32 devices in a mesh: dp: 4 (over x, core), row: 2 (over y), col: 4 (over z).
Axes of the slice: x: 2, y: 2, z: 4, core: 2. Of those that a mesh axis runs over, the one named last changes fastest.
Arguments:
- inputs: bfloat16 [8192, 1536], P(('dp', 'col'), 'row'), may hold values from -6 to 6
- norm_gain: float32 [1536], P('row'), may hold values from 0.25 to 1.75
- query_weight: bfloat16 [1536, 1536], P('row', 'col'), may hold values from -0.15625 to 0.15625
- key_value_matrix: bfloat16 [1536, 512], P('row', 'col'), may hold values from -0.15625 to 0.15625
- output_weight: bfloat16 [1536, 1536], P('col', 'row'), may hold values from -0.625 to 0.625
- mixer_gain: float32 [1536], P('row'), may hold values from 0.25 to 1.75
- gate_weight: bfloat16 [8, 1536, 768], P(None, 'row', 'col'), may hold values from -0.15625 to 0.15625
- up_weight: bfloat16 [8, 1536, 768], P(None, 'row', 'col'), may hold values from -0.15625 to 0.15625
- down_weight: bfloat16 [8, 768, 1536], P(None, 'col', 'row'), may hold values from -0.4375 to 0.4375
- lengths: int32 [8, 4], P(('dp', 'row')), may hold values from 1 to 512, 1024 in all within a row
- routes: int32 [8192, 4], P('dp'), may hold values from 0 to 7, all different within a row; in each aligned block of 2048 rows (0 to 2047, 2048 to 4095, ...) at most 1536 rows name the same one
- route_gates: float32 [8192, 4], P('dp'), may hold values from 0.1 to 1
- cotangent: bfloat16 [8192, 1536], P(('dp', 'col'), 'row'), may hold values from -6 to 6
Outputs:
- outputs: bfloat16 [8192, 1536], P(('dp', 'col'), 'row')
- input_grad: bfloat16 [8192, 1536], P(('dp', 'col'), 'row')
- norm_gain_grad: float32 [1536], P('row')
- query_weight_grad: float32 [1536, 1536], P('row', 'col')
- key_value_weight_grad: float32 [1536, 512], P('row', 'col')
- output_weight_grad: float32 [1536, 1536], P('col', 'row')
- mixer_gain_grad: float32 [1536], P('row')
- gate_weight_grad: float32 [8, 1536, 768], P(None, 'row', 'col')
- up_weight_grad: float32 [8, 1536, 768], P(None, 'row', 'col')
- down_weight_grad: float32 [8, 768, 1536], P(None, 'col', 'row')
The draws below stay inside these ranges and needn't reach their ends.
Inputs may be any that keep to these rules, and one draw needn't show every extreme that they name: Each row holds the lengths of the 4 sequences of one block in order; they sum to 1024 and the longest is exactly 512. `routes`: A token's 4 experts differ. Within the rows of one data index (aligned blocks of 2048 rows) no expert is named more than 1536 times, a bound that some block reaches.
All inputs are finite; a program needn't handle non-finite values.
Results may differ from the reference program's by a relative error of at most 0.025.
Values may be sent and summed in bfloat16 or wider, within the bound.
A program may use at most 320 MiB of HBM per device.

```python
import math
import jax
import jax.numpy as jnp
import numpy as np
from jax import lax

MODEL_DIM = 1536
QUERY_HEADS = 12
KEY_VALUE_HEADS = 2
HEAD_SIZE = 128
FE = 768
TOP = 4
EXPERTS = 8
GROUP = 2048
HALF = 1024
TOKENS = 8192
LONGEST = 512
SEQS = 4
CAP = 1536
N_DP = 4
N_ROW = 2


def steps_of(own_key, shape, shards, smallest, largest):
    factor_of = 1.0
    for axis_at, shards_of in shards:
        draws = jax.random.uniform(jax.random.fold_in(jax.random.fold_in(own_key, 6), axis_at), (shards_of,), jnp.float32, smallest / len(shards), largest / len(shards))
        factor_of = factor_of * jnp.repeat(jnp.exp(draws), shape[axis_at] // shards_of).reshape((-1,) + (1,) * (len(shape) - 1 - axis_at))
    return factor_of


def length_profile(count, total, limit, skew):
    portions = [(1 << 20) // math.isqrt(standing ** skew) + 1 for standing in range(2, count + 1)]
    surplus, counts = total - limit - (count - 1), [1] * (count - 1)
    while surplus > 0:
        free = [i for i in range(count - 1) if counts[i] < limit]
        pool, budget = sum([portions[i] for i in free]), surplus
        for i in free:
            addition = min(limit - counts[i], max(1, budget * portions[i] // pool), surplus)
            counts[i] = counts[i] + addition
            surplus = surplus - addition
    return np.array([limit] + counts)


def ragged_sizes(key, number_of, total, reach, skew):
    if number_of == 2:
        one = jax.random.randint(key, (), max(1, total - reach), min(reach, total - 1) + 1)
        return jnp.stack([one, total - one])
    sizes = jnp.asarray(length_profile(number_of, total, reach, skew), jnp.int32)
    couples = (number_of - 1) // 2
    giver, taker = sizes[1:1 + 2 * couples:2], sizes[2:2 + 2 * couples:2]
    room = jnp.minimum(giver - 1, reach - taker)
    moved = jax.random.randint(jax.random.fold_in(key, 1), (couples,), 0, 1 << 20) % (room + 1)
    sizes = sizes.at[1:1 + 2 * couples:2].set(giver - moved).at[2:2 + 2 * couples:2].set(taker + moved)
    return sizes[jax.random.permutation(jax.random.fold_in(key, 2), number_of)]


def shared_out(own_key, own, number, rows, count, top, limit, lean):
    ranking = jax.random.permutation(own_key, count)
    packed, usual = portions_of(count, rows * top, limit, lean, True), portions_of(count, rows * top, limit, lean, False)
    places = jnp.arange(count)

    def named(sizes, offset_by):
        used = int((sizes > 0).sum())
        fixed = max(1, used // 4)
        shifted = fixed + (places - fixed + offset_by * (used - fixed)) % max(1, count - fixed)
        return jnp.zeros((count,), jnp.int32).at[ranking[jnp.where(places < fixed, places, shifted)]].set(jnp.asarray(sizes, jnp.int32))

    sizes = jnp.where(number % 4 == 0, named(packed, number // 4), named(usual, number - number // 4 - 1))
    mixed = jax.random.permutation(jax.random.fold_in(own, 3), count)
    giver, sink = mixed[0:count // 2 * 2:2], mixed[1:count // 2 * 2:2]
    slack = jnp.minimum(sizes[giver] - 1, limit - sizes[sink]) // 2
    slack = jnp.where((giver == ranking[0]) | (sink == ranking[0]) | (sizes[sink] == 0), 0, jnp.maximum(slack, 0))
    shifted = jax.random.randint(jax.random.fold_in(own, 4), (count // 2,), 0, 1 << 20) % (slack + 1)
    sizes = sizes.at[giver].add(-shifted).at[sink].add(shifted)
    items = jnp.searchsorted(jnp.cumsum(sizes), jnp.arange(rows * top), side="right").astype(jnp.int32)
    listing = items.reshape(top, rows).T
    listing = listing[jax.random.permutation(jax.random.fold_in(own, 1), rows)]
    offset_by = jax.random.randint(jax.random.fold_in(own, 2), (rows, 1), 0, top)
    return jnp.take_along_axis(listing, (jnp.arange(top)[None, :] + offset_by) % top, axis=1)


def portions_of(count, total, reach, lean, full):
    portions = [(1 << 20) // math.isqrt(rank ** lean) + 1 for rank in range(1, count + 1)]
    largest = reach if full else min(reach, max(-(-total // count), total * portions[0] // sum(portions)))
    least = 1 if total - largest >= count - 1 else 0
    holding, surplus = [largest] + [least] * (count - 1), total - largest - least * (count - 1)
    while surplus > 0:
        candidates = [i for i in range(1, count) if holding[i] < largest] or [i for i in range(1, count) if holding[i] < reach]
        pool, left = sum([portions[i] for i in candidates]), surplus
        for i in candidates:
            more = min(reach - holding[i], max(1, left * portions[i] // pool), surplus)
            holding[i] = holding[i] + more
            surplus = surplus - more
    return np.array(holding)


def centred(own_key, dims, width, most, split=(), kind=jnp.bfloat16):
    values = jax.random.normal(own_key, dims, jnp.float32) * width
    if len(split) > 0:
        values = steps_of(own_key, dims, split, -0.22, 0.18) * values
    return jnp.clip(values, min=-most, max=most).astype(kind)


def setup_inputs(seed: int = 0) -> dict:
    key_list = jax.random.split(jax.random.key(seed), 14)
    inputs = centred(key_list[0], (TOKENS, MODEL_DIM), 1.0, 6.0, ((0, 16), (1, 2)))
    norm_gain = jnp.clip(1.0 + 0.15 * jax.random.normal(key_list[1], (MODEL_DIM,), jnp.float32), 0.25, 1.75)
    query_weight = centred(key_list[2], (MODEL_DIM, QUERY_HEADS * HEAD_SIZE), MODEL_DIM ** -0.5, 0.15625, ((0, 2), (1, 4)))
    key_value_matrix = centred(key_list[3], (MODEL_DIM, 2 * KEY_VALUE_HEADS * HEAD_SIZE), MODEL_DIM ** -0.5, 0.15625, ((0, 2), (1, 4)))
    output_weight = centred(key_list[4], (QUERY_HEADS * HEAD_SIZE, MODEL_DIM), (QUERY_HEADS * HEAD_SIZE // 16) ** -0.5, 0.625, ((0, 4), (1, 2)))
    mixer_gain = jnp.clip(1.0 + 0.15 * jax.random.normal(key_list[5], (MODEL_DIM,), jnp.float32), 0.25, 1.75)
    gate_weight = centred(key_list[6], (EXPERTS, MODEL_DIM, FE), MODEL_DIM ** -0.5, 0.15625, ((1, 2), (2, 4)))
    up_weight = centred(key_list[7], (EXPERTS, MODEL_DIM, FE), MODEL_DIM ** -0.5, 0.15625, ((1, 2), (2, 4)))
    down_weight = centred(key_list[8], (EXPERTS, FE, MODEL_DIM), (FE // 4) ** -0.5, 0.4375, ((1, 4), (2, 2)))
    lengths = jax.vmap(lambda own: ragged_sizes(own, SEQS, HALF, LONGEST, 2))(jax.random.split(key_list[9], (N_DP * N_ROW))).reshape((N_DP * N_ROW, SEQS)).astype(jnp.int32)
    routes_keys = jax.random.split(jax.random.fold_in(key_list[10], 1), TOKENS // GROUP)
    routes_turns = jax.random.permutation(jax.random.fold_in(key_list[10], 3), TOKENS // GROUP)
    routes = jax.vmap(lambda own, number: shared_out(jax.random.fold_in(key_list[10], 2), own, number, GROUP, EXPERTS, TOP, CAP, 1))(routes_keys, routes_turns).reshape((TOKENS, TOP))
    route_gates = jnp.clip(0.1 + 0.9 * jax.random.uniform(key_list[11], (TOKENS, TOP), jnp.float32) ** steps_of(key_list[11], (TOKENS, TOP), ((0, 4),), -0.2, 0.2), 0.1, 1.0)
    cotangent = centred(key_list[12], (TOKENS, MODEL_DIM), 1.0, 6.0, ((0, 16), (1, 2)))
    return dict(inputs=inputs, norm_gain=norm_gain, query_weight=query_weight, key_value_matrix=key_value_matrix, output_weight=output_weight, mixer_gain=mixer_gain, gate_weight=gate_weight, up_weight=up_weight, down_weight=down_weight, lengths=lengths, routes=routes, route_gates=route_gates, cotangent=cotangent)


epsilon = 1e-06
rope_base = 1000000.0
highest = lax.Precision.HIGHEST

@jax.custom_vjp
def low(v):
    return lax.optimization_barrier(v.astype(jnp.bfloat16)).astype(jnp.float32)

@jax.custom_vjp
def low_back(v):
    return v

def low_keep(v):
    return (low(v), None)

def low_pass(kept, grad):
    return (grad,)

def back_keep(v):
    return (v, None)

def back_low(kept, grad):
    return (low(grad),)
low.defvjp(low_keep, low_pass)
low_back.defvjp(back_keep, back_low)

def rms_scale(matrix):
    return lax.rsqrt(lax.optimization_barrier(jnp.mean(matrix * matrix, axis=-1, keepdims=True)) + epsilon)

def frequencies():
    return rope_base ** (-jnp.arange(0, HEAD_SIZE, 2, dtype=jnp.float32) / HEAD_SIZE)

def rotate(matrix, cosine, sine_rows):
    half_dim = matrix.shape[-1] // 2
    first_half = matrix[..., :half_dim]
    second = matrix[..., half_dim:]
    return jnp.concatenate([first_half * cosine - second * sine_rows, second * cosine + first_half * sine_rows], axis=-1)

def positions(lengths_row, per_half_columns):
    seq_ends = jnp.cumsum(lengths_row).astype(jnp.int32)
    token_index = jnp.arange(per_half_columns, dtype=jnp.int32)
    segment = lax.optimization_barrier(jnp.sum((token_index[:, None] >= seq_ends[None, :]).astype(jnp.int32), axis=1))
    starts = seq_ends - lengths_row
    picked = segment[:, None] == jnp.arange(lengths_row.shape[0], dtype=jnp.int32)[None, :]
    seq_begin = lax.optimization_barrier(jnp.sum(jnp.where(picked, starts[None, :], 0), axis=1)).astype(jnp.int32)
    return (segment, token_index - seq_begin)

def attend_half(member):
    query_half, key_value_halves, lengths_row = member
    per_half_columns = query_half.shape[0]
    segment, position = positions(lengths_row, per_half_columns)
    angles = position.astype(jnp.float32)[:, None] * frequencies()[None, :]
    cosine = jnp.cos(angles)[:, None, :]
    sine_rows = jnp.sin(angles)[:, None, :]
    query_rot = low(rotate(low_back(query_half.reshape(per_half_columns, QUERY_HEADS, HEAD_SIZE)), cosine, sine_rows))
    key_value_pairs = key_value_halves.reshape(per_half_columns, KEY_VALUE_HEADS, 2, HEAD_SIZE)
    key_rot = low(rotate(low_back(key_value_pairs[:, :, 0]), cosine, sine_rows))
    value_rows = low(low_back(key_value_pairs[:, :, 1]))
    grouped_heads = QUERY_HEADS // KEY_VALUE_HEADS
    key_all = jnp.repeat(key_rot, grouped_heads, axis=1)
    value_all = jnp.repeat(value_rows, grouped_heads, axis=1)
    raw_scores = low_back(jnp.einsum('qhd,khd->hqk', query_rot, key_all, precision=highest))
    allowed = (segment[:, None] == segment[None, :]) & (position[None, :] <= position[:, None])
    scores = jnp.where(allowed[None], raw_scores * HEAD_SIZE ** (-0.5), -1e+30)
    probs = jax.nn.softmax(scores, axis=-1)
    mixed_rows = jnp.einsum('hqk,khd->qhd', low(probs), value_all, precision=highest)
    return mixed_rows.reshape(per_half_columns, QUERY_HEADS * HEAD_SIZE)

def layer(inputs, norm_gain, query_weight, key_value_matrix, output_weight, mixer_gain, gate_weight, up_weight, down_weight, lengths, routes, route_gates):
    normed = low(inputs * rms_scale(inputs) * norm_gain)
    queries = jnp.dot(normed, query_weight, precision=highest)
    keyvals = jnp.dot(normed, key_value_matrix, precision=highest)
    halves = lengths.shape[0]
    per_half_columns = queries.shape[0] // halves
    attention = lax.map(jax.checkpoint(attend_half), (queries.reshape(halves, per_half_columns, -1), keyvals.reshape(halves, per_half_columns, -1), lengths))
    attended = low(low_back(attention.reshape(queries.shape[0], QUERY_HEADS * HEAD_SIZE)))
    branch = low_back(jnp.dot(attended, output_weight, precision=highest))
    middle = inputs + branch
    expert_in = low(middle * rms_scale(middle) * mixer_gain)
    chosen = routes[:, :, None] == jnp.arange(EXPERTS, dtype=jnp.int32)[None, None, :]
    gate_table = lax.optimization_barrier(jnp.sum(jnp.where(chosen, route_gates[:, :, None], 0.0), axis=1))

    def expert_step(running, member):
        gate_block, up_block, down_block, column = member
        gate_rows = low_back(jnp.dot(expert_in, gate_block, precision=highest))
        up_rows = low_back(jnp.dot(expert_in, up_block, precision=highest))
        hidden = low(jax.nn.silu(gate_rows) * up_rows)
        result = low_back(jnp.dot(hidden, down_block, precision=highest))
        return (running + column[:, None] * result, None)
    experts_out, unused = lax.scan(jax.checkpoint(expert_step), jnp.zeros_like(middle), (gate_weight, up_weight, down_weight, gate_table.T))
    return middle + experts_out

def reference(inputs, norm_gain, query_weight, key_value_matrix, output_weight, mixer_gain, gate_weight, up_weight, down_weight, lengths, routes, route_gates, cotangent):
    floats = tuple((matrix.astype(jnp.float32) for matrix in (inputs, norm_gain, query_weight, key_value_matrix, output_weight, mixer_gain, gate_weight, up_weight, down_weight)))

    def wrapped(inputs_f, norm_f, query_f, keyval_f, output_f, mixer_f, gate_f, up_f, down_f):
        return layer(inputs_f, norm_f, query_f, keyval_f, output_f, mixer_f, gate_f, up_f, down_f, lengths, routes, route_gates.astype(jnp.float32))
    outputs, pullback = jax.vjp(wrapped, *floats)
    grads = pullback(cotangent.astype(jnp.float32))
    return (outputs.astype(jnp.bfloat16), grads[0].astype(jnp.bfloat16), grads[1], grads[2], grads[3], grads[4], grads[5], grads[6], grads[7], grads[8])
```

```python
import functools

import jax
import jax.numpy as jnp
from jax import lax
from jax.experimental import pallas as pl
from jax.experimental.pallas import tpu as pltpu
from jax.sharding import PartitionSpec as P

epsilon = 1e-06
rope_base = 1000000.0
head_dim = 128
low = jnp.bfloat16
full = jnp.float32


def swap(block, axis, bit):
    count = lax.axis_size(axis)
    return lax.ppermute(block, axis, [(i, i ^ bit) for i in range(count)])


def pair(bit, own, other, axis):
    first = jnp.where(bit == 0, own, other)
    second = jnp.where(bit == 0, other, own)
    return jnp.concatenate([first, second], axis=axis)


def dot(left, right, left_dim=1, right_dim=0):
    return lax.dot_general(
        left, right, (((left_dim,), (right_dim,)), ((), ())), preferred_element_type=full
    )


def gather_col(block, col):
    count = lax.axis_size("col")
    from_left, from_right = [block], [block]
    for step in range(1, count):
        from_left.append(
            lax.ppermute(from_left[-1], "col", [(i, i + 1) for i in range(step - 1, count - 1)])
        )
        from_right.append(
            lax.ppermute(from_right[-1], "col", [(i + 1, i) for i in range(count - step)])
        )
    slots = [block]
    for k in range(1, count):
        chosen = None
        for at in range(count):
            there = at ^ k
            value = from_right[there - at] if there > at else from_left[at - there]
            chosen = value if chosen is None else jnp.where(col == at, value, chosen)
        slots.append(chosen)
    return slots


def scatter_col(stack, col):
    count = lax.axis_size("col")

    def term(block):
        return lax.dynamic_index_in_dim(stack, col ^ jnp.clip(block, 0, count - 1), 0, False)

    right, left = None, None
    for step in range(1, count):
        to_right = term(col + count - step)
        to_left = term(col - count + step)
        if right is not None:
            to_right = (to_right.astype(full) + right.astype(full)).astype(low)
            to_left = (to_left.astype(full) + left.astype(full)).astype(low)
        right = lax.ppermute(to_right, "col", [(i, i + 1) for i in range(min(step, count - 1))])
        left = lax.ppermute(
            to_left, "col", [(i, i - 1) for i in range(count - 1, count - 1 - step, -1)]
        )
    return stack[0].astype(full) + right.astype(full) + left.astype(full)


def halves_sum(parts, core, axis):
    size = parts.shape[axis] // 2
    mine = lax.dynamic_slice_in_dim(parts, core * size, size, axis)
    theirs = lax.dynamic_slice_in_dim(parts, (1 - core) * size, size, axis)
    return (mine.astype(full) + swap(theirs, "dp", 1).astype(full)).astype(low)


def others_sum(block):
    bit = 2
    while bit < lax.axis_size("dp"):
        block = (block.astype(full) + swap(block, "dp", bit).astype(full)).astype(low)
        bit *= 2
    return block


def quarter_of(block, quarter):
    size = block.shape[0] // 4
    return lax.dynamic_slice_in_dim(block, quarter * size, size, 0)


def quarters_all(block, core, side):
    across = swap(block, "dp", 2)
    two = [jnp.where(side == 0, block, across), jnp.where(side == 0, across, block)]
    both = jnp.stack(two)
    near = swap(both, "dp", 1)
    result = []
    for at in range(2):
        result.append(jnp.where(core == 0, both[at], near[at]))
        result.append(jnp.where(core == 0, near[at], both[at]))
    return result


def attention_forward_kernel(
    pre_ref, cosine_ref, sine_ref, key_ref, value_ref, start_ref, out_ref, rot_ref, *, window, tile
):
    rows = pre_ref.shape[0]
    pre = pre_ref[...]
    rot = (pre * cosine_ref[...] + pltpu.roll(pre, head_dim // 2, 1) * sine_ref[...]).astype(low)
    rot_ref[...] = rot
    for at in range(rows // tile):
        first = at * tile
        keys = key_ref[first : first + window, :]
        values = value_ref[first : first + window, :]
        scores = dot(rot[first : first + tile], keys, 1, 1) * head_dim ** (-0.5)
        place = lax.broadcasted_iota(jnp.int32, scores.shape, 1) + first
        query = lax.broadcasted_iota(jnp.int32, scores.shape, 0) + (first + rows)
        allowed = (place <= query) & (place >= start_ref[first : first + tile, :])
        scores = jnp.where(allowed, scores, -1e30)
        exponent = jnp.exp(scores - jnp.max(scores, axis=1, keepdims=True))
        weights = exponent / jnp.sum(exponent, axis=1, keepdims=True)
        out_ref[first : first + tile, :] = dot(weights.astype(low), values).astype(low)


def attention_backward_kernel(
    rot_ref,
    cosine_ref,
    sine_ref,
    key_ref,
    value_ref,
    start_ref,
    grad_ref,
    query_grad_ref,
    key_grad_ref,
    value_grad_ref,
    *,
    window,
    tile,
):
    rows = rot_ref.shape[0]

    @pl.when(pl.program_id(0) == 0)
    def _():
        key_grad_ref[...] = jnp.zeros_like(key_grad_ref)
        value_grad_ref[...] = jnp.zeros_like(value_grad_ref)

    for at in range(rows // tile):
        first = at * tile
        rot = rot_ref[first : first + tile, :]
        grad = grad_ref[first : first + tile, :]
        keys = key_ref[first : first + window, :]
        values = value_ref[first : first + window, :]
        scores = dot(rot, keys, 1, 1) * head_dim ** (-0.5)
        place = lax.broadcasted_iota(jnp.int32, scores.shape, 1) + first
        query = lax.broadcasted_iota(jnp.int32, scores.shape, 0) + (first + rows)
        allowed = (place <= query) & (place >= start_ref[first : first + tile, :])
        scores = jnp.where(allowed, scores, -1e30)
        exponent = jnp.exp(scores - jnp.max(scores, axis=1, keepdims=True))
        probs = exponent / jnp.sum(exponent, axis=1, keepdims=True)
        prob_grad = dot(grad, values, 1, 1)
        inner = jnp.sum(probs * prob_grad, axis=1, keepdims=True)
        score_grad = (probs * (prob_grad - inner) * head_dim ** (-0.5)).astype(low)
        rot_grad = dot(score_grad, keys)
        cosine = cosine_ref[first : first + tile, :]
        sine = sine_ref[first : first + tile, :]
        query_grad_ref[first : first + tile, :] = (
            rot_grad * cosine - pltpu.roll(rot_grad, head_dim // 2, 1) * sine
        ).astype(low)
        key_grad_ref[first : first + window, :] += dot(score_grad, rot, 0, 0)
        value_grad_ref[first : first + window, :] += dot(probs.astype(low), grad, 0, 0)


def attention_forward(pre, cosine, sine, keys, values, start, heads):
    rows, reach = pre.shape[0], keys.shape[0]
    whole = lambda shape: pl.BlockSpec(shape, lambda h: (0, 0))
    head = pl.BlockSpec((rows, head_dim), lambda h: (0, h))
    shape = jax.ShapeDtypeStruct((rows, heads * head_dim), low)
    per_half = heads // 2
    return pl.pallas_call(
        functools.partial(attention_forward_kernel, window=reach - rows // 2, tile=rows // 2),
        grid=(heads,),
        in_specs=[
            pl.BlockSpec((rows, head_dim), lambda h: (0, h + h // per_half)),
            whole((rows, head_dim)),
            whole((rows, head_dim)),
            whole((reach, head_dim)),
            whole((reach, head_dim)),
            whole((rows, 1)),
        ],
        out_specs=[head, head],
        out_shape=[shape, shape],
        compiler_params=pltpu.CompilerParams(vmem_limit_bytes=32 * 2**20),
        cost_estimate=pl.CostEstimate(
            flops=heads * rows * reach * 3 * head_dim,
            bytes_accessed=heads * rows * head_dim * 8,
            transcendentals=heads * rows * reach,
        ),
    )(pre, cosine, sine, keys, values, start)


def attention_backward(rot, cosine, sine, keys, values, start, grad, heads):
    rows, reach = rot.shape[0], keys.shape[0]
    whole = lambda shape: pl.BlockSpec(shape, lambda h: (0, 0))
    head = pl.BlockSpec((rows, head_dim), lambda h: (0, h))
    return pl.pallas_call(
        functools.partial(attention_backward_kernel, window=reach - rows // 2, tile=rows // 2),
        grid=(heads,),
        in_specs=[
            head,
            whole((rows, head_dim)),
            whole((rows, head_dim)),
            whole((reach, head_dim)),
            whole((reach, head_dim)),
            whole((rows, 1)),
            head,
        ],
        out_specs=[head, whole((reach, head_dim)), whole((reach, head_dim))],
        out_shape=[
            jax.ShapeDtypeStruct((rows, heads * head_dim), low),
            jax.ShapeDtypeStruct((reach, head_dim), full),
            jax.ShapeDtypeStruct((reach, head_dim), full),
        ],
        compiler_params=pltpu.CompilerParams(vmem_limit_bytes=32 * 2**20),
        cost_estimate=pl.CostEstimate(
            flops=heads * rows * reach * 8 * head_dim,
            bytes_accessed=heads * rows * head_dim * 8,
            transcendentals=heads * rows * reach,
        ),
    )(rot, cosine, sine, keys, values, start, grad)


def rotate(matrix, cosine, sine):
    return matrix * cosine + jnp.roll(matrix, head_dim // 2, axis=1) * sine


def shards(
    inputs,
    norm_gain,
    query_weight,
    key_value_matrix,
    output_weight,
    mixer_gain,
    gate_weight,
    up_weight,
    down_weight,
    lengths,
    routes,
    route_gates,
    cotangent,
):
    row, col, dp = lax.axis_index("row"), lax.axis_index("col"), lax.axis_index("dp")
    core, side, quarter = dp % 2, (dp // 2) % 2, dp % 4
    cols = lax.axis_size("col")
    tokens, part_width = inputs.shape
    width = 2 * part_width
    own_tokens = tokens // 2
    experts, _, units = gate_weight.shape
    hidden_width = experts * units
    query_block, keyval_block = query_weight.shape[1], key_value_matrix.shape[1]
    heads = 2 * query_block // head_dim

    inputs_all = pair(row, inputs, swap(inputs, "row", 1), 1)
    gains = jnp.stack([norm_gain, mixer_gain])
    gains = pair(row, gains, swap(gains, "row", 1), 1)
    norm_all, mixer_all = gains[0], gains[1]
    lengths_all = pair(row, lengths, swap(lengths, "row", 1), 0)
    lengths_row = jnp.where(col < cols // 2, lengths_all[0], lengths_all[1])

    blocks = 2 * cols
    joint = jnp.concatenate([query_weight, key_value_matrix], axis=1)
    joint_part = quarter_of(joint, quarter)
    output_part = quarter_of(output_weight, quarter)

    def spread(part):
        arrived = []
        for k in range(cols):
            route = []
            for index in range(blocks):
                from_row, from_col = index // cols, index % cols
                to_row, to_col = from_col // 2, (2 * from_row + from_col % 2) ^ k
                route.append((index, to_row * cols + to_col))
            arrived.append(lax.ppermute(part, ("row", "col"), route))
        for bit in (1, 2):
            arrived = [
                jnp.where(col & bit == 0, arrived[k], arrived[k ^ bit]) for k in range(cols)
            ]
        return jnp.stack(arrived)

    joint_quarters = quarters_all(spread(joint_part), core, side)
    output_quarters = quarters_all(spread(output_part), core, side)
    joint_weight = jnp.concatenate(
        [
            jnp.concatenate(
                [piece[2 * r + b] for r in range(2) for piece in joint_quarters], axis=0
            )
            for b in range(2)
        ],
        axis=1,
    )
    head_output = jnp.concatenate(
        [
            jnp.concatenate(
                [piece[2 * r + b] for b in range(2) for piece in output_quarters], axis=0
            )
            for r in range(2)
        ],
        axis=1,
    )

    def flat_units(weight):
        return weight.transpose(1, 0, 2).reshape(part_width, hidden_width)

    gate_flat, up_flat = flat_units(gate_weight), flat_units(up_weight)
    down_flat = down_weight.reshape(hidden_width, part_width)

    def partner_of(flat):
        part = swap(quarter_of(flat, quarter), "row", 1)
        return jnp.concatenate(quarters_all(part, core, side), axis=0)

    gate_all = pair(row, gate_flat, partner_of(gate_flat), 0)
    up_all = pair(row, up_flat, partner_of(up_flat), 0)
    down_all = pair(row, down_flat, partner_of(down_flat), 1)

    kept = lax.dynamic_slice_in_dim(cotangent, row * own_tokens, own_tokens, 0)
    sent = lax.dynamic_slice_in_dim(cotangent, (1 - row) * own_tokens, own_tokens, 0)
    cot_own = pair(row, kept, swap(sent, "row", 1), 1)
    cot_all = jnp.concatenate(gather_col(cot_own, col), axis=0)

    chosen = routes[:, :, None] == jnp.arange(experts, dtype=jnp.int32)[None, None, :]
    table = jnp.sum(jnp.where(chosen, route_gates[:, :, None], 0.0), axis=1)
    slot_tables = [
        lax.dynamic_slice_in_dim(table, (col ^ k) * tokens + row * own_tokens, own_tokens, 0)
        for k in range(cols)
    ]
    widen = jnp.repeat(jnp.eye(experts, dtype=full), units, axis=1)
    gates = jnp.dot(
        jnp.concatenate(slot_tables, axis=0), widen, precision=lax.Precision.HIGHEST
    )

    inputs_full = inputs_all.astype(full)
    first_scale = lax.rsqrt(jnp.mean(inputs_full * inputs_full, axis=1, keepdims=True) + epsilon)
    normed = (inputs_full * first_scale * norm_all[None, :]).astype(low)
    projected = dot(normed, joint_weight)
    ends = jnp.cumsum(lengths_row)
    starts = ends - lengths_row
    odd = col % 2
    place = odd * tokens + jnp.arange(tokens, dtype=jnp.int32)
    begin = jnp.max(jnp.where(starts[None, :] <= place[:, None], starts[None, :], 0), axis=1)
    position = place - begin
    start = (begin + (1 - odd) * tokens)[:, None]
    theta = rope_base ** (-jnp.arange(0, head_dim, 2, dtype=full) / head_dim)
    angles = position.astype(full)[:, None] * theta[None, :]
    cosine, sine = jnp.cos(angles), jnp.sin(angles)
    cosine = jnp.concatenate([cosine, cosine], axis=1)
    sine = jnp.concatenate([-sine, sine], axis=1)
    key_at = query_block
    value_at = 2 * query_block + keyval_block
    key_own = rotate(projected[:, key_at : key_at + head_dim], cosine, sine).astype(low)
    value_own = projected[:, value_at : value_at + head_dim].astype(low)
    own_pair = jnp.concatenate([key_own, value_own], axis=1)
    before = lax.ppermute(own_pair, "col", [(i, i + 1) for i in range(0, cols, 2)])
    pairs = jnp.concatenate([before, own_pair], axis=0)
    keys, values = pairs[:, :head_dim], pairs[:, head_dim:]
    attended, rot = attention_forward(projected, cosine, sine, keys, values, start, heads)

    branch_part = dot(attended, head_output).astype(low)
    kept = lax.dynamic_slice_in_dim(branch_part, row * own_tokens, own_tokens, 0)
    sent = lax.dynamic_slice_in_dim(branch_part, (1 - row) * own_tokens, own_tokens, 0)
    branch = kept.astype(full) + swap(sent, "row", 1).astype(full)
    inputs_own = lax.dynamic_slice_in_dim(inputs_all, row * own_tokens, own_tokens, 0)
    middle = inputs_own.astype(full) + branch
    second_scale = lax.rsqrt(jnp.mean(middle * middle, axis=1, keepdims=True) + epsilon)
    expert_own = (middle * second_scale * mixer_all[None, :]).astype(low)
    expert_in = jnp.concatenate(gather_col(expert_own, col), axis=0)

    gate = dot(expert_in, gate_all)
    up = dot(expert_in, up_all)
    hidden_grad = dot(cot_all, down_all, 1, 1) * gates
    sigmoid = jax.nn.sigmoid(gate)
    silu = gate * sigmoid
    hidden = (silu * up * gates).astype(low)
    gate_grad = (hidden_grad * up * (sigmoid * (1.0 + gate * (1.0 - sigmoid)))).astype(low)
    up_grad = (hidden_grad * silu).astype(low)
    in_part = (dot(gate_grad, gate_all, 1, 1) + dot(up_grad, up_all, 1, 1)).astype(low)
    second_grad = scatter_col(in_part.reshape(cols, own_tokens, width), col)
    out_part = dot(hidden, down_all).astype(low)
    experts_out = scatter_col(out_part.reshape(cols, own_tokens, width), col)
    outputs_own = (middle + experts_out).astype(low)
    theirs = lax.dynamic_slice_in_dim(outputs_own, (1 - row) * part_width, part_width, 1)
    mine = lax.dynamic_slice_in_dim(outputs_own, row * part_width, part_width, 1)
    outputs = pair(row, mine, swap(theirs, "row", 1), 0)

    gate_part = dot(expert_in, gate_grad, 0, 0).astype(low)
    up_part = dot(expert_in, up_grad, 0, 0).astype(low)
    down_part = dot(hidden, cot_all, 0, 0).astype(low)

    def expert_total(part, hidden_axis):
        half = halves_sum(part, core, hidden_axis)
        axis = 1 - hidden_axis
        mine = lax.dynamic_slice_in_dim(half, row * part_width, part_width, axis)
        theirs = lax.dynamic_slice_in_dim(half, (1 - row) * part_width, part_width, axis)
        block = (mine.astype(full) + swap(theirs, "row", 1).astype(full)).astype(low)
        block = others_sum(block)
        return pair(core, block, swap(block, "dp", 1), hidden_axis).astype(full)

    def by_expert(flat):
        return flat.reshape(part_width, experts, units).transpose(1, 0, 2)

    gate_total = by_expert(expert_total(gate_part, 1))
    up_total = by_expert(expert_total(up_part, 1))
    down_total = expert_total(down_part, 0).reshape(experts, units, part_width)

    weighted = mixer_all[None, :] * second_grad
    inner = jnp.sum(weighted * middle, axis=1, keepdims=True)
    cube = second_scale * second_scale * second_scale
    middle_grad = cot_own.astype(full) + second_scale * weighted - middle * cube * inner / width
    mixer_partial = jnp.sum(second_grad * middle * second_scale, axis=0)
    branch_own = middle_grad.astype(low)
    branch_grad = pair(row, branch_own, swap(branch_own, "row", 1), 0)

    attended_grad = dot(branch_grad, head_output, 1, 1).astype(low)
    output_part_grad = dot(attended, branch_grad, 0, 0).astype(low)
    query_grad, key_grad, value_grad = attention_backward(
        rot, cosine, sine, keys, values, start, attended_grad, heads
    )
    pair_grad = jnp.concatenate([key_grad, value_grad], axis=1)
    returned = lax.ppermute(
        pair_grad[:tokens].astype(low), "col", [(i + 1, i) for i in range(0, cols, 2)]
    )
    pair_grad = pair_grad[tokens:] + returned.astype(full)
    key_pre = rotate(pair_grad[:, :head_dim], cosine, -sine).astype(low)
    value_pre = pair_grad[:, head_dim:].astype(low)
    joint_grad = jnp.concatenate(
        [query_grad[:, :query_block], key_pre, query_grad[:, query_block:], value_pre], axis=1
    )
    normed_part = dot(joint_grad, joint_weight, 1, 1).astype(low)
    mine = lax.dynamic_slice_in_dim(normed_part, row * part_width, part_width, 1)
    theirs = lax.dynamic_slice_in_dim(normed_part, (1 - row) * part_width, part_width, 1)
    normed_grad = mine.astype(full) + swap(theirs, "row", 1).astype(full)
    weighted = norm_gain[None, :] * normed_grad
    inputs_part = inputs.astype(full)
    inner = jnp.sum(weighted * inputs_part, axis=1)
    inner = (inner + swap(inner, "row", 1))[:, None]
    cube = first_scale * first_scale * first_scale
    middle_part = lax.dynamic_slice_in_dim(branch_grad, row * part_width, part_width, 1)
    input_grad = (
        middle_part.astype(full) + first_scale * weighted - inputs_part * cube * inner / width
    ).astype(low)
    norm_partial = jnp.sum(normed_grad * inputs_part * first_scale, axis=0)

    joint_weight_grad = dot(normed, joint_grad, 0, 0).astype(low)

    def block_total(part, block_axis):
        half = halves_sum(part, core, 2 + block_axis)
        mine = lax.dynamic_index_in_dim(half, row, 0, False)
        theirs = swap(lax.dynamic_index_in_dim(half, 1 - row, 0, False), "row", 1)
        by_col = pair(row, mine, theirs, 0)
        stack = jnp.stack(
            [lax.dynamic_index_in_dim(by_col, col ^ k, 0, False) for k in range(cols)]
        )
        block = others_sum(scatter_col(stack, col).astype(low))
        return pair(core, block, swap(block, "dp", 1), block_axis).astype(full)

    both = query_block + keyval_block
    joint_total = block_total(
        joint_weight_grad.reshape(2, part_width, 2, both).transpose(0, 2, 1, 3), 0
    )
    output_total = block_total(
        output_part_grad.reshape(2, query_block, 2, part_width).transpose(2, 0, 1, 3), 0
    )
    query_total, keyval_total = joint_total[:, :query_block], joint_total[:, query_block:]

    norm_total = lax.psum(norm_partial, ("dp", "col"))
    mixer_sum = lax.psum(mixer_partial, ("dp", "row", "col"))
    mixer_total = lax.dynamic_slice_in_dim(mixer_sum, row * part_width, part_width, 0)
    return (
        outputs,
        input_grad,
        norm_total,
        query_total,
        keyval_total,
        output_total,
        mixer_total,
        gate_total,
        up_total,
        down_total,
    )


def solution(mesh):
    return jax.shard_map(
        shards,
        mesh=mesh,
        in_specs=(
            P(("dp", "col"), "row"),
            P("row"),
            P("row", "col"),
            P("row", "col"),
            P("col", "row"),
            P("row"),
            P(None, "row", "col"),
            P(None, "row", "col"),
            P(None, "col", "row"),
            P(("dp", "row"), None),
            P("dp", None),
            P("dp", None),
            P(("dp", "col"), "row"),
        ),
        out_specs=(
            P(("dp", "col"), "row"),
            P(("dp", "col"), "row"),
            P("row"),
            P("row", "col"),
            P("row", "col"),
            P("col", "row"),
            P("row"),
            P(None, "row", "col"),
            P(None, "row", "col"),
            P(None, "col", "row"),
        ),
        check_vma=False,
    )
```

```python
import functools

import jax
import jax.numpy as jnp
from jax import lax
from jax.experimental import pallas as pl
from jax.experimental.pallas import tpu as pltpu
from jax.sharding import PartitionSpec as P

epsilon = 1e-06
rope_base = 1000000.0
head_dim = 128
low = jnp.bfloat16
full = jnp.float32


def swap(block, axis, bit):
    count = lax.axis_size(axis)
    return lax.ppermute(block, axis, [(i, i ^ bit) for i in range(count)])


def pair(bit, own, other, axis):
    first = jnp.where(bit == 0, own, other)
    second = jnp.where(bit == 0, other, own)
    return jnp.concatenate([first, second], axis=axis)


def dot(left, right, left_dim=1, right_dim=0):
    return lax.dot_general(
        left, right, (((left_dim,), (right_dim,)), ((), ())), preferred_element_type=full
    )


def gather_col(block, col):
    count = lax.axis_size("col")
    from_left, from_right = [block], [block]
    for step in range(1, count):
        from_left.append(
            lax.ppermute(from_left[-1], "col", [(i, i + 1) for i in range(step - 1, count - 1)])
        )
        from_right.append(
            lax.ppermute(from_right[-1], "col", [(i + 1, i) for i in range(count - step)])
        )
    slots = [block]
    for k in range(1, count):
        chosen = None
        for at in range(count):
            there = at ^ k
            value = from_right[there - at] if there > at else from_left[at - there]
            chosen = value if chosen is None else jnp.where(col == at, value, chosen)
        slots.append(chosen)
    return slots


def scatter_col(stack, col):
    count = lax.axis_size("col")

    def term(block):
        return lax.dynamic_index_in_dim(stack, col ^ jnp.clip(block, 0, count - 1), 0, False)

    right, left = None, None
    for step in range(1, count):
        to_right = term(col + count - step)
        to_left = term(col - count + step)
        if right is not None:
            to_right = (to_right.astype(full) + right.astype(full)).astype(low)
            to_left = (to_left.astype(full) + left.astype(full)).astype(low)
        right = lax.ppermute(to_right, "col", [(i, i + 1) for i in range(min(step, count - 1))])
        left = lax.ppermute(
            to_left, "col", [(i, i - 1) for i in range(count - 1, count - 1 - step, -1)]
        )
    return stack[0].astype(full) + right.astype(full) + left.astype(full)


def halves_sum(parts, core, axis):
    size = parts.shape[axis] // 2
    mine = lax.dynamic_slice_in_dim(parts, core * size, size, axis)
    theirs = lax.dynamic_slice_in_dim(parts, (1 - core) * size, size, axis)
    return (mine.astype(full) + swap(theirs, "dp", 1).astype(full)).astype(low)


def others_sum(block):
    bit = 2
    while bit < lax.axis_size("dp"):
        block = (block.astype(full) + swap(block, "dp", bit).astype(full)).astype(low)
        bit *= 2
    return block


def quarter_of(block, quarter):
    size = block.shape[0] // 4
    return lax.dynamic_slice_in_dim(block, quarter * size, size, 0)


def quarters_all(block, core, side):
    across = swap(block, "dp", 2)
    two = [jnp.where(side == 0, block, across), jnp.where(side == 0, across, block)]
    both = jnp.stack(two)
    near = swap(both, "dp", 1)
    result = []
    for at in range(2):
        result.append(jnp.where(core == 0, both[at], near[at]))
        result.append(jnp.where(core == 0, near[at], both[at]))
    return result


def attention_forward_kernel(
    pre_ref, cosine_ref, sine_ref, key_ref, value_ref, start_ref, out_ref, rot_ref, *, window, tile
):
    rows = pre_ref.shape[0]
    pre = pre_ref[...]
    rot = (pre * cosine_ref[...] + pltpu.roll(pre, head_dim // 2, 1) * sine_ref[...]).astype(low)
    rot_ref[...] = rot
    for at in range(rows // tile):
        first = at * tile
        keys = key_ref[first : first + window, :]
        values = value_ref[first : first + window, :]
        scores = dot(rot[first : first + tile], keys, 1, 1) * head_dim ** (-0.5)
        place = lax.broadcasted_iota(jnp.int32, scores.shape, 1) + first
        query = lax.broadcasted_iota(jnp.int32, scores.shape, 0) + (first + rows)
        allowed = (place <= query) & (place >= start_ref[first : first + tile, :])
        scores = jnp.where(allowed, scores, -1e30)
        exponent = jnp.exp(scores - jnp.max(scores, axis=1, keepdims=True))
        weights = exponent / jnp.sum(exponent, axis=1, keepdims=True)
        out_ref[first : first + tile, :] = dot(weights.astype(low), values).astype(low)


def attention_backward_kernel(
    rot_ref,
    cosine_ref,
    sine_ref,
    key_ref,
    value_ref,
    start_ref,
    grad_ref,
    query_grad_ref,
    key_grad_ref,
    value_grad_ref,
    *,
    window,
    tile,
):
    rows = rot_ref.shape[0]

    @pl.when(pl.program_id(0) == 0)
    def _():
        key_grad_ref[...] = jnp.zeros_like(key_grad_ref)
        value_grad_ref[...] = jnp.zeros_like(value_grad_ref)

    for at in range(rows // tile):
        first = at * tile
        rot = rot_ref[first : first + tile, :]
        grad = grad_ref[first : first + tile, :]
        keys = key_ref[first : first + window, :]
        values = value_ref[first : first + window, :]
        scores = dot(rot, keys, 1, 1) * head_dim ** (-0.5)
        place = lax.broadcasted_iota(jnp.int32, scores.shape, 1) + first
        query = lax.broadcasted_iota(jnp.int32, scores.shape, 0) + (first + rows)
        allowed = (place <= query) & (place >= start_ref[first : first + tile, :])
        scores = jnp.where(allowed, scores, -1e30)
        exponent = jnp.exp(scores - jnp.max(scores, axis=1, keepdims=True))
        probs = exponent / jnp.sum(exponent, axis=1, keepdims=True)
        prob_grad = dot(grad, values, 1, 1)
        inner = jnp.sum(probs * prob_grad, axis=1, keepdims=True)
        score_grad = (probs * (prob_grad - inner) * head_dim ** (-0.5)).astype(low)
        rot_grad = dot(score_grad, keys)
        cosine = cosine_ref[first : first + tile, :]
        sine = sine_ref[first : first + tile, :]
        query_grad_ref[first : first + tile, :] = (
            rot_grad * cosine - pltpu.roll(rot_grad, head_dim // 2, 1) * sine
        ).astype(low)
        key_grad_ref[first : first + window, :] += dot(score_grad, rot, 0, 0)
        value_grad_ref[first : first + window, :] += dot(probs.astype(low), grad, 0, 0)


def attention_forward(pre, cosine, sine, keys, values, start, heads):
    rows, reach = pre.shape[0], keys.shape[0]
    whole = lambda shape: pl.BlockSpec(shape, lambda h: (0, 0))
    head = pl.BlockSpec((rows, head_dim), lambda h: (0, h))
    shape = jax.ShapeDtypeStruct((rows, heads * head_dim), low)
    per_half = heads // 2
    return pl.pallas_call(
        functools.partial(attention_forward_kernel, window=reach - rows // 2, tile=rows // 2),
        grid=(heads,),
        in_specs=[
            pl.BlockSpec((rows, head_dim), lambda h: (0, h + h // per_half)),
            whole((rows, head_dim)),
            whole((rows, head_dim)),
            whole((reach, head_dim)),
            whole((reach, head_dim)),
            whole((rows, 1)),
        ],
        out_specs=[head, head],
        out_shape=[shape, shape],
        compiler_params=pltpu.CompilerParams(vmem_limit_bytes=32 * 2**20),
        cost_estimate=pl.CostEstimate(
            flops=heads * rows * reach * 3 * head_dim,
            bytes_accessed=heads * rows * head_dim * 8,
            transcendentals=heads * rows * reach,
        ),
    )(pre, cosine, sine, keys, values, start)


def attention_backward(rot, cosine, sine, keys, values, start, grad, heads):
    rows, reach = rot.shape[0], keys.shape[0]
    whole = lambda shape: pl.BlockSpec(shape, lambda h: (0, 0))
    head = pl.BlockSpec((rows, head_dim), lambda h: (0, h))
    return pl.pallas_call(
        functools.partial(attention_backward_kernel, window=reach - rows // 2, tile=rows // 2),
        grid=(heads,),
        in_specs=[
            head,
            whole((rows, head_dim)),
            whole((rows, head_dim)),
            whole((reach, head_dim)),
            whole((reach, head_dim)),
            whole((rows, 1)),
            head,
        ],
        out_specs=[head, whole((reach, head_dim)), whole((reach, head_dim))],
        out_shape=[
            jax.ShapeDtypeStruct((rows, heads * head_dim), low),
            jax.ShapeDtypeStruct((reach, head_dim), full),
            jax.ShapeDtypeStruct((reach, head_dim), full),
        ],
        compiler_params=pltpu.CompilerParams(vmem_limit_bytes=32 * 2**20),
        cost_estimate=pl.CostEstimate(
            flops=heads * rows * reach * 8 * head_dim,
            bytes_accessed=heads * rows * head_dim * 8,
            transcendentals=heads * rows * reach,
        ),
    )(rot, cosine, sine, keys, values, start, grad)


def experts_kernel(
    own_ref,
    cot_ref,
    table_ref,
    gate_ref,
    up_ref,
    down_ref,
    sum_ref,
    out_part_ref,
    mine_ref,
    theirs_ref,
    mine_down_ref,
    theirs_down_ref,
    expert_in,
    gate_grad,
    up_grad,
    hidden,
    send_stage,
    arrived,
    stage,
    stage_down,
    ag_recv,
    ag_right,
    ag_left,
    rs_recv,
    rs_send,
    local_sem,
    core_send,
    core_recv,
    down_local,
    down_send,
    down_recv,
):
    col, dp = lax.axis_index("col"), lax.axis_index("dp")
    core = dp % 2
    last = cot_ref.shape[0] - 1
    rows, width = own_ref.shape
    half = width // 2
    inner = (col > 0) & (col < last)

    barrier = pltpu.get_barrier_semaphore()

    def greet(device):
        pl.semaphore_signal(barrier, inc=1, device_id=device, device_id_type=pl.DeviceIdType.MESH)

    greet({"dp": dp + 1 - 2 * core})
    pl.when(col > 0)(lambda: greet({"col": col - 1}))
    pl.when(col < last)(lambda: greet({"col": col + 1}))
    expert_in[col] = own_ref[...]
    pl.when(inner)(lambda: pl.semaphore_wait(barrier, 3))
    pl.when(jnp.logical_not(inner))(lambda: pl.semaphore_wait(barrier, 2))

    def ag_copy(block, right):
        return pltpu.make_async_remote_copy(
            src_ref=expert_in.at[block],
            dst_ref=expert_in.at[block],
            send_sem=(ag_right if right else ag_left).at[block],
            recv_sem=ag_recv.at[block],
            device_id={"col": col + 1 if right else col - 1},
            device_id_type=pl.DeviceIdType.MESH,
        )

    def rs_copy(block, part, right):
        neighbour = col + 1 if right else col - 1
        slot = block if right else jnp.where(block == neighbour, last + 1, block)
        return pltpu.make_async_remote_copy(
            src_ref=send_stage.at[block, part],
            dst_ref=arrived.at[slot, part],
            send_sem=rs_send.at[block, part],
            recv_sem=rs_recv.at[slot, part],
            device_id={"col": neighbour},
            device_id_type=pl.DeviceIdType.MESH,
        )

    def rs_wait(slot, part):
        pltpu.make_async_remote_copy(
            src_ref=arrived.at[slot, part],
            dst_ref=arrived.at[slot, part],
            send_sem=rs_send.at[0, part],
            recv_sem=rs_recv.at[slot, part],
            device_id={"col": jnp.where(col > 0, col - 1, col + 1)},
            device_id_type=pl.DeviceIdType.MESH,
        ).wait_recv()

    pl.when(col < last)(lambda: ag_copy(col, True).start())
    pl.when(col > 0)(lambda: ag_copy(col, False).start())

    def compute(block):
        tokens = expert_in[block]
        grads = cot_ref[block]
        table = table_ref[block]
        experts = table.shape[1]
        units = width // experts
        for g in range(2):
            cols = slice(g * half, (g + 1) * half)
            gate = dot(tokens, gate_ref[:, cols])
            up = dot(tokens, up_ref[:, cols])
            grad = dot(grads, down_ref[cols, :], 1, 1)
            lane = lax.broadcasted_iota(jnp.int32, gate.shape, 1)
            first = g * experts // 2
            chosen = jnp.broadcast_to(table[:, first : first + 1], gate.shape)
            for e in range(1, experts // 2):
                chosen = jnp.where(lane >= e * units, table[:, first + e : first + e + 1], chosen)
            sigmoid = 1.0 / (1.0 + jnp.exp(-gate))
            silu = gate * sigmoid
            grad = grad * chosen
            hidden[block, :, cols] = (silu * up * chosen).astype(low)
            gate_grad[block, :, cols] = (
                grad * up * (sigmoid * (1.0 + gate * (1.0 - sigmoid)))
            ).astype(low)
            up_grad[block, :, cols] = (grad * silu).astype(low)
        gates_now, ups_now = gate_grad[block], up_grad[block]
        for part in range(2):
            cols = slice(part * half, (part + 1) * half)
            total = dot(gates_now, gate_ref[cols, :], 1, 1) + dot(ups_now, up_ref[cols, :], 1, 1)
            send_stage[block, part] = total.astype(low)
            pl.when((col == 0) & (block != col))(lambda: rs_copy(block, part, True).start())
            pl.when((col == last) & (block != col))(lambda: rs_copy(block, part, False).start())
        out_part_ref[block] = dot(hidden[block], down_ref[...]).astype(low)

    def step(i, carry):
        apart = (i + 1) // 2
        from_left = i % 2 == 1

        @pl.when(from_left & (col - apart >= 0))
        def _():
            block = col - apart
            ag_copy(block, True).wait_recv()
            pl.when(col < last)(lambda: ag_copy(block, True).start())

        @pl.when(from_left & (col + apart <= last))
        def _():
            block = col + apart
            ag_copy(block, False).wait_recv()
            pl.when(col > 0)(lambda: ag_copy(block, False).start())

        block = jnp.where(from_left, col - apart, col + apart)
        pl.when((block >= 0) & (block <= last))(lambda: compute(block))
        return carry

    lax.fori_loop(0, 2 * last + 1, step, 0)

    def forward(block, right):
        for part in range(2):
            rs_wait(block, part)
            send_stage[block, part] = (
                send_stage[block, part].astype(full) + arrived[block, part].astype(full)
            ).astype(low)
            rs_copy(block, part, right).start()

    def event(number):
        blocks = ((2, 1), (3, 0), (0, 3))[number]
        pl.when(col == 1)(lambda: forward(blocks[0], number < 2))
        pl.when(col == 2)(lambda: forward(blocks[1], number == 2))

    def to_partner(source, target, send_sem, recv_sem):
        return pltpu.make_async_remote_copy(
            src_ref=source,
            dst_ref=target,
            send_sem=send_sem,
            recv_sem=recv_sem,
            device_id={"dp": dp + 1 - 2 * core},
            device_id_type=pl.DeviceIdType.MESH,
        )

    size = stage.shape[1]
    tiles = width // size
    flat_in = expert_in[...].reshape((last + 1) * rows, width)

    def weight_copies(which, tile):
        at = which * tiles + tile
        slot = at % 2
        target = pl.ds(tile * size, size)
        return (
            to_partner(
                stage.at[2 * slot], theirs_ref.at[which, target], core_send.at[at], core_recv.at[at]
            ),
            pltpu.make_async_copy(
                stage.at[2 * slot + 1], mine_ref.at[which, target], local_sem.at[at]
            ),
        )

    def weight_tile(which, tile):
        right = (gate_grad, up_grad)[which]
        at = which * tiles + tile
        if at >= 2:
            before = weight_copies((at - 2) // tiles, (at - 2) % tiles)
            before[0].wait_send()
            before[1].wait()
        left = expert_in[:, :, tile * size : (tile + 1) * size].reshape(-1, size)
        for order in range(2):
            which_half = 1 - core if order == 0 else core
            cols = pl.ds(pl.multiple_of(which_half * half, half), half)
            stage[2 * (at % 2) + order] = dot(
                left, right[:, :, cols].reshape(-1, half), 0, 0
            ).astype(low)
        for copy in weight_copies(which, tile):
            copy.start()

    size_down = stage_down.shape[1]
    tiles_down = half // size_down

    def down_copy(order, tile):
        at = order * tiles_down + tile
        target = pl.ds(tile * size_down, size_down)
        if order == 0:
            return to_partner(
                stage_down.at[at], theirs_down_ref.at[target], down_send.at[tile], down_recv.at[tile]
            )
        return pltpu.make_async_copy(
            stage_down.at[at], mine_down_ref.at[target], down_local.at[tile]
        )

    def down_tile(order, tile):
        which_half = 1 - core if order == 0 else core
        first = pl.multiple_of(which_half * half + tile * size_down, 128)
        left = hidden[:, :, pl.ds(first, size_down)].reshape(-1, size_down)
        stage_down[order * tiles_down + tile] = dot(
            left, cot_ref[...].reshape(-1, width), 0, 0
        ).astype(low)
        down_copy(order, tile).start()

    for tile in range(tiles):
        weight_tile(0, tile)
    event(0)
    for tile in range(tiles):
        weight_tile(1, tile)
    for tile in range(tiles_down):
        down_tile(0, tile)
    event(1)
    for tile in range(tiles_down):
        down_tile(1, tile)
    event(2)

    for part in range(2):
        cols = slice(part * half, (part + 1) * half)
        sum_ref[:, cols] = send_stage[col, part].astype(full)

        @pl.when(col > 0)
        def _():
            rs_wait(col, part)
            sum_ref[:, cols] += arrived[col, part].astype(full)

        @pl.when(col < last)
        def _():
            rs_wait(last + 1, part)
            sum_ref[:, cols] += arrived[last + 1, part].astype(full)

    for block in range(last + 1):
        pl.when((block <= col) & (col < last))(lambda: ag_copy(block, True).wait_send())
        pl.when((block >= col) & (col > 0))(lambda: ag_copy(block, False).wait_send())
        for part in range(2):
            pl.when(block > col)(lambda: rs_copy(block, part, True).wait_send())
            pl.when(block < col)(lambda: rs_copy(block, part, False).wait_send())
    for at in range(2 * tiles):
        remote, local = weight_copies(at // tiles, at % tiles)
        remote.wait_recv()
        if at >= 2 * tiles - 2:
            remote.wait_send()
            local.wait()
    for tile in range(tiles_down):
        down_copy(0, tile).wait()
        down_copy(1, tile).wait()


def experts_call(own, cot, table, gate_all, up_all, down_all):
    rows, width = own.shape
    blocks, half = cot.shape[0], width // 2
    vmem = pl.BlockSpec(memory_space=pltpu.VMEM)
    anywhere = pl.BlockSpec(memory_space=pl.ANY)
    dma = pltpu.SemaphoreType.DMA
    size, size_down = width // 3, half // 2
    return pl.pallas_call(
        experts_kernel,
        in_specs=[vmem] * 6,
        out_specs=[vmem, vmem] + [anywhere] * 4,
        out_shape=[
            jax.ShapeDtypeStruct((rows, width), full),
            jax.ShapeDtypeStruct((blocks, rows, width), low),
            jax.ShapeDtypeStruct((2, width, half), low),
            jax.ShapeDtypeStruct((2, width, half), low),
            jax.ShapeDtypeStruct((half, width), low),
            jax.ShapeDtypeStruct((half, width), low),
        ],
        scratch_shapes=[pltpu.VMEM((blocks, rows, width), low)] * 4
        + [
            pltpu.VMEM((blocks, 2, rows, half), low),
            pltpu.VMEM((blocks + 1, 2, rows, half), low),
            pltpu.VMEM((4, size, half), low),
            pltpu.VMEM((4, size_down, width), low),
            dma((blocks,)),
            dma((blocks,)),
            dma((blocks,)),
            dma((blocks + 1, 2)),
            dma((blocks, 2)),
            dma((6,)),
            dma((6,)),
            dma((6,)),
            dma((2,)),
            dma((2,)),
            dma((2,)),
        ],
        compiler_params=pltpu.CompilerParams(
            collective_id=1, has_side_effects=True, vmem_limit_bytes=60 * 2**20
        ),
        cost_estimate=pl.CostEstimate(
            flops=9 * 2 * blocks * rows * width * width,
            bytes_accessed=12 * width * width,
            transcendentals=blocks * rows * width,
        ),
    )(own, cot, table, gate_all, up_all, down_all)


def rotate(matrix, cosine, sine):
    return matrix * cosine + jnp.roll(matrix, head_dim // 2, axis=1) * sine


def shards(
    inputs,
    norm_gain,
    query_weight,
    key_value_matrix,
    output_weight,
    mixer_gain,
    gate_weight,
    up_weight,
    down_weight,
    lengths,
    routes,
    route_gates,
    cotangent,
):
    row, col, dp = lax.axis_index("row"), lax.axis_index("col"), lax.axis_index("dp")
    core, side, quarter = dp % 2, (dp // 2) % 2, dp % 4
    cols = lax.axis_size("col")
    tokens, part_width = inputs.shape
    width = 2 * part_width
    own_tokens = tokens // 2
    experts, _, units = gate_weight.shape
    hidden_width = experts * units
    query_block, keyval_block = query_weight.shape[1], key_value_matrix.shape[1]
    heads = 2 * query_block // head_dim

    inputs_all = pair(row, inputs, swap(inputs, "row", 1), 1)
    gains = jnp.stack([norm_gain, mixer_gain])
    gains = pair(row, gains, swap(gains, "row", 1), 1)
    norm_all, mixer_all = gains[0], gains[1]
    lengths_all = pair(row, lengths, swap(lengths, "row", 1), 0)
    lengths_row = jnp.where(col < cols // 2, lengths_all[0], lengths_all[1])

    blocks = 2 * cols
    joint = jnp.concatenate([query_weight, key_value_matrix], axis=1)
    joint_part = quarter_of(joint, quarter)
    output_part = quarter_of(output_weight, quarter)

    def spread(part):
        arrived = []
        for k in range(cols):
            route = []
            for index in range(blocks):
                from_row, from_col = index // cols, index % cols
                to_row, to_col = from_col // 2, (2 * from_row + from_col % 2) ^ k
                route.append((index, to_row * cols + to_col))
            arrived.append(lax.ppermute(part, ("row", "col"), route))
        for bit in (1, 2):
            arrived = [
                jnp.where(col & bit == 0, arrived[k], arrived[k ^ bit]) for k in range(cols)
            ]
        return jnp.stack(arrived)

    joint_quarters = quarters_all(spread(joint_part), core, side)
    output_quarters = quarters_all(spread(output_part), core, side)
    joint_weight = jnp.concatenate(
        [
            jnp.concatenate(
                [piece[2 * r + b] for r in range(2) for piece in joint_quarters], axis=0
            )
            for b in range(2)
        ],
        axis=1,
    )
    head_output = jnp.concatenate(
        [
            jnp.concatenate(
                [piece[2 * r + b] for b in range(2) for piece in output_quarters], axis=0
            )
            for r in range(2)
        ],
        axis=1,
    )

    def flat_units(weight):
        return weight.transpose(1, 0, 2).reshape(part_width, hidden_width)

    gate_flat, up_flat = flat_units(gate_weight), flat_units(up_weight)
    down_flat = down_weight.reshape(hidden_width, part_width)

    def partner_of(flat):
        part = swap(quarter_of(flat, quarter), "row", 1)
        return jnp.concatenate(quarters_all(part, core, side), axis=0)

    gate_all = pair(row, gate_flat, partner_of(gate_flat), 0)
    up_all = pair(row, up_flat, partner_of(up_flat), 0)
    down_all = pair(row, down_flat, partner_of(down_flat), 1)

    kept = lax.dynamic_slice_in_dim(cotangent, row * own_tokens, own_tokens, 0)
    sent = lax.dynamic_slice_in_dim(cotangent, (1 - row) * own_tokens, own_tokens, 0)
    cot_own = pair(row, kept, swap(sent, "row", 1), 1)
    cot_slots = gather_col(cot_own, col)
    for bit in (1, 2):
        cot_slots = [
            jnp.where(col & bit == 0, cot_slots[k], cot_slots[k ^ bit]) for k in range(cols)
        ]
    cot_all = jnp.stack(cot_slots)

    chosen = routes[:, :, None] == jnp.arange(experts, dtype=jnp.int32)[None, None, :]
    table = jnp.sum(jnp.where(chosen, route_gates[:, :, None], 0.0), axis=1)
    tables = lax.dynamic_index_in_dim(
        table.reshape(cols, 2, own_tokens, experts), row, 1, False
    )

    inputs_full = inputs_all.astype(full)
    first_scale = lax.rsqrt(jnp.mean(inputs_full * inputs_full, axis=1, keepdims=True) + epsilon)
    normed = (inputs_full * first_scale * norm_all[None, :]).astype(low)
    projected = dot(normed, joint_weight)
    ends = jnp.cumsum(lengths_row)
    starts = ends - lengths_row
    odd = col % 2
    place = odd * tokens + jnp.arange(tokens, dtype=jnp.int32)
    begin = jnp.max(jnp.where(starts[None, :] <= place[:, None], starts[None, :], 0), axis=1)
    position = place - begin
    start = (begin + (1 - odd) * tokens)[:, None]
    theta = rope_base ** (-jnp.arange(0, head_dim, 2, dtype=full) / head_dim)
    angles = position.astype(full)[:, None] * theta[None, :]
    cosine, sine = jnp.cos(angles), jnp.sin(angles)
    cosine = jnp.concatenate([cosine, cosine], axis=1)
    sine = jnp.concatenate([-sine, sine], axis=1)
    key_at = query_block
    value_at = 2 * query_block + keyval_block
    key_own = rotate(projected[:, key_at : key_at + head_dim], cosine, sine).astype(low)
    value_own = projected[:, value_at : value_at + head_dim].astype(low)
    own_pair = jnp.concatenate([key_own, value_own], axis=1)
    before = lax.ppermute(own_pair, "col", [(i, i + 1) for i in range(0, cols, 2)])
    pairs = jnp.concatenate([before, own_pair], axis=0)
    keys, values = pairs[:, :head_dim], pairs[:, head_dim:]
    attended, rot = attention_forward(projected, cosine, sine, keys, values, start, heads)

    branch_part = dot(attended, head_output).astype(low)
    kept = lax.dynamic_slice_in_dim(branch_part, row * own_tokens, own_tokens, 0)
    sent = lax.dynamic_slice_in_dim(branch_part, (1 - row) * own_tokens, own_tokens, 0)
    branch = kept.astype(full) + swap(sent, "row", 1).astype(full)
    inputs_own = lax.dynamic_slice_in_dim(inputs_all, row * own_tokens, own_tokens, 0)
    middle = inputs_own.astype(full) + branch
    second_scale = lax.rsqrt(jnp.mean(middle * middle, axis=1, keepdims=True) + epsilon)
    expert_own = (middle * second_scale * mixer_all[None, :]).astype(low)
    (
        second_grad,
        out_part,
        mine_parts,
        their_parts,
        mine_down,
        their_down,
    ) = experts_call(expert_own, cot_all, tables, gate_all, up_all, down_all)
    by_slot = jnp.stack(
        [lax.dynamic_index_in_dim(out_part, col ^ k, 0, False) for k in range(cols)]
    )
    experts_out = scatter_col(by_slot, col)
    outputs_own = (middle + experts_out).astype(low)
    theirs = lax.dynamic_slice_in_dim(outputs_own, (1 - row) * part_width, part_width, 1)
    mine = lax.dynamic_slice_in_dim(outputs_own, row * part_width, part_width, 1)
    outputs = pair(row, mine, swap(theirs, "row", 1), 0)
    both_parts = (mine_parts.astype(full) + their_parts.astype(full)).astype(low)
    both_down = (mine_down.astype(full) + their_down.astype(full)).astype(low)

    def expert_total(half, hidden_axis):
        axis = 1 - hidden_axis
        mine = lax.dynamic_slice_in_dim(half, row * part_width, part_width, axis)
        theirs = lax.dynamic_slice_in_dim(half, (1 - row) * part_width, part_width, axis)
        block = (mine.astype(full) + swap(theirs, "row", 1).astype(full)).astype(low)
        block = others_sum(block)
        return pair(core, block, swap(block, "dp", 1), hidden_axis).astype(full)

    def by_expert(flat):
        return flat.reshape(part_width, experts, units).transpose(1, 0, 2)

    gate_total = by_expert(expert_total(both_parts[0], 1))
    up_total = by_expert(expert_total(both_parts[1], 1))
    down_total = expert_total(both_down, 0).reshape(experts, units, part_width)

    weighted = mixer_all[None, :] * second_grad
    inner = jnp.sum(weighted * middle, axis=1, keepdims=True)
    cube = second_scale * second_scale * second_scale
    middle_grad = cot_own.astype(full) + second_scale * weighted - middle * cube * inner / width
    mixer_partial = jnp.sum(second_grad * middle * second_scale, axis=0)
    branch_own = middle_grad.astype(low)
    branch_grad = pair(row, branch_own, swap(branch_own, "row", 1), 0)

    attended_grad = dot(branch_grad, head_output, 1, 1).astype(low)
    output_part_grad = dot(attended, branch_grad, 0, 0).astype(low)
    query_grad, key_grad, value_grad = attention_backward(
        rot, cosine, sine, keys, values, start, attended_grad, heads
    )
    pair_grad = jnp.concatenate([key_grad, value_grad], axis=1)
    returned = lax.ppermute(
        pair_grad[:tokens].astype(low), "col", [(i + 1, i) for i in range(0, cols, 2)]
    )
    pair_grad = pair_grad[tokens:] + returned.astype(full)
    key_pre = rotate(pair_grad[:, :head_dim], cosine, -sine).astype(low)
    value_pre = pair_grad[:, head_dim:].astype(low)
    joint_grad = jnp.concatenate(
        [query_grad[:, :query_block], key_pre, query_grad[:, query_block:], value_pre], axis=1
    )
    normed_part = dot(joint_grad, joint_weight, 1, 1).astype(low)
    mine = lax.dynamic_slice_in_dim(normed_part, row * part_width, part_width, 1)
    theirs = lax.dynamic_slice_in_dim(normed_part, (1 - row) * part_width, part_width, 1)
    normed_grad = mine.astype(full) + swap(theirs, "row", 1).astype(full)
    weighted = norm_gain[None, :] * normed_grad
    inputs_part = inputs.astype(full)
    inner = jnp.sum(weighted * inputs_part, axis=1)
    inner = (inner + swap(inner, "row", 1))[:, None]
    cube = first_scale * first_scale * first_scale
    middle_part = lax.dynamic_slice_in_dim(branch_grad, row * part_width, part_width, 1)
    input_grad = (
        middle_part.astype(full) + first_scale * weighted - inputs_part * cube * inner / width
    ).astype(low)
    norm_partial = jnp.sum(normed_grad * inputs_part * first_scale, axis=0)

    joint_weight_grad = dot(normed, joint_grad, 0, 0).astype(low)

    def block_total(part, block_axis):
        half = halves_sum(part, core, 2 + block_axis)
        mine = lax.dynamic_index_in_dim(half, row, 0, False)
        theirs = swap(lax.dynamic_index_in_dim(half, 1 - row, 0, False), "row", 1)
        by_col = pair(row, mine, theirs, 0)
        stack = jnp.stack(
            [lax.dynamic_index_in_dim(by_col, col ^ k, 0, False) for k in range(cols)]
        )
        block = others_sum(scatter_col(stack, col).astype(low))
        return pair(core, block, swap(block, "dp", 1), block_axis).astype(full)

    both = query_block + keyval_block
    joint_total = block_total(
        joint_weight_grad.reshape(2, part_width, 2, both).transpose(0, 2, 1, 3), 0
    )
    output_total = block_total(
        output_part_grad.reshape(2, query_block, 2, part_width).transpose(2, 0, 1, 3), 0
    )
    query_total, keyval_total = joint_total[:, :query_block], joint_total[:, query_block:]

    spread_norm = jnp.where(
        jnp.arange(2)[:, None] == row, norm_partial[None, :], 0.0
    ).reshape(width)
    gain_sums = lax.psum(jnp.stack([spread_norm, mixer_partial]), ("dp", "row", "col"))
    gain_sums = lax.dynamic_slice_in_dim(gain_sums, row * part_width, part_width, 1)
    norm_total, mixer_total = gain_sums[0], gain_sums[1]
    return (
        outputs,
        input_grad,
        norm_total,
        query_total,
        keyval_total,
        output_total,
        mixer_total,
        gate_total,
        up_total,
        down_total,
    )


def solution(mesh):
    return jax.shard_map(
        shards,
        mesh=mesh,
        in_specs=(
            P(("dp", "col"), "row"),
            P("row"),
            P("row", "col"),
            P("row", "col"),
            P("col", "row"),
            P("row"),
            P(None, "row", "col"),
            P(None, "row", "col"),
            P(None, "col", "row"),
            P(("dp", "row"), None),
            P("dp", None),
            P("dp", None),
            P(("dp", "col"), "row"),
        ),
        out_specs=(
            P(("dp", "col"), "row"),
            P(("dp", "col"), "row"),
            P("row"),
            P("row", "col"),
            P("row", "col"),
            P("col", "row"),
            P("row"),
            P(None, "row", "col"),
            P(None, "row", "col"),
            P(None, "col", "row"),
        ),
        check_vma=False,
    )
```

```python
import functools

import jax
import jax.numpy as jnp
from jax import lax
from jax.experimental import pallas as pl
from jax.experimental.pallas import tpu as pltpu
from jax.sharding import PartitionSpec as P

epsilon = 1e-06
rope_base = 1000000.0
head_dim = 128
low = jnp.bfloat16
full = jnp.float32


def swap(block, axis, bit):
    count = lax.axis_size(axis)
    return lax.ppermute(block, axis, [(i, i ^ bit) for i in range(count)])


def pair(bit, own, other, axis):
    first = jnp.where(bit == 0, own, other)
    second = jnp.where(bit == 0, other, own)
    return jnp.concatenate([first, second], axis=axis)


def dot(left, right, left_dim=1, right_dim=0):
    return lax.dot_general(
        left, right, (((left_dim,), (right_dim,)), ((), ())), preferred_element_type=full
    )


def gather_col(block, col):
    count = lax.axis_size("col")
    from_left, from_right = [block], [block]
    for step in range(1, count):
        from_left.append(
            lax.ppermute(from_left[-1], "col", [(i, i + 1) for i in range(step - 1, count - 1)])
        )
        from_right.append(
            lax.ppermute(from_right[-1], "col", [(i + 1, i) for i in range(count - step)])
        )
    slots = [block]
    for k in range(1, count):
        chosen = None
        for at in range(count):
            there = at ^ k
            value = from_right[there - at] if there > at else from_left[at - there]
            chosen = value if chosen is None else jnp.where(col == at, value, chosen)
        slots.append(chosen)
    return slots


def quarter_of(block, quarter):
    size = block.shape[0] // 4
    return lax.dynamic_slice_in_dim(block, quarter * size, size, 0)


def quarters_all(block, core, side):
    across = swap(block, "dp", 2)
    two = [jnp.where(side == 0, block, across), jnp.where(side == 0, across, block)]
    both = jnp.stack(two)
    near = swap(both, "dp", 1)
    result = []
    for at in range(2):
        result.append(jnp.where(core == 0, both[at], near[at]))
        result.append(jnp.where(core == 0, near[at], both[at]))
    return result


def attention_forward_kernel(
    pre_ref, cosine_ref, sine_ref, key_ref, value_ref, start_ref, out_ref, rot_ref, *, window, tile
):
    rows = pre_ref.shape[0]
    pre = pre_ref[...]
    rot = (pre * cosine_ref[...] + pltpu.roll(pre, head_dim // 2, 1) * sine_ref[...]).astype(low)
    rot_ref[...] = rot
    for at in range(rows // tile):
        first = at * tile
        keys = key_ref[first : first + window, :]
        values = value_ref[first : first + window, :]
        scores = dot(rot[first : first + tile], keys, 1, 1) * head_dim ** (-0.5)
        place = lax.broadcasted_iota(jnp.int32, scores.shape, 1) + first
        query = lax.broadcasted_iota(jnp.int32, scores.shape, 0) + (first + rows)
        allowed = (place <= query) & (place >= start_ref[first : first + tile, :])
        scores = jnp.where(allowed, scores, -1e30)
        exponent = jnp.exp(scores - jnp.max(scores, axis=1, keepdims=True))
        weights = exponent / jnp.sum(exponent, axis=1, keepdims=True)
        out_ref[first : first + tile, :] = dot(weights.astype(low), values).astype(low)


def attention_forward(pre, cosine, sine, keys, values, start, heads):
    rows, reach = pre.shape[0], keys.shape[0]
    whole = lambda shape: pl.BlockSpec(shape, lambda h: (0, 0))
    head = pl.BlockSpec((rows, head_dim), lambda h: (0, h))
    shape = jax.ShapeDtypeStruct((rows, heads * head_dim), low)
    per_half = heads // 2
    return pl.pallas_call(
        functools.partial(attention_forward_kernel, window=reach - rows // 2, tile=rows // 2),
        grid=(heads,),
        in_specs=[
            pl.BlockSpec((rows, head_dim), lambda h: (0, h + h // per_half)),
            whole((rows, head_dim)),
            whole((rows, head_dim)),
            whole((reach, head_dim)),
            whole((reach, head_dim)),
            whole((rows, 1)),
        ],
        out_specs=[head, head],
        out_shape=[shape, shape],
        compiler_params=pltpu.CompilerParams(vmem_limit_bytes=32 * 2**20),
        cost_estimate=pl.CostEstimate(
            flops=heads * rows * reach * 3 * head_dim,
            bytes_accessed=heads * rows * head_dim * 8,
            transcendentals=heads * rows * reach,
        ),
    )(pre, cosine, sine, keys, values, start)


def remote_copy(source, target, send_sem, recv_sem, **device):
    return pltpu.make_async_remote_copy(
        src_ref=source,
        dst_ref=target,
        send_sem=send_sem,
        recv_sem=recv_sem,
        device_id=device,
        device_id_type=pl.DeviceIdType.MESH,
    )


def add_low(left, right):
    return (left.astype(full) + right.astype(full)).astype(low)


class ColSum:
    def __init__(self, stack, arrived, send_sem, recv_sem, col):
        self.stack, self.arrived, self.send_sem, self.recv_sem, self.col = (
            stack,
            arrived,
            send_sem,
            recv_sem,
            col,
        )
        self.last = stack.shape[0] - 1

    def copy(self, block, at, right):
        neighbour = at + 1 if right else at - 1
        slot = block if right or block != neighbour else self.last + 1
        return remote_copy(
            self.stack.at[block],
            self.arrived.at[slot],
            self.send_sem.at[block],
            self.recv_sem.at[slot],
            col=neighbour,
        )

    def wait(self, slot, at):
        remote_copy(
            self.arrived.at[slot],
            self.arrived.at[slot],
            self.send_sem.at[0],
            self.recv_sem.at[slot],
            col=at + 1 if at == 0 else at - 1,
        ).wait_recv()

    def step(self, number):
        for at in range(self.last + 1):

            @pl.when(self.col == at)
            def _(at=at):
                for right in (True, False):
                    block = at + self.last + 1 - number if right else at - self.last - 1 + number
                    if not 0 <= block <= self.last:
                        continue
                    if 0 < at < self.last:
                        self.wait(block, at)
                        self.stack[block] = add_low(self.stack[block], self.arrived[block])
                    self.copy(block, at, right).start()

    def total(self, part):
        for at in range(self.last + 1):

            @pl.when(self.col == at)
            def _(at=at):
                if at > 0:
                    self.wait(at, at)
                if at < self.last:
                    self.wait(self.last + 1, at)
                value = self.stack[at].astype(full)
                if at > 0:
                    value += self.arrived[at].astype(full)
                if at < self.last:
                    value += self.arrived[self.last + 1].astype(full)
                part(value)

    def end(self):
        for at in range(self.last + 1):

            @pl.when(self.col == at)
            def _(at=at):
                for block in range(self.last + 1):
                    if block != at:
                        self.copy(block, at, block > at).wait_send()


def experts_kernel(
    own_ref,
    cot_ref,
    table_ref,
    gate_hbm,
    up_hbm,
    down_hbm,
    sum_ref,
    out_part_ref,
    gate_total_ref,
    up_own_ref,
    up_row_ref,
    up_other_ref,
    down_half_ref,
    weights,
    expert_in,
    gate_grad,
    up_grad,
    hidden,
    send_stage,
    arrived,
    parts,
    stage,
    weights_sem,
    ready,
    ag_recv,
    ag_right,
    ag_left,
    rs_recv,
    rs_send,
    core_send,
    core_recv,
    row_send,
    row_recv,
    side_send,
    side_recv,
    final_sem,
    local_sem,
):
    row, col, dp = lax.axis_index("row"), lax.axis_index("col"), lax.axis_index("dp")
    dps = lax.axis_size("dp")
    core, other = dp % 2, 1 - row
    core_partner = dp + 1 - 2 * core
    side_bits = list(range(1, dps.bit_length() - 1))
    sides = len(side_bits)
    last = cot_ref.shape[0] - 1
    rows, width = own_ref.shape
    half = width // 2
    size = half // 2
    inner = (col > 0) & (col < last)

    def across(bit):
        on = (dp // (1 << bit)) % 2
        return dp + (1 << bit) * (1 - 2 * on)

    gate_ref, up_ref, down_ref = weights.at[0], weights.at[1], weights.at[2]
    loads = [
        pltpu.make_async_copy(source, weights.at[i], weights_sem.at[i])
        for i, source in enumerate((gate_hbm, up_hbm, down_hbm))
    ]
    for copy in loads:
        copy.start()

    barrier = pltpu.get_barrier_semaphore()

    def greet(semaphore, **device):
        pl.semaphore_signal(
            semaphore, inc=1, device_id=device, device_id_type=pl.DeviceIdType.MESH
        )

    greet(barrier, dp=core_partner)
    greet(barrier, row=other)
    for bit in side_bits:
        greet(barrier, dp=across(bit))
    pl.when(col > 0)(lambda: greet(barrier, col=col - 1))
    pl.when(col < last)(lambda: greet(barrier, col=col + 1))
    expert_in[col] = own_ref[...]
    pl.when(inner)(lambda: pl.semaphore_wait(barrier, 4 + sides))
    pl.when(jnp.logical_not(inner))(lambda: pl.semaphore_wait(barrier, 3 + sides))

    def ag_copy(block, right):
        return remote_copy(
            expert_in.at[block],
            expert_in.at[block],
            (ag_right if right else ag_left).at[block],
            ag_recv.at[block],
            col=col + 1 if right else col - 1,
        )

    def rs_copy(block, part, right):
        neighbour = col + 1 if right else col - 1
        slot = block if right else jnp.where(block == neighbour, last + 1, block)
        return remote_copy(
            send_stage.at[block, part],
            arrived.at[slot, part],
            rs_send.at[block, part],
            rs_recv.at[slot, part],
            col=neighbour,
        )

    def rs_wait(slot, part):
        remote_copy(
            arrived.at[slot, part],
            arrived.at[slot, part],
            rs_send.at[0, part],
            rs_recv.at[slot, part],
            col=jnp.where(col > 0, col - 1, col + 1),
        ).wait_recv()

    pl.when(col < last)(lambda: ag_copy(col, True).start())
    pl.when(col > 0)(lambda: ag_copy(col, False).start())
    for copy in loads:
        copy.wait()

    def compute(block):
        tokens = expert_in[block]
        grads = cot_ref[block]
        table = table_ref[block]
        experts = table.shape[1]
        units = width // experts
        for g in range(2):
            cols = slice(g * half, (g + 1) * half)
            gate = dot(tokens, gate_ref[:, cols])
            up = dot(tokens, up_ref[:, cols])
            grad = dot(grads, down_ref[cols, :], 1, 1)
            lane = lax.broadcasted_iota(jnp.int32, gate.shape, 1)
            first = g * experts // 2
            chosen = jnp.broadcast_to(table[:, first : first + 1], gate.shape)
            for e in range(1, experts // 2):
                chosen = jnp.where(lane >= e * units, table[:, first + e : first + e + 1], chosen)
            sigmoid = 1.0 / (1.0 + jnp.exp(-gate))
            silu = gate * sigmoid
            grad = grad * chosen
            hidden[block, :, cols] = (silu * up * chosen).astype(low)
            gate_grad[block, :, cols] = (
                grad * up * (sigmoid * (1.0 + gate * (1.0 - sigmoid)))
            ).astype(low)
            up_grad[block, :, cols] = (grad * silu).astype(low)
        gates_now, ups_now = gate_grad[block], up_grad[block]
        for part in range(2):
            cols = slice(part * half, (part + 1) * half)
            total = dot(gates_now, gate_ref[cols, :], 1, 1) + dot(ups_now, up_ref[cols, :], 1, 1)
            send_stage[block, part] = total.astype(low)
            pl.when((col == 0) & (block != col))(lambda: rs_copy(block, part, True).start())
            pl.when((col == last) & (block != col))(lambda: rs_copy(block, part, False).start())
        out_part_ref[block] = dot(hidden[block], down_ref[...]).astype(low)

    def step(i, carry):
        apart = (i + 1) // 2
        from_left = i % 2 == 1

        @pl.when(from_left & (col - apart >= 0))
        def _():
            block = col - apart
            ag_copy(block, True).wait_recv()
            pl.when(col < last)(lambda: ag_copy(block, True).start())

        @pl.when(from_left & (col + apart <= last))
        def _():
            block = col + apart
            ag_copy(block, False).wait_recv()
            pl.when(col > 0)(lambda: ag_copy(block, False).start())

        block = jnp.where(from_left, col - apart, col + apart)
        pl.when((block >= 0) & (block <= last))(lambda: compute(block))
        return carry

    lax.fori_loop(0, 2 * last + 1, step, 0)

    greet(ready.at[0], dp=core_partner)
    greet(ready.at[1], row=other)
    for number, bit in enumerate(side_bits):
        greet(ready.at[2 + number], dp=across(bit))

    def room(which, down, right):
        return weights.at[
            which, pl.ds(down * half, half), pl.ds(right * half, half)
        ]

    def forward(block, right):
        for part in range(2):
            rs_wait(block, part)
            send_stage[block, part] = add_low(send_stage[block, part], arrived[block, part])
            rs_copy(block, part, right).start()

    def event(number):
        blocks = ((2, 1), (3, 0), (0, 3))[number]
        pl.when(col == 1)(lambda: forward(blocks[0], number < 2))
        pl.when(col == 2)(lambda: forward(blocks[1], number == 2))

    def core_copy(at):
        if at < 4:
            target = room(at // 2, 0, at % 2)
        else:
            target = room(2, 0, at - 4)
        return remote_copy(
            stage.at[at % 2], target, core_send.at[at], core_recv.at[at], dp=core_partner
        )

    def stage_free(at):
        if at >= 2:
            core_copy(at - 2).wait_send()

    def half_lanes(which):
        return pl.ds(pl.multiple_of(which * half, half), half)

    def core_dot(at):
        right = (gate_grad, up_grad)[at // 2]
        left = expert_in[:, :, half_lanes(row if at % 2 else other)].reshape(-1, half)
        stage_free(at)
        stage[at % 2] = dot(
            left, right[:, :, half_lanes(1 - core)].reshape(-1, half), 0, 0
        ).astype(low)
        core_copy(at).start()
        parts[at] = dot(left, right[:, :, half_lanes(core)].reshape(-1, half), 0, 0).astype(low)

    def core_sum(at):
        core_copy(at).wait_recv()
        parts[at] = add_low(parts[at], room(at // 2, 0, at % 2)[...])

    def down_dot():
        left = hidden[:, :, half_lanes(1 - core)].reshape(-1, half)
        for part in range(2):
            lanes = slice(part * half, (part + 1) * half)
            right = cot_ref[:, :, lanes].reshape(-1, half)
            stage_free(4 + part)
            stage[part] = dot(left, right, 0, 0).astype(low)
            core_copy(4 + part).start()
        left = hidden[:, :, half_lanes(core)].reshape(-1, half)
        for part in range(2):
            lanes = slice(part * half, (part + 1) * half)
            right = cot_ref[:, :, lanes].reshape(-1, half)
            room(2, 1, part)[...] = dot(left, right, 0, 0).astype(low)

    def down_sum():
        for part in range(2):
            core_copy(4 + part).wait_recv()
            room(2, 1, part)[...] = add_low(room(2, 1, part)[...], room(2, 0, part)[...])

    down_out = pltpu.make_async_copy(
        weights.at[2, pl.ds(half, half)], down_half_ref, local_sem.at[0]
    )
    up_out = pltpu.make_async_copy(parts.at[3], up_own_ref, local_sem.at[1])
    up_rest = pltpu.make_async_copy(
        parts.at[2, pl.ds(size, size)], up_other_ref, local_sem.at[2]
    )

    def chunk_rows(chunk):
        return pl.ds(chunk * size, size)

    def row_copy(chunk):
        if chunk < 2:
            source = parts.at[0, chunk_rows(chunk)]
            target = weights.at[0, pl.ds(half + chunk * size, size), pl.ds(0, half)]
        else:
            source, target = parts.at[2, chunk_rows(0)], up_row_ref
        return remote_copy(source, target, row_send.at[chunk], row_recv.at[chunk], row=other)

    def side_room(number, chunk):
        which, right = ((0, 1), (1, 0), (1, 1))[number]
        return weights.at[
            which, pl.ds(half + chunk * size, size), pl.ds(right * half, half)
        ]

    def side_copy(chunk, number):
        return remote_copy(
            parts.at[1 - number % 2, chunk_rows(chunk)],
            side_room(number, chunk),
            side_send.at[chunk, number],
            side_recv.at[chunk, number],
            dp=across(side_bits[number]),
        )

    def after_row(chunk):
        copy = row_copy(chunk)
        copy.wait_recv()
        copy.wait_send()
        here = chunk_rows(chunk)
        landed = weights.at[0, pl.ds(half + chunk * size, size), pl.ds(0, half)]
        parts[1, here] = add_low(parts[1, here], landed[...])
        if sides:
            if chunk == 0:
                for number in range(sides):
                    pl.semaphore_wait(ready.at[2 + number], 1)
            side_copy(chunk, 0).start()

    def final_copies(chunk):
        source = parts.at[1 - sides % 2, chunk_rows(chunk)]
        target = gate_total_ref.at[chunk_rows(chunk), half_lanes(core)]
        return (
            remote_copy(
                source, target, final_sem.at[chunk, 0], final_sem.at[chunk, 1], dp=core_partner
            ),
            pltpu.make_async_copy(source, target, final_sem.at[chunk, 2]),
        )

    def after_side(chunk):
        here = chunk_rows(chunk)
        for number in range(sides):
            copy = side_copy(chunk, number)
            copy.wait_recv()
            copy.wait_send()
            parts[number % 2, here] = add_low(
                parts[1 - number % 2, here], side_room(number, chunk)[...]
            )
            if number + 1 < sides:
                side_copy(chunk, number + 1).start()
        for copy in final_copies(chunk):
            copy.start()

    pl.semaphore_wait(ready.at[0], 1)
    core_dot(0)
    core_dot(1)
    core_sum(0)
    pl.semaphore_wait(ready.at[1], 1)
    row_copy(0).start()
    row_copy(1).start()
    event(0)
    core_dot(2)
    core_sum(1)
    core_sum(2)
    row_copy(2).start()
    up_rest.start()
    core_dot(3)
    down_dot()
    core_sum(3)
    up_out.start()
    event(1)
    after_row(0)
    down_sum()
    down_out.start()
    event(2)
    after_row(1)

    for part in range(2):
        cols = slice(part * half, (part + 1) * half)
        sum_ref[:, cols] = send_stage[col, part].astype(full)

        @pl.when(col > 0)
        def _():
            rs_wait(col, part)
            sum_ref[:, cols] += arrived[col, part].astype(full)

        @pl.when(col < last)
        def _():
            rs_wait(last + 1, part)
            sum_ref[:, cols] += arrived[last + 1, part].astype(full)

    after_side(0)
    after_side(1)

    for block in range(last + 1):
        pl.when((block <= col) & (col < last))(lambda: ag_copy(block, True).wait_send())
        pl.when((block >= col) & (col > 0))(lambda: ag_copy(block, False).wait_send())
        for part in range(2):
            pl.when(block > col)(lambda: rs_copy(block, part, True).wait_send())
            pl.when(block < col)(lambda: rs_copy(block, part, False).wait_send())
    for at in range(4, 6):
        core_copy(at).wait_send()
    row_copy(2).wait()
    for copy in (down_out, up_out, up_rest):
        copy.wait()
    for chunk in range(2):
        remote, local = final_copies(chunk)
        remote.wait()
        local.wait()


def experts_call(own, cot, table, gate_all, up_all, down_all):
    rows, width = own.shape
    blocks, half = cot.shape[0], width // 2
    sides = lax.axis_size("dp").bit_length() - 2
    vmem = pl.BlockSpec(memory_space=pltpu.VMEM)
    anywhere = pl.BlockSpec(memory_space=pl.ANY)
    dma = pltpu.SemaphoreType.DMA
    shape = jax.ShapeDtypeStruct
    return pl.pallas_call(
        experts_kernel,
        in_specs=[vmem] * 3 + [anywhere] * 3,
        out_specs=[vmem, vmem] + [anywhere] * 5,
        out_shape=[
            shape((rows, width), full),
            shape((blocks, rows, width), low),
            shape((half, width), low),
            shape((half, half), low),
            shape((half // 2, half), low),
            shape((half // 2, half), low),
            shape((half, width), low),
        ],
        scratch_shapes=[pltpu.VMEM((3, width, width), low)]
        + [pltpu.VMEM((blocks, rows, width), low)] * 4
        + [
            pltpu.VMEM((blocks, 2, rows, half), low),
            pltpu.VMEM((blocks + 1, 2, rows, half), low),
            pltpu.VMEM((4, half, half), low),
            pltpu.VMEM((2, half, half), low),
            dma((3,)),
            pltpu.SemaphoreType.REGULAR((2 + max(sides, 1),)),
            dma((blocks,)),
            dma((blocks,)),
            dma((blocks,)),
            dma((blocks + 1, 2)),
            dma((blocks, 2)),
            dma((6,)),
            dma((6,)),
            dma((3,)),
            dma((3,)),
            dma((2, max(sides, 1))),
            dma((2, max(sides, 1))),
            dma((2, 3)),
            dma((3,)),
        ],
        compiler_params=pltpu.CompilerParams(
            collective_id=1, has_side_effects=True, vmem_limit_bytes=60 * 2**20
        ),
        cost_estimate=pl.CostEstimate(
            flops=9 * 2 * blocks * rows * width * width,
            bytes_accessed=12 * width * width,
            transcendentals=blocks * rows * width,
        ),
    )(own, cot, table, gate_all, up_all, down_all)


def finish_kernel(
    sum_ref,
    middle_ref,
    cot_ref,
    mixer_ref,
    gain_ref,
    scale_ref,
    inputs_ref,
    attended_ref,
    rot_ref,
    key_ref,
    value_ref,
    cosine_ref,
    sine_ref,
    start_ref,
    head_output_ref,
    joint_ref,
    normed_ref,
    out_part_ref,
    up_own_ref,
    up_row_ref,
    up_other_ref,
    down_half_ref,
    outputs_ref,
    input_grad_ref,
    gains_ref,
    output_total_ref,
    joint_total_ref,
    up_total_ref,
    down_total_ref,
    item_side,
    branch,
    branch_sem,
    out_stack,
    out_arrived,
    out_load,
    out_send,
    out_recv,
    own_out_sem,
    grad_heads,
    joint_grad,
    key_grad,
    value_grad,
    pair_stage,
    pair_arrived,
    pair_sem,
    normed_arrived,
    normed_own,
    normed_sem,
    inner_stage,
    inner_arrived,
    inner_sem,
    sums,
    sums_arrived,
    sums_sem,
    item_mine,
    item_other,
    item_row,
    item_sem,
    item_load_sem,
    wo_parts,
    wo_core,
    wo_row,
    wo_stack,
    wo_arrived,
    wo_side,
    wo_sem,
    wo_send,
    wo_recv,
    wa_parts,
    wa_core,
    wa_row,
    wa_stack,
    wa_arrived,
    wa_side,
    wa_sem,
    wa_send,
    wa_recv,
):
    row, col, dp = lax.axis_index("row"), lax.axis_index("col"), lax.axis_index("dp")
    cols, dps = lax.axis_size("col"), lax.axis_size("dp")
    core, other = dp % 2, 1 - row
    core_partner = dp + 1 - 2 * core
    side_bits = [bit for bit in range(1, dps.bit_length() - 1)]

    def across(bit):
        on = (dp // (1 << bit)) % 2
        return dp + (1 << bit) * (1 - 2 * on)

    rows, width = middle_ref.shape
    tokens, part_width = inputs_ref.shape
    heads = attended_ref.shape[1] // head_dim
    per_block = heads // 2

    barrier = pltpu.get_barrier_semaphore()

    def greet(**device):
        pl.semaphore_signal(
            barrier, inc=1, device_id=device, device_id_type=pl.DeviceIdType.MESH
        )

    greet(row=other)
    for apart in range(1, cols):
        greet(col=(col + apart) % cols)
    greet(dp=core_partner)
    for bit in side_bits:
        greet(dp=across(bit))

    out_copy = pltpu.make_async_copy(out_part_ref, out_stack, out_load)
    out_copy.start()
    size = item_mine.shape[1]
    items = item_mine.shape[0]

    def item_loads(at):
        chunk = at % 2
        place = pl.ds(chunk * size, size)
        if at < 2:
            sources = (up_own_ref.at[place], (up_row_ref, up_other_ref)[chunk])
        else:
            sources = [
                down_half_ref.at[place, pl.ds(pl.multiple_of(which * part_width, 128), part_width)]
                for which in (row, other)
            ]
        targets = (item_mine.at[at], item_row.at[at] if at == 0 else item_other.at[at])
        return [
            pltpu.make_async_copy(source, target, item_load_sem.at[at, number])
            for number, (source, target) in enumerate(zip(sources, targets))
        ]

    for at in range(items):
        for copy in item_loads(at):
            copy.start()

    pl.semaphore_wait(barrier, cols + 1 + len(side_bits))

    sums[0] = jnp.zeros_like(sums[0])
    piece = 64

    def norm_piece(at, mixer_sum):
        place = pl.ds(pl.multiple_of(at * piece, piece), piece)
        middle = middle_ref[place, :]
        second = sum_ref[place, :]
        scale = lax.rsqrt(jnp.mean(middle * middle, axis=1, keepdims=True) + epsilon)
        weighted = mixer_ref[...] * second
        inner = jnp.sum(weighted * middle, axis=1, keepdims=True)
        grad = (
            cot_ref[place, :].astype(full)
            + scale * weighted
            - middle * (scale * scale * scale) * (inner / width)
        )
        branch[row, place, :] = grad.astype(low)
        return mixer_sum + jnp.sum(second * middle * scale, axis=0, keepdims=True)

    mixer_sum = lax.fori_loop(0, rows // piece, norm_piece, jnp.zeros((1, width), full))
    sums[0, 1:2, :] = mixer_sum
    branch_copy = remote_copy(
        branch.at[row], branch.at[row], branch_sem.at[0], branch_sem.at[1], row=other
    )
    branch_copy.start()

    outs = ColSum(out_stack, out_arrived, out_send, out_recv, col)
    out_copy.wait()
    outs.step(1)
    for at in range(items):
        for copy in item_loads(at):
            copy.wait()

    def item_row_copy(at):
        return remote_copy(
            item_other.at[at], item_row.at[at], item_sem.at[at, 0], item_sem.at[at, 1], row=other
        )

    def item_side_copy(at, number):
        source = item_mine if number % 2 == 0 else item_other
        return remote_copy(
            source.at[at],
            item_side.at[at, number],
            item_sem.at[at, 2 + 2 * number],
            item_sem.at[at, 3 + 2 * number],
            dp=across(side_bits[number]),
        )

    last_side = len(side_bits)

    def item_value(at):
        return item_mine if last_side % 2 == 0 else item_other

    def item_places(at):
        which, chunk = at // 2, at % 2
        total = (up_total_ref, down_total_ref)[which]
        if which < 1:
            lanes = pl.ds(pl.multiple_of(core * part_width, 128), part_width)
            return total.at[pl.ds(chunk * size, size), lanes]
        return total.at[pl.ds(pl.multiple_of(core * part_width + chunk * size, 128), size), :]

    def item_core_copies(at):
        source, target = item_value(at).at[at], item_places(at)
        base = 2 + 2 * last_side
        return (
            remote_copy(
                source, target, item_sem.at[at, base], item_sem.at[at, base + 1], dp=core_partner
            ),
            pltpu.make_async_copy(source, target, item_sem.at[at, base + 2]),
        )

    def item_after_row(at):
        if at > 0:
            copy = item_row_copy(at)
            copy.wait_recv()
            copy.wait_send()
        item_mine[at] = add_low(item_mine[at], item_row[at])
        if last_side:
            item_side_copy(at, 0).start()

    def item_after_side(at):
        for number in range(last_side):
            copy = item_side_copy(at, number)
            copy.wait_recv()
            landed = pltpu.make_async_copy(
                item_side.at[at, number], item_row.at[at], item_load_sem.at[at, 0]
            )
            landed.start()
            copy.wait_send()
            landed.wait()
            source = item_mine if number % 2 == 0 else item_other
            target = item_other if number % 2 == 0 else item_mine
            target[at] = add_low(source[at], item_row[at])
            if number + 1 < last_side:
                item_side_copy(at, number + 1).start()
        for copy in item_core_copies(at):
            copy.start()

    def item_end(at):
        remote, local = item_core_copies(at)
        remote.wait_recv()
        remote.wait_send()
        local.wait()

    item_after_row(0)

    branch_copy.wait_recv()
    branch_all = branch[...].reshape(tokens, width)
    half_lanes = heads * head_dim // 2
    for part in range(2):
        lanes = slice(part * half_lanes, (part + 1) * half_lanes)
        grad_heads[:, lanes] = dot(branch_all, head_output_ref[lanes, :], 1, 1).astype(low)
    item_row_copy(1).start()

    wo_size = wo_parts.shape[2]
    for b in range(2):
        lanes = slice(b * half_lanes, (b + 1) * half_lanes)
        value = dot(attended_ref[:, lanes], branch_all, 0, 0).astype(low)
        for part in range(2):
            wo_parts[b, part] = value[part * wo_size : (part + 1) * wo_size, :]

    def wo_core_copy(b):
        return remote_copy(
            wo_parts.at[b, 1 - core], wo_core.at[b], wo_sem.at[0, b], wo_sem.at[1, b], dp=core_partner
        )

    for b in range(2):
        wo_core_copy(b).start()
    outs.step(2)

    key_grad[...] = jnp.zeros_like(key_grad)
    value_grad[...] = jnp.zeros_like(value_grad)
    tile = tokens // 2
    window = key_ref.shape[0] - tile

    def head_step(head, carry):
        here = pl.ds(pl.multiple_of(head * head_dim, head_dim), head_dim)
        there = pl.ds(
            pl.multiple_of((head + head // per_block) * head_dim, head_dim), head_dim
        )
        for at in range(tokens // tile):
            first = at * tile
            rot = rot_ref[first : first + tile, here]
            grad = grad_heads[first : first + tile, here]
            keys = key_ref[first : first + window, :]
            values = value_ref[first : first + window, :]
            scores = dot(rot, keys, 1, 1) * head_dim ** (-0.5)
            place = lax.broadcasted_iota(jnp.int32, scores.shape, 1) + first
            query = lax.broadcasted_iota(jnp.int32, scores.shape, 0) + (first + tokens)
            allowed = (place <= query) & (place >= start_ref[first : first + tile, :])
            scores = jnp.where(allowed, scores, -1e30)
            exponent = jnp.exp(scores - jnp.max(scores, axis=1, keepdims=True))
            probs = exponent / jnp.sum(exponent, axis=1, keepdims=True)
            prob_grad = dot(grad, values, 1, 1)
            inner = jnp.sum(probs * prob_grad, axis=1, keepdims=True)
            score_grad = (probs * (prob_grad - inner) * head_dim ** (-0.5)).astype(low)
            rot_grad = dot(score_grad, keys)
            joint_grad[first : first + tile, there] = (
                rot_grad * cosine_ref[first : first + tile, :]
                - pltpu.roll(rot_grad, head_dim // 2, 1) * sine_ref[first : first + tile, :]
            ).astype(low)
            key_grad[first : first + window, :] += dot(score_grad, rot, 0, 0)
            value_grad[first : first + window, :] += dot(probs.astype(low), grad, 0, 0)
        return carry

    lax.fori_loop(0, heads, head_step, 0)

    pair_stage[:, :head_dim] = key_grad[:tokens, :].astype(low)
    pair_stage[:, head_dim:] = value_grad[:tokens, :].astype(low)
    odd = col % 2 == 1

    def pair_copy():
        return remote_copy(
            pair_stage, pair_arrived, pair_sem.at[0], pair_sem.at[1], col=col + 1 - 2 * (col % 2)
        )

    pl.when(odd)(lambda: pair_copy().start())

    def wo_row_copy(b):
        lanes = pl.ds(pl.multiple_of(other * part_width, 128), part_width)
        return remote_copy(
            wo_parts.at[b, core, :, lanes],
            wo_row.at[b],
            wo_sem.at[2, b],
            wo_sem.at[3, b],
            row=other,
        )

    for b in range(2):
        wo_core_copy(b).wait_recv()
        wo_parts[b, core] = add_low(wo_parts[b, core], wo_core[b])
        wo_row_copy(b).start()
    item_after_row(1)

    @pl.when(jnp.logical_not(odd))
    def _():
        pair_copy().wait_recv()
        key_grad[tokens:, :] += pair_arrived[:, :head_dim].astype(full)
        value_grad[tokens:, :] += pair_arrived[:, head_dim:].astype(full)

    key_total = key_grad[tokens:, :]
    key_lanes = slice(per_block * head_dim, (per_block + 1) * head_dim)
    value_lanes = slice((2 * per_block + 1) * head_dim, (2 * per_block + 2) * head_dim)
    joint_grad[:, key_lanes] = (
        key_total * cosine_ref[...] - pltpu.roll(key_total, head_dim // 2, 1) * sine_ref[...]
    ).astype(low)
    joint_grad[:, value_lanes] = value_grad[tokens:, :].astype(low)

    wa_size = wa_core.shape[1]

    def wa_core_copy(r0):
        return remote_copy(
            wa_parts.at[r0, 1 - core], wa_core.at[r0], wa_sem.at[0, r0], wa_sem.at[1, r0], dp=core_partner
        )

    def wa_dot(r0, which):
        first = pl.multiple_of(r0 * part_width + which * wa_size, 128)
        wa_parts[r0, which] = dot(
            normed_ref[:, pl.ds(first, wa_size)], joint_grad[...], 0, 0
        ).astype(low)

    wa_dot(other, 1 - core)
    wa_core_copy(other).start()
    wa_dot(row, 1 - core)
    wa_core_copy(row).start()
    wa_dot(other, core)
    wa_dot(row, core)
    chunk_rows = wa_size // 2

    def wa_row_copy(chunk):
        return remote_copy(
            wa_parts.at[other, core, pl.ds(chunk * chunk_rows, chunk_rows)],
            wa_row.at[chunk],
            wa_sem.at[2, chunk],
            wa_sem.at[3, chunk],
            row=other,
        )

    wa_core_copy(other).wait_recv()
    wa_parts[other, core] = add_low(wa_parts[other, core], wa_core[other])
    for chunk in range(2):
        wa_row_copy(chunk).start()

    def normed_dot(which):
        place = pl.ds(pl.multiple_of(which * part_width, 128), part_width)
        return dot(joint_grad[...], joint_ref[place, :], 1, 1)

    normed_stage = grad_heads
    normed_stage[...] = normed_dot(other).astype(low)
    normed_copy = remote_copy(
        normed_stage, normed_arrived, normed_sem.at[0], normed_sem.at[1], row=other
    )
    normed_copy.start()
    normed_own[...] = normed_dot(row)
    wa_core_copy(row).wait_recv()
    wa_parts[row, core] = add_low(wa_parts[row, core], wa_core[row])

    wo_total = ColSum(wo_stack, wo_arrived, wo_send, wo_recv, col)
    for b in range(2):
        wo_row_copy(b).wait_recv()
        lanes = pl.ds(pl.multiple_of(row * part_width, 128), part_width)
        wo_stack[2 * row + b] = wo_parts[b, core, :, lanes]
        wo_stack[2 * other + b] = wo_row[b]
    wo_total.step(1)
    item_after_side(0)
    item_row_copy(2).start()
    outs.step(3)
    wo_total.step(2)

    wa_total = [
        ColSum(wa_stack.at[c], wa_arrived.at[c], wa_send.at[c], wa_recv.at[c], col)
        for c in range(2)
    ]
    block_lanes = wa_stack.shape[3]
    for chunk in range(2):
        wa_row_copy(chunk).wait_recv()
        place = pl.ds(chunk * chunk_rows, chunk_rows)
        for b in range(2):
            lanes = slice(b * block_lanes, (b + 1) * block_lanes)
            wa_stack[chunk, 2 * row + b] = wa_parts[row, core, place, lanes]
            wa_stack[chunk, 2 * other + b] = wa_row[chunk, :, lanes]
        wa_total[chunk].step(1)
    wo_total.step(3)
    for chunk in range(2):
        wa_total[chunk].step(2)

    normed_copy.wait_recv()
    scale = scale_ref[...]
    normed_own[...] += normed_arrived[...].astype(full)
    inner = jnp.sum(
        gain_ref[...] * normed_own[...] * inputs_ref[...].astype(full), axis=1, keepdims=True
    )
    inner_stage[...] = jnp.transpose(jnp.broadcast_to(inner, (tokens, head_dim)))[:8, :]
    inner_copy = remote_copy(
        inner_stage, inner_arrived, inner_sem.at[0], inner_sem.at[1], row=other
    )
    inner_copy.start()
    for chunk in range(2):
        wa_total[chunk].step(3)
    sums[0, 0:1, pl.ds(pl.multiple_of(row * part_width, 128), part_width)] = jnp.sum(
        normed_own[...] * inputs_ref[...].astype(full) * scale, axis=0, keepdims=True
    )
    inner_copy.wait_recv()
    both = inner_stage[...] + inner_arrived[...]
    inner = jnp.transpose(jnp.concatenate([both] * (head_dim // 8), axis=0))[:, 0:1]
    lanes = pl.ds(pl.multiple_of(row * part_width, 128), part_width)
    input_grad_ref[...] = (
        branch[:, :, lanes].reshape(tokens, part_width).astype(full)
        + scale * (gain_ref[...] * normed_own[...])
        - inputs_ref[...].astype(full) * (scale * scale * scale) * (inner / width)
    ).astype(low)

    partners = [dict(row=other), dict(col=col + 1 - 2 * (col % 2))]
    partners.append(dict(col=col + 2 - 4 * ((col // 2) % 2)))
    partners.append(dict(dp=core_partner))
    partners += [dict(dp=across(bit)) for bit in side_bits]

    def sums_copy(number):
        return remote_copy(
            sums.at[number],
            sums_arrived.at[number],
            sums_sem.at[number, 0],
            sums_sem.at[number, 1],
            **partners[number],
        )

    def sums_step(number):
        sums_copy(number).wait_recv()
        sums[number + 1] = sums[number] + sums_arrived[number]
        if number + 1 < len(partners):
            sums_copy(number + 1).start()

    sums_copy(0).start()

    def own_tokens(value):
        total = (middle_ref[...] + value).astype(low)
        out_stack[col] = total

    outs.total(own_tokens)

    def outputs_copy():
        place = pl.ds(pl.multiple_of(row * rows, rows), rows)
        lanes = pl.ds(pl.multiple_of(other * part_width, 128), part_width)
        return remote_copy(
            out_stack.at[col, :, lanes],
            outputs_ref.at[place],
            own_out_sem.at[0],
            own_out_sem.at[1],
            row=other,
        )

    outputs_copy().start()
    outputs_ref[pl.ds(pl.multiple_of(row * rows, rows), rows), :] = out_stack[
        col, :, pl.ds(pl.multiple_of(row * part_width, 128), part_width)
    ]
    sums_step(0)
    for at in range(3, items):
        item_row_copy(at).start()

    def over_dp(side, sems):
        def copy(number):
            return remote_copy(
                side.at[number % 2],
                side.at[2 + number],
                sems.at[2 * number],
                sems.at[2 * number + 1],
                dp=across(side_bits[number]),
            )

        def start(number):
            copy(number).start()

        def finish(number):
            copy(number).wait()
            side[1 - number % 2] = add_low(side[number % 2], side[2 + number])
            if number + 1 < last_side:
                start(number + 1)

        return copy, start, finish

    def set_side(side):
        def part(value):
            side[0] = value.astype(low)

        return part

    chains = [(wo_total, wo_side, wo_sem.at[4])] + [
        (wa_total[c], wa_side.at[c], wa_sem.at[4 + c]) for c in range(2)
    ]
    steps = []
    for total, side, sems in chains:
        total.total(set_side(side))
        steps.append(over_dp(side, sems))
        if last_side:
            steps[-1][1](0)
    sums_step(1)
    item_after_side(1)
    item_after_row(2)
    for _, _, finish in steps:
        for number in range(last_side):
            finish(number)
    sums_step(2)

    def block_copies(number):
        _, side, sems = chains[number]
        base, value = 2 * last_side, side.at[last_side % 2]
        if number == 0:
            target = output_total_ref.at[pl.ds(pl.multiple_of(core * wo_size, 16), wo_size)]
        else:
            first = pl.multiple_of(core * wa_size + (number - 1) * chunk_rows, 16)
            target = joint_total_ref.at[pl.ds(first, chunk_rows)]
        return (
            remote_copy(
                value, target, sems.at[base], sems.at[base + 1], dp=core_partner
            ),
            pltpu.make_async_copy(value, target, sems.at[base + 2]),
        )

    for number in range(3):
        for copy in block_copies(number):
            copy.start()
    for number in range(3, len(partners)):
        sums_step(number)
    gains_ref[...] = sums[len(partners)]

    item_after_side(2)
    item_after_row(3)
    item_after_side(3)

    branch_copy.wait_send()
    pl.when(odd)(lambda: pair_copy().wait_send())
    for b in range(2):
        wo_core_copy(b).wait_send()
        wo_row_copy(b).wait_send()
        wa_core_copy(b).wait_send()
        wa_row_copy(b).wait_send()
    normed_copy.wait_send()
    inner_copy.wait_send()
    outputs_copy().wait()
    for number in range(len(partners)):
        sums_copy(number).wait_send()
    for total in [outs, wo_total] + wa_total:
        total.end()
    for number in range(3):
        remote, local = block_copies(number)
        remote.wait()
        local.wait()
    for at in range(items):
        item_end(at)


def finish_call(
    sums, middle, cot, mixer, gain, scale, inputs, attended, rot, keys, values, cosine, sine,
    start, head_output, joint_weight, normed, out_part, up_own, up_row, up_other, down_half,
    query_block, both_block,
):
    rows, width = middle.shape
    tokens, part_width = inputs.shape
    cols, dps = lax.axis_size("col"), lax.axis_size("dp")
    sides = dps.bit_length() - 2
    heads_width = attended.shape[1]
    reach = keys.shape[0]
    vmem = pl.BlockSpec(memory_space=pltpu.VMEM)
    anywhere = pl.BlockSpec(memory_space=pl.ANY)
    dma = pltpu.SemaphoreType.DMA
    hidden = 2 * up_own.shape[1]
    size = part_width // 2
    items = 4
    wo_size, wa_size = query_block // 2, part_width // 2
    shape = jax.ShapeDtypeStruct
    sums_count = 4 + sides
    return pl.pallas_call(
        finish_kernel,
        in_specs=[vmem] * 17 + [anywhere] * 5,
        out_specs=[vmem] * 5 + [anywhere] * 3,
        out_shape=[
            shape((tokens, part_width), low),
            shape((tokens, part_width), low),
            shape((8, width), full),
            shape((query_block, part_width), low),
            shape((part_width, both_block), low),
            shape((part_width, hidden), low),
            shape((hidden, part_width), low),
            shape((items, max(sides, 1), size, part_width), low),
        ],
        scratch_shapes=[
            pltpu.VMEM((2, rows, width), low),
            dma((2,)),
            pltpu.VMEM((cols, rows, width), low),
            pltpu.VMEM((cols + 1, rows, width), low),
            dma,
            dma((cols,)),
            dma((cols + 1,)),
            dma((2,)),
            pltpu.VMEM((tokens, heads_width), low),
            pltpu.VMEM((tokens, 2 * both_block), low),
            pltpu.VMEM((reach, head_dim), full),
            pltpu.VMEM((reach, head_dim), full),
            pltpu.VMEM((tokens, 2 * head_dim), low),
            pltpu.VMEM((tokens, 2 * head_dim), low),
            dma((2,)),
            pltpu.VMEM((tokens, part_width), low),
            pltpu.VMEM((tokens, part_width), full),
            dma((2,)),
            pltpu.VMEM((8, tokens), full),
            pltpu.VMEM((8, tokens), full),
            dma((2,)),
            pltpu.VMEM((sums_count + 1, 8, width), full),
            pltpu.VMEM((sums_count, 8, width), full),
            dma((sums_count, 2)),
            pltpu.VMEM((items, size, part_width), low),
            pltpu.VMEM((items, size, part_width), low),
            pltpu.VMEM((items, size, part_width), low),
            dma((items, 5 + 2 * sides)),
            dma((items, 2)),
            pltpu.VMEM((2, 2, wo_size, width), low),
            pltpu.VMEM((2, wo_size, width), low),
            pltpu.VMEM((2, wo_size, part_width), low),
            pltpu.VMEM((cols, wo_size, part_width), low),
            pltpu.VMEM((cols + 1, wo_size, part_width), low),
            pltpu.VMEM((2 + sides, wo_size, part_width), low),
            dma((5, 3 + 2 * sides)),
            dma((cols,)),
            dma((cols + 1,)),
            pltpu.VMEM((2, 2, wa_size, 2 * both_block), low),
            pltpu.VMEM((2, wa_size, 2 * both_block), low),
            pltpu.VMEM((2, wa_size // 2, 2 * both_block), low),
            pltpu.VMEM((2, cols, wa_size // 2, both_block), low),
            pltpu.VMEM((2, cols + 1, wa_size // 2, both_block), low),
            pltpu.VMEM((2, 2 + sides, wa_size // 2, both_block), low),
            dma((6, 3 + 2 * sides)),
            dma((2, cols)),
            dma((2, cols + 1)),
        ],
        compiler_params=pltpu.CompilerParams(
            collective_id=2, has_side_effects=True, vmem_limit_bytes=63 * 2**20
        ),
        cost_estimate=pl.CostEstimate(
            flops=10 * 10**9, bytes_accessed=40 * 10**6, transcendentals=4 * 10**6
        ),
    )(
        sums, middle, cot, mixer, gain, scale, inputs, attended, rot, keys, values, cosine, sine,
        start, head_output, joint_weight, normed, out_part, up_own, up_row, up_other, down_half,
    )


def rotate(matrix, cosine, sine):
    return matrix * cosine + jnp.roll(matrix, head_dim // 2, axis=1) * sine


def shards(
    inputs,
    norm_gain,
    query_weight,
    key_value_matrix,
    output_weight,
    mixer_gain,
    gate_weight,
    up_weight,
    down_weight,
    lengths,
    routes,
    route_gates,
    cotangent,
):
    row, col, dp = lax.axis_index("row"), lax.axis_index("col"), lax.axis_index("dp")
    core, side, quarter = dp % 2, (dp // 2) % 2, dp % 4
    cols = lax.axis_size("col")
    tokens, part_width = inputs.shape
    width = 2 * part_width
    own_tokens = tokens // 2
    experts, _, units = gate_weight.shape
    hidden_width = experts * units
    query_block, keyval_block = query_weight.shape[1], key_value_matrix.shape[1]
    heads = 2 * query_block // head_dim

    inputs_all = pair(row, inputs, swap(inputs, "row", 1), 1)
    gains = jnp.stack([norm_gain, mixer_gain])
    gains = pair(row, gains, swap(gains, "row", 1), 1)
    norm_all, mixer_all = gains[0], gains[1]
    lengths_all = pair(row, lengths, swap(lengths, "row", 1), 0)
    lengths_row = jnp.where(col < cols // 2, lengths_all[0], lengths_all[1])

    blocks = 2 * cols
    joint = jnp.concatenate([query_weight, key_value_matrix], axis=1)
    joint_part = quarter_of(joint, quarter)
    output_part = quarter_of(output_weight, quarter)

    def spread(part):
        arrived = []
        for k in range(cols):
            route = []
            for index in range(blocks):
                from_row, from_col = index // cols, index % cols
                to_row, to_col = from_col // 2, (2 * from_row + from_col % 2) ^ k
                route.append((index, to_row * cols + to_col))
            arrived.append(lax.ppermute(part, ("row", "col"), route))
        for bit in (1, 2):
            arrived = [
                jnp.where(col & bit == 0, arrived[k], arrived[k ^ bit]) for k in range(cols)
            ]
        return jnp.stack(arrived)

    joint_quarters = quarters_all(spread(joint_part), core, side)
    output_quarters = quarters_all(spread(output_part), core, side)
    joint_weight = jnp.concatenate(
        [
            jnp.concatenate(
                [piece[2 * r + b] for r in range(2) for piece in joint_quarters], axis=0
            )
            for b in range(2)
        ],
        axis=1,
    )
    head_output = jnp.concatenate(
        [
            jnp.concatenate(
                [piece[2 * r + b] for b in range(2) for piece in output_quarters], axis=0
            )
            for r in range(2)
        ],
        axis=1,
    )

    def flat_units(weight):
        return weight.transpose(1, 0, 2).reshape(part_width, hidden_width)

    gate_flat, up_flat = flat_units(gate_weight), flat_units(up_weight)
    down_flat = down_weight.reshape(hidden_width, part_width)

    def partner_of(flat):
        part = swap(quarter_of(flat, quarter), "row", 1)
        return jnp.concatenate(quarters_all(part, core, side), axis=0)

    gate_all = pair(row, gate_flat, partner_of(gate_flat), 0)
    up_all = pair(row, up_flat, partner_of(up_flat), 0)
    down_all = pair(row, down_flat, partner_of(down_flat), 1)

    kept = lax.dynamic_slice_in_dim(cotangent, row * own_tokens, own_tokens, 0)
    sent = lax.dynamic_slice_in_dim(cotangent, (1 - row) * own_tokens, own_tokens, 0)
    cot_own = pair(row, kept, swap(sent, "row", 1), 1)
    cot_slots = gather_col(cot_own, col)
    for bit in (1, 2):
        cot_slots = [
            jnp.where(col & bit == 0, cot_slots[k], cot_slots[k ^ bit]) for k in range(cols)
        ]
    cot_all = jnp.stack(cot_slots)

    chosen = routes[:, :, None] == jnp.arange(experts, dtype=jnp.int32)[None, None, :]
    table = jnp.sum(jnp.where(chosen, route_gates[:, :, None], 0.0), axis=1)
    tables = lax.dynamic_index_in_dim(
        table.reshape(cols, 2, own_tokens, experts), row, 1, False
    )

    inputs_full = inputs_all.astype(full)
    first_scale = lax.rsqrt(jnp.mean(inputs_full * inputs_full, axis=1, keepdims=True) + epsilon)
    normed = (inputs_full * first_scale * norm_all[None, :]).astype(low)
    projected = dot(normed, joint_weight)
    ends = jnp.cumsum(lengths_row)
    starts = ends - lengths_row
    odd = col % 2
    place = odd * tokens + jnp.arange(tokens, dtype=jnp.int32)
    begin = jnp.max(jnp.where(starts[None, :] <= place[:, None], starts[None, :], 0), axis=1)
    position = place - begin
    start = (begin + (1 - odd) * tokens)[:, None]
    theta = rope_base ** (-jnp.arange(0, head_dim, 2, dtype=full) / head_dim)
    angles = position.astype(full)[:, None] * theta[None, :]
    cosine, sine = jnp.cos(angles), jnp.sin(angles)
    cosine = jnp.concatenate([cosine, cosine], axis=1)
    sine = jnp.concatenate([-sine, sine], axis=1)
    key_at = query_block
    value_at = 2 * query_block + keyval_block
    key_own = rotate(projected[:, key_at : key_at + head_dim], cosine, sine).astype(low)
    value_own = projected[:, value_at : value_at + head_dim].astype(low)
    own_pair = jnp.concatenate([key_own, value_own], axis=1)
    before = lax.ppermute(own_pair, "col", [(i, i + 1) for i in range(0, cols, 2)])
    pairs = jnp.concatenate([before, own_pair], axis=0)
    keys, values = pairs[:, :head_dim], pairs[:, head_dim:]
    attended, rot = attention_forward(projected, cosine, sine, keys, values, start, heads)

    branch_part = dot(attended, head_output).astype(low)
    kept = lax.dynamic_slice_in_dim(branch_part, row * own_tokens, own_tokens, 0)
    sent = lax.dynamic_slice_in_dim(branch_part, (1 - row) * own_tokens, own_tokens, 0)
    branch = kept.astype(full) + swap(sent, "row", 1).astype(full)
    inputs_own = lax.dynamic_slice_in_dim(inputs_all, row * own_tokens, own_tokens, 0)
    middle = inputs_own.astype(full) + branch
    second_scale = lax.rsqrt(jnp.mean(middle * middle, axis=1, keepdims=True) + epsilon)
    expert_own = (middle * second_scale * mixer_all[None, :]).astype(low)
    second_grad, out_part, gate_total, up_own, up_row, up_other, down_half = experts_call(
        expert_own, cot_all, tables, gate_all, up_all, down_all
    )

    both_block = query_block + keyval_block
    (
        outputs,
        input_grad,
        gain_sums,
        output_total,
        joint_total,
        up_total,
        down_total,
        _,
    ) = finish_call(
        second_grad, middle, cot_own, mixer_all[None, :], norm_gain[None, :], first_scale, inputs,
        attended, rot, keys, values, cosine, sine, start, head_output, joint_weight, normed,
        out_part, up_own, up_row, up_other, down_half, query_block, both_block,
    )
    gain_sums = lax.dynamic_slice_in_dim(gain_sums, row * part_width, part_width, 1)
    norm_total, mixer_total = gain_sums[0], gain_sums[1]

    def by_expert(flat):
        return flat.reshape(part_width, experts, units).transpose(1, 0, 2).astype(full)

    gate_total, up_total = by_expert(gate_total), by_expert(up_total)
    down_total = down_total.reshape(experts, units, part_width).astype(full)
    output_total = output_total.astype(full)
    joint_total = joint_total.astype(full)
    query_total, keyval_total = joint_total[:, :query_block], joint_total[:, query_block:]
    return (
        outputs,
        input_grad,
        norm_total,
        query_total,
        keyval_total,
        output_total,
        mixer_total,
        gate_total,
        up_total,
        down_total,
    )


def solution(mesh):
    return jax.shard_map(
        shards,
        mesh=mesh,
        in_specs=(
            P(("dp", "col"), "row"),
            P("row"),
            P("row", "col"),
            P("row", "col"),
            P("col", "row"),
            P("row"),
            P(None, "row", "col"),
            P(None, "row", "col"),
            P(None, "col", "row"),
            P(("dp", "row"), None),
            P("dp", None),
            P("dp", None),
            P(("dp", "col"), "row"),
        ),
        out_specs=(
            P(("dp", "col"), "row"),
            P(("dp", "col"), "row"),
            P("row"),
            P("row", "col"),
            P("row", "col"),
            P("col", "row"),
            P("row"),
            P(None, "row", "col"),
            P(None, "row", "col"),
            P(None, "col", "row"),
        ),
        check_vma=False,
    )
```

```python
import functools

import jax
import jax.numpy as jnp
from jax import lax
from jax.experimental import pallas as pl
from jax.experimental.pallas import tpu as pltpu
from jax.sharding import PartitionSpec as P

epsilon = 1e-06
rope_base = 1000000.0
head_dim = 128
low = jnp.bfloat16
full = jnp.float32


def dot(left, right, left_dim=1, right_dim=0):
    return lax.dot_general(
        left, right, (((left_dim,), (right_dim,)), ((), ())), preferred_element_type=full
    )


def remote_copy(source, target, send_sem, recv_sem, **device):
    return pltpu.make_async_remote_copy(
        src_ref=source,
        dst_ref=target,
        send_sem=send_sem,
        recv_sem=recv_sem,
        device_id=device,
        device_id_type=pl.DeviceIdType.MESH,
    )


def add_low(left, right):
    return (left.astype(full) + right.astype(full)).astype(low)


class ColSum:
    def __init__(self, stack, arrived, send_sem, recv_sem, col):
        self.stack, self.arrived, self.send_sem, self.recv_sem, self.col = (
            stack,
            arrived,
            send_sem,
            recv_sem,
            col,
        )
        self.last = stack.shape[0] - 1

    def copy(self, block, at, right):
        neighbour = at + 1 if right else at - 1
        slot = block if right or block != neighbour else self.last + 1
        return remote_copy(
            self.stack.at[block],
            self.arrived.at[slot],
            self.send_sem.at[block],
            self.recv_sem.at[slot],
            col=neighbour,
        )

    def wait(self, slot, at):
        remote_copy(
            self.arrived.at[slot],
            self.arrived.at[slot],
            self.send_sem.at[0],
            self.recv_sem.at[slot],
            col=at + 1 if at == 0 else at - 1,
        ).wait_recv()

    def step(self, number):
        for at in range(self.last + 1):

            @pl.when(self.col == at)
            def _(at=at):
                for right in (True, False):
                    block = at + self.last + 1 - number if right else at - self.last - 1 + number
                    if not 0 <= block <= self.last:
                        continue
                    if 0 < at < self.last:
                        self.wait(block, at)
                        self.stack[block] = add_low(self.stack[block], self.arrived[block])
                    self.copy(block, at, right).start()

    def total(self, part):
        for at in range(self.last + 1):

            @pl.when(self.col == at)
            def _(at=at):
                if at > 0:
                    self.wait(at, at)
                if at < self.last:
                    self.wait(self.last + 1, at)
                value = self.stack[at].astype(full)
                if at > 0:
                    value += self.arrived[at].astype(full)
                if at < self.last:
                    value += self.arrived[self.last + 1].astype(full)
                part(value)

    def end(self):
        for at in range(self.last + 1):

            @pl.when(self.col == at)
            def _(at=at):
                for block in range(self.last + 1):
                    if block != at:
                        self.copy(block, at, block > at).wait_send()


def experts_kernel(
    own_ref,
    cot_ref,
    table_ref,
    gate_hbm,
    up_hbm,
    down_hbm,
    sum_ref,
    out_part_ref,
    gate_total_ref,
    up_own_ref,
    up_row_ref,
    up_other_ref,
    down_half_ref,
    weights,
    expert_in,
    gate_grad,
    up_grad,
    hidden,
    send_stage,
    arrived,
    parts,
    stage,
    weights_sem,
    ready,
    ag_recv,
    ag_right,
    ag_left,
    rs_recv,
    rs_send,
    core_send,
    core_recv,
    row_send,
    row_recv,
    side_send,
    side_recv,
    final_sem,
    local_sem,
):
    row, col, dp = lax.axis_index("row"), lax.axis_index("col"), lax.axis_index("dp")
    dps = lax.axis_size("dp")
    core, other = dp % 2, 1 - row
    core_partner = dp + 1 - 2 * core
    side_bits = list(range(1, dps.bit_length() - 1))
    sides = len(side_bits)
    last = cot_ref.shape[0] - 1
    rows, width = own_ref.shape
    half = width // 2
    size = half // 2
    inner = (col > 0) & (col < last)

    def across(bit):
        on = (dp // (1 << bit)) % 2
        return dp + (1 << bit) * (1 - 2 * on)

    gate_ref, up_ref, down_ref = weights.at[0], weights.at[1], weights.at[2]
    loads = [
        pltpu.make_async_copy(source, weights.at[i], weights_sem.at[i])
        for i, source in enumerate((gate_hbm, up_hbm, down_hbm))
    ]
    for copy in loads:
        copy.start()

    barrier = pltpu.get_barrier_semaphore()

    def greet(semaphore, **device):
        pl.semaphore_signal(
            semaphore, inc=1, device_id=device, device_id_type=pl.DeviceIdType.MESH
        )

    greet(barrier, dp=core_partner)
    greet(barrier, row=other)
    for bit in side_bits:
        greet(barrier, dp=across(bit))
    pl.when(col > 0)(lambda: greet(barrier, col=col - 1))
    pl.when(col < last)(lambda: greet(barrier, col=col + 1))
    expert_in[col] = own_ref[...]
    pl.when(inner)(lambda: pl.semaphore_wait(barrier, 4 + sides))
    pl.when(jnp.logical_not(inner))(lambda: pl.semaphore_wait(barrier, 3 + sides))

    def ag_copy(block, right):
        return remote_copy(
            expert_in.at[block],
            expert_in.at[block],
            (ag_right if right else ag_left).at[block],
            ag_recv.at[block],
            col=col + 1 if right else col - 1,
        )

    def rs_copy(block, part, right):
        neighbour = col + 1 if right else col - 1
        slot = block if right else jnp.where(block == neighbour, last + 1, block)
        return remote_copy(
            send_stage.at[block, part],
            arrived.at[slot, part],
            rs_send.at[block, part],
            rs_recv.at[slot, part],
            col=neighbour,
        )

    def rs_wait(slot, part):
        remote_copy(
            arrived.at[slot, part],
            arrived.at[slot, part],
            rs_send.at[0, part],
            rs_recv.at[slot, part],
            col=jnp.where(col > 0, col - 1, col + 1),
        ).wait_recv()

    pl.when(col < last)(lambda: ag_copy(col, True).start())
    pl.when(col > 0)(lambda: ag_copy(col, False).start())
    for copy in loads:
        copy.wait()

    def compute(block):
        tokens = expert_in[block]
        grads = cot_ref[block]
        table = table_ref[block]
        experts = table.shape[1]
        units = width // experts
        for g in range(2):
            cols = slice(g * half, (g + 1) * half)
            gate = dot(tokens, gate_ref[:, cols])
            up = dot(tokens, up_ref[:, cols])
            grad = dot(grads, down_ref[cols, :], 1, 1)
            lane = lax.broadcasted_iota(jnp.int32, gate.shape, 1)
            first = g * experts // 2
            chosen = jnp.broadcast_to(table[:, first : first + 1], gate.shape)
            for e in range(1, experts // 2):
                chosen = jnp.where(lane >= e * units, table[:, first + e : first + e + 1], chosen)
            sigmoid = 1.0 / (1.0 + jnp.exp(-gate))
            silu = gate * sigmoid
            grad = grad * chosen
            hidden[block, :, cols] = (silu * up * chosen).astype(low)
            gate_grad[block, :, cols] = (
                grad * up * (sigmoid * (1.0 + gate * (1.0 - sigmoid)))
            ).astype(low)
            up_grad[block, :, cols] = (grad * silu).astype(low)
        gates_now, ups_now = gate_grad[block], up_grad[block]
        for part in range(2):
            cols = slice(part * half, (part + 1) * half)
            total = dot(gates_now, gate_ref[cols, :], 1, 1) + dot(ups_now, up_ref[cols, :], 1, 1)
            send_stage[block, part] = total.astype(low)
            pl.when((col == 0) & (block != col))(lambda: rs_copy(block, part, True).start())
            pl.when((col == last) & (block != col))(lambda: rs_copy(block, part, False).start())
        out_part_ref[block] = dot(hidden[block], down_ref[...]).astype(low)

    def step(i, carry):
        apart = (i + 1) // 2
        from_left = i % 2 == 1

        @pl.when(from_left & (col - apart >= 0))
        def _():
            block = col - apart
            ag_copy(block, True).wait_recv()
            pl.when(col < last)(lambda: ag_copy(block, True).start())

        @pl.when(from_left & (col + apart <= last))
        def _():
            block = col + apart
            ag_copy(block, False).wait_recv()
            pl.when(col > 0)(lambda: ag_copy(block, False).start())

        block = jnp.where(from_left, col - apart, col + apart)
        pl.when((block >= 0) & (block <= last))(lambda: compute(block))
        return carry

    lax.fori_loop(0, 2 * last + 1, step, 0)

    greet(ready.at[0], dp=core_partner)
    greet(ready.at[1], row=other)
    for number, bit in enumerate(side_bits):
        greet(ready.at[2 + number], dp=across(bit))

    def room(which, down, right):
        return weights.at[
            which, pl.ds(down * half, half), pl.ds(right * half, half)
        ]

    def forward(block, right):
        for part in range(2):
            rs_wait(block, part)
            send_stage[block, part] = add_low(send_stage[block, part], arrived[block, part])
            rs_copy(block, part, right).start()

    def event(number):
        blocks = ((2, 1), (3, 0), (0, 3))[number]
        pl.when(col == 1)(lambda: forward(blocks[0], number < 2))
        pl.when(col == 2)(lambda: forward(blocks[1], number == 2))

    def core_copy(at):
        if at < 4:
            target = room(at // 2, 0, at % 2)
        else:
            target = room(2, 0, at - 4)
        return remote_copy(
            stage.at[at % 2], target, core_send.at[at], core_recv.at[at], dp=core_partner
        )

    def stage_free(at):
        if at >= 2:
            core_copy(at - 2).wait_send()

    def half_lanes(which):
        return pl.ds(pl.multiple_of(which * half, half), half)

    def core_dot(at):
        right = (gate_grad, up_grad)[at // 2]
        left = expert_in[:, :, half_lanes(row if at % 2 else other)].reshape(-1, half)
        stage_free(at)
        stage[at % 2] = dot(
            left, right[:, :, half_lanes(1 - core)].reshape(-1, half), 0, 0
        ).astype(low)
        core_copy(at).start()
        parts[at] = dot(left, right[:, :, half_lanes(core)].reshape(-1, half), 0, 0).astype(low)

    def core_sum(at):
        core_copy(at).wait_recv()
        parts[at] = add_low(parts[at], room(at // 2, 0, at % 2)[...])

    def down_dot():
        left = hidden[:, :, half_lanes(1 - core)].reshape(-1, half)
        for part in range(2):
            lanes = slice(part * half, (part + 1) * half)
            right = cot_ref[:, :, lanes].reshape(-1, half)
            stage_free(4 + part)
            stage[part] = dot(left, right, 0, 0).astype(low)
            core_copy(4 + part).start()
        left = hidden[:, :, half_lanes(core)].reshape(-1, half)
        for part in range(2):
            lanes = slice(part * half, (part + 1) * half)
            right = cot_ref[:, :, lanes].reshape(-1, half)
            room(2, 1, part)[...] = dot(left, right, 0, 0).astype(low)

    def down_sum():
        for part in range(2):
            core_copy(4 + part).wait_recv()
            room(2, 1, part)[...] = add_low(room(2, 1, part)[...], room(2, 0, part)[...])

    down_out = pltpu.make_async_copy(
        weights.at[2, pl.ds(half, half)], down_half_ref, local_sem.at[0]
    )
    up_out = pltpu.make_async_copy(parts.at[3], up_own_ref, local_sem.at[1])
    up_rest = pltpu.make_async_copy(
        parts.at[2, pl.ds(size, size)], up_other_ref, local_sem.at[2]
    )

    def chunk_rows(chunk):
        return pl.ds(chunk * size, size)

    def row_copy(chunk):
        if chunk < 2:
            source = parts.at[0, chunk_rows(chunk)]
            target = weights.at[0, pl.ds(half + chunk * size, size), pl.ds(0, half)]
        else:
            source, target = parts.at[2, chunk_rows(0)], up_row_ref
        return remote_copy(source, target, row_send.at[chunk], row_recv.at[chunk], row=other)

    def side_room(number, chunk):
        which, right = ((0, 1), (1, 0), (1, 1))[number]
        return weights.at[
            which, pl.ds(half + chunk * size, size), pl.ds(right * half, half)
        ]

    def side_copy(chunk, number):
        return remote_copy(
            parts.at[1 - number % 2, chunk_rows(chunk)],
            side_room(number, chunk),
            side_send.at[chunk, number],
            side_recv.at[chunk, number],
            dp=across(side_bits[number]),
        )

    def after_row(chunk):
        copy = row_copy(chunk)
        copy.wait_recv()
        copy.wait_send()
        here = chunk_rows(chunk)
        landed = weights.at[0, pl.ds(half + chunk * size, size), pl.ds(0, half)]
        parts[1, here] = add_low(parts[1, here], landed[...])
        if sides:
            if chunk == 0:
                for number in range(sides):
                    pl.semaphore_wait(ready.at[2 + number], 1)
            side_copy(chunk, 0).start()

    def final_copies(chunk):
        source = parts.at[1 - sides % 2, chunk_rows(chunk)]
        target = gate_total_ref.at[chunk_rows(chunk), half_lanes(core)]
        return (
            remote_copy(
                source, target, final_sem.at[chunk, 0], final_sem.at[chunk, 1], dp=core_partner
            ),
            pltpu.make_async_copy(source, target, final_sem.at[chunk, 2]),
        )

    def after_side(chunk):
        here = chunk_rows(chunk)
        for number in range(sides):
            copy = side_copy(chunk, number)
            copy.wait_recv()
            copy.wait_send()
            parts[number % 2, here] = add_low(
                parts[1 - number % 2, here], side_room(number, chunk)[...]
            )
            if number + 1 < sides:
                side_copy(chunk, number + 1).start()
        for copy in final_copies(chunk):
            copy.start()

    pl.semaphore_wait(ready.at[0], 1)
    core_dot(0)
    core_dot(1)
    core_sum(0)
    pl.semaphore_wait(ready.at[1], 1)
    row_copy(0).start()
    row_copy(1).start()
    event(0)
    core_dot(2)
    core_sum(1)
    core_sum(2)
    row_copy(2).start()
    up_rest.start()
    core_dot(3)
    down_dot()
    core_sum(3)
    up_out.start()
    event(1)
    after_row(0)
    down_sum()
    down_out.start()
    event(2)
    after_row(1)

    for part in range(2):
        cols = slice(part * half, (part + 1) * half)
        sum_ref[:, cols] = send_stage[col, part].astype(full)

        @pl.when(col > 0)
        def _():
            rs_wait(col, part)
            sum_ref[:, cols] += arrived[col, part].astype(full)

        @pl.when(col < last)
        def _():
            rs_wait(last + 1, part)
            sum_ref[:, cols] += arrived[last + 1, part].astype(full)

    after_side(0)
    after_side(1)

    for block in range(last + 1):
        pl.when((block <= col) & (col < last))(lambda: ag_copy(block, True).wait_send())
        pl.when((block >= col) & (col > 0))(lambda: ag_copy(block, False).wait_send())
        for part in range(2):
            pl.when(block > col)(lambda: rs_copy(block, part, True).wait_send())
            pl.when(block < col)(lambda: rs_copy(block, part, False).wait_send())
    for at in range(4, 6):
        core_copy(at).wait_send()
    row_copy(2).wait()
    for copy in (down_out, up_out, up_rest):
        copy.wait()
    for chunk in range(2):
        remote, local = final_copies(chunk)
        remote.wait()
        local.wait()


def experts_call(own, cot, table, gate_all, up_all, down_all):
    rows, width = own.shape
    blocks, half = cot.shape[0], width // 2
    sides = lax.axis_size("dp").bit_length() - 2
    vmem = pl.BlockSpec(memory_space=pltpu.VMEM)
    anywhere = pl.BlockSpec(memory_space=pl.ANY)
    dma = pltpu.SemaphoreType.DMA
    shape = jax.ShapeDtypeStruct
    return pl.pallas_call(
        experts_kernel,
        in_specs=[vmem] * 3 + [anywhere] * 3,
        out_specs=[vmem, vmem] + [anywhere] * 5,
        out_shape=[
            shape((rows, width), full),
            shape((blocks, rows, width), low),
            shape((half, width), low),
            shape((half, half), low),
            shape((half // 2, half), low),
            shape((half // 2, half), low),
            shape((half, width), low),
        ],
        scratch_shapes=[pltpu.VMEM((3, width, width), low)]
        + [pltpu.VMEM((blocks, rows, width), low)] * 4
        + [
            pltpu.VMEM((blocks, 2, rows, half), low),
            pltpu.VMEM((blocks + 1, 2, rows, half), low),
            pltpu.VMEM((4, half, half), low),
            pltpu.VMEM((2, half, half), low),
            dma((3,)),
            pltpu.SemaphoreType.REGULAR((2 + max(sides, 1),)),
            dma((blocks,)),
            dma((blocks,)),
            dma((blocks,)),
            dma((blocks + 1, 2)),
            dma((blocks, 2)),
            dma((6,)),
            dma((6,)),
            dma((3,)),
            dma((3,)),
            dma((2, max(sides, 1))),
            dma((2, max(sides, 1))),
            dma((2, 3)),
            dma((3,)),
        ],
        compiler_params=pltpu.CompilerParams(
            collective_id=1, has_side_effects=True, vmem_limit_bytes=60 * 2**20
        ),
        cost_estimate=pl.CostEstimate(
            flops=9 * 2 * blocks * rows * width * width,
            bytes_accessed=12 * width * width,
            transcendentals=blocks * rows * width,
        ),
    )(own, cot, table, gate_all, up_all, down_all)


def prologue_kernel(
    inputs_ref,
    small_ref,
    theta_ref,
    routes_ref,
    route_gates_ref,
    query_hbm,
    keyval_hbm,
    output_hbm,
    gate_hbm,
    up_hbm,
    down_hbm,
    cot_hbm,
    normed_ref,
    scale_ref,
    mixer_ref,
    key_ref,
    value_ref,
    cosine_ref,
    sine_ref,
    start_ref,
    attended_ref,
    rot_ref,
    joint_ref,
    head_output_ref,
    middle_ref,
    expert_ref,
    table_ref,
    cot_all_ref,
    gate_all_ref,
    up_all_ref,
    down_all_ref,
    inputs_all,
    inputs_sem,
    small,
    small_sem,
    raw,
    raw_sem,
    flat,
    flat_sem,
    projected,
    branch_own,
    branch_stage,
    branch_arrived,
    branch_sem,
    pair_sem,
    joint_uni,
    joint_side,
    joint_core,
    output_uni,
    output_side,
    output_core,
    expert_row,
    expert_side,
    expert_core,
    cot_sem,
    cot_recv,
    cot_send,
    *,
    sequences,
):
    row, col, dp = lax.axis_index("row"), lax.axis_index("col"), lax.axis_index("dp")
    cols = lax.axis_size("col")
    last = cols - 1
    core, side, other = dp % 2, (dp // 2) % 2, 1 - row
    quarter = dp % 4
    core_partner, side_partner = dp + 1 - 2 * core, dp + 2 - 4 * side
    tokens, part_width = inputs_ref.shape
    width, rows = 2 * part_width, tokens // 2
    query_block, keyval_block = query_hbm.shape[1], keyval_hbm.shape[1]
    block = query_block + keyval_block
    experts, units = gate_hbm.shape[0], gate_hbm.shape[2]

    raws = [
        pltpu.make_async_copy(source, raw.at[i], raw_sem.at[i])
        for i, source in enumerate((gate_hbm, up_hbm))
    ]
    for copy in raws:
        copy.start()

    barrier = pltpu.get_barrier_semaphore()

    def greet(**device):
        pl.semaphore_signal(
            barrier, inc=1, device_id=device, device_id_type=pl.DeviceIdType.MESH
        )

    for there in range(1, 2 * cols):
        greet(row=(row + there // cols) % 2, col=(col + there % cols) % cols)
    greet(dp=core_partner)
    greet(dp=side_partner)

    def part_lanes(which):
        return pl.ds(pl.multiple_of(which * part_width, 128), part_width)

    inputs_all[:, part_lanes(row)] = inputs_ref[...]
    small[row] = small_ref[...]
    pl.semaphore_wait(barrier, 2 * cols + 1)

    inputs_copy = remote_copy(
        inputs_ref,
        inputs_all.at[:, part_lanes(row)],
        inputs_sem.at[0],
        inputs_sem.at[1],
        row=other,
    )
    small_copy = remote_copy(
        small.at[row], small.at[row], small_sem.at[0], small_sem.at[1], row=other
    )
    inputs_copy.start()
    small_copy.start()

    joint_size, output_size = query_hbm.shape[0] // 4, output_hbm.shape[0] // 4

    def joint_region(r0, b, which):
        return joint_ref.at[
            pl.ds(pl.multiple_of(r0 * part_width + which * joint_size, 16), joint_size),
            pl.ds(pl.multiple_of(b * block, 128), block),
        ]

    def output_region(r0, b, which):
        return head_output_ref.at[
            pl.ds(pl.multiple_of(b * query_block + which * output_size, 16), output_size),
            part_lanes(r0),
        ]

    def own_joint():
        b = col % 2
        first = pl.ds(pl.multiple_of(quarter * joint_size, 16), joint_size)
        at = pl.ds(pl.multiple_of(row * part_width + quarter * joint_size, 16), joint_size)
        return (
            (
                query_hbm.at[first],
                joint_ref.at[at, pl.ds(pl.multiple_of(b * block, 128), query_block)],
            ),
            (
                keyval_hbm.at[first],
                joint_ref.at[
                    at, pl.ds(pl.multiple_of(b * block + query_block, 128), keyval_block)
                ],
            ),
        )

    def own_output():
        first = pl.ds(pl.multiple_of(quarter * output_size, 16), output_size)
        return ((output_hbm.at[first], output_region(row, col % 2, quarter)),)

    def spread(pieces, sems):
        def copies(k):
            to_row, to_col = col // 2, (2 * row + col % 2 + k) % cols
            return [
                remote_copy(
                    source, target, sems.at[k, 2 * n], sems.at[k, 2 * n + 1], row=to_row, col=to_col
                )
                for n, (source, target) in enumerate(pieces)
            ]

        def here():
            return [
                pltpu.make_async_copy(source, target, sems.at[0, 2 * n + 1])
                for n, (source, target) in enumerate(pieces)
            ]

        home = col // 2 == row

        def start():
            for k in range(cols):
                if k == 0:

                    @pl.when(home)
                    def _():
                        for copy in here():
                            copy.start()

                    @pl.when(jnp.logical_not(home))
                    def _():
                        for copy in copies(0):
                            copy.start()

                else:
                    for copy in copies(k):
                        copy.start()

        def wait_recv(k):
            if k == 0:

                @pl.when(home)
                def _():
                    for copy in here():
                        copy.wait()

                @pl.when(jnp.logical_not(home))
                def _():
                    for copy in copies(0):
                        copy.wait_recv()

            else:
                for copy in copies(k):
                    copy.wait_recv()

        def wait_send():
            for k in range(cols):
                if k == 0:

                    @pl.when(jnp.logical_not(home))
                    def _():
                        for copy in copies(0):
                            copy.wait_send()

                else:
                    for copy in copies(k):
                        copy.wait_send()

        return start, wait_recv, wait_send

    def came_from(k):
        j = (col - k + cols) % cols
        return j // 2, j % 2

    def relay(region, side_sems, core_sems):
        def side_copy(k):
            there = region(*came_from(k), quarter)
            return remote_copy(
                there, there, side_sems.at[k, 0], side_sems.at[k, 1], dp=side_partner
            )

        def core_copies(k):
            result = []
            for n in range(2):
                there = region(*came_from(k), core + 2 * n)
                result.append(
                    remote_copy(
                        there,
                        there,
                        core_sems.at[k, 2 * n],
                        core_sems.at[k, 2 * n + 1],
                        dp=core_partner,
                    )
                )
            return result

        return side_copy, core_copies

    joint_start, joint_wait, joint_sent = spread(own_joint(), joint_uni)
    output_start, output_wait, output_sent = spread(own_output(), output_uni)
    joint_side_copy, joint_core_copies = relay(joint_region, joint_side, joint_core)
    output_side_copy, output_core_copies = relay(output_region, output_side, output_core)
    joint_start()

    expert_size = part_width // 4
    down_size = down_hbm.shape[0] // 4

    def flatten(which):
        raws[which].wait()
        for e in range(0, experts, 2):
            flat[which, :, e * units : (e + 2) * units] = jnp.concatenate(
                [raw[which, e], raw[which, e + 1]], axis=1
            )

    totals = (gate_all_ref, up_all_ref, down_all_ref)

    def expert_region(which, of_row, of_quarter):
        if which < 2:
            first = pl.multiple_of(of_row * part_width + of_quarter * expert_size, 16)
            return totals[which].at[pl.ds(first, expert_size)]
        first = pl.multiple_of(of_quarter * down_size, 16)
        return totals[2].at[pl.ds(first, down_size), part_lanes(of_row)]

    def expert_local(which):
        if which < 2:
            target = totals[which].at[pl.ds(pl.multiple_of(row * part_width, 16), part_width)]
            return pltpu.make_async_copy(flat.at[which], target, flat_sem.at[which])
        return pltpu.make_async_copy(down_hbm, totals[2].at[:, part_lanes(row)], flat_sem.at[2])

    def expert_row_copy(which):
        if which < 2:
            source = flat.at[which, pl.ds(pl.multiple_of(quarter * expert_size, 16), expert_size)]
        else:
            source = down_hbm.at[pl.ds(pl.multiple_of(quarter * down_size, 16), down_size)]
        return remote_copy(
            source,
            expert_region(which, row, quarter),
            expert_row.at[which, 0],
            expert_row.at[which, 1],
            row=other,
        )

    def expert_side_copy(which):
        there = expert_region(which, other, quarter)
        return remote_copy(
            there, there, expert_side.at[which, 0], expert_side.at[which, 1], dp=side_partner
        )

    def expert_core_copies(which):
        result = []
        for n in range(2):
            there = expert_region(which, other, core + 2 * n)
            result.append(
                remote_copy(
                    there,
                    there,
                    expert_core.at[which, 2 * n],
                    expert_core.at[which, 2 * n + 1],
                    dp=core_partner,
                )
            )
        return result

    def expert_after_row(which):
        expert_row_copy(which).wait_recv()
        expert_side_copy(which).start()

    def expert_after_side(which):
        expert_side_copy(which).wait_recv()
        for copy in expert_core_copies(which):
            copy.start()

    def token_rows(which):
        return pl.ds(pl.multiple_of(which * rows, 16), rows)

    cot_target = cot_all_ref.at[col, :, part_lanes(row)]
    cot_local = pltpu.make_async_copy(cot_hbm.at[token_rows(row)], cot_target, cot_sem.at[0])
    cot_row = remote_copy(
        cot_hbm.at[token_rows(other)], cot_target, cot_sem.at[1], cot_sem.at[2], row=other
    )

    def cot_copy(block_at, right):
        return remote_copy(
            cot_all_ref.at[block_at],
            cot_all_ref.at[block_at],
            cot_send.at[block_at, 1 if right else 0],
            cot_recv.at[block_at],
            col=col + 1 if right else col - 1,
        )

    def cot_first():
        cot_local.wait()
        cot_row.wait_recv()
        pl.when(col < last)(lambda: cot_copy(col, True).start())
        pl.when(col > 0)(lambda: cot_copy(col, False).start())

    def cot_pass(apart):
        @pl.when(col - apart >= 0)
        def _():
            cot_copy(col - apart, True).wait_recv()
            pl.when(col < last)(lambda: cot_copy(col - apart, True).start())

        @pl.when(col + apart <= last)
        def _():
            cot_copy(col + apart, False).wait_recv()
            pl.when(col > 0)(lambda: cot_copy(col + apart, False).start())

    cot_local.start()
    expert_local(2).start()

    for at in range(cols):
        place = pl.ds(pl.multiple_of(at * tokens + row * rows, 16), rows)
        chosen, gates = routes_ref[place, :], route_gates_ref[place, :]
        lane = lax.broadcasted_iota(jnp.int32, (rows, experts), 1)
        table = jnp.zeros((rows, experts), full)
        for k in range(chosen.shape[1]):
            table += jnp.where(chosen[:, k : k + 1] == lane, gates[:, k : k + 1], 0.0)
        table_ref[at] = table

    for which in range(2):
        flatten(which)
        expert_local(which).start()

    small_copy.wait_recv()
    mixer_ref[:, :part_width] = small[0, 1:2, :]
    mixer_ref[:, part_width:] = small[1, 1:2, :]
    half = col // 2
    lens = small[half, 2:3, :]
    odd = (col % 2).astype(full)
    place = lax.broadcasted_iota(jnp.int32, (tokens, 1), 0).astype(full) + odd * tokens
    begin = jnp.zeros((tokens, 1), full)
    total = lens[:, 0:1]
    for n in range(1, sequences):
        begin = jnp.where(place >= total, total, begin)
        total = total + lens[:, n : n + 1]
    start_ref[...] = begin + (1.0 - odd) * tokens
    angles = (place - begin) * theta_ref[...]
    cosine_ref[...] = jnp.cos(angles)
    sine = jnp.sin(angles)
    lane = lax.broadcasted_iota(jnp.int32, sine.shape, 1)
    sine_ref[...] = jnp.where(lane < head_dim // 2, -sine, sine)

    for k in range(cols):
        joint_wait(k)
        joint_side_copy(k).start()
    inputs_copy.wait_recv()
    cot_row.start()
    output_start()
    expert_row_copy(0).start()

    piece = 64

    def norm_piece(at, carry):
        here = pl.ds(pl.multiple_of(at * piece, piece), piece)
        values = inputs_all[here, :].astype(full)
        scale = lax.rsqrt(jnp.mean(values * values, axis=1, keepdims=True) + epsilon)
        scale_ref[here, :] = scale
        for which in range(2):
            lanes = slice(which * part_width, (which + 1) * part_width)
            normed_ref[here, lanes] = (values[:, lanes] * scale * small[which, 0:1, :]).astype(low)
        return carry

    lax.fori_loop(0, tokens // piece, norm_piece, 0)
    for k in range(cols):
        joint_side_copy(k).wait_recv()
        for copy in joint_core_copies(k):
            copy.start()
    expert_row_copy(1).start()
    for k in range(cols):
        for copy in joint_core_copies(k):
            copy.wait_recv()

    projected[...] = dot(normed_ref[...], joint_ref[...])
    own = slice(tokens, 2 * tokens)
    key = projected[:, query_block : query_block + head_dim]
    key_ref[own, :] = (
        key * cosine_ref[...] + pltpu.roll(key, head_dim // 2, 1) * sine_ref[...]
    ).astype(low)
    value_ref[own, :] = projected[:, block + query_block : block + query_block + head_dim].astype(low)

    def pair_copies():
        return [
            remote_copy(
                ref.at[pl.ds(tokens, tokens)],
                ref.at[pl.ds(0, tokens)],
                pair_sem.at[n, 0],
                pair_sem.at[n, 1],
                col=col + 1 - 2 * (col % 2),
            )
            for n, ref in enumerate((key_ref, value_ref))
        ]

    @pl.when(col % 2 == 0)
    def _():
        for copy in pair_copies():
            copy.start()
        key_ref[:tokens, :] = jnp.zeros((tokens, head_dim), low)
        value_ref[:tokens, :] = jnp.zeros((tokens, head_dim), low)

    for k in range(cols):
        output_wait(k)
        output_side_copy(k).start()
    cot_first()
    expert_row_copy(2).start()

    @pl.when(col % 2 == 1)
    def _():
        for copy in pair_copies():
            copy.wait_recv()

    heads = 2 * query_block // head_dim
    per_block = heads // 2
    tile = tokens // 2
    window = key_ref.shape[0] - tile

    def head_step(head, carry):
        here = pl.ds(pl.multiple_of(head * head_dim, head_dim), head_dim)
        there = pl.ds(
            pl.multiple_of((head + head // per_block) * head_dim, head_dim), head_dim
        )
        pre = projected[:, there]
        rot = (pre * cosine_ref[...] + pltpu.roll(pre, head_dim // 2, 1) * sine_ref[...]).astype(low)
        rot_ref[:, here] = rot
        for at in range(tokens // tile):
            first = at * tile
            keys = key_ref[first : first + window, :]
            values = value_ref[first : first + window, :]
            scores = dot(rot[first : first + tile], keys, 1, 1) * head_dim ** (-0.5)
            key_place = lax.broadcasted_iota(jnp.int32, scores.shape, 1) + first
            query_place = lax.broadcasted_iota(jnp.int32, scores.shape, 0) + (first + tokens)
            allowed = (key_place <= query_place) & (
                key_place.astype(full) >= start_ref[first : first + tile, :]
            )
            scores = jnp.where(allowed, scores, -1e30)
            exponent = jnp.exp(scores - jnp.max(scores, axis=1, keepdims=True))
            weights = exponent / jnp.sum(exponent, axis=1, keepdims=True)
            attended_ref[first : first + tile, here] = dot(weights.astype(low), values).astype(low)
        return carry

    lax.fori_loop(0, heads, head_step, 0)

    for k in range(cols):
        output_side_copy(k).wait_recv()
        for copy in output_core_copies(k):
            copy.start()
    expert_after_row(0)
    cot_pass(1)
    for k in range(cols):
        for copy in output_core_copies(k):
            copy.wait_recv()

    def branch_copy(part):
        return remote_copy(
            branch_stage.at[part],
            branch_arrived.at[part],
            branch_sem.at[part, 0],
            branch_sem.at[part, 1],
            row=other,
        )

    theirs = attended_ref[token_rows(other), :]
    for part in range(2):
        lanes = slice(part * part_width, (part + 1) * part_width)
        branch_stage[part] = dot(theirs, head_output_ref[:, lanes]).astype(low)
        branch_copy(part).start()
    mine = attended_ref[token_rows(row), :]
    branch_own[...] = dot(mine, head_output_ref[...])
    expert_after_row(1)
    expert_after_side(0)
    cot_pass(2)
    expert_after_row(2)
    for part in range(2):
        lanes = slice(part * part_width, (part + 1) * part_width)
        branch_copy(part).wait_recv()
        middle_ref[:, lanes] = (
            inputs_all[token_rows(row), lanes].astype(full)
            + branch_own[:, lanes]
            + branch_arrived[part].astype(full)
        )

    def second_piece(at, carry):
        here = pl.ds(pl.multiple_of(at * piece, piece), piece)
        values = middle_ref[here, :]
        scale = lax.rsqrt(jnp.mean(values * values, axis=1, keepdims=True) + epsilon)
        expert_ref[here, :] = (values * scale * mixer_ref[...]).astype(low)
        return carry

    lax.fori_loop(0, rows // piece, second_piece, 0)
    expert_after_side(1)
    cot_pass(3)
    expert_after_side(2)

    inputs_copy.wait_send()
    small_copy.wait_send()
    joint_sent()
    output_sent()
    for k in range(cols):
        for copy in [joint_side_copy(k), output_side_copy(k)]:
            copy.wait_send()
        for copy in joint_core_copies(k) + output_core_copies(k):
            copy.wait_send()
    for which in range(3):
        expert_local(which).wait()
        expert_row_copy(which).wait_send()
        expert_side_copy(which).wait_send()
        for copy in expert_core_copies(which):
            copy.wait()
    cot_row.wait_send()
    for at in range(cols):
        pl.when((at <= col) & (col < last))(lambda: cot_copy(at, True).wait_send())
        pl.when((at >= col) & (col > 0))(lambda: cot_copy(at, False).wait_send())

    @pl.when(col % 2 == 0)
    def _():
        for copy in pair_copies():
            copy.wait_send()

    for part in range(2):
        branch_copy(part).wait_send()


def prologue_call(
    inputs, small, theta, routes, route_gates, query_weight, key_value_matrix, output_weight,
    gate_weight, up_weight, down_flat, cotangent, sequences,
):
    tokens, part_width = inputs.shape
    cols = lax.axis_size("col")
    width, rows = 2 * part_width, tokens // 2
    query_block, keyval_block = query_weight.shape[1], key_value_matrix.shape[1]
    block = query_block + keyval_block
    experts, _, units = gate_weight.shape
    hidden = experts * units
    vmem = pl.BlockSpec(memory_space=pltpu.VMEM)
    anywhere = pl.BlockSpec(memory_space=pl.ANY)
    dma = pltpu.SemaphoreType.DMA
    shape = jax.ShapeDtypeStruct
    return pl.pallas_call(
        functools.partial(prologue_kernel, sequences=sequences),
        in_specs=[vmem] * 5 + [anywhere] * 7,
        out_specs=[vmem] * 15 + [anywhere] * 4,
        out_shape=[
            shape((tokens, width), low),
            shape((tokens, 1), full),
            shape((1, width), full),
            shape((2 * tokens, head_dim), low),
            shape((2 * tokens, head_dim), low),
            shape((tokens, head_dim), full),
            shape((tokens, head_dim), full),
            shape((tokens, 1), full),
            shape((tokens, 2 * query_block), low),
            shape((tokens, 2 * query_block), low),
            shape((width, 2 * block), low),
            shape((2 * query_block, width), low),
            shape((rows, width), full),
            shape((rows, width), low),
            shape((cols, rows, experts), full),
            shape((cols, rows, width), low),
            shape((width, hidden), low),
            shape((width, hidden), low),
            shape((hidden, width), low),
        ],
        scratch_shapes=[
            pltpu.VMEM((tokens, width), low),
            dma((2,)),
            pltpu.VMEM((2,) + small.shape, full),
            dma((2,)),
            pltpu.VMEM((2,) + gate_weight.shape, low),
            dma((2,)),
            pltpu.VMEM((2, part_width, hidden), low),
            dma((3,)),
            pltpu.VMEM((tokens, 2 * block), full),
            pltpu.VMEM((rows, width), full),
            pltpu.VMEM((2, rows, part_width), low),
            pltpu.VMEM((2, rows, part_width), low),
            dma((2, 2)),
            dma((2, 2)),
            dma((cols, 4)),
            dma((cols, 2)),
            dma((cols, 4)),
            dma((cols, 2)),
            dma((cols, 2)),
            dma((cols, 4)),
            dma((3, 2)),
            dma((3, 2)),
            dma((3, 4)),
            dma((3,)),
            dma((cols,)),
            dma((cols, 2)),
        ],
        compiler_params=pltpu.CompilerParams(
            collective_id=3, has_side_effects=True, vmem_limit_bytes=60 * 2**20
        ),
        cost_estimate=pl.CostEstimate(
            flops=5 * 10**9, bytes_accessed=30 * 10**6, transcendentals=3 * 10**6
        ),
    )(
        inputs, small, theta, routes, route_gates, query_weight, key_value_matrix, output_weight,
        gate_weight, up_weight, down_flat, cotangent,
    )


def finish_kernel(
    sum_ref,
    middle_ref,
    cot_ref,
    mixer_ref,
    gain_ref,
    scale_ref,
    inputs_ref,
    attended_ref,
    rot_ref,
    key_ref,
    value_ref,
    cosine_ref,
    sine_ref,
    start_ref,
    head_output_ref,
    joint_ref,
    normed_ref,
    out_part_ref,
    up_own_ref,
    up_row_ref,
    up_other_ref,
    down_half_ref,
    outputs_ref,
    input_grad_ref,
    gains_ref,
    output_total_ref,
    joint_total_ref,
    up_total_ref,
    down_total_ref,
    item_side,
    branch,
    branch_sem,
    out_stack,
    out_arrived,
    out_load,
    out_send,
    out_recv,
    own_out_sem,
    grad_heads,
    joint_grad,
    key_grad,
    value_grad,
    pair_stage,
    pair_arrived,
    pair_sem,
    normed_arrived,
    normed_own,
    normed_sem,
    inner_stage,
    inner_arrived,
    inner_sem,
    sums,
    sums_arrived,
    sums_sem,
    item_mine,
    item_other,
    item_row,
    item_sem,
    item_load_sem,
    wo_parts,
    wo_core,
    wo_row,
    wo_stack,
    wo_arrived,
    wo_side,
    wo_sem,
    wo_send,
    wo_recv,
    wa_parts,
    wa_core,
    wa_row,
    wa_stack,
    wa_arrived,
    wa_side,
    wa_sem,
    wa_send,
    wa_recv,
):
    row, col, dp = lax.axis_index("row"), lax.axis_index("col"), lax.axis_index("dp")
    cols, dps = lax.axis_size("col"), lax.axis_size("dp")
    core, other = dp % 2, 1 - row
    core_partner = dp + 1 - 2 * core
    side_bits = [bit for bit in range(1, dps.bit_length() - 1)]

    def across(bit):
        on = (dp // (1 << bit)) % 2
        return dp + (1 << bit) * (1 - 2 * on)

    rows, width = middle_ref.shape
    tokens, part_width = inputs_ref.shape
    heads = attended_ref.shape[1] // head_dim
    per_block = heads // 2

    barrier = pltpu.get_barrier_semaphore()

    def greet(**device):
        pl.semaphore_signal(
            barrier, inc=1, device_id=device, device_id_type=pl.DeviceIdType.MESH
        )

    greet(row=other)
    for apart in range(1, cols):
        greet(col=(col + apart) % cols)
    greet(dp=core_partner)
    for bit in side_bits:
        greet(dp=across(bit))

    out_copy = pltpu.make_async_copy(out_part_ref, out_stack, out_load)
    out_copy.start()
    size = item_mine.shape[1]
    items = item_mine.shape[0]

    def item_loads(at):
        chunk = at % 2
        place = pl.ds(chunk * size, size)
        if at < 2:
            sources = (up_own_ref.at[place], (up_row_ref, up_other_ref)[chunk])
        else:
            sources = [
                down_half_ref.at[place, pl.ds(pl.multiple_of(which * part_width, 128), part_width)]
                for which in (row, other)
            ]
        targets = (item_mine.at[at], item_row.at[at] if at == 0 else item_other.at[at])
        return [
            pltpu.make_async_copy(source, target, item_load_sem.at[at, number])
            for number, (source, target) in enumerate(zip(sources, targets))
        ]

    for at in range(items):
        for copy in item_loads(at):
            copy.start()

    pl.semaphore_wait(barrier, cols + 1 + len(side_bits))

    sums[0] = jnp.zeros_like(sums[0])
    piece = 64

    def norm_piece(at, mixer_sum):
        place = pl.ds(pl.multiple_of(at * piece, piece), piece)
        middle = middle_ref[place, :]
        second = sum_ref[place, :]
        scale = lax.rsqrt(jnp.mean(middle * middle, axis=1, keepdims=True) + epsilon)
        weighted = mixer_ref[...] * second
        inner = jnp.sum(weighted * middle, axis=1, keepdims=True)
        grad = (
            cot_ref[place, :].astype(full)
            + scale * weighted
            - middle * (scale * scale * scale) * (inner / width)
        )
        branch[row, place, :] = grad.astype(low)
        return mixer_sum + jnp.sum(second * middle * scale, axis=0, keepdims=True)

    mixer_sum = lax.fori_loop(0, rows // piece, norm_piece, jnp.zeros((1, width), full))
    sums[0, 1:2, :] = mixer_sum
    branch_copy = remote_copy(
        branch.at[row], branch.at[row], branch_sem.at[0], branch_sem.at[1], row=other
    )
    branch_copy.start()

    outs = ColSum(out_stack, out_arrived, out_send, out_recv, col)
    out_copy.wait()
    outs.step(1)
    for at in range(items):
        for copy in item_loads(at):
            copy.wait()

    def item_row_copy(at):
        return remote_copy(
            item_other.at[at], item_row.at[at], item_sem.at[at, 0], item_sem.at[at, 1], row=other
        )

    def item_side_copy(at, number):
        source = item_mine if number % 2 == 0 else item_other
        return remote_copy(
            source.at[at],
            item_side.at[at, number],
            item_sem.at[at, 2 + 2 * number],
            item_sem.at[at, 3 + 2 * number],
            dp=across(side_bits[number]),
        )

    last_side = len(side_bits)

    def item_value(at):
        return item_mine if last_side % 2 == 0 else item_other

    def item_places(at):
        which, chunk = at // 2, at % 2
        total = (up_total_ref, down_total_ref)[which]
        if which < 1:
            lanes = pl.ds(pl.multiple_of(core * part_width, 128), part_width)
            return total.at[pl.ds(chunk * size, size), lanes]
        return total.at[pl.ds(pl.multiple_of(core * part_width + chunk * size, 128), size), :]

    def item_core_copies(at):
        source, target = item_value(at).at[at], item_places(at)
        base = 2 + 2 * last_side
        return (
            remote_copy(
                source, target, item_sem.at[at, base], item_sem.at[at, base + 1], dp=core_partner
            ),
            pltpu.make_async_copy(source, target, item_sem.at[at, base + 2]),
        )

    def item_after_row(at):
        if at > 0:
            copy = item_row_copy(at)
            copy.wait_recv()
            copy.wait_send()
        item_mine[at] = add_low(item_mine[at], item_row[at])
        if last_side:
            item_side_copy(at, 0).start()

    def item_after_side(at):
        for number in range(last_side):
            copy = item_side_copy(at, number)
            copy.wait_recv()
            landed = pltpu.make_async_copy(
                item_side.at[at, number], item_row.at[at], item_load_sem.at[at, 0]
            )
            landed.start()
            copy.wait_send()
            landed.wait()
            source = item_mine if number % 2 == 0 else item_other
            target = item_other if number % 2 == 0 else item_mine
            target[at] = add_low(source[at], item_row[at])
            if number + 1 < last_side:
                item_side_copy(at, number + 1).start()
        for copy in item_core_copies(at):
            copy.start()

    def item_end(at):
        remote, local = item_core_copies(at)
        remote.wait_recv()
        remote.wait_send()
        local.wait()

    item_after_row(0)

    branch_copy.wait_recv()
    branch_all = branch[...].reshape(tokens, width)
    half_lanes = heads * head_dim // 2
    for part in range(2):
        lanes = slice(part * half_lanes, (part + 1) * half_lanes)
        grad_heads[:, lanes] = dot(branch_all, head_output_ref[lanes, :], 1, 1).astype(low)
    item_row_copy(1).start()

    wo_size = wo_parts.shape[2]
    for b in range(2):
        lanes = slice(b * half_lanes, (b + 1) * half_lanes)
        value = dot(attended_ref[:, lanes], branch_all, 0, 0).astype(low)
        for part in range(2):
            wo_parts[b, part] = value[part * wo_size : (part + 1) * wo_size, :]

    def wo_core_copy(b):
        return remote_copy(
            wo_parts.at[b, 1 - core], wo_core.at[b], wo_sem.at[0, b], wo_sem.at[1, b], dp=core_partner
        )

    for b in range(2):
        wo_core_copy(b).start()
    outs.step(2)

    key_grad[...] = jnp.zeros_like(key_grad)
    value_grad[...] = jnp.zeros_like(value_grad)
    tile = tokens // 2
    window = key_ref.shape[0] - tile

    def head_step(head, carry):
        here = pl.ds(pl.multiple_of(head * head_dim, head_dim), head_dim)
        there = pl.ds(
            pl.multiple_of((head + head // per_block) * head_dim, head_dim), head_dim
        )
        for at in range(tokens // tile):
            first = at * tile
            rot = rot_ref[first : first + tile, here]
            grad = grad_heads[first : first + tile, here]
            keys = key_ref[first : first + window, :]
            values = value_ref[first : first + window, :]
            scores = dot(rot, keys, 1, 1) * head_dim ** (-0.5)
            place = lax.broadcasted_iota(jnp.int32, scores.shape, 1) + first
            query = lax.broadcasted_iota(jnp.int32, scores.shape, 0) + (first + tokens)
            allowed = (place <= query) & (place.astype(full) >= start_ref[first : first + tile, :])
            scores = jnp.where(allowed, scores, -1e30)
            exponent = jnp.exp(scores - jnp.max(scores, axis=1, keepdims=True))
            probs = exponent / jnp.sum(exponent, axis=1, keepdims=True)
            prob_grad = dot(grad, values, 1, 1)
            inner = jnp.sum(probs * prob_grad, axis=1, keepdims=True)
            score_grad = (probs * (prob_grad - inner) * head_dim ** (-0.5)).astype(low)
            rot_grad = dot(score_grad, keys)
            joint_grad[first : first + tile, there] = (
                rot_grad * cosine_ref[first : first + tile, :]
                - pltpu.roll(rot_grad, head_dim // 2, 1) * sine_ref[first : first + tile, :]
            ).astype(low)
            key_grad[first : first + window, :] += dot(score_grad, rot, 0, 0)
            value_grad[first : first + window, :] += dot(probs.astype(low), grad, 0, 0)
        return carry

    lax.fori_loop(0, heads, head_step, 0)

    pair_stage[:, :head_dim] = key_grad[:tokens, :].astype(low)
    pair_stage[:, head_dim:] = value_grad[:tokens, :].astype(low)
    odd = col % 2 == 1

    def pair_copy():
        return remote_copy(
            pair_stage, pair_arrived, pair_sem.at[0], pair_sem.at[1], col=col + 1 - 2 * (col % 2)
        )

    pl.when(odd)(lambda: pair_copy().start())

    def wo_row_copy(b):
        lanes = pl.ds(pl.multiple_of(other * part_width, 128), part_width)
        return remote_copy(
            wo_parts.at[b, core, :, lanes],
            wo_row.at[b],
            wo_sem.at[2, b],
            wo_sem.at[3, b],
            row=other,
        )

    for b in range(2):
        wo_core_copy(b).wait_recv()
        wo_parts[b, core] = add_low(wo_parts[b, core], wo_core[b])
        wo_row_copy(b).start()
    item_after_row(1)

    @pl.when(jnp.logical_not(odd))
    def _():
        pair_copy().wait_recv()
        key_grad[tokens:, :] += pair_arrived[:, :head_dim].astype(full)
        value_grad[tokens:, :] += pair_arrived[:, head_dim:].astype(full)

    key_total = key_grad[tokens:, :]
    key_lanes = slice(per_block * head_dim, (per_block + 1) * head_dim)
    value_lanes = slice((2 * per_block + 1) * head_dim, (2 * per_block + 2) * head_dim)
    joint_grad[:, key_lanes] = (
        key_total * cosine_ref[...] - pltpu.roll(key_total, head_dim // 2, 1) * sine_ref[...]
    ).astype(low)
    joint_grad[:, value_lanes] = value_grad[tokens:, :].astype(low)

    wa_size = wa_core.shape[1]

    def wa_core_copy(r0):
        return remote_copy(
            wa_parts.at[r0, 1 - core], wa_core.at[r0], wa_sem.at[0, r0], wa_sem.at[1, r0], dp=core_partner
        )

    def wa_dot(r0, which):
        first = pl.multiple_of(r0 * part_width + which * wa_size, 128)
        wa_parts[r0, which] = dot(
            normed_ref[:, pl.ds(first, wa_size)], joint_grad[...], 0, 0
        ).astype(low)

    wa_dot(other, 1 - core)
    wa_core_copy(other).start()
    wa_dot(row, 1 - core)
    wa_core_copy(row).start()
    wa_dot(other, core)
    wa_dot(row, core)
    chunk_rows = wa_size // 2

    def wa_row_copy(chunk):
        return remote_copy(
            wa_parts.at[other, core, pl.ds(chunk * chunk_rows, chunk_rows)],
            wa_row.at[chunk],
            wa_sem.at[2, chunk],
            wa_sem.at[3, chunk],
            row=other,
        )

    wa_core_copy(other).wait_recv()
    wa_parts[other, core] = add_low(wa_parts[other, core], wa_core[other])
    for chunk in range(2):
        wa_row_copy(chunk).start()

    def normed_dot(which):
        place = pl.ds(pl.multiple_of(which * part_width, 128), part_width)
        return dot(joint_grad[...], joint_ref[place, :], 1, 1)

    normed_stage = grad_heads
    normed_stage[...] = normed_dot(other).astype(low)
    normed_copy = remote_copy(
        normed_stage, normed_arrived, normed_sem.at[0], normed_sem.at[1], row=other
    )
    normed_copy.start()
    normed_own[...] = normed_dot(row)
    wa_core_copy(row).wait_recv()
    wa_parts[row, core] = add_low(wa_parts[row, core], wa_core[row])

    wo_total = ColSum(wo_stack, wo_arrived, wo_send, wo_recv, col)
    for b in range(2):
        wo_row_copy(b).wait_recv()
        lanes = pl.ds(pl.multiple_of(row * part_width, 128), part_width)
        wo_stack[2 * row + b] = wo_parts[b, core, :, lanes]
        wo_stack[2 * other + b] = wo_row[b]
    wo_total.step(1)
    item_after_side(0)
    item_row_copy(2).start()
    outs.step(3)
    wo_total.step(2)

    wa_total = [
        ColSum(wa_stack.at[c], wa_arrived.at[c], wa_send.at[c], wa_recv.at[c], col)
        for c in range(2)
    ]
    block_lanes = wa_stack.shape[3]
    for chunk in range(2):
        wa_row_copy(chunk).wait_recv()
        place = pl.ds(chunk * chunk_rows, chunk_rows)
        for b in range(2):
            lanes = slice(b * block_lanes, (b + 1) * block_lanes)
            wa_stack[chunk, 2 * row + b] = wa_parts[row, core, place, lanes]
            wa_stack[chunk, 2 * other + b] = wa_row[chunk, :, lanes]
        wa_total[chunk].step(1)
    wo_total.step(3)
    for chunk in range(2):
        wa_total[chunk].step(2)

    normed_copy.wait_recv()
    scale = scale_ref[...]
    normed_own[...] += normed_arrived[...].astype(full)
    inner = jnp.sum(
        gain_ref[...] * normed_own[...] * inputs_ref[...].astype(full), axis=1, keepdims=True
    )
    inner_stage[...] = jnp.transpose(jnp.broadcast_to(inner, (tokens, head_dim)))[:8, :]
    inner_copy = remote_copy(
        inner_stage, inner_arrived, inner_sem.at[0], inner_sem.at[1], row=other
    )
    inner_copy.start()
    for chunk in range(2):
        wa_total[chunk].step(3)
    sums[0, 0:1, pl.ds(pl.multiple_of(row * part_width, 128), part_width)] = jnp.sum(
        normed_own[...] * inputs_ref[...].astype(full) * scale, axis=0, keepdims=True
    )
    inner_copy.wait_recv()
    both = inner_stage[...] + inner_arrived[...]
    inner = jnp.transpose(jnp.concatenate([both] * (head_dim // 8), axis=0))[:, 0:1]
    lanes = pl.ds(pl.multiple_of(row * part_width, 128), part_width)
    input_grad_ref[...] = (
        branch[:, :, lanes].reshape(tokens, part_width).astype(full)
        + scale * (gain_ref[...] * normed_own[...])
        - inputs_ref[...].astype(full) * (scale * scale * scale) * (inner / width)
    ).astype(low)

    partners = [dict(row=other), dict(col=col + 1 - 2 * (col % 2))]
    partners.append(dict(col=col + 2 - 4 * ((col // 2) % 2)))
    partners.append(dict(dp=core_partner))
    partners += [dict(dp=across(bit)) for bit in side_bits]

    def sums_copy(number):
        return remote_copy(
            sums.at[number],
            sums_arrived.at[number],
            sums_sem.at[number, 0],
            sums_sem.at[number, 1],
            **partners[number],
        )

    def sums_step(number):
        sums_copy(number).wait_recv()
        sums[number + 1] = sums[number] + sums_arrived[number]
        if number + 1 < len(partners):
            sums_copy(number + 1).start()

    sums_copy(0).start()

    def own_tokens(value):
        total = (middle_ref[...] + value).astype(low)
        out_stack[col] = total

    outs.total(own_tokens)

    def outputs_copy():
        place = pl.ds(pl.multiple_of(row * rows, rows), rows)
        lanes = pl.ds(pl.multiple_of(other * part_width, 128), part_width)
        return remote_copy(
            out_stack.at[col, :, lanes],
            outputs_ref.at[place],
            own_out_sem.at[0],
            own_out_sem.at[1],
            row=other,
        )

    outputs_copy().start()
    outputs_ref[pl.ds(pl.multiple_of(row * rows, rows), rows), :] = out_stack[
        col, :, pl.ds(pl.multiple_of(row * part_width, 128), part_width)
    ]
    sums_step(0)
    for at in range(3, items):
        item_row_copy(at).start()

    def over_dp(side, sems):
        def copy(number):
            return remote_copy(
                side.at[number % 2],
                side.at[2 + number],
                sems.at[2 * number],
                sems.at[2 * number + 1],
                dp=across(side_bits[number]),
            )

        def start(number):
            copy(number).start()

        def finish(number):
            copy(number).wait()
            side[1 - number % 2] = add_low(side[number % 2], side[2 + number])
            if number + 1 < last_side:
                start(number + 1)

        return copy, start, finish

    def set_side(side):
        def part(value):
            side[0] = value.astype(low)

        return part

    chains = [(wo_total, wo_side, wo_sem.at[4])] + [
        (wa_total[c], wa_side.at[c], wa_sem.at[4 + c]) for c in range(2)
    ]
    steps = []
    for total, side, sems in chains:
        total.total(set_side(side))
        steps.append(over_dp(side, sems))
        if last_side:
            steps[-1][1](0)
    sums_step(1)
    item_after_side(1)
    item_after_row(2)
    for _, _, finish in steps:
        for number in range(last_side):
            finish(number)
    sums_step(2)

    def block_copies(number):
        _, side, sems = chains[number]
        base, value = 2 * last_side, side.at[last_side % 2]
        if number == 0:
            target = output_total_ref.at[pl.ds(pl.multiple_of(core * wo_size, 16), wo_size)]
        else:
            first = pl.multiple_of(core * wa_size + (number - 1) * chunk_rows, 16)
            target = joint_total_ref.at[pl.ds(first, chunk_rows)]
        return (
            remote_copy(
                value, target, sems.at[base], sems.at[base + 1], dp=core_partner
            ),
            pltpu.make_async_copy(value, target, sems.at[base + 2]),
        )

    for number in range(3):
        for copy in block_copies(number):
            copy.start()
    for number in range(3, len(partners)):
        sums_step(number)
    gains_ref[...] = sums[len(partners)]

    item_after_side(2)
    item_after_row(3)
    item_after_side(3)

    branch_copy.wait_send()
    pl.when(odd)(lambda: pair_copy().wait_send())
    for b in range(2):
        wo_core_copy(b).wait_send()
        wo_row_copy(b).wait_send()
        wa_core_copy(b).wait_send()
        wa_row_copy(b).wait_send()
    normed_copy.wait_send()
    inner_copy.wait_send()
    outputs_copy().wait()
    for number in range(len(partners)):
        sums_copy(number).wait_send()
    for total in [outs, wo_total] + wa_total:
        total.end()
    for number in range(3):
        remote, local = block_copies(number)
        remote.wait()
        local.wait()
    for at in range(items):
        item_end(at)


def finish_call(
    sums, middle, cot, mixer, gain, scale, inputs, attended, rot, keys, values, cosine, sine,
    start, head_output, joint_weight, normed, out_part, up_own, up_row, up_other, down_half,
    query_block, both_block,
):
    rows, width = middle.shape
    tokens, part_width = inputs.shape
    cols, dps = lax.axis_size("col"), lax.axis_size("dp")
    sides = dps.bit_length() - 2
    heads_width = attended.shape[1]
    reach = keys.shape[0]
    vmem = pl.BlockSpec(memory_space=pltpu.VMEM)
    anywhere = pl.BlockSpec(memory_space=pl.ANY)
    dma = pltpu.SemaphoreType.DMA
    hidden = 2 * up_own.shape[1]
    size = part_width // 2
    items = 4
    wo_size, wa_size = query_block // 2, part_width // 2
    shape = jax.ShapeDtypeStruct
    sums_count = 4 + sides
    return pl.pallas_call(
        finish_kernel,
        in_specs=[vmem] * 17 + [anywhere] * 5,
        out_specs=[vmem] * 5 + [anywhere] * 3,
        out_shape=[
            shape((tokens, part_width), low),
            shape((tokens, part_width), low),
            shape((8, width), full),
            shape((query_block, part_width), low),
            shape((part_width, both_block), low),
            shape((part_width, hidden), low),
            shape((hidden, part_width), low),
            shape((items, max(sides, 1), size, part_width), low),
        ],
        scratch_shapes=[
            pltpu.VMEM((2, rows, width), low),
            dma((2,)),
            pltpu.VMEM((cols, rows, width), low),
            pltpu.VMEM((cols + 1, rows, width), low),
            dma,
            dma((cols,)),
            dma((cols + 1,)),
            dma((2,)),
            pltpu.VMEM((tokens, heads_width), low),
            pltpu.VMEM((tokens, 2 * both_block), low),
            pltpu.VMEM((reach, head_dim), full),
            pltpu.VMEM((reach, head_dim), full),
            pltpu.VMEM((tokens, 2 * head_dim), low),
            pltpu.VMEM((tokens, 2 * head_dim), low),
            dma((2,)),
            pltpu.VMEM((tokens, part_width), low),
            pltpu.VMEM((tokens, part_width), full),
            dma((2,)),
            pltpu.VMEM((8, tokens), full),
            pltpu.VMEM((8, tokens), full),
            dma((2,)),
            pltpu.VMEM((sums_count + 1, 8, width), full),
            pltpu.VMEM((sums_count, 8, width), full),
            dma((sums_count, 2)),
            pltpu.VMEM((items, size, part_width), low),
            pltpu.VMEM((items, size, part_width), low),
            pltpu.VMEM((items, size, part_width), low),
            dma((items, 5 + 2 * sides)),
            dma((items, 2)),
            pltpu.VMEM((2, 2, wo_size, width), low),
            pltpu.VMEM((2, wo_size, width), low),
            pltpu.VMEM((2, wo_size, part_width), low),
            pltpu.VMEM((cols, wo_size, part_width), low),
            pltpu.VMEM((cols + 1, wo_size, part_width), low),
            pltpu.VMEM((2 + sides, wo_size, part_width), low),
            dma((5, 3 + 2 * sides)),
            dma((cols,)),
            dma((cols + 1,)),
            pltpu.VMEM((2, 2, wa_size, 2 * both_block), low),
            pltpu.VMEM((2, wa_size, 2 * both_block), low),
            pltpu.VMEM((2, wa_size // 2, 2 * both_block), low),
            pltpu.VMEM((2, cols, wa_size // 2, both_block), low),
            pltpu.VMEM((2, cols + 1, wa_size // 2, both_block), low),
            pltpu.VMEM((2, 2 + sides, wa_size // 2, both_block), low),
            dma((6, 3 + 2 * sides)),
            dma((2, cols)),
            dma((2, cols + 1)),
        ],
        compiler_params=pltpu.CompilerParams(
            collective_id=2, has_side_effects=True, vmem_limit_bytes=63 * 2**20
        ),
        cost_estimate=pl.CostEstimate(
            flops=10 * 10**9, bytes_accessed=40 * 10**6, transcendentals=4 * 10**6
        ),
    )(
        sums, middle, cot, mixer, gain, scale, inputs, attended, rot, keys, values, cosine, sine,
        start, head_output, joint_weight, normed, out_part, up_own, up_row, up_other, down_half,
    )


def shards(
    inputs,
    norm_gain,
    query_weight,
    key_value_matrix,
    output_weight,
    mixer_gain,
    gate_weight,
    up_weight,
    down_weight,
    lengths,
    routes,
    route_gates,
    cotangent,
):
    row, col = lax.axis_index("row"), lax.axis_index("col")
    part_width = inputs.shape[1]
    experts, _, units = gate_weight.shape
    hidden_width = experts * units
    query_block, keyval_block = query_weight.shape[1], key_value_matrix.shape[1]
    small = jnp.zeros((8, part_width), full)
    small = small.at[0].set(norm_gain).at[1].set(mixer_gain)
    sequences = lengths.shape[1]
    small = small.at[2, :sequences].set(lengths[0].astype(full))
    theta = rope_base ** (-jnp.arange(0, head_dim, 2, dtype=full) / head_dim)
    theta = jnp.concatenate([theta, theta])[None, :]
    (
        normed,
        first_scale,
        mixer_all,
        keys,
        values,
        cosine,
        sine,
        start,
        attended,
        rot,
        joint_weight,
        head_output,
        middle,
        expert_own,
        tables,
        cot_all,
        gate_all,
        up_all,
        down_all,
    ) = prologue_call(
        inputs, small, theta, routes, route_gates, query_weight, key_value_matrix, output_weight,
        gate_weight, up_weight, down_weight.reshape(hidden_width, part_width), cotangent, sequences,
    )
    cot_own = lax.dynamic_index_in_dim(cot_all, col, 0, False)
    second_grad, out_part, gate_total, up_own, up_row, up_other, down_half = experts_call(
        expert_own, cot_all, tables, gate_all, up_all, down_all
    )

    both_block = query_block + keyval_block
    (
        outputs,
        input_grad,
        gain_sums,
        output_total,
        joint_total,
        up_total,
        down_total,
        _,
    ) = finish_call(
        second_grad, middle, cot_own, mixer_all, norm_gain[None, :], first_scale, inputs,
        attended, rot, keys, values, cosine, sine, start, head_output, joint_weight, normed,
        out_part, up_own, up_row, up_other, down_half, query_block, both_block,
    )
    gain_sums = lax.dynamic_slice_in_dim(gain_sums, row * part_width, part_width, 1)
    norm_total, mixer_total = gain_sums[0], gain_sums[1]

    def by_expert(flat):
        return flat.reshape(part_width, experts, units).transpose(1, 0, 2).astype(full)

    gate_total, up_total = by_expert(gate_total), by_expert(up_total)
    down_total = down_total.reshape(experts, units, part_width).astype(full)
    output_total = output_total.astype(full)
    joint_total = joint_total.astype(full)
    query_total, keyval_total = joint_total[:, :query_block], joint_total[:, query_block:]
    return (
        outputs,
        input_grad,
        norm_total,
        query_total,
        keyval_total,
        output_total,
        mixer_total,
        gate_total,
        up_total,
        down_total,
    )


def solution(mesh):
    return jax.shard_map(
        shards,
        mesh=mesh,
        in_specs=(
            P(("dp", "col"), "row"),
            P("row"),
            P("row", "col"),
            P("row", "col"),
            P("col", "row"),
            P("row"),
            P(None, "row", "col"),
            P(None, "row", "col"),
            P(None, "col", "row"),
            P(("dp", "row"), None),
            P("dp", None),
            P("dp", None),
            P(("dp", "col"), "row"),
        ),
        out_specs=(
            P(("dp", "col"), "row"),
            P(("dp", "col"), "row"),
            P("row"),
            P("row", "col"),
            P("row", "col"),
            P("col", "row"),
            P("row"),
            P(None, "row", "col"),
            P(None, "row", "col"),
            P(None, "col", "row"),
        ),
        check_vma=False,
    )
```

```python
import functools

import jax
import jax.numpy as jnp
from jax import lax
from jax.experimental import pallas as pl
from jax.experimental.pallas import tpu as pltpu
from jax.sharding import PartitionSpec as P

epsilon = 1e-06
rope_base = 1000000.0
head_dim = 128
low = jnp.bfloat16
full = jnp.float32


def dot(left, right, left_dim=1, right_dim=0):
    return lax.dot_general(
        left, right, (((left_dim,), (right_dim,)), ((), ())), preferred_element_type=full
    )


def remote_copy(source, target, send_sem, recv_sem, **device):
    return pltpu.make_async_remote_copy(
        src_ref=source,
        dst_ref=target,
        send_sem=send_sem,
        recv_sem=recv_sem,
        device_id=device,
        device_id_type=pl.DeviceIdType.MESH,
    )


def add_low(left, right):
    return (left.astype(full) + right.astype(full)).astype(low)


class ColSum:
    def __init__(self, stack, arrived, send_sem, recv_sem, col, count, blocks):
        self.stack, self.arrived, self.send_sem, self.recv_sem = stack, arrived, send_sem, recv_sem
        self.col, self.last, self.blocks = col, count - 1, list(blocks)

    def copy(self, block, at, right):
        neighbour = at + 1 if right else at - 1
        n = self.blocks.index(block)
        slot = n if right or block != neighbour else len(self.blocks)
        return remote_copy(
            self.stack.at[n],
            self.arrived.at[slot],
            self.send_sem.at[n],
            self.recv_sem.at[slot],
            col=neighbour,
        )

    def wait(self, slot, at):
        remote_copy(
            self.arrived.at[slot],
            self.arrived.at[slot],
            self.send_sem.at[0],
            self.recv_sem.at[slot],
            col=at + 1 if at == 0 else at - 1,
        ).wait_recv()

    def step(self, number, placed=False):
        for at in range(self.last + 1):
            ways = []
            for right in (True, False):
                block = at + self.last + 1 - number if right else at - self.last - 1 + number
                if block in self.blocks:
                    ways.append((block, right))
            if not ways:
                continue

            @pl.when(self.col == at)
            def _(at=at, ways=ways):
                for block, right in ways:
                    n = self.blocks.index(block)
                    if 0 < at < self.last:
                        if not placed:
                            self.wait(n, at)
                        self.stack[n] = add_low(self.stack[n], self.arrived[n])
                    self.copy(block, at, right).start()

    def total(self, part):
        for n, at in enumerate(self.blocks):

            @pl.when(self.col == at)
            def _(n=n, at=at):
                value = self.stack[n].astype(full)
                if at > 0:
                    self.wait(n, at)
                    value += self.arrived[n].astype(full)
                if at < self.last:
                    self.wait(len(self.blocks), at)
                    value += self.arrived[len(self.blocks)].astype(full)
                part(value)

    def end(self, first=True):
        for at in range(self.last + 1):

            @pl.when(self.col == at)
            def _(at=at):
                for block in self.blocks:
                    if block != at and (first or abs(block - at) < self.last):
                        self.copy(block, at, block > at).wait_send()


def experts_kernel(
    own_ref,
    cot_ref,
    table_ref,
    gate_hbm,
    gate_other_hbm,
    up_hbm,
    up_other_hbm,
    down_hbm,
    down_other_hbm,
    sum_ref,
    out_part_ref,
    gate_total_ref,
    up_own_ref,
    up_row_ref,
    up_other_ref,
    down_half_ref,
    out_first_ref,
    weights,
    expert_in,
    gate_grad,
    up_grad,
    hidden,
    send_stage,
    arrived,
    parts,
    stage,
    weights_sem,
    down_sem,
    ready,
    ag_recv,
    ag_right,
    ag_left,
    rs_recv,
    rs_send,
    core_send,
    core_recv,
    row_send,
    row_recv,
    side_send,
    side_recv,
    final_sem,
    local_sem,
    out_sem,
):
    row, col, dp = lax.axis_index("row"), lax.axis_index("col"), lax.axis_index("dp")
    dps = lax.axis_size("dp")
    core, other = dp % 2, 1 - row
    core_partner = dp + 1 - 2 * core
    side_bits = list(range(1, dps.bit_length() - 1))
    sides = len(side_bits)
    last = cot_ref.shape[0] - 1
    rows, width = own_ref.shape
    half = width // 2
    size = half // 2
    inner = (col > 0) & (col < last)

    def across(bit):
        on = (dp // (1 << bit)) % 2
        return dp + (1 << bit) * (1 - 2 * on)

    def half_lanes(which):
        return pl.ds(pl.multiple_of(which * half, half), half)

    gate_ref, up_ref, down_ref = weights.at[0], weights.at[1], weights.at[2]
    sources = (gate_hbm, gate_other_hbm, up_hbm, up_other_hbm, down_hbm, down_other_hbm)
    loads = [
        pltpu.make_async_copy(
            source,
            weights.at[i // 2, :, half_lanes((row, other)[i % 2])],
            weights_sem.at[i],
        )
        for i, source in enumerate(sources)
    ]
    for copy in loads[:5]:
        copy.start()

    barrier = pltpu.get_barrier_semaphore()

    def greet(semaphore, **device):
        pl.semaphore_signal(
            semaphore, inc=1, device_id=device, device_id_type=pl.DeviceIdType.MESH
        )

    greet(barrier, dp=core_partner)
    greet(barrier, row=other)
    for bit in side_bits:
        greet(barrier, dp=across(bit))
    pl.when(col > 0)(lambda: greet(barrier, col=col - 1))
    pl.when(col < last)(lambda: greet(barrier, col=col + 1))
    expert_in[col] = own_ref[...]
    pl.when(inner)(lambda: pl.semaphore_wait(barrier, 4 + sides))
    pl.when(jnp.logical_not(inner))(lambda: pl.semaphore_wait(barrier, 3 + sides))

    def ag_copy(block, right):
        return remote_copy(
            expert_in.at[block],
            expert_in.at[block],
            (ag_right if right else ag_left).at[block],
            ag_recv.at[block],
            col=col + 1 if right else col - 1,
        )

    def rs_copy(block, part, right):
        neighbour = col + 1 if right else col - 1
        slot = block if right else jnp.where(block == neighbour, last + 1, block)
        return remote_copy(
            send_stage.at[block, part],
            arrived.at[slot, part],
            rs_send.at[block, part],
            rs_recv.at[slot, part],
            col=neighbour,
        )

    def rs_wait(slot, part):
        remote_copy(
            arrived.at[slot, part],
            arrived.at[slot, part],
            rs_send.at[0, part],
            rs_recv.at[slot, part],
            col=jnp.where(col > 0, col - 1, col + 1),
        ).wait_recv()

    pl.when(col < last)(lambda: ag_copy(col, True).start())
    pl.when(col > 0)(lambda: ag_copy(col, False).start())
    quarter_size = down_other_hbm.shape[0] // 4

    def down_quarter(which):
        return down_other_hbm.at[
            pl.ds(pl.multiple_of(which * quarter_size, 16), quarter_size)
        ]

    def down_room(which):
        first = pl.multiple_of(which * quarter_size, 16)
        return weights.at[2, pl.ds(first, quarter_size), half_lanes(other)]

    quarter = dp % 4
    down_side = remote_copy(
        down_quarter(quarter), down_room(quarter), down_sem.at[0], down_sem.at[1], dp=across(1)
    )
    down_own = pltpu.make_async_copy(down_quarter(quarter), down_room(quarter), weights_sem.at[5])

    def down_core(n):
        there = down_room(core + 2 * n)
        return remote_copy(
            there, there, down_sem.at[2 + 2 * n], down_sem.at[3 + 2 * n], dp=core_partner
        )

    down_side.start()
    down_own.start()
    for copy in loads[:5]:
        copy.wait()
    down_own.wait()
    down_side.wait_recv()
    for n in range(2):
        down_core(n).start()
    for n in range(2):
        down_core(n).wait()
    down_side.wait_send()

    def compute(block):
        tokens = expert_in[block]
        grads = cot_ref[block]
        table = table_ref[block]
        experts = table.shape[1]
        units = width // experts
        for g in range(2):
            cols = slice(g * half, (g + 1) * half)
            gate = dot(tokens, gate_ref[cols, :], 1, 1)
            up = dot(tokens, up_ref[cols, :], 1, 1)
            grad = dot(grads, down_ref[cols, :], 1, 1)
            lane = lax.broadcasted_iota(jnp.int32, gate.shape, 1)
            first = g * experts // 2
            chosen = jnp.broadcast_to(table[:, first : first + 1], gate.shape)
            for e in range(1, experts // 2):
                chosen = jnp.where(lane >= e * units, table[:, first + e : first + e + 1], chosen)
            sigmoid = 1.0 / (1.0 + jnp.exp(-gate))
            silu = gate * sigmoid
            grad = grad * chosen
            hidden[block, :, cols] = (silu * up * chosen).astype(low)
            gate_grad[block, :, cols] = (
                grad * up * (sigmoid * (1.0 + gate * (1.0 - sigmoid)))
            ).astype(low)
            up_grad[block, :, cols] = (grad * silu).astype(low)
        gates_now, ups_now = gate_grad[block], up_grad[block]
        for part in range(2):
            cols = slice(part * half, (part + 1) * half)
            total = dot(gates_now, gate_ref[:, cols]) + dot(ups_now, up_ref[:, cols])
            send_stage[block, part] = total.astype(low)
            pl.when((col == 0) & (block != col))(lambda: rs_copy(block, part, True).start())
            pl.when((col == last) & (block != col))(lambda: rs_copy(block, part, False).start())
        out_part_ref[block] = dot(hidden[block], down_ref[...]).astype(low)

    def step(i, carry):
        apart = (i + 1) // 2
        from_left = i % 2 == 1

        @pl.when(from_left & (col - apart >= 0))
        def _():
            block = col - apart
            ag_copy(block, True).wait_recv()
            pl.when(col < last)(lambda: ag_copy(block, True).start())

        @pl.when(from_left & (col + apart <= last))
        def _():
            block = col + apart
            ag_copy(block, False).wait_recv()
            pl.when(col > 0)(lambda: ag_copy(block, False).start())

        block = jnp.where(from_left, col - apart, col + apart)
        pl.when((block >= 0) & (block <= last))(lambda: compute(block))
        return carry

    lax.fori_loop(0, 2 * last + 1, step, 0)

    greet(ready.at[0], dp=core_partner)
    greet(ready.at[1], row=other)
    for number, bit in enumerate(side_bits):
        greet(ready.at[2 + number], dp=across(bit))

    def room(which, down, right):
        return weights.at[
            which, pl.ds(down * half, half), pl.ds(right * half, half)
        ]

    def forward(block, right):
        for part in range(2):
            rs_wait(block, part)
            send_stage[block, part] = add_low(send_stage[block, part], arrived[block, part])
            rs_copy(block, part, right).start()

    def event(number):
        blocks = ((2, 1), (3, 0), (0, 3))[number]
        pl.when(col == 1)(lambda: forward(blocks[0], number < 2))
        pl.when(col == 2)(lambda: forward(blocks[1], number == 2))

    def core_copy(at):
        if at < 4:
            target = room(at // 2, 0, at % 2)
        else:
            target = room(2, 0, at - 4)
        return remote_copy(
            stage.at[at % 2], target, core_send.at[at], core_recv.at[at], dp=core_partner
        )

    def stage_free(at):
        if at >= 2:
            core_copy(at - 2).wait_send()

    def core_dot(at):
        left = (gate_grad, up_grad)[at // 2]
        right = expert_in[:, :, half_lanes(row if at % 2 else other)].reshape(-1, half)
        stage_free(at)
        stage[at % 2] = dot(
            left[:, :, half_lanes(1 - core)].reshape(-1, half), right, 0, 0
        ).astype(low)
        core_copy(at).start()
        parts[at] = dot(left[:, :, half_lanes(core)].reshape(-1, half), right, 0, 0).astype(low)

    def core_sum(at):
        core_copy(at).wait_recv()
        parts[at] = add_low(parts[at], room(at // 2, 0, at % 2)[...])

    def down_dot_partner():
        left = hidden[:, :, half_lanes(1 - core)].reshape(-1, half)
        for part in range(2):
            lanes = slice(part * half, (part + 1) * half)
            right = cot_ref[:, :, lanes].reshape(-1, half)
            stage_free(4 + part)
            stage[part] = dot(left, right, 0, 0).astype(low)
            core_copy(4 + part).start()

    def down_dot_own():
        left = hidden[:, :, half_lanes(core)].reshape(-1, half)
        for part in range(2):
            lanes = slice(part * half, (part + 1) * half)
            right = cot_ref[:, :, lanes].reshape(-1, half)
            room(2, 1, part)[...] = dot(left, right, 0, 0).astype(low)

    def down_sum():
        for part in range(2):
            core_copy(4 + part).wait_recv()
            room(2, 1, part)[...] = add_low(room(2, 1, part)[...], room(2, 0, part)[...])

    down_out = pltpu.make_async_copy(
        weights.at[2, pl.ds(half, half)], down_half_ref, local_sem.at[0]
    )
    up_out = pltpu.make_async_copy(parts.at[3], up_own_ref, local_sem.at[1])
    up_rest = pltpu.make_async_copy(
        parts.at[2, pl.ds(size, size)], up_other_ref, local_sem.at[2]
    )

    def chunk_rows(chunk):
        return pl.ds(chunk * size, size)

    def row_copy(chunk):
        if chunk < 2:
            source = parts.at[0, chunk_rows(chunk)]
            target = weights.at[0, pl.ds(half + chunk * size, size), pl.ds(0, half)]
        else:
            source, target = parts.at[2, chunk_rows(0)], up_row_ref
        return remote_copy(source, target, row_send.at[chunk], row_recv.at[chunk], row=other)

    def side_room(number, chunk):
        which, right = ((0, 1), (1, 0), (1, 1))[number]
        return weights.at[
            which, pl.ds(half + chunk * size, size), pl.ds(right * half, half)
        ]

    def side_copy(chunk, number):
        return remote_copy(
            parts.at[1 - number % 2, chunk_rows(chunk)],
            side_room(number, chunk),
            side_send.at[chunk, number],
            side_recv.at[chunk, number],
            dp=across(side_bits[number]),
        )

    def after_row(chunk):
        copy = row_copy(chunk)
        copy.wait_recv()
        copy.wait_send()
        here = chunk_rows(chunk)
        landed = weights.at[0, pl.ds(half + chunk * size, size), pl.ds(0, half)]
        parts[1, here] = add_low(parts[1, here], landed[...])
        if sides:
            if chunk == 0:
                for number in range(sides):
                    pl.semaphore_wait(ready.at[2 + number], 1)
            side_copy(chunk, 0).start()

    def final_copies(chunk):
        source = parts.at[1 - sides % 2, chunk_rows(chunk)]
        first = pl.multiple_of(core * half + chunk * size, 16)
        target = gate_total_ref.at[pl.ds(first, size)]
        return (
            remote_copy(
                source, target, final_sem.at[chunk, 0], final_sem.at[chunk, 1], dp=core_partner
            ),
            pltpu.make_async_copy(source, target, final_sem.at[chunk, 2]),
        )

    def after_side(chunk):
        here = chunk_rows(chunk)
        for number in range(sides):
            copy = side_copy(chunk, number)
            copy.wait_recv()
            copy.wait_send()
            parts[number % 2, here] = add_low(
                parts[1 - number % 2, here], side_room(number, chunk)[...]
            )
            if number + 1 < sides:
                side_copy(chunk, number + 1).start()
        for copy in final_copies(chunk):
            copy.start()

    def out_copy(right):
        return remote_copy(
            out_part_ref.at[last if right else 0],
            out_first_ref,
            out_sem.at[0],
            out_sem.at[1],
            col=col + 1 if right else col - 1,
        )

    pl.semaphore_wait(ready.at[0], 1)
    core_dot(0)
    event(0)
    core_dot(1)
    core_sum(0)
    pl.semaphore_wait(ready.at[1], 1)
    row_copy(0).start()
    core_dot(2)
    core_sum(1)
    core_sum(2)
    up_rest.start()
    core_dot(3)
    event(1)
    pl.when(col == 0)(lambda: out_copy(True).start())
    pl.when(col == last)(lambda: out_copy(False).start())
    down_dot_partner()
    after_row(0)
    row_copy(1).start()
    core_sum(3)
    up_out.start()
    event(2)
    down_dot_own()
    down_sum()
    down_out.start()

    for part in range(2):
        sum_ref[part] = send_stage[col, part].astype(full)

        @pl.when(col > 0)
        def _():
            rs_wait(col, part)
            sum_ref[part] += arrived[col, part].astype(full)

        @pl.when(col < last)
        def _():
            rs_wait(last + 1, part)
            sum_ref[part] += arrived[last + 1, part].astype(full)

    after_row(1)
    row_copy(2).start()
    after_side(0)
    after_side(1)

    for block in range(last + 1):
        pl.when((block <= col) & (col < last))(lambda: ag_copy(block, True).wait_send())
        pl.when((block >= col) & (col > 0))(lambda: ag_copy(block, False).wait_send())
        for part in range(2):
            pl.when(block > col)(lambda: rs_copy(block, part, True).wait_send())
            pl.when(block < col)(lambda: rs_copy(block, part, False).wait_send())
    for at in range(4, 6):
        core_copy(at).wait_send()
    row_copy(2).wait()
    pl.when(col == 0)(lambda: out_copy(True).wait_send())
    pl.when(col == last)(lambda: out_copy(False).wait_send())
    pl.when(inner)(lambda: out_copy(False).wait_recv())
    for copy in (down_out, up_out, up_rest):
        copy.wait()
    for chunk in range(2):
        remote, local = final_copies(chunk)
        remote.wait()
        local.wait()


def experts_call(own, cot, table, *halves):
    rows, width = own.shape
    blocks, half = cot.shape[0], width // 2
    sides = lax.axis_size("dp").bit_length() - 2
    vmem = pl.BlockSpec(memory_space=pltpu.VMEM)
    anywhere = pl.BlockSpec(memory_space=pl.ANY)
    dma = pltpu.SemaphoreType.DMA
    shape = jax.ShapeDtypeStruct
    return pl.pallas_call(
        experts_kernel,
        in_specs=[vmem] * 3 + [anywhere] * 6,
        out_specs=[vmem, vmem] + [anywhere] * 6,
        out_shape=[
            shape((2, rows, half), full),
            shape((blocks, rows, width), low),
            shape((width, half), low),
            shape((half, half), low),
            shape((half // 2, half), low),
            shape((half // 2, half), low),
            shape((half, width), low),
            shape((rows, width), low),
        ],
        scratch_shapes=[pltpu.VMEM((3, width, width), low)]
        + [pltpu.VMEM((blocks, rows, width), low)] * 4
        + [
            pltpu.VMEM((blocks, 2, rows, half), low),
            pltpu.VMEM((blocks + 1, 2, rows, half), low),
            pltpu.VMEM((4, half, half), low),
            pltpu.VMEM((2, half, half), low),
            dma((6,)),
            dma((6,)),
            pltpu.SemaphoreType.REGULAR((2 + max(sides, 1),)),
            dma((blocks,)),
            dma((blocks,)),
            dma((blocks,)),
            dma((blocks + 1, 2)),
            dma((blocks, 2)),
            dma((6,)),
            dma((6,)),
            dma((3,)),
            dma((3,)),
            dma((2, max(sides, 1))),
            dma((2, max(sides, 1))),
            dma((2, 3)),
            dma((3,)),
            dma((2,)),
        ],
        compiler_params=pltpu.CompilerParams(
            collective_id=1, has_side_effects=True, vmem_limit_bytes=60 * 2**20
        ),
        cost_estimate=pl.CostEstimate(
            flops=9 * 2 * blocks * rows * width * width,
            bytes_accessed=12 * width * width,
            transcendentals=blocks * rows * width,
        ),
    )(own, cot, table, *halves)


def prologue_kernel(
    inputs_ref,
    small_ref,
    theta_ref,
    routes_ref,
    route_gates_ref,
    cot_ref,
    query_hbm,
    keyval_hbm,
    output_hbm,
    gate_hbm,
    up_hbm,
    down_hbm,
    normed_ref,
    scale_ref,
    gains_ref,
    key_ref,
    value_ref,
    cosine_ref,
    sine_ref,
    start_ref,
    attended_ref,
    rot_ref,
    joint_ref,
    head_output_ref,
    middle_ref,
    expert_ref,
    table_ref,
    cot_all_ref,
    gate_all_ref,
    up_all_ref,
    down_all_ref,
    inputs_all,
    inputs_sem,
    small,
    small_sem,
    projected,
    branch_own,
    branch_stage,
    branch_arrived,
    branch_sem,
    pair_sem,
    joint_line,
    joint_load,
    joint_hop,
    joint_row,
    joint_side,
    joint_core,
    output_line,
    output_load,
    output_hop,
    output_row,
    output_side,
    output_core,
    expert_row,
    expert_side,
    expert_core,
    cot_sem,
    cot_recv,
    cot_send,
    *,
    sequences,
):
    row, col, dp = lax.axis_index("row"), lax.axis_index("col"), lax.axis_index("dp")
    cols = lax.axis_size("col")
    last = cols - 1
    core, side, other = dp % 2, (dp // 2) % 2, 1 - row
    quarter = dp % 4
    core_partner, side_partner = dp + 1 - 2 * core, dp + 2 - 4 * side
    tokens, part_width = inputs_ref.shape
    width, rows = 2 * part_width, tokens // 2
    query_block, keyval_block = query_hbm.shape[1], keyval_hbm.shape[1]
    block = query_block + keyval_block
    experts = table_ref.shape[2]

    barrier = pltpu.get_barrier_semaphore()

    def greet(**device):
        pl.semaphore_signal(
            barrier, inc=1, device_id=device, device_id_type=pl.DeviceIdType.MESH
        )

    greet(row=other)
    for apart in range(1, cols):
        greet(col=(col + apart) % cols)
    greet(dp=core_partner)
    greet(dp=side_partner)

    def part_lanes(which):
        return pl.ds(pl.multiple_of(which * part_width, 128), part_width)

    inputs_all[:, part_lanes(row)] = inputs_ref[...]
    small[row] = small_ref[...]
    inputs_copy = remote_copy(
        inputs_ref,
        inputs_all.at[:, part_lanes(row)],
        inputs_sem.at[0],
        inputs_sem.at[1],
        row=other,
    )
    small_copy = remote_copy(
        small.at[row], small.at[row], small_sem.at[0], small_sem.at[1], row=other
    )

    joint_size, output_size = query_hbm.shape[0] // 4, output_hbm.shape[0] // 4

    def joint_region(r0, b, which):
        return joint_ref.at[
            pl.ds(pl.multiple_of(r0 * part_width + which * joint_size, 16), joint_size),
            pl.ds(pl.multiple_of(b * block, 128), block),
        ]

    def output_region(r0, b, which):
        return head_output_ref.at[
            pl.ds(pl.multiple_of(b * query_block + which * output_size, 16), output_size),
            part_lanes(r0),
        ]

    class Gather:
        def __init__(self, line, pieces, load, hop, row_sems, side_sems, core_sems, region):
            self.line, self.region, self.hop, self.row_sems = line, region, hop, row_sems
            self.side_sems, self.core_sems = side_sems, core_sems
            self.loads = [
                pltpu.make_async_copy(source, target, load.at[n])
                for n, (source, target) in enumerate(pieces)
            ]

        def copy(self, at, right):
            return remote_copy(
                self.line.at[at],
                self.line.at[at],
                self.hop.at[at, 1 if right else 0],
                self.hop.at[at, 2],
                col=col + 1 if right else col - 1,
            )

        def row_copy(self, b):
            return remote_copy(
                self.line.at[2 * other + b],
                self.region(row, b, quarter),
                self.row_sems.at[b, 0],
                self.row_sems.at[b, 1],
                row=other,
            )

        def side_copy(self, n):
            there = self.region((row, other)[n // 2], n % 2, quarter)
            return remote_copy(
                there, there, self.side_sems.at[n, 0], self.side_sems.at[n, 1], dp=side_partner
            )

        def core_copies(self, n):
            result = []
            for part in range(2):
                there = self.region((row, other)[n // 2], n % 2, core + 2 * part)
                result.append(
                    remote_copy(
                        there,
                        there,
                        self.core_sems.at[n, 2 * part],
                        self.core_sems.at[n, 2 * part + 1],
                        dp=core_partner,
                    )
                )
            return result

        def use(self, at):
            for b in range(2):

                @pl.when(at == 2 * row + b)
                def _(b=b):
                    there = self.region(row, b, quarter)
                    there[...] = self.line[at]
                    self.side_copy(b).start()

                @pl.when(at == 2 * other + b)
                def _(b=b):
                    self.row_copy(b).start()

        def load(self):
            for copy in self.loads:
                copy.start()

        def first(self):
            for copy in self.loads:
                copy.wait()
            pl.when(col < last)(lambda: self.copy(col, True).start())
            pl.when(col > 0)(lambda: self.copy(col, False).start())
            self.use(col)

        def step(self, apart):
            @pl.when(col - apart >= 0)
            def _():
                self.copy(col - apart, True).wait_recv()
                pl.when(col < last)(lambda: self.copy(col - apart, True).start())
                self.use(col - apart)

            @pl.when(col + apart <= last)
            def _():
                self.copy(col + apart, False).wait_recv()
                pl.when(col > 0)(lambda: self.copy(col + apart, False).start())
                self.use(col + apart)

        def from_row(self):
            for b in range(2):
                self.row_copy(b).wait_recv()
                self.side_copy(2 + b).start()

        def to_core(self):
            for n in range(4):
                self.side_copy(n).wait_recv()
                for copy in self.core_copies(n):
                    copy.start()

        def ready(self):
            for n in range(4):
                for copy in self.core_copies(n):
                    copy.wait_recv()

        def end(self):
            for at in range(cols):
                pl.when((at <= col) & (col < last))(lambda: self.copy(at, True).wait_send())
                pl.when((at >= col) & (col > 0))(lambda: self.copy(at, False).wait_send())
            for b in range(2):
                self.row_copy(b).wait_send()
            for n in range(4):
                self.side_copy(n).wait_send()
                for copy in self.core_copies(n):
                    copy.wait_send()

    first_joint = pl.ds(pl.multiple_of(quarter * joint_size, 16), joint_size)
    first_output = pl.ds(pl.multiple_of(quarter * output_size, 16), output_size)
    joint = Gather(
        joint_line,
        (
            (query_hbm.at[first_joint], joint_line.at[col, :, pl.ds(0, query_block)]),
            (keyval_hbm.at[first_joint], joint_line.at[col, :, pl.ds(query_block, keyval_block)]),
        ),
        joint_load,
        joint_hop,
        joint_row,
        joint_side,
        joint_core,
        joint_region,
    )
    output = Gather(
        output_line,
        ((output_hbm.at[first_output], output_line.at[col]),),
        output_load,
        output_hop,
        output_row,
        output_side,
        output_core,
        output_region,
    )

    def token_rows(which):
        return pl.ds(pl.multiple_of(which * rows, 16), rows)

    cot_row = remote_copy(
        cot_ref.at[token_rows(other)],
        cot_all_ref.at[col, :, part_lanes(row)],
        cot_sem.at[0],
        cot_sem.at[1],
        row=other,
    )

    def cot_copy(block_at, right):
        return remote_copy(
            cot_all_ref.at[block_at],
            cot_all_ref.at[block_at],
            cot_send.at[block_at, 1 if right else 0],
            cot_recv.at[block_at],
            col=col + 1 if right else col - 1,
        )

    def cot_first():
        cot_row.wait_recv()
        pl.when(col < last)(lambda: cot_copy(col, True).start())
        pl.when(col > 0)(lambda: cot_copy(col, False).start())

    def cot_pass(apart):
        @pl.when(col - apart >= 0)
        def _():
            cot_copy(col - apart, True).wait_recv()
            pl.when(col < last)(lambda: cot_copy(col - apart, True).start())

        @pl.when(col + apart <= last)
        def _():
            cot_copy(col + apart, False).wait_recv()
            pl.when(col > 0)(lambda: cot_copy(col + apart, False).start())

    joint.load()
    output.load()
    pl.semaphore_wait(barrier, cols + 2)
    joint.first()
    small_copy.start()
    inputs_copy.start()
    cot_row.start()

    expert_size = down_hbm.shape[0] // 4
    weights = (gate_hbm, up_hbm, down_hbm)
    totals = (gate_all_ref, up_all_ref, down_all_ref)

    def expert_region(which, of_quarter):
        first = pl.multiple_of(of_quarter * expert_size, 16)
        return totals[which].at[pl.ds(first, expert_size)]

    def expert_row_copy(which):
        first = pl.multiple_of(quarter * expert_size, 16)
        return remote_copy(
            weights[which].at[pl.ds(first, expert_size)],
            expert_region(which, quarter),
            expert_row.at[which, 0],
            expert_row.at[which, 1],
            row=other,
        )

    def expert_side_copy(which):
        there = expert_region(which, quarter)
        return remote_copy(
            there, there, expert_side.at[which, 0], expert_side.at[which, 1], dp=side_partner
        )

    def expert_core_copies(which):
        result = []
        for n in range(2):
            there = expert_region(which, core + 2 * n)
            result.append(
                remote_copy(
                    there,
                    there,
                    expert_core.at[which, 2 * n],
                    expert_core.at[which, 2 * n + 1],
                    dp=core_partner,
                )
            )
        return result

    def expert_after_row(which):
        expert_row_copy(which).wait_recv()
        expert_side_copy(which).start()

    def expert_after_side(which):
        expert_side_copy(which).wait_recv()
        for copy in expert_core_copies(which):
            copy.start()

    cot_all_ref[col, :, part_lanes(row)] = cot_ref[token_rows(row), :]

    for at in range(cols):
        place = pl.ds(pl.multiple_of(at * tokens + row * rows, 128), rows)
        chosen, gates = routes_ref[:, place], route_gates_ref[:, place]
        expert = lax.broadcasted_iota(jnp.int32, (experts, rows), 0)
        table = jnp.zeros((experts, rows), full)
        for k in range(chosen.shape[0]):
            table += jnp.where(chosen[k : k + 1, :] == expert, gates[k : k + 1, :], 0.0)
        table_ref[at] = jnp.transpose(table)

    joint.step(1)
    joint.step(2)
    joint.step(3)
    output.first()
    joint.from_row()
    cot_first()

    small_copy.wait_recv()
    gains_ref[:, :part_width] = small[0, 0:2, :]
    gains_ref[:, part_width:] = small[1, 0:2, :]
    half = col // 2
    lens = small[half, 2:3, :]
    odd = (col % 2).astype(full)
    place = lax.broadcasted_iota(jnp.int32, (tokens, 1), 0).astype(full) + odd * tokens
    begin = jnp.zeros((tokens, 1), full)
    total = lens[:, 0:1]
    for n in range(1, sequences):
        begin = jnp.where(place >= total, total, begin)
        total = total + lens[:, n : n + 1]
    start_ref[...] = begin + (1.0 - odd) * tokens
    angles = (place - begin) * theta_ref[...]
    cosine_ref[...] = jnp.cos(angles)
    sine = jnp.sin(angles)
    lane = lax.broadcasted_iota(jnp.int32, sine.shape, 1)
    sine_ref[...] = jnp.where(lane < head_dim // 2, -sine, sine)

    output.step(1)
    inputs_copy.wait_recv()
    expert_row_copy(0).start()

    piece = 64

    def norm_piece(at, carry):
        here = pl.ds(pl.multiple_of(at * piece, piece), piece)
        values = inputs_all[here, :].astype(full)
        scale = lax.rsqrt(jnp.mean(values * values, axis=1, keepdims=True) + epsilon)
        scale_ref[here, :] = scale
        for which in range(2):
            lanes = slice(which * part_width, (which + 1) * part_width)
            normed_ref[here, lanes] = (values[:, lanes] * scale * small[which, 0:1, :]).astype(low)
        return carry

    lax.fori_loop(0, tokens // piece, norm_piece, 0)
    output.step(2)
    joint.to_core()
    output.step(3)
    joint.ready()

    projected[...] = dot(normed_ref[...], joint_ref[...])
    own = slice(tokens, 2 * tokens)
    key = projected[:, query_block : query_block + head_dim]
    key_ref[own, :] = (
        key * cosine_ref[...] + pltpu.roll(key, head_dim // 2, 1) * sine_ref[...]
    ).astype(low)
    value_ref[own, :] = projected[:, block + query_block : block + query_block + head_dim].astype(low)

    def pair_copies():
        return [
            remote_copy(
                ref.at[pl.ds(tokens, tokens)],
                ref.at[pl.ds(0, tokens)],
                pair_sem.at[n, 0],
                pair_sem.at[n, 1],
                col=col + 1 - 2 * (col % 2),
            )
            for n, ref in enumerate((key_ref, value_ref))
        ]

    @pl.when(col % 2 == 0)
    def _():
        for copy in pair_copies():
            copy.start()
        key_ref[:tokens, :] = jnp.zeros((tokens, head_dim), low)
        value_ref[:tokens, :] = jnp.zeros((tokens, head_dim), low)

    expert_row_copy(1).start()
    output.from_row()
    cot_pass(1)
    output.to_core()

    @pl.when(col % 2 == 1)
    def _():
        for copy in pair_copies():
            copy.wait_recv()

    heads = 2 * query_block // head_dim
    per_block = heads // 2
    tile = tokens // 2
    window = key_ref.shape[0] - tile

    def head_step(head, carry):
        here = pl.ds(pl.multiple_of(head * head_dim, head_dim), head_dim)
        there = pl.ds(
            pl.multiple_of((head + head // per_block) * head_dim, head_dim), head_dim
        )
        pre = projected[:, there]
        rot = (pre * cosine_ref[...] + pltpu.roll(pre, head_dim // 2, 1) * sine_ref[...]).astype(low)
        rot_ref[:, here] = rot
        for at in range(tokens // tile):
            first = at * tile
            keys = key_ref[first : first + window, :]
            values = value_ref[first : first + window, :]
            scores = dot(rot[first : first + tile], keys, 1, 1) * head_dim ** (-0.5)
            key_place = lax.broadcasted_iota(jnp.int32, scores.shape, 1) + first
            query_place = lax.broadcasted_iota(jnp.int32, scores.shape, 0) + (first + tokens)
            allowed = (key_place <= query_place) & (
                key_place.astype(full) >= start_ref[first : first + tile, :]
            )
            scores = jnp.where(allowed, scores, -1e30)
            exponent = jnp.exp(scores - jnp.max(scores, axis=1, keepdims=True))
            weights = exponent / jnp.sum(exponent, axis=1, keepdims=True)
            attended_ref[first : first + tile, here] = dot(weights.astype(low), values).astype(low)
        return carry

    lax.fori_loop(0, heads, head_step, 0)

    expert_after_row(0)
    output.ready()

    def branch_copy(part):
        return remote_copy(
            branch_stage.at[part],
            branch_arrived.at[part],
            branch_sem.at[part, 0],
            branch_sem.at[part, 1],
            row=other,
        )

    theirs = attended_ref[token_rows(other), :]
    for part in range(2):
        lanes = slice(part * part_width, (part + 1) * part_width)
        branch_stage[part] = dot(theirs, head_output_ref[:, lanes]).astype(low)
        branch_copy(part).start()
    expert_row_copy(2).start()
    cot_pass(2)
    mine = attended_ref[token_rows(row), :]
    branch_own[...] = dot(mine, head_output_ref[...])
    expert_after_row(1)
    expert_after_side(0)
    for part in range(2):
        lanes = slice(part * part_width, (part + 1) * part_width)
        branch_copy(part).wait_recv()
        middle_ref[:, lanes] = (
            inputs_all[token_rows(row), lanes].astype(full)
            + branch_own[:, lanes]
            + branch_arrived[part].astype(full)
        )

    def second_piece(at, carry):
        here = pl.ds(pl.multiple_of(at * piece, piece), piece)
        values = middle_ref[here, :]
        scale = lax.rsqrt(jnp.mean(values * values, axis=1, keepdims=True) + epsilon)
        expert_ref[here, :] = (values * scale * gains_ref[1:2, :]).astype(low)
        return carry

    lax.fori_loop(0, rows // piece, second_piece, 0)
    expert_after_side(1)
    cot_pass(3)

    inputs_copy.wait_send()
    small_copy.wait_send()
    joint.end()
    output.end()
    for which in range(3):
        expert_row_copy(which).wait_send()
        if which == 2:
            expert_row_copy(which).wait_recv()
            continue
        expert_side_copy(which).wait_send()
        for copy in expert_core_copies(which):
            copy.wait()
    cot_row.wait_send()
    for at in range(cols):
        pl.when((at <= col) & (col < last))(lambda: cot_copy(at, True).wait_send())
        pl.when((at >= col) & (col > 0))(lambda: cot_copy(at, False).wait_send())

    @pl.when(col % 2 == 0)
    def _():
        for copy in pair_copies():
            copy.wait_send()

    for part in range(2):
        branch_copy(part).wait_send()


def prologue_call(
    inputs, small, theta, routes, route_gates, cotangent, query_weight, key_value_matrix,
    output_weight, gate_flat, up_flat, down_flat, sequences, experts,
):
    tokens, part_width = inputs.shape
    cols = lax.axis_size("col")
    width, rows = 2 * part_width, tokens // 2
    query_block, keyval_block = query_weight.shape[1], key_value_matrix.shape[1]
    block = query_block + keyval_block
    hidden = down_flat.shape[0]
    vmem = pl.BlockSpec(memory_space=pltpu.VMEM)
    anywhere = pl.BlockSpec(memory_space=pl.ANY)
    dma = pltpu.SemaphoreType.DMA
    shape = jax.ShapeDtypeStruct
    return pl.pallas_call(
        functools.partial(prologue_kernel, sequences=sequences),
        in_specs=[vmem] * 6 + [anywhere] * 6,
        out_specs=[vmem] * 16 + [anywhere] * 3,
        out_shape=[
            shape((tokens, width), low),
            shape((tokens, 1), full),
            shape((2, width), full),
            shape((2 * tokens, head_dim), low),
            shape((2 * tokens, head_dim), low),
            shape((tokens, head_dim), full),
            shape((tokens, head_dim), full),
            shape((tokens, 1), full),
            shape((tokens, 2 * query_block), low),
            shape((tokens, 2 * query_block), low),
            shape((width, 2 * block), low),
            shape((2 * query_block, width), low),
            shape((rows, width), full),
            shape((rows, width), low),
            shape((cols, rows, experts), full),
            shape((cols, rows, width), low),
            shape((hidden, part_width), low),
            shape((hidden, part_width), low),
            shape((hidden, part_width), low),
        ],
        scratch_shapes=[
            pltpu.VMEM((tokens, width), low),
            dma((2,)),
            pltpu.VMEM((2,) + small.shape, full),
            dma((2,)),
            pltpu.VMEM((tokens, 2 * block), full),
            pltpu.VMEM((rows, width), full),
            pltpu.VMEM((2, rows, part_width), low),
            pltpu.VMEM((2, rows, part_width), low),
            dma((2, 2)),
            dma((2, 2)),
            pltpu.VMEM((cols, part_width // 4, block), low),
            dma((2,)),
            dma((cols, 3)),
            dma((2, 2)),
            dma((4, 2)),
            dma((4, 4)),
            pltpu.VMEM((cols, query_block // 4, part_width), low),
            dma((1,)),
            dma((cols, 3)),
            dma((2, 2)),
            dma((4, 2)),
            dma((4, 4)),
            dma((3, 2)),
            dma((3, 2)),
            dma((3, 4)),
            dma((2,)),
            dma((cols,)),
            dma((cols, 2)),
        ],
        compiler_params=pltpu.CompilerParams(
            collective_id=3, has_side_effects=True, vmem_limit_bytes=60 * 2**20
        ),
        cost_estimate=pl.CostEstimate(
            flops=5 * 10**9, bytes_accessed=30 * 10**6, transcendentals=3 * 10**6
        ),
    )(
        inputs, small, theta, routes, route_gates, cotangent, query_weight, key_value_matrix,
        output_weight, gate_flat, up_flat, down_flat,
    )


def finish_kernel(
    middle_ref,
    gains_ref,
    scale_ref,
    start_ref,
    sum_hbm,
    inputs_hbm,
    attended_hbm,
    rot_hbm,
    key_hbm,
    value_hbm,
    cosine_hbm,
    sine_hbm,
    head_output_hbm,
    joint_hbm,
    normed_hbm,
    cot_all_hbm,
    out_part_hbm,
    up_own_hbm,
    up_row_hbm,
    up_other_hbm,
    down_half_hbm,
    out_first_hbm,
    outputs_ref,
    input_grad_ref,
    gain_sums_ref,
    output_total_ref,
    query_total_ref,
    keyval_total_ref,
    up_total_ref,
    down_total_ref,
    further,
    work,
    cot_ref,
    inputs_ref,
    attended_ref,
    rot_ref,
    key_ref,
    value_ref,
    cosine_ref,
    sine_ref,
    head_output_ref,
    joint_ref,
    normed_ref,
    loads,
    branch,
    branch_sem,
    out_stack,
    out_arrived,
    out_send,
    out_recv,
    own_out_sem,
    grad_heads,
    joint_grad,
    key_grad,
    value_grad,
    pair_stage,
    pair_arrived,
    pair_sem,
    normed_arrived,
    normed_sem,
    inner_stage,
    inner_arrived,
    inner_sem,
    sums,
    sums_arrived,
    sums_sem,
    item_mine,
    item_other,
    item_side,
    item_row,
    item_last,
    item_sem,
    item_load_sem,
    wo_parts,
    wo_core,
    wo_row,
    wo_stack,
    wo_arrived,
    wo_side,
    wo_sem,
    wo_send,
    wo_recv,
    wq_parts,
    wq_core,
    wq_row,
    wq_stack,
    wq_arrived,
    wq_side,
    wq_sem,
    wq_side_sem,
    wq_send,
    wq_recv,
    wk_parts,
    wk_core,
    wk_row,
    wk_stack,
    wk_arrived,
    wk_side,
    wk_sem,
    wk_send,
    wk_recv,
):
    row, col, dp = lax.axis_index("row"), lax.axis_index("col"), lax.axis_index("dp")
    cols, dps = lax.axis_size("col"), lax.axis_size("dp")
    core, side, other = dp % 2, (dp // 2) % 2, 1 - row
    core_partner = dp + 1 - 2 * core
    bits = list(range(1, dps.bit_length() - 1))
    sides = len(bits)

    def across(bit):
        on = (dp // (1 << bit)) % 2
        return dp + (1 << bit) * (1 - 2 * on)

    rows, width = middle_ref.shape
    tokens, part_width = inputs_ref.shape
    heads = attended_ref.shape[1] // head_dim
    per_block = heads // 2
    query_lanes, key_lanes = query_total_ref.shape[1], keyval_total_ref.shape[1]
    block_lanes = query_lanes + key_lanes

    def part_lanes(which):
        return pl.ds(pl.multiple_of(which * part_width, 128), part_width)

    size = item_mine.shape[1]
    items = item_mine.shape[0]
    load_pairs = [
        (sum_hbm, work),
        (cot_all_hbm.at[col], cot_ref),
        (out_part_hbm, out_stack),
        (head_output_hbm, head_output_ref),
        (attended_hbm, attended_ref),
        (rot_hbm, rot_ref),
        (key_hbm, key_ref),
        (value_hbm, value_ref),
        (cosine_hbm, cosine_ref),
        (sine_hbm, sine_ref),
        (joint_hbm, joint_ref),
        (normed_hbm, normed_ref),
        (inputs_hbm, inputs_ref),
    ]
    load = [
        pltpu.make_async_copy(source, target, loads.at[n])
        for n, (source, target) in enumerate(load_pairs)
    ]

    def item_loads(at):
        chunk = at % 2
        place = pl.ds(chunk * size, size)
        if at < 2:
            sources = (up_own_hbm.at[place], (up_row_hbm, up_other_hbm)[chunk])
        else:
            sources = [down_half_hbm.at[place, part_lanes(which)] for which in (row, other)]
        return [
            pltpu.make_async_copy(source, target.at[at], item_load_sem.at[at, number])
            for number, (source, target) in enumerate(zip(sources, (item_mine, item_other)))
        ]

    inner_col = (col > 0) & (col < cols - 1)
    first_load = pltpu.make_async_copy(
        out_first_hbm, out_arrived.at[(cols - 1) * (2 - col) % cols], loads.at[13]
    )
    for copy in load[:3]:
        copy.start()
    pl.when(inner_col)(lambda: first_load.start())
    for copy in item_loads(1) + load[3:]:
        copy.start()
    for at in (2, 3, 0):
        for copy in item_loads(at):
            copy.start()

    barrier = pltpu.get_barrier_semaphore()

    def greet(**device):
        pl.semaphore_signal(
            barrier, inc=1, device_id=device, device_id_type=pl.DeviceIdType.MESH
        )

    plane = [
        dict(row=(row + there // cols) % 2, col=(col + there % cols) % cols)
        for there in range(1, 2 * cols)
    ]
    copies = [dict(dp=(dp + apart) % dps) for apart in range(1, dps)]
    for device in plane + copies:
        greet(**device)

    outs = ColSum(out_stack, out_arrived, out_send, out_recv, col, cols, range(cols))
    load[2].wait()
    pl.when(inner_col)(lambda: first_load.wait())
    pl.semaphore_wait(barrier, len(plane) + len(copies))
    outs.step(2, placed=True)

    for copy in load[:2]:
        copy.wait()
    piece = 64
    halves = [slice(h * part_width, (h + 1) * part_width) for h in range(2)]

    def norm_piece(at, mixer_sum):
        place = pl.ds(pl.multiple_of(at * piece, piece), piece)
        middle = middle_ref[place, :]
        second = jnp.concatenate([work[h, place, :] for h in range(2)], axis=1)
        scale = lax.rsqrt(jnp.mean(middle * middle, axis=1, keepdims=True) + epsilon)
        weighted = gains_ref[1:2, :] * second
        inner = jnp.sum(weighted * middle, axis=1, keepdims=True)
        grad = (
            cot_ref[place, :].astype(full)
            + scale * weighted
            - middle * (scale * scale * scale) * (inner / width)
        )
        branch[row, place, :] = grad.astype(low)
        return mixer_sum + jnp.sum(second * middle * scale, axis=0, keepdims=True)

    mixer_sum = lax.fori_loop(0, rows // piece, norm_piece, jnp.zeros((1, width), full))
    quarter_lanes = sums.shape[2]
    parts = width // quarter_lanes
    for n in range(parts):
        sums[0, parts + n : parts + n + 1, :] = mixer_sum[
            :, n * quarter_lanes : (n + 1) * quarter_lanes
        ]
    branch_copy = remote_copy(
        branch.at[row], branch.at[row], branch_sem.at[0], branch_sem.at[1], row=other
    )
    branch_copy.start()

    half_size = size // 2

    def side_rows(which):
        return pl.ds(pl.multiple_of(which * half_size, 16), half_size)

    def item_first_copies(at):
        if at == 0:
            pairs = [(item_mine.at[0], item_side.at[0])]
        else:
            there = side_rows(1 - side)
            pairs = [
                (item_mine.at[at, there], item_side.at[at, side_rows(0)]),
                (item_other.at[at, there], item_side.at[at, side_rows(1)]),
            ]
        return [
            remote_copy(
                source, target, item_sem.at[at, 2 * n], item_sem.at[at, 2 * n + 1], dp=across(1)
            )
            for n, (source, target) in enumerate(pairs)
        ]

    def item_start(at):
        for copy in item_loads(at):
            copy.wait()
        if at == 0:
            item_mine[0] = add_low(item_mine[0], item_other[0])
        for copy in item_first_copies(at):
            copy.start()

    def item_row_copy(at):
        return remote_copy(
            item_other.at[at, side_rows(side)],
            item_row.at[at],
            item_sem.at[at, 4],
            item_sem.at[at, 5],
            row=other,
        )

    def item_to_row(at):
        for copy in item_first_copies(at):
            copy.wait_recv()
        here = side_rows(side)
        item_other[at, here] = add_low(item_other[at, here], item_side[at, side_rows(1)])
        item_row_copy(at).start()
        item_mine[at, here] = add_low(item_mine[at, here], item_side[at, side_rows(0)])

    def item_extent(at):
        return pl.ds(0, size) if at == 0 else side_rows(side)

    def item_further_copy(at, number):
        extent = pl.ds(0, size if at == 0 else half_size)
        return remote_copy(
            item_mine.at[at, item_extent(at)],
            further.at[at, number - 1, extent],
            item_sem.at[at, 4 + 2 * number],
            item_sem.at[at, 5 + 2 * number],
            dp=across(bits[number]),
        )

    def item_further(at):
        extent = pl.ds(0, size if at == 0 else half_size)
        for number in range(1, sides):
            copy = item_further_copy(at, number)
            copy.start()
            copy.wait()
            landed = pltpu.make_async_copy(
                further.at[at, number - 1, extent],
                item_side.at[at, extent],
                item_load_sem.at[at, 0],
            )
            landed.start()
            landed.wait()
            here = item_extent(at)
            item_mine[at, here] = add_low(item_mine[at, here], item_side[at, extent])

    def item_last_copy(at):
        return remote_copy(
            item_mine.at[at, side_rows(side)],
            item_last.at[at],
            item_sem.at[at, 4 + 2 * sides],
            item_sem.at[at, 5 + 2 * sides],
            dp=across(1),
        )

    def item_after_row(at):
        item_row_copy(at).wait_recv()
        here = side_rows(side)
        for copy in item_first_copies(at):
            copy.wait_send()
        item_mine[at, here] = add_low(item_mine[at, here], item_row[at])
        item_further(at)
        item_last_copy(at).start()

    def item_core_copies(at):
        which, chunk = at // 2, at % 2
        total = (up_total_ref, down_total_ref)[which]
        first = core * part_width + chunk * size
        if at == 0:
            pieces = [(item_mine.at[0], pl.ds(pl.multiple_of(first, 16), size))]
        else:
            pieces = [
                (source, pl.ds(pl.multiple_of(first + of_side * half_size, 16), half_size))
                for source, of_side in (
                    (item_mine.at[at, side_rows(side)], side),
                    (item_last.at[at], 1 - side),
                )
            ]
        result = []
        for n, (source, place) in enumerate(pieces):
            base = 6 + 2 * sides + 3 * n
            result.append(
                remote_copy(
                    source,
                    total.at[place],
                    item_sem.at[at, base],
                    item_sem.at[at, base + 1],
                    dp=core_partner,
                )
            )
            result.append(
                pltpu.make_async_copy(source, total.at[place], item_sem.at[at, base + 2])
            )
        return result

    def item_finish(at):
        if at == 0:
            for copy in item_first_copies(0):
                copy.wait()
            item_mine[0] = add_low(item_mine[0], item_side[0])
            item_further(0)
        else:
            item_last_copy(at).wait_recv()
        for copy in item_core_copies(at):
            copy.start()

    def item_end(at):
        if at > 0:
            item_row_copy(at).wait_send()
            item_last_copy(at).wait_send()
        for copy in item_core_copies(at):
            copy.wait()

    item_start(1)
    for copy in load[3:]:
        copy.wait()

    branch_copy.wait_recv()
    item_to_row(1)
    item_start(0)
    outs.step(3)
    branch_all = branch[...].reshape(tokens, width)
    half_lanes = heads * head_dim // 2
    for part in range(2):
        lanes = slice(part * half_lanes, (part + 1) * half_lanes)
        grad_heads[:, lanes] = dot(branch_all, head_output_ref[lanes, :], 1, 1).astype(low)

    wo_size = wo_parts.shape[2]
    for b in range(2):
        lanes = slice(b * half_lanes, (b + 1) * half_lanes)
        value = dot(attended_ref[:, lanes], branch_all, 0, 0).astype(low)
        for part in range(2):
            wo_parts[b, part] = value[part * wo_size : (part + 1) * wo_size, :]

    def wo_core_copy(b):
        return remote_copy(
            wo_parts.at[b, 1 - core],
            wo_core.at[b],
            wo_sem.at[0, b],
            wo_sem.at[1, b],
            dp=core_partner,
        )

    for b in range(2):
        wo_core_copy(b).start()

    key_grad[...] = jnp.zeros_like(key_grad)
    value_grad[...] = jnp.zeros_like(value_grad)
    tile = tokens // 2
    window = key_ref.shape[0] - tile

    def head_step(head, carry):
        here = pl.ds(pl.multiple_of(head * head_dim, head_dim), head_dim)
        there = pl.ds(
            pl.multiple_of((head + head // per_block) * head_dim, head_dim), head_dim
        )
        for at in range(tokens // tile):
            first = at * tile
            rot = rot_ref[first : first + tile, here]
            grad = grad_heads[first : first + tile, here]
            keys = key_ref[first : first + window, :]
            values = value_ref[first : first + window, :]
            scores = dot(rot, keys, 1, 1) * head_dim ** (-0.5)
            place = lax.broadcasted_iota(jnp.int32, scores.shape, 1) + first
            query = lax.broadcasted_iota(jnp.int32, scores.shape, 0) + (first + tokens)
            allowed = (place <= query) & (place.astype(full) >= start_ref[first : first + tile, :])
            scores = jnp.where(allowed, scores, -1e30)
            exponent = jnp.exp(scores - jnp.max(scores, axis=1, keepdims=True))
            probs = exponent / jnp.sum(exponent, axis=1, keepdims=True)
            prob_grad = dot(grad, values, 1, 1)
            inner = jnp.sum(probs * prob_grad, axis=1, keepdims=True)
            score_grad = (probs * (prob_grad - inner) * head_dim ** (-0.5)).astype(low)
            rot_grad = dot(score_grad, keys)
            joint_grad[first : first + tile, there] = (
                rot_grad * cosine_ref[first : first + tile, :]
                - pltpu.roll(rot_grad, head_dim // 2, 1) * sine_ref[first : first + tile, :]
            ).astype(low)
            key_grad[first : first + window, :] += dot(score_grad, rot, 0, 0)
            value_grad[first : first + window, :] += dot(probs.astype(low), grad, 0, 0)
        return carry

    wa_size = part_width // 2
    chunk_rows = wa_size // 2

    class Lanes:
        def __init__(self, parts, core_room, row_room, sems, stretches, chunks):
            self.parts, self.core_room, self.row_room, self.sems = parts, core_room, row_room, sems
            self.stretches, self.chunks = stretches, chunks

        def core_copy(self, r0):
            return remote_copy(
                self.parts.at[r0, 1 - core],
                self.core_room.at[r0],
                self.sems.at[0, r0],
                self.sems.at[1, r0],
                dp=core_partner,
            )

        def dot(self, r0, which):
            first = pl.multiple_of(r0 * part_width + which * wa_size, 128)
            left = normed_ref[:, pl.ds(first, wa_size)]
            right = [joint_grad[:, lanes] for lanes in self.stretches]
            right = right[0] if len(right) == 1 else jnp.concatenate(right, axis=1)
            self.parts[r0, which] = dot(left, right, 0, 0).astype(low)

        def first(self):
            for r0 in (other, row):
                self.dot(r0, 1 - core)
                self.core_copy(r0).start()
            for r0 in (other, row):
                self.dot(r0, core)

        def row_copy(self, chunk):
            count = wa_size // self.chunks
            return remote_copy(
                self.parts.at[other, core, pl.ds(chunk * count, count)],
                self.row_room.at[chunk],
                self.sems.at[2, chunk],
                self.sems.at[3, chunk],
                row=other,
            )

        def to_row(self):
            self.core_copy(other).wait_recv()
            self.parts[other, core] = add_low(self.parts[other, core], self.core_room[other])
            for chunk in range(self.chunks):
                self.row_copy(chunk).start()
            self.core_copy(row).wait_recv()
            self.parts[row, core] = add_low(self.parts[row, core], self.core_room[row])

        def end(self):
            for r0 in range(2):
                self.core_copy(r0).wait_send()
            for chunk in range(self.chunks):
                self.row_copy(chunk).wait_send()

    stretches = [
        slice(b * block_lanes, b * block_lanes + query_lanes) for b in range(2)
    ]
    key_stretch = slice(query_lanes, block_lanes)
    value_stretch = slice(block_lanes + query_lanes, 2 * block_lanes)
    wq = [
        Lanes(
            wq_parts.at[b], wq_core.at[b], wq_row.at[b], wq_sem.at[b], [stretches[b]], 2
        )
        for b in range(2)
    ]
    wk = Lanes(wk_parts, wk_core, wk_row, wk_sem, [key_stretch, value_stretch], 1)

    def wo_row_copy(b):
        return remote_copy(
            wo_parts.at[b, core, :, part_lanes(other)],
            wo_row.at[b],
            wo_sem.at[2, b],
            wo_sem.at[3, b],
            row=other,
        )

    lax.fori_loop(0, 1, head_step, 0)
    for b in range(2):
        wo_core_copy(b).wait_recv()
        wo_parts[b, core] = add_low(wo_parts[b, core], wo_core[b])
        wo_row_copy(b).start()
    lax.fori_loop(1, per_block, head_step, 0)
    item_start(2)
    wq[0].first()
    lax.fori_loop(per_block, per_block + 1, head_step, 0)
    wq[0].to_row()
    lax.fori_loop(per_block + 1, heads, head_step, 0)
    pair_stage[:, :head_dim] = key_grad[:tokens, :].astype(low)
    pair_stage[:, head_dim:] = value_grad[:tokens, :].astype(low)
    odd = col % 2 == 1

    def pair_copy():
        return remote_copy(
            pair_stage, pair_arrived, pair_sem.at[0], pair_sem.at[1], col=col + 1 - 2 * (col % 2)
        )

    pl.when(odd)(lambda: pair_copy().start())
    wq[1].first()
    item_start(3)

    def over_col(lanes, stacks, arrived, send, recv, chunk, blocks):
        return ColSum(
            stacks.at[chunk], arrived.at[chunk], send.at[chunk], recv.at[chunk], col, cols, blocks
        )

    wq_total = [
        [
            over_col(
                wq[b], wq_stack.at[b], wq_arrived.at[b], wq_send.at[b], wq_recv.at[b], c, (b, 2 + b)
            )
            for c in range(2)
        ]
        for b in range(2)
    ]

    def wq_to_col(b):
        for chunk in range(2):
            wq[b].row_copy(chunk).wait_recv()
            place = pl.ds(chunk * chunk_rows, chunk_rows)
            wq_stack[b, chunk, row] = wq_parts[b, row, core, place]
            wq_stack[b, chunk, other] = wq_row[b, chunk]
            wq_total[b][chunk].step(1)

    def wq_step(b, number):
        for chunk in range(2):
            wq_total[b][chunk].step(number)

    wq[1].to_row()
    item_finish(0)
    wo_total = ColSum(wo_stack, wo_arrived, wo_send, wo_recv, col, cols, range(cols))
    for b in range(2):
        wo_row_copy(b).wait_recv()
        wo_stack[2 * row + b] = wo_parts[b, core, :, part_lanes(row)]
        wo_stack[2 * other + b] = wo_row[b]
    wo_total.step(1)
    wq_to_col(0)

    @pl.when(jnp.logical_not(odd))
    def _():
        pair_copy().wait_recv()
        key_grad[tokens:, :] += pair_arrived[:, :head_dim].astype(full)
        value_grad[tokens:, :] += pair_arrived[:, head_dim:].astype(full)

    key_total = key_grad[tokens:, :]
    joint_grad[:, key_stretch] = (
        key_total * cosine_ref[...] - pltpu.roll(key_total, head_dim // 2, 1) * sine_ref[...]
    ).astype(low)
    joint_grad[:, value_stretch] = value_grad[tokens:, :].astype(low)
    wk.first()

    normed_own = work

    def normed_dot(which):
        return dot(joint_grad[...], joint_ref[part_lanes(which), :], 1, 1)

    def normed_sums(which, value):
        product = value * normed_ref[:, part_lanes(which)].astype(full)
        gain = gains_ref[0:1, part_lanes(which)]
        total = jnp.sum(product, axis=0, keepdims=True) / gain
        for n in range(parts // 2):
            sums[0, pl.ds(which * (parts // 2) + n, 1), :] = total[
                :, n * quarter_lanes : (n + 1) * quarter_lanes
            ]
        return jnp.sum(product, axis=1, keepdims=True)

    wk.to_row()
    item_to_row(2)
    value = normed_dot(other)
    grad_heads[...] = value.astype(low)
    normed_copy = remote_copy(
        grad_heads, normed_arrived, normed_sem.at[0], normed_sem.at[1], row=other
    )
    inner = normed_sums(other, value)
    value = normed_dot(row)
    inner += normed_sums(row, value)
    for h in range(2):
        normed_own[h] = value[h * rows : (h + 1) * rows]
    inner_stage[...] = jnp.transpose(jnp.broadcast_to(inner, (tokens, head_dim)))[:8, :]
    inner_copy = remote_copy(
        inner_stage, inner_arrived, inner_sem.at[0], inner_sem.at[1], row=other
    )
    inner_copy.start()

    def sums_copies(stage):
        base = 0 if stage == 0 else len(plane)
        return [
            remote_copy(
                sums.at[stage],
                sums_arrived.at[base + n],
                sums_sem.at[base + n, 0],
                sums_sem.at[base + n, 1],
                **device,
            )
            for n, device in enumerate((plane, copies)[stage])
        ]

    def sums_start(stage):
        for copy in sums_copies(stage):
            copy.start()

    def sums_finish(stage):
        base = 0 if stage == 0 else len(plane)
        total = sums[stage]
        for n, copy in enumerate(sums_copies(stage)):
            copy.wait_recv()
            total += sums_arrived[base + n]
        sums[stage + 1] = total

    sums_start(0)
    wq_to_col(1)
    wq_step(0, 2)
    wo_total.step(2)
    wk_total = ColSum(wk_stack, wk_arrived, wk_send, wk_recv, col, cols, range(cols))
    wk.row_copy(0).wait_recv()
    for b in range(2):
        lanes = slice(b * key_lanes, (b + 1) * key_lanes)
        wk_stack[2 * row + b] = wk_parts[row, core, :, lanes]
        wk_stack[2 * other + b] = wk_row[0, :, lanes]
    wk_total.step(1)
    item_to_row(3)
    wq_step(1, 2)
    wq_step(0, 3)
    wk_total.step(2)
    normed_copy.start()
    sums_finish(0)
    sums_start(1)
    wo_total.step(3)
    wq_step(1, 3)
    wk_total.step(3)
    item_after_row(1)
    item_after_row(2)

    class Owned:
        def __init__(self, side_room, sems, targets):
            self.room, self.sems, self.targets = side_room, sems, targets

        def copy(self, number):
            return remote_copy(
                self.room.at[number % 2],
                self.room.at[2 + number],
                self.sems.at[2 * number],
                self.sems.at[2 * number + 1],
                dp=across(bits[number]),
            )

        def start(self, value):
            self.room[0] = value.astype(low)
            if sides:
                self.copy(0).start()

        def core_copies(self):
            result = []
            base, value = 2 * sides, self.room.at[sides % 2]
            return (
                remote_copy(
                    value,
                    self.targets,
                    self.sems.at[base],
                    self.sems.at[base + 1],
                    dp=core_partner,
                ),
                pltpu.make_async_copy(value, self.targets, self.sems.at[base + 2]),
            )

        def finish(self):
            for number in range(sides):
                self.copy(number).wait()
                self.room[1 - number % 2] = add_low(
                    self.room[number % 2], self.room[2 + number]
                )
                if number + 1 < sides:
                    self.copy(number + 1).start()
            for copy in self.core_copies():
                copy.start()

        def end(self):
            for copy in self.core_copies():
                copy.wait()

    def own_place(chunk, count):
        return pl.ds(pl.multiple_of(core * wa_size + chunk * count, 16), count)

    wk_owned = Owned(wk_side, wk_sem.at[4], keyval_total_ref.at[own_place(0, wa_size)])
    wq_owned = [
        Owned(wq_side.at[c], wq_side_sem.at[c], query_total_ref.at[own_place(c, chunk_rows)])
        for c in range(2)
    ]
    wo_owned = Owned(
        wo_side,
        wo_sem.at[4],
        output_total_ref.at[pl.ds(pl.multiple_of(core * wo_size, 16), wo_size)],
    )
    for b in range(2):
        for c in range(2):
            wq_total[b][c].total(wq_owned[c].start)
    wo_total.total(wo_owned.start)
    wk_total.total(wk_owned.start)

    def own_tokens(value):
        out_stack[col] = (middle_ref[...] + value).astype(low)

    outs.total(own_tokens)

    def outputs_copy():
        place = pl.ds(pl.multiple_of(row * rows, rows), rows)
        return remote_copy(
            out_stack.at[col, :, part_lanes(other)],
            outputs_ref.at[place],
            own_out_sem.at[0],
            own_out_sem.at[1],
            row=other,
        )

    outputs_copy().start()
    outputs_ref[pl.ds(pl.multiple_of(row * rows, rows), rows), :] = out_stack[
        col, :, part_lanes(row)
    ]
    item_after_row(3)
    item_finish(1)
    for c in range(2):
        wq_owned[c].finish()
    wk_owned.finish()
    wo_owned.finish()
    item_finish(2)
    sums_finish(1)
    for n in range(parts // 2):
        place = pl.ds(row * (parts // 2) + n, 1)
        lanes = slice(n * quarter_lanes, (n + 1) * quarter_lanes)
        gain_sums_ref[0:1, lanes] = sums[2, place, :]
        place = pl.ds(parts + row * (parts // 2) + n, 1)
        gain_sums_ref[1:2, lanes] = sums[2, place, :]
    item_finish(3)

    normed_copy.wait_recv()
    inner_copy.wait_recv()
    both = inner_stage[...] + inner_arrived[...]
    inner = jnp.transpose(jnp.concatenate([both] * (head_dim // 8), axis=0))[:, 0:1]
    for h in range(2):
        place = slice(h * rows, (h + 1) * rows)
        scale = scale_ref[place, :]
        normed_grad = normed_own[h] + normed_arrived[place, :].astype(full)
        input_grad_ref[place, :] = (
            branch[h, :, part_lanes(row)].astype(full)
            + scale * (gains_ref[0:1, part_lanes(row)] * normed_grad)
            - inputs_ref[place, :].astype(full) * (scale * scale) * (inner[place, :] / width)
        ).astype(low)

    branch_copy.wait_send()
    pl.when(odd)(lambda: pair_copy().wait_send())
    for b in range(2):
        wo_core_copy(b).wait_send()
        wo_row_copy(b).wait_send()
    for lanes in wq + [wk]:
        lanes.end()
    normed_copy.wait_send()
    inner_copy.wait_send()
    outputs_copy().wait()
    for stage in range(2):
        for copy in sums_copies(stage):
            copy.wait_send()
    outs.end(first=False)
    for total in [wo_total, wk_total] + wq_total[0] + wq_total[1]:
        total.end()
    for owned in wq_owned + [wk_owned, wo_owned]:
        owned.end()
    for at in range(items):
        item_end(at)


def finish_call(
    middle, gains, scale, start, sums, inputs, attended, rot, keys, values, cosine, sine,
    head_output, joint_weight, normed, cot_all, out_part, up_own, up_row, up_other, down_half, out_first,
    query_block, both_block,
):
    rows, width = middle.shape
    tokens, part_width = inputs.shape
    cols, dps = lax.axis_size("col"), lax.axis_size("dp")
    sides = dps.bit_length() - 2
    heads_width = attended.shape[1]
    reach = keys.shape[0]
    vmem = pl.BlockSpec(memory_space=pltpu.VMEM)
    anywhere = pl.BlockSpec(memory_space=pl.ANY)
    dma = pltpu.SemaphoreType.DMA
    hidden = 2 * up_own.shape[0]
    size = part_width // 2
    items = 4
    key_block = both_block - query_block
    wo_size, wa_size = query_block // 2, part_width // 2
    chunk = wa_size // 2
    shape = jax.ShapeDtypeStruct
    sums_count = 2 * cols - 1 + dps - 1
    return pl.pallas_call(
        finish_kernel,
        in_specs=[vmem] * 4 + [anywhere] * 18,
        out_specs=[vmem] * 6 + [anywhere] * 3,
        out_shape=[
            shape((tokens, part_width), low),
            shape((tokens, part_width), low),
            shape((2, part_width), full),
            shape((query_block, part_width), low),
            shape((part_width, query_block), low),
            shape((part_width, key_block), low),
            shape((hidden, part_width), low),
            shape((hidden, part_width), low),
            shape((items, max(sides - 1, 1), size, part_width), low),
        ],
        scratch_shapes=[
            pltpu.VMEM((2, rows, part_width), full),
            pltpu.VMEM((rows, width), low),
            pltpu.VMEM((tokens, part_width), low),
            pltpu.VMEM((tokens, heads_width), low),
            pltpu.VMEM((tokens, heads_width), low),
            pltpu.VMEM((reach, head_dim), low),
            pltpu.VMEM((reach, head_dim), low),
            pltpu.VMEM((tokens, head_dim), full),
            pltpu.VMEM((tokens, head_dim), full),
            pltpu.VMEM((heads_width, width), low),
            pltpu.VMEM((width, 2 * both_block), low),
            pltpu.VMEM((tokens, width), low),
            dma((14,)),
            pltpu.VMEM((2, rows, width), low),
            dma((2,)),
            pltpu.VMEM((cols, rows, width), low),
            pltpu.VMEM((cols + 1, rows, width), low),
            dma((cols,)),
            dma((cols + 1,)),
            dma((2,)),
            pltpu.VMEM((tokens, heads_width), low),
            pltpu.VMEM((tokens, 2 * both_block), low),
            pltpu.VMEM((reach, head_dim), full),
            pltpu.VMEM((reach, head_dim), full),
            pltpu.VMEM((tokens, 2 * head_dim), low),
            pltpu.VMEM((tokens, 2 * head_dim), low),
            dma((2,)),
            pltpu.VMEM((tokens, part_width), low),
            dma((2,)),
            pltpu.VMEM((8, tokens), full),
            pltpu.VMEM((8, tokens), full),
            dma((2,)),
            pltpu.VMEM((3, 8, width // 4), full),
            pltpu.VMEM((sums_count, 8, width // 4), full),
            dma((sums_count, 2)),
            pltpu.VMEM((items, size, part_width), low),
            pltpu.VMEM((items, size, part_width), low),
            pltpu.VMEM((items, size, part_width), low),
            pltpu.VMEM((items, size // 2, part_width), low),
            pltpu.VMEM((items, size // 2, part_width), low),
            dma((items, 12 + 2 * sides)),
            dma((items, 2)),
            pltpu.VMEM((2, 2, wo_size, width), low),
            pltpu.VMEM((2, wo_size, width), low),
            pltpu.VMEM((2, wo_size, part_width), low),
            pltpu.VMEM((cols, wo_size, part_width), low),
            pltpu.VMEM((cols + 1, wo_size, part_width), low),
            pltpu.VMEM((2 + sides, wo_size, part_width), low),
            dma((5, 3 + 2 * sides)),
            dma((cols,)),
            dma((cols + 1,)),
            pltpu.VMEM((2, 2, 2, wa_size, query_block), low),
            pltpu.VMEM((2, 2, wa_size, query_block), low),
            pltpu.VMEM((2, 2, chunk, query_block), low),
            pltpu.VMEM((2, 2, 2, chunk, query_block), low),
            pltpu.VMEM((2, 2, 3, chunk, query_block), low),
            pltpu.VMEM((2, 2 + sides, chunk, query_block), low),
            dma((2, 4, 2)),
            dma((2, 3 + 2 * sides)),
            dma((2, 2, 2)),
            dma((2, 2, 3)),
            pltpu.VMEM((2, 2, wa_size, 2 * key_block), low),
            pltpu.VMEM((2, wa_size, 2 * key_block), low),
            pltpu.VMEM((1, wa_size, 2 * key_block), low),
            pltpu.VMEM((cols, wa_size, key_block), low),
            pltpu.VMEM((cols + 1, wa_size, key_block), low),
            pltpu.VMEM((2 + sides, wa_size, key_block), low),
            dma((5, 3 + 2 * sides)),
            dma((cols,)),
            dma((cols + 1,)),
        ],
        compiler_params=pltpu.CompilerParams(
            collective_id=2, has_side_effects=True, vmem_limit_bytes=63 * 2**20
        ),
        cost_estimate=pl.CostEstimate(
            flops=10 * 10**9, bytes_accessed=40 * 10**6, transcendentals=4 * 10**6
        ),
    )(
        middle, gains, scale, start, sums, inputs, attended, rot, keys, values, cosine, sine,
        head_output, joint_weight, normed, cot_all, out_part, up_own, up_row, up_other, down_half, out_first,
    )


def shards(
    inputs,
    norm_gain,
    query_weight,
    key_value_matrix,
    output_weight,
    mixer_gain,
    gate_weight,
    up_weight,
    down_weight,
    lengths,
    routes,
    route_gates,
    cotangent,
):
    row, col = lax.axis_index("row"), lax.axis_index("col")
    part_width = inputs.shape[1]
    experts, _, units = gate_weight.shape
    hidden_width = experts * units
    query_block, keyval_block = query_weight.shape[1], key_value_matrix.shape[1]
    small = jnp.zeros((8, part_width), full)
    small = small.at[0].set(norm_gain).at[1].set(mixer_gain)
    sequences = lengths.shape[1]
    small = small.at[2, :sequences].set(lengths[0].astype(full))
    theta = rope_base ** (-jnp.arange(0, head_dim, 2, dtype=full) / head_dim)
    theta = jnp.concatenate([theta, theta])[None, :]
    gate_flat = gate_weight.swapaxes(1, 2).reshape(hidden_width, part_width)
    up_flat = up_weight.swapaxes(1, 2).reshape(hidden_width, part_width)
    down_flat = down_weight.reshape(hidden_width, part_width)
    (
        normed,
        first_scale,
        gains,
        keys,
        values,
        cosine,
        sine,
        start,
        attended,
        rot,
        joint_weight,
        head_output,
        middle,
        expert_own,
        tables,
        cot_all,
        gate_other,
        up_other_half,
        down_other,
    ) = prologue_call(
        inputs, small, theta, routes.T, route_gates.T, cotangent, query_weight, key_value_matrix,
        output_weight, gate_flat, up_flat, down_flat, sequences, experts,
    )
    second_grad, out_part, gate_total, up_own, up_row, up_other, down_half, out_first = experts_call(
        expert_own, cot_all, tables, gate_flat, gate_other, up_flat, up_other_half, down_flat, down_other
    )

    both_block = query_block + keyval_block
    (
        outputs,
        input_grad,
        gain_sums,
        output_total,
        query_total,
        keyval_total,
        up_total,
        down_total,
        _,
    ) = finish_call(
        middle, gains, first_scale, start, second_grad, inputs, attended, rot, keys, values,
        cosine, sine, head_output, joint_weight, normed, cot_all, out_part, up_own, up_row,
        up_other, down_half, out_first, query_block, both_block,
    )
    norm_total, mixer_total = gain_sums[0], gain_sums[1]

    def by_expert(flat):
        return flat.astype(full).reshape(experts, units, part_width).swapaxes(1, 2)

    gate_total, up_total = by_expert(gate_total), by_expert(up_total)
    down_total = down_total.reshape(experts, units, part_width).astype(full)
    output_total = output_total.astype(full)
    query_total, keyval_total = query_total.astype(full), keyval_total.astype(full)
    return (
        outputs,
        input_grad,
        norm_total,
        query_total,
        keyval_total,
        output_total,
        mixer_total,
        gate_total,
        up_total,
        down_total,
    )


def solution(mesh):
    return jax.shard_map(
        shards,
        mesh=mesh,
        in_specs=(
            P(("dp", "col"), "row"),
            P("row"),
            P("row", "col"),
            P("row", "col"),
            P("col", "row"),
            P("row"),
            P(None, "row", "col"),
            P(None, "row", "col"),
            P(None, "col", "row"),
            P(("dp", "row"), None),
            P("dp", None),
            P("dp", None),
            P(("dp", "col"), "row"),
        ),
        out_specs=(
            P(("dp", "col"), "row"),
            P(("dp", "col"), "row"),
            P("row"),
            P("row", "col"),
            P("row", "col"),
            P("col", "row"),
            P("row"),
            P(None, "row", "col"),
            P(None, "row", "col"),
            P(None, "col", "row"),
        ),
        check_vma=False,
    )
```

```python
import functools

import jax
import jax.numpy as jnp
from jax import lax
from jax.experimental import pallas as pl
from jax.experimental.pallas import tpu as pltpu
from jax.sharding import PartitionSpec as P

epsilon = 1e-06
rope_base = 1000000.0
head_dim = 128
low = jnp.bfloat16
full = jnp.float32


def dot(left, right, left_dim=1, right_dim=0):
    return lax.dot_general(
        left, right, (((left_dim,), (right_dim,)), ((), ())), preferred_element_type=full
    )


def remote_copy(source, target, send_sem, recv_sem, **device):
    return pltpu.make_async_remote_copy(
        src_ref=source,
        dst_ref=target,
        send_sem=send_sem,
        recv_sem=recv_sem,
        device_id=device,
        device_id_type=pl.DeviceIdType.MESH,
    )


def add_low(left, right):
    return (left.astype(full) + right.astype(full)).astype(low)


class ColSum:
    def __init__(self, stack, arrived, send_sem, recv_sem, col, count, blocks):
        self.stack, self.arrived, self.send_sem, self.recv_sem = stack, arrived, send_sem, recv_sem
        self.col, self.last, self.blocks = col, count - 1, list(blocks)

    def copy(self, block, at, right):
        neighbour = at + 1 if right else at - 1
        n = self.blocks.index(block)
        slot = n if right or block != neighbour else len(self.blocks)
        return remote_copy(
            self.stack.at[n],
            self.arrived.at[slot],
            self.send_sem.at[n],
            self.recv_sem.at[slot],
            col=neighbour,
        )

    def wait(self, slot, at):
        remote_copy(
            self.arrived.at[slot],
            self.arrived.at[slot],
            self.send_sem.at[0],
            self.recv_sem.at[slot],
            col=at + 1 if at == 0 else at - 1,
        ).wait_recv()

    def step(self, number, placed=False):
        for at in range(self.last + 1):
            ways = []
            for right in (True, False):
                block = at + self.last + 1 - number if right else at - self.last - 1 + number
                if block in self.blocks:
                    ways.append((block, right))
            if not ways:
                continue

            @pl.when(self.col == at)
            def _(at=at, ways=ways):
                for block, right in ways:
                    n = self.blocks.index(block)
                    if 0 < at < self.last:
                        if not placed:
                            self.wait(n, at)
                        self.stack[n] = add_low(self.stack[n], self.arrived[n])
                    self.copy(block, at, right).start()

    def total(self, part):
        for n, at in enumerate(self.blocks):

            @pl.when(self.col == at)
            def _(n=n, at=at):
                value = self.stack[n].astype(full)
                if at > 0:
                    self.wait(n, at)
                    value += self.arrived[n].astype(full)
                if at < self.last:
                    self.wait(len(self.blocks), at)
                    value += self.arrived[len(self.blocks)].astype(full)
                part(value)

    def end(self, first=True):
        for at in range(self.last + 1):

            @pl.when(self.col == at)
            def _(at=at):
                for block in self.blocks:
                    if block != at and (first or abs(block - at) < self.last):
                        self.copy(block, at, block > at).wait_send()


def experts_kernel(
    own_ref,
    cot_ref,
    table_ref,
    gate_hbm,
    gate_other_hbm,
    up_hbm,
    up_other_hbm,
    down_hbm,
    down_quarter_hbm,
    sum_ref,
    out_part_ref,
    gate_total_ref,
    up_own_ref,
    up_row_ref,
    up_other_ref,
    down_half_ref,
    out_first_ref,
    weights,
    expert_in,
    gate_grad,
    up_grad,
    hidden,
    send_stage,
    arrived,
    parts,
    stage,
    weights_sem,
    down_sem,
    ready,
    ag_recv,
    ag_right,
    ag_left,
    rs_recv,
    rs_send,
    core_send,
    core_recv,
    row_send,
    row_recv,
    side_send,
    side_recv,
    final_sem,
    local_sem,
    out_sem,
):
    row, col, dp = lax.axis_index("row"), lax.axis_index("col"), lax.axis_index("dp")
    dps = lax.axis_size("dp")
    core, other = dp % 2, 1 - row
    core_partner = dp + 1 - 2 * core
    side_bits = list(range(1, dps.bit_length() - 1))
    sides = len(side_bits)
    last = cot_ref.shape[0] - 1
    rows, width = own_ref.shape
    half = width // 2
    size = half // 2
    inner = (col > 0) & (col < last)

    def across(bit):
        on = (dp // (1 << bit)) % 2
        return dp + (1 << bit) * (1 - 2 * on)

    def half_lanes(which):
        return pl.ds(pl.multiple_of(which * half, half), half)

    gate_ref, up_ref, down_ref = weights.at[0], weights.at[1], weights.at[2]
    sources = (gate_hbm, gate_other_hbm, up_hbm, up_other_hbm, down_hbm)
    loads = [
        pltpu.make_async_copy(
            source,
            weights.at[i // 2, :, half_lanes((row, other)[i % 2])],
            weights_sem.at[i],
        )
        for i, source in enumerate(sources)
    ]
    for copy in loads:
        copy.start()

    barrier = pltpu.get_barrier_semaphore()

    def greet(semaphore, **device):
        pl.semaphore_signal(
            semaphore, inc=1, device_id=device, device_id_type=pl.DeviceIdType.MESH
        )

    greet(barrier, dp=core_partner)
    greet(barrier, row=other)
    for bit in side_bits:
        greet(barrier, dp=across(bit))
    pl.when(col > 0)(lambda: greet(barrier, col=col - 1))
    pl.when(col < last)(lambda: greet(barrier, col=col + 1))
    expert_in[col] = own_ref[...]
    pl.when(inner)(lambda: pl.semaphore_wait(barrier, 4 + sides))
    pl.when(jnp.logical_not(inner))(lambda: pl.semaphore_wait(barrier, 3 + sides))

    def ag_copy(block, right):
        return remote_copy(
            expert_in.at[block],
            expert_in.at[block],
            (ag_right if right else ag_left).at[block],
            ag_recv.at[block],
            col=col + 1 if right else col - 1,
        )

    def rs_copy(block, part, right):
        neighbour = col + 1 if right else col - 1
        slot = block if right else jnp.where(block == neighbour, last + 1, block)
        return remote_copy(
            send_stage.at[block, part],
            arrived.at[slot, part],
            rs_send.at[block, part],
            rs_recv.at[slot, part],
            col=neighbour,
        )

    def rs_wait(slot, part):
        remote_copy(
            arrived.at[slot, part],
            arrived.at[slot, part],
            rs_send.at[0, part],
            rs_recv.at[slot, part],
            col=jnp.where(col > 0, col - 1, col + 1),
        ).wait_recv()

    pl.when(col < last)(lambda: ag_copy(col, True).start())
    pl.when(col > 0)(lambda: ag_copy(col, False).start())
    quarter_size = down_hbm.shape[0] // 4
    quarter = dp % 4

    def down_place(which, piece):
        first = which * quarter_size + piece * (quarter_size // 2)
        return pl.ds(pl.multiple_of(first, 16), quarter_size // 2)

    def down_piece(piece):
        return down_quarter_hbm.at[pl.ds(piece * (quarter_size // 2), quarter_size // 2)]

    def down_side(piece):
        return remote_copy(
            down_piece(piece),
            weights.at[2, down_place(quarter, piece), half_lanes(other)],
            down_sem.at[piece, 2],
            down_sem.at[piece, 3],
            dp=across(1),
        )

    def down_here(piece):
        there = weights.at[2, down_place(quarter, piece), half_lanes(other)]
        return pltpu.make_async_copy(down_piece(piece), there, down_sem.at[piece, 0])

    def down_core(piece, n):
        there = weights.at[2, down_place(core + 2 * n, piece), half_lanes(other)]
        return remote_copy(
            there,
            there,
            down_sem.at[piece, 4 + 2 * n],
            down_sem.at[piece, 5 + 2 * n],
            dp=core_partner,
        )

    for piece in range(2):
        down_side(piece).start()
        down_here(piece).start()
    for copy in loads[:4]:
        copy.wait()

    def products(block):
        tokens = expert_in[block]
        table = table_ref[block]
        experts = table.shape[1]
        units = width // experts
        for g in range(2):
            cols = slice(g * half, (g + 1) * half)
            gate = dot(tokens, gate_ref[cols, :], 1, 1)
            up = dot(tokens, up_ref[cols, :], 1, 1)
            lane = lax.broadcasted_iota(jnp.int32, gate.shape, 1)
            first = g * experts // 2
            chosen = jnp.broadcast_to(table[:, first : first + 1], gate.shape)
            for e in range(1, experts // 2):
                chosen = jnp.where(lane >= e * units, table[:, first + e : first + e + 1], chosen)
            sigmoid = 1.0 / (1.0 + jnp.exp(-gate))
            silu = gate * sigmoid
            up = up * chosen
            hidden[block, :, cols] = (silu * up).astype(low)
            gate_grad[block, :, cols] = (up * (sigmoid * (1.0 + gate * (1.0 - sigmoid)))).astype(low)
            up_grad[block, :, cols] = (silu * chosen).astype(low)

    def gradients(block):
        grads = cot_ref[block]
        for g in range(2):
            cols = slice(g * half, (g + 1) * half)
            grad = dot(grads, down_ref[cols, :], 1, 1)
            gate_grad[block, :, cols] = (grad * gate_grad[block, :, cols].astype(full)).astype(low)
            up_grad[block, :, cols] = (grad * up_grad[block, :, cols].astype(full)).astype(low)
        gates_now, ups_now = gate_grad[block], up_grad[block]
        for part in range(2):
            cols = slice(part * half, (part + 1) * half)
            total = dot(gates_now, gate_ref[:, cols]) + dot(ups_now, up_ref[:, cols])
            send_stage[block, part] = total.astype(low)
            pl.when((col == 0) & (block != col))(lambda: rs_copy(block, part, True).start())
            pl.when((col == last) & (block != col))(lambda: rs_copy(block, part, False).start())
        out_part_ref[block] = dot(hidden[block], down_ref[...]).astype(low)

    def block_of(i):
        return jnp.where(i % 2 == 1, col - (i + 1) // 2, col + (i + 1) // 2)

    def pass_on(apart):
        @pl.when(col - apart >= 0)
        def _():
            ag_copy(col - apart, True).wait_recv()
            pl.when(col < last)(lambda: ag_copy(col - apart, True).start())

        @pl.when(col + apart <= last)
        def _():
            ag_copy(col + apart, False).wait_recv()
            pl.when(col > 0)(lambda: ag_copy(col + apart, False).start())

    def present(block):
        return (block >= 0) & (block <= last)

    def near_products(i, carry):
        pl.when(i == 1)(lambda: pass_on(1))
        pl.when(present(block_of(i)))(lambda: products(block_of(i)))
        return carry

    lax.fori_loop(0, 3, near_products, 0)
    for piece in range(2):
        down_here(piece).wait()
        down_side(piece).wait_recv()
        for n in range(2):
            down_core(piece, n).start()
    loads[4].wait()
    for piece in range(2):
        for n in range(2):
            down_core(piece, n).wait_recv()

    def near_gradients(n, carry):
        i = (n + 1) % 3
        pl.when(i == 0)(lambda: pass_on(2))
        pl.when(present(block_of(i)))(lambda: gradients(block_of(i)))
        return carry

    lax.fori_loop(0, 3, near_gradients, 0)

    def far_blocks(i, carry):
        pl.when(i == 5)(lambda: pass_on(3))

        @pl.when(present(block_of(i)))
        def _():
            products(block_of(i))
            gradients(block_of(i))

        return carry

    lax.fori_loop(3, 2 * last + 1, far_blocks, 0)
    for piece in range(2):
        down_side(piece).wait_send()
        for n in range(2):
            down_core(piece, n).wait_send()

    greet(ready.at[0], dp=core_partner)
    greet(ready.at[1], row=other)
    for number, bit in enumerate(side_bits):
        greet(ready.at[2 + number], dp=across(bit))

    def room(which, down, right):
        return weights.at[
            which, pl.ds(down * half, half), pl.ds(right * half, half)
        ]

    def forward(block, part, right):
        rs_wait(block, part)
        send_stage[block, part] = add_low(send_stage[block, part], arrived[block, part])
        rs_copy(block, part, right).start()

    def event(number, part):
        blocks = ((2, 1), (3, 0), (0, 3))[number]
        pl.when(col == 1)(lambda: forward(blocks[0], part, number < 2))
        pl.when(col == 2)(lambda: forward(blocks[1], part, number == 2))

    def core_copy(at):
        if at < 4:
            target = room(at // 2, 0, at % 2)
        else:
            target = room(2, 0, at - 4)
        return remote_copy(
            stage.at[at % 2], target, core_send.at[at], core_recv.at[at], dp=core_partner
        )

    def stage_free(at):
        if at >= 2:
            core_copy(at - 2).wait_send()

    def core_dot(at):
        left = (gate_grad, up_grad)[at // 2]
        right = expert_in[:, :, half_lanes(row if at % 2 else other)].reshape(-1, half)
        stage_free(at)
        stage[at % 2] = dot(
            left[:, :, half_lanes(1 - core)].reshape(-1, half), right, 0, 0
        ).astype(low)
        core_copy(at).start()
        parts[at] = dot(left[:, :, half_lanes(core)].reshape(-1, half), right, 0, 0).astype(low)

    def core_sum(at):
        core_copy(at).wait_recv()
        parts[at] = add_low(parts[at], room(at // 2, 0, at % 2)[...])

    def down_dot_partner():
        left = hidden[:, :, half_lanes(1 - core)].reshape(-1, half)
        for part in range(2):
            lanes = slice(part * half, (part + 1) * half)
            right = cot_ref[:, :, lanes].reshape(-1, half)
            stage_free(4 + part)
            stage[part] = dot(left, right, 0, 0).astype(low)
            core_copy(4 + part).start()

    def down_dot_own():
        left = hidden[:, :, half_lanes(core)].reshape(-1, half)
        for part in range(2):
            lanes = slice(part * half, (part + 1) * half)
            right = cot_ref[:, :, lanes].reshape(-1, half)
            room(2, 1, part)[...] = dot(left, right, 0, 0).astype(low)

    def down_sum():
        for part in range(2):
            core_copy(4 + part).wait_recv()
            room(2, 1, part)[...] = add_low(room(2, 1, part)[...], room(2, 0, part)[...])

    down_out = pltpu.make_async_copy(
        weights.at[2, pl.ds(half, half)], down_half_ref, local_sem.at[0]
    )
    up_out = pltpu.make_async_copy(parts.at[3], up_own_ref, local_sem.at[1])
    up_rest = pltpu.make_async_copy(
        parts.at[2, pl.ds(size, size)], up_other_ref, local_sem.at[2]
    )

    def chunk_rows(chunk):
        return pl.ds(chunk * size, size)

    def row_copy(chunk):
        if chunk < 2:
            source = parts.at[0, chunk_rows(chunk)]
            target = weights.at[0, pl.ds(half + chunk * size, size), pl.ds(0, half)]
        else:
            source, target = parts.at[2, chunk_rows(0)], up_row_ref
        return remote_copy(source, target, row_send.at[chunk], row_recv.at[chunk], row=other)

    def side_room(number, chunk):
        which, right = ((0, 1), (1, 0), (1, 1))[number]
        return weights.at[
            which, pl.ds(half + chunk * size, size), pl.ds(right * half, half)
        ]

    def side_copy(chunk, number):
        return remote_copy(
            parts.at[1 - number % 2, chunk_rows(chunk)],
            side_room(number, chunk),
            side_send.at[chunk, number],
            side_recv.at[chunk, number],
            dp=across(side_bits[number]),
        )

    def after_row(chunk):
        copy = row_copy(chunk)
        copy.wait_recv()
        copy.wait_send()
        here = chunk_rows(chunk)
        landed = weights.at[0, pl.ds(half + chunk * size, size), pl.ds(0, half)]
        parts[1, here] = add_low(parts[1, here], landed[...])
        if chunk == 0 and sides:
            for number in range(sides):
                pl.semaphore_wait(ready.at[2 + number], 1)
        if sides:
            side_copy(chunk, 0).start()

    def final_copies(chunk):
        source = parts.at[1 - sides % 2, chunk_rows(chunk)]
        first = pl.multiple_of(core * half + chunk * size, 16)
        target = gate_total_ref.at[pl.ds(first, size)]
        return (
            remote_copy(
                source, target, final_sem.at[chunk, 0], final_sem.at[chunk, 1], dp=core_partner
            ),
            pltpu.make_async_copy(source, target, final_sem.at[chunk, 2]),
        )

    def after_side(chunk):
        here = chunk_rows(chunk)
        for number in range(sides):
            copy = side_copy(chunk, number)
            copy.wait_recv()
            copy.wait_send()
            parts[number % 2, here] = add_low(
                parts[1 - number % 2, here], side_room(number, chunk)[...]
            )
            if number + 1 < sides:
                side_copy(chunk, number + 1).start()
        for copy in final_copies(chunk):
            copy.start()

    def out_copy(right):
        return remote_copy(
            out_part_ref.at[last if right else 0],
            out_first_ref,
            out_sem.at[0],
            out_sem.at[1],
            col=col + 1 if right else col - 1,
        )

    pl.semaphore_wait(ready.at[0], 1)
    core_dot(0)
    event(0, 0)
    core_sum(0)
    pl.semaphore_wait(ready.at[1], 1)
    row_copy(0).start()
    event(0, 1)
    core_dot(1)
    core_sum(1)
    core_dot(2)
    event(1, 0)
    core_dot(3)
    core_sum(2)
    up_rest.start()
    core_sum(3)
    up_out.start()
    event(1, 1)
    event(2, 0)
    after_row(0)
    row_copy(1).start()
    pl.when(col == 0)(lambda: out_copy(True).start())
    pl.when(col == last)(lambda: out_copy(False).start())
    down_dot_partner()
    event(2, 1)
    down_dot_own()
    down_sum()
    down_out.start()
    after_row(1)
    row_copy(2).start()
    after_side(0)

    for part in range(2):
        sum_ref[part] = send_stage[col, part].astype(full)

        @pl.when(col > 0)
        def _():
            rs_wait(col, part)
            sum_ref[part] += arrived[col, part].astype(full)

        @pl.when(col < last)
        def _():
            rs_wait(last + 1, part)
            sum_ref[part] += arrived[last + 1, part].astype(full)

    after_side(1)

    for block in range(last + 1):
        pl.when((block <= col) & (col < last))(lambda: ag_copy(block, True).wait_send())
        pl.when((block >= col) & (col > 0))(lambda: ag_copy(block, False).wait_send())
        for part in range(2):
            pl.when(block > col)(lambda: rs_copy(block, part, True).wait_send())
            pl.when(block < col)(lambda: rs_copy(block, part, False).wait_send())
    for at in range(4, 6):
        core_copy(at).wait_send()
    row_copy(2).wait()
    pl.when(col == 0)(lambda: out_copy(True).wait_send())
    pl.when(col == last)(lambda: out_copy(False).wait_send())
    pl.when(inner)(lambda: out_copy(False).wait_recv())
    for copy in (down_out, up_out, up_rest):
        copy.wait()
    for chunk in range(2):
        for copy in final_copies(chunk):
            copy.wait()


def experts_call(own, cot, table, *halves):
    rows, width = own.shape
    blocks, half = cot.shape[0], width // 2
    sides = lax.axis_size("dp").bit_length() - 2
    vmem = pl.BlockSpec(memory_space=pltpu.VMEM)
    anywhere = pl.BlockSpec(memory_space=pl.ANY)
    dma = pltpu.SemaphoreType.DMA
    shape = jax.ShapeDtypeStruct
    return pl.pallas_call(
        experts_kernel,
        in_specs=[vmem] * 3 + [anywhere] * 6,
        out_specs=[vmem, vmem] + [anywhere] * 6,
        out_shape=[
            shape((2, rows, half), full),
            shape((blocks, rows, width), low),
            shape((width, half), low),
            shape((half, half), low),
            shape((half // 2, half), low),
            shape((half // 2, half), low),
            shape((half, width), low),
            shape((rows, width), low),
        ],
        scratch_shapes=[pltpu.VMEM((3, width, width), low)]
        + [pltpu.VMEM((blocks, rows, width), low)] * 4
        + [
            pltpu.VMEM((blocks, 2, rows, half), low),
            pltpu.VMEM((blocks + 1, 2, rows, half), low),
            pltpu.VMEM((4, half, half), low),
            pltpu.VMEM((2, half, half), low),
            dma((5,)),
            dma((2, 8)),
            pltpu.SemaphoreType.REGULAR((2 + max(sides, 1),)),
            dma((blocks,)),
            dma((blocks,)),
            dma((blocks,)),
            dma((blocks + 1, 2)),
            dma((blocks, 2)),
            dma((6,)),
            dma((6,)),
            dma((3,)),
            dma((3,)),
            dma((2, max(sides, 1))),
            dma((2, max(sides, 1))),
            dma((2, 3)),
            dma((3,)),
            dma((2,)),
        ],
        compiler_params=pltpu.CompilerParams(
            collective_id=1, has_side_effects=True, vmem_limit_bytes=60 * 2**20
        ),
        cost_estimate=pl.CostEstimate(
            flops=9 * 2 * blocks * rows * width * width,
            bytes_accessed=12 * width * width,
            transcendentals=blocks * rows * width,
        ),
    )(own, cot, table, *halves)


def prologue_kernel(
    inputs_ref,
    small_ref,
    theta_ref,
    routes_ref,
    route_gates_ref,
    cot_ref,
    query_hbm,
    keyval_hbm,
    output_hbm,
    gate_hbm,
    up_hbm,
    down_hbm,
    normed_hbm,
    scale_ref,
    gains_ref,
    key_hbm,
    value_hbm,
    cosine_ref,
    sine_ref,
    start_ref,
    logsum_ref,
    attended_hbm,
    rot_hbm,
    joint_hbm,
    head_output_hbm,
    middle_ref,
    expert_ref,
    table_ref,
    cot_all_ref,
    gate_all_ref,
    up_all_ref,
    down_quarter_ref,
    normed_ref,
    key_ref,
    value_ref,
    attended_ref,
    rot_ref,
    joint_ref,
    head_output_ref,
    store_sem,
    inputs_all,
    inputs_sem,
    small,
    small_sem,
    projected,
    branch_own,
    branch_stage,
    branch_arrived,
    branch_sem,
    pair_sem,
    joint_line,
    joint_load,
    joint_hop,
    joint_row,
    joint_side,
    joint_core,
    output_line,
    output_load,
    output_hop,
    output_row,
    output_side,
    output_core,
    expert_row,
    expert_side,
    expert_core,
    cot_sem,
    cot_recv,
    cot_send,
    *,
    sequences,
):
    row, col, dp = lax.axis_index("row"), lax.axis_index("col"), lax.axis_index("dp")
    cols = lax.axis_size("col")
    last = cols - 1
    core, side, other = dp % 2, (dp // 2) % 2, 1 - row
    quarter = dp % 4
    core_partner, side_partner = dp + 1 - 2 * core, dp + 2 - 4 * side
    tokens, part_width = inputs_ref.shape
    width, rows = 2 * part_width, tokens // 2
    query_block, keyval_block = query_hbm.shape[1], keyval_hbm.shape[1]
    block = query_block + keyval_block
    experts = table_ref.shape[2]

    barrier = pltpu.get_barrier_semaphore()

    def greet(**device):
        pl.semaphore_signal(
            barrier, inc=1, device_id=device, device_id_type=pl.DeviceIdType.MESH
        )

    greet(row=other)
    for apart in range(1, cols):
        greet(col=(col + apart) % cols)
    greet(dp=core_partner)
    greet(dp=side_partner)

    def part_lanes(which):
        return pl.ds(pl.multiple_of(which * part_width, 128), part_width)

    inputs_all[:, part_lanes(row)] = inputs_ref[...]
    small[row] = small_ref[...]
    inputs_copy = remote_copy(
        inputs_ref,
        inputs_all.at[:, part_lanes(row)],
        inputs_sem.at[0],
        inputs_sem.at[1],
        row=other,
    )
    small_copy = remote_copy(
        small.at[row], small.at[row], small_sem.at[0], small_sem.at[1], row=other
    )

    joint_size, output_size = query_hbm.shape[0] // 4, output_hbm.shape[0] // 4

    def joint_region(r0, b, which):
        return joint_ref.at[
            pl.ds(pl.multiple_of(r0 * part_width + which * joint_size, 16), joint_size),
            pl.ds(pl.multiple_of(b * block, 128), block),
        ]

    def output_region(r0, b, which):
        return head_output_ref.at[
            pl.ds(pl.multiple_of(b * query_block + which * output_size, 16), output_size),
            part_lanes(r0),
        ]

    class Gather:
        def __init__(self, line, pieces, load, hop, row_sems, side_sems, core_sems, region):
            self.line, self.region, self.hop, self.row_sems = line, region, hop, row_sems
            self.side_sems, self.core_sems = side_sems, core_sems
            self.loads = [
                pltpu.make_async_copy(source, target, load.at[n])
                for n, (source, target) in enumerate(pieces)
            ]

        def copy(self, at, right):
            return remote_copy(
                self.line.at[at],
                self.line.at[at],
                self.hop.at[at, 1 if right else 0],
                self.hop.at[at, 2],
                col=col + 1 if right else col - 1,
            )

        def row_copy(self, b):
            return remote_copy(
                self.line.at[2 * other + b],
                self.region(row, b, quarter),
                self.row_sems.at[b, 0],
                self.row_sems.at[b, 1],
                row=other,
            )

        def side_copy(self, n):
            there = self.region((row, other)[n // 2], n % 2, quarter)
            return remote_copy(
                there, there, self.side_sems.at[n, 0], self.side_sems.at[n, 1], dp=side_partner
            )

        def core_copies(self, n):
            result = []
            for part in range(2):
                there = self.region((row, other)[n // 2], n % 2, core + 2 * part)
                result.append(
                    remote_copy(
                        there,
                        there,
                        self.core_sems.at[n, 2 * part],
                        self.core_sems.at[n, 2 * part + 1],
                        dp=core_partner,
                    )
                )
            return result

        def use(self, at):
            for b in range(2):

                @pl.when(at == 2 * row + b)
                def _(b=b):
                    there = self.region(row, b, quarter)
                    there[...] = self.line[at]
                    self.side_copy(b).start()

                @pl.when(at == 2 * other + b)
                def _(b=b):
                    self.row_copy(b).start()

        def load(self):
            for copy in self.loads:
                copy.start()

        def first(self):
            for copy in self.loads:
                copy.wait()
            pl.when(col < last)(lambda: self.copy(col, True).start())
            pl.when(col > 0)(lambda: self.copy(col, False).start())
            self.use(col)

        def step(self, apart):
            @pl.when(col - apart >= 0)
            def _():
                self.copy(col - apart, True).wait_recv()
                pl.when(col < last)(lambda: self.copy(col - apart, True).start())
                self.use(col - apart)

            @pl.when(col + apart <= last)
            def _():
                self.copy(col + apart, False).wait_recv()
                pl.when(col > 0)(lambda: self.copy(col + apart, False).start())
                self.use(col + apart)

        def from_row(self):
            for b in range(2):
                self.row_copy(b).wait_recv()
                self.side_copy(2 + b).start()

        def to_core(self):
            for n in range(4):
                self.side_copy(n).wait_recv()
                for copy in self.core_copies(n):
                    copy.start()

        def ready(self):
            for n in range(4):
                for copy in self.core_copies(n):
                    copy.wait_recv()

        def end(self):
            for at in range(cols):
                pl.when((at <= col) & (col < last))(lambda: self.copy(at, True).wait_send())
                pl.when((at >= col) & (col > 0))(lambda: self.copy(at, False).wait_send())
            for b in range(2):
                self.row_copy(b).wait_send()
            for n in range(4):
                self.side_copy(n).wait_send()
                for copy in self.core_copies(n):
                    copy.wait_send()

    first_joint = pl.ds(pl.multiple_of(quarter * joint_size, 16), joint_size)
    first_output = pl.ds(pl.multiple_of(quarter * output_size, 16), output_size)
    joint = Gather(
        joint_line,
        (
            (query_hbm.at[first_joint], joint_line.at[col, :, pl.ds(0, query_block)]),
            (keyval_hbm.at[first_joint], joint_line.at[col, :, pl.ds(query_block, keyval_block)]),
        ),
        joint_load,
        joint_hop,
        joint_row,
        joint_side,
        joint_core,
        joint_region,
    )
    output = Gather(
        output_line,
        ((output_hbm.at[first_output], output_line.at[col]),),
        output_load,
        output_hop,
        output_row,
        output_side,
        output_core,
        output_region,
    )

    def token_rows(which):
        return pl.ds(pl.multiple_of(which * rows, 16), rows)

    cot_row = remote_copy(
        cot_ref.at[token_rows(other)],
        cot_all_ref.at[col, :, part_lanes(row)],
        cot_sem.at[0],
        cot_sem.at[1],
        row=other,
    )

    def cot_copy(block_at, right):
        return remote_copy(
            cot_all_ref.at[block_at],
            cot_all_ref.at[block_at],
            cot_send.at[block_at, 1 if right else 0],
            cot_recv.at[block_at],
            col=col + 1 if right else col - 1,
        )

    def cot_first():
        cot_row.wait_recv()
        pl.when(col < last)(lambda: cot_copy(col, True).start())
        pl.when(col > 0)(lambda: cot_copy(col, False).start())

    def cot_pass(apart):
        @pl.when(col - apart >= 0)
        def _():
            cot_copy(col - apart, True).wait_recv()
            pl.when(col < last)(lambda: cot_copy(col - apart, True).start())

        @pl.when(col + apart <= last)
        def _():
            cot_copy(col + apart, False).wait_recv()
            pl.when(col > 0)(lambda: cot_copy(col + apart, False).start())

    expert_size = gate_hbm.shape[0] // 4
    weights = (gate_hbm, up_hbm)
    totals = (gate_all_ref, up_all_ref)

    def expert_region(which, of_quarter):
        first = pl.multiple_of(of_quarter * expert_size, 16)
        return totals[which].at[pl.ds(first, expert_size)]

    def expert_row_copy(which):
        first = pl.multiple_of(quarter * expert_size, 16)
        return remote_copy(
            weights[which].at[pl.ds(first, expert_size)],
            expert_region(which, quarter),
            expert_row.at[which, 0],
            expert_row.at[which, 1],
            row=other,
        )

    def down_row_copy():
        first = pl.multiple_of(quarter * expert_size, 16)
        return remote_copy(
            down_hbm.at[pl.ds(first, expert_size)],
            down_quarter_ref,
            expert_row.at[2, 0],
            expert_row.at[2, 1],
            row=other,
        )

    def expert_side_copy(which):
        there = expert_region(which, quarter)
        return remote_copy(
            there, there, expert_side.at[which, 0], expert_side.at[which, 1], dp=side_partner
        )

    def expert_core_copies(which):
        result = []
        for n in range(2):
            there = expert_region(which, core + 2 * n)
            result.append(
                remote_copy(
                    there,
                    there,
                    expert_core.at[which, 2 * n],
                    expert_core.at[which, 2 * n + 1],
                    dp=core_partner,
                )
            )
        return result

    def expert_after_row(which):
        expert_row_copy(which).wait_recv()
        expert_side_copy(which).start()

    def expert_after_side(which):
        expert_side_copy(which).wait_recv()
        for copy in expert_core_copies(which):
            copy.start()

    store_pairs = (
        (normed_ref, normed_hbm),
        (key_ref, key_hbm),
        (value_ref, value_hbm),
        (attended_ref, attended_hbm),
        (rot_ref, rot_hbm),
        (joint_ref, joint_hbm),
        (head_output_ref, head_output_hbm),
    )
    stores = [
        pltpu.make_async_copy(source, target, store_sem.at[n])
        for n, (source, target) in enumerate(store_pairs)
    ]
    joint.load()
    output.load()
    pl.semaphore_wait(barrier, cols + 2)
    joint.first()
    small_copy.start()
    cot_row.start()
    cot_all_ref[col, :, part_lanes(row)] = cot_ref[token_rows(row), :]

    for at in range(cols):
        place = pl.ds(pl.multiple_of(at * tokens + row * rows, 128), rows)
        chosen, gates = routes_ref[:, place], route_gates_ref[:, place]
        expert = lax.broadcasted_iota(jnp.int32, (experts, rows), 0)
        table = jnp.zeros((experts, rows), full)
        for k in range(chosen.shape[0]):
            table += jnp.where(chosen[k : k + 1, :] == expert, gates[k : k + 1, :], 0.0)
        table_ref[at] = jnp.transpose(table)
    joint.step(1)

    small_copy.wait_recv()
    gains_ref[:, :part_width] = small[0, 0:2, :]
    gains_ref[:, part_width:] = small[1, 0:2, :]
    half = col // 2
    lens = small[half, 2:3, :]
    odd = (col % 2).astype(full)
    place = lax.broadcasted_iota(jnp.int32, (tokens, 1), 0).astype(full) + odd * tokens
    begin = jnp.zeros((tokens, 1), full)
    total = lens[:, 0:1]
    for n in range(1, sequences):
        begin = jnp.where(place >= total, total, begin)
        total = total + lens[:, n : n + 1]
    start_ref[...] = begin + (1.0 - odd) * tokens
    cot_first()
    inputs_copy.start()
    angles = (place - begin) * theta_ref[...]
    cosine_ref[...] = jnp.cos(angles)
    sine = jnp.sin(angles)
    lane = lax.broadcasted_iota(jnp.int32, sine.shape, 1)
    sine_ref[...] = jnp.where(lane < head_dim // 2, -sine, sine)

    joint.step(2)
    joint.step(3)
    output.first()
    joint.from_row()
    output.step(1)
    inputs_copy.wait_recv()
    expert_row_copy(0).start()

    piece = 64

    def norm_piece(at, carry):
        here = pl.ds(pl.multiple_of(at * piece, piece), piece)
        values = inputs_all[here, :].astype(full)
        scale = lax.rsqrt(jnp.mean(values * values, axis=1, keepdims=True) + epsilon)
        scale_ref[here, :] = scale
        for which in range(2):
            lanes = slice(which * part_width, (which + 1) * part_width)
            normed_ref[here, lanes] = (values[:, lanes] * scale * small[which, 0:1, :]).astype(low)
        return carry

    lax.fori_loop(0, tokens // piece, norm_piece, 0)
    joint.to_core()
    output.step(2)
    cot_pass(1)
    joint.ready()
    stores[0].start()
    stores[5].start()

    own = pl.ds(tokens, tokens)
    key = dot(normed_ref[...], joint_ref[:, query_block:block])
    key_ref[own, :] = (
        key * cosine_ref[...] + pltpu.roll(key, head_dim // 2, 1) * sine_ref[...]
    ).astype(low)
    value_ref[own, :] = dot(normed_ref[...], joint_ref[:, block + query_block :]).astype(low)

    def pair_copies():
        return [
            remote_copy(
                ref.at[own],
                ref.at[pl.ds(0, tokens)],
                pair_sem.at[n, 0],
                pair_sem.at[n, 1],
                col=col + 1 - 2 * (col % 2),
            )
            for n, ref in enumerate((key_ref, value_ref))
        ]

    @pl.when(col % 2 == 0)
    def _():
        for copy in pair_copies():
            copy.start()
        key_ref[:tokens, :] = jnp.zeros((tokens, head_dim), low)
        value_ref[:tokens, :] = jnp.zeros((tokens, head_dim), low)

    for b in range(2):
        lanes = slice(b * query_block, (b + 1) * query_block)
        projected[:, lanes] = dot(
            normed_ref[...], joint_ref[:, b * block : b * block + query_block]
        )
    output.step(3)
    output.from_row()
    expert_after_row(0)
    expert_row_copy(1).start()
    output.to_core()

    @pl.when(col % 2 == 1)
    def _():
        for copy in pair_copies():
            copy.wait_recv()

    heads = 2 * query_block // head_dim
    tile = rows
    window = key_ref.shape[0] - tile

    def attend(which):
        first = which * tile
        here = pl.ds(pl.multiple_of(first, 16), tile)
        reach = pl.ds(pl.multiple_of(first, 16), window)

        def head_step(head, carry):
            lanes = pl.ds(pl.multiple_of(head * head_dim, head_dim), head_dim)
            pre = projected[here, lanes]
            rot = (
                pre * cosine_ref[here, :] + pltpu.roll(pre, head_dim // 2, 1) * sine_ref[here, :]
            ).astype(low)
            rot_ref[here, lanes] = rot
            scores = dot(rot, key_ref[reach, :], 1, 1) * head_dim ** (-0.5)
            key_place = lax.broadcasted_iota(jnp.int32, scores.shape, 1) + first
            query_place = lax.broadcasted_iota(jnp.int32, scores.shape, 0) + (first + tokens)
            allowed = (key_place <= query_place) & (
                key_place.astype(full) >= start_ref[here, :]
            )
            scores = jnp.where(allowed, scores, -1e30)
            most = jnp.max(scores, axis=1, keepdims=True)
            exponent = jnp.exp(scores - most)
            total = jnp.sum(exponent, axis=1, keepdims=True)
            weights = exponent / total
            attended_ref[here, lanes] = dot(weights.astype(low), value_ref[reach, :]).astype(low)
            lane = lax.broadcasted_iota(jnp.int32, (tile, head_dim), 1)
            logsum_ref[here, :] = jnp.where(
                lane == head, most + jnp.log(total), logsum_ref[here, :]
            )
            return carry

        lax.fori_loop(0, heads, head_step, 0)

    logsum_ref[...] = jnp.zeros_like(logsum_ref)
    attend(other)
    output.ready()

    def branch_copy(part):
        return remote_copy(
            branch_stage.at[part],
            branch_arrived.at[part],
            branch_sem.at[part, 0],
            branch_sem.at[part, 1],
            row=other,
        )

    theirs = attended_ref[token_rows(other), :]
    for part in range(2):
        lanes = slice(part * part_width, (part + 1) * part_width)
        branch_stage[part] = dot(theirs, head_output_ref[:, lanes]).astype(low)
        branch_copy(part).start()
    cot_pass(2)
    attend(row)
    mine = attended_ref[token_rows(row), :]
    branch_own[...] = dot(mine, head_output_ref[...])
    for n in (1, 2, 3, 4, 6):
        stores[n].start()
    expert_after_row(1)
    expert_after_side(0)
    for part in range(2):
        lanes = slice(part * part_width, (part + 1) * part_width)
        branch_copy(part).wait_recv()
        middle_ref[:, lanes] = (
            inputs_all[token_rows(row), lanes].astype(full)
            + branch_own[:, lanes]
            + branch_arrived[part].astype(full)
        )

    down_row_copy().start()

    def second_piece(at, carry):
        here = pl.ds(pl.multiple_of(at * piece, piece), piece)
        values = middle_ref[here, :]
        scale = lax.rsqrt(jnp.mean(values * values, axis=1, keepdims=True) + epsilon)
        expert_ref[here, :] = (values * scale * gains_ref[1:2, :]).astype(low)
        return carry

    lax.fori_loop(0, rows // piece, second_piece, 0)
    cot_pass(3)
    expert_after_side(1)

    inputs_copy.wait_send()
    small_copy.wait_send()
    joint.end()
    output.end()
    for copy in stores:
        copy.wait()
    down_row_copy().wait()
    for which in range(2):
        expert_row_copy(which).wait_send()
        expert_side_copy(which).wait_send()
        for copy in expert_core_copies(which):
            copy.wait()
    cot_row.wait_send()
    for at in range(cols):
        pl.when((at <= col) & (col < last))(lambda: cot_copy(at, True).wait_send())
        pl.when((at >= col) & (col > 0))(lambda: cot_copy(at, False).wait_send())

    @pl.when(col % 2 == 0)
    def _():
        for copy in pair_copies():
            copy.wait_send()

    for part in range(2):
        branch_copy(part).wait_send()


def prologue_call(
    inputs, small, theta, routes, route_gates, cotangent, query_weight, key_value_matrix,
    output_weight, gate_flat, up_flat, down_flat, sequences, experts,
):
    tokens, part_width = inputs.shape
    cols = lax.axis_size("col")
    width, rows = 2 * part_width, tokens // 2
    query_block, keyval_block = query_weight.shape[1], key_value_matrix.shape[1]
    block = query_block + keyval_block
    hidden = gate_flat.shape[0]
    vmem = pl.BlockSpec(memory_space=pltpu.VMEM)
    anywhere = pl.BlockSpec(memory_space=pl.ANY)
    dma = pltpu.SemaphoreType.DMA
    shape = jax.ShapeDtypeStruct
    return pl.pallas_call(
        functools.partial(prologue_kernel, sequences=sequences),
        in_specs=[vmem] * 6 + [anywhere] * 6,
        out_specs=[anywhere]
        + [vmem] * 2
        + [anywhere] * 2
        + [vmem] * 4
        + [anywhere] * 4
        + [vmem] * 4
        + [anywhere] * 3,
        out_shape=[
            shape((tokens, width), low),
            shape((tokens, 1), full),
            shape((2, width), full),
            shape((2 * tokens, head_dim), low),
            shape((2 * tokens, head_dim), low),
            shape((tokens, head_dim), full),
            shape((tokens, head_dim), full),
            shape((tokens, 1), full),
            shape((tokens, head_dim), full),
            shape((tokens, 2 * query_block), low),
            shape((tokens, 2 * query_block), low),
            shape((width, 2 * block), low),
            shape((2 * query_block, width), low),
            shape((rows, width), full),
            shape((rows, width), low),
            shape((cols, rows, experts), full),
            shape((cols, rows, width), low),
            shape((hidden, part_width), low),
            shape((hidden, part_width), low),
            shape((hidden // 4, part_width), low),
        ],
        scratch_shapes=[
            pltpu.VMEM((tokens, width), low),
            pltpu.VMEM((2 * tokens, head_dim), low),
            pltpu.VMEM((2 * tokens, head_dim), low),
            pltpu.VMEM((tokens, 2 * query_block), low),
            pltpu.VMEM((tokens, 2 * query_block), low),
            pltpu.VMEM((width, 2 * block), low),
            pltpu.VMEM((2 * query_block, width), low),
            dma((7,)),
            pltpu.VMEM((tokens, width), low),
            dma((2,)),
            pltpu.VMEM((2,) + small.shape, full),
            dma((2,)),
            pltpu.VMEM((tokens, 2 * query_block), full),
            pltpu.VMEM((rows, width), full),
            pltpu.VMEM((2, rows, part_width), low),
            pltpu.VMEM((2, rows, part_width), low),
            dma((2, 2)),
            dma((2, 2)),
            pltpu.VMEM((cols, part_width // 4, block), low),
            dma((2,)),
            dma((cols, 3)),
            dma((2, 2)),
            dma((4, 2)),
            dma((4, 4)),
            pltpu.VMEM((cols, query_block // 4, part_width), low),
            dma((1,)),
            dma((cols, 3)),
            dma((2, 2)),
            dma((4, 2)),
            dma((4, 4)),
            dma((3, 2)),
            dma((2, 2)),
            dma((2, 4)),
            dma((2,)),
            dma((cols,)),
            dma((cols, 2)),
        ],
        compiler_params=pltpu.CompilerParams(
            collective_id=3, has_side_effects=True, vmem_limit_bytes=60 * 2**20
        ),
        cost_estimate=pl.CostEstimate(
            flops=5 * 10**9, bytes_accessed=30 * 10**6, transcendentals=3 * 10**6
        ),
    )(
        inputs, small, theta, routes, route_gates, cotangent, query_weight, key_value_matrix,
        output_weight, gate_flat, up_flat, down_flat,
    )


def finish_kernel(
    middle_ref,
    gains_ref,
    scale_ref,
    start_ref,
    logsum_ref,
    sum_hbm,
    inputs_hbm,
    attended_hbm,
    rot_hbm,
    key_hbm,
    value_hbm,
    cosine_hbm,
    sine_hbm,
    head_output_hbm,
    joint_hbm,
    normed_hbm,
    cot_all_hbm,
    out_part_hbm,
    up_own_hbm,
    up_row_hbm,
    up_other_hbm,
    down_half_hbm,
    out_first_hbm,
    outputs_ref,
    input_grad_ref,
    gain_sums_ref,
    output_total_ref,
    query_total_ref,
    keyval_total_ref,
    up_total_ref,
    down_total_ref,
    further,
    work,
    cot_ref,
    inputs_ref,
    attended_ref,
    rot_ref,
    key_ref,
    value_ref,
    cosine_ref,
    sine_ref,
    head_output_ref,
    joint_ref,
    normed_ref,
    loads,
    branch,
    branch_sem,
    out_stack,
    out_arrived,
    out_send,
    out_recv,
    own_out_sem,
    grad_heads,
    joint_grad,
    key_grad,
    value_grad,
    pair_stage,
    pair_arrived,
    pair_sem,
    normed_arrived,
    normed_sem,
    inner_stage,
    inner_arrived,
    inner_sem,
    sums,
    sums_arrived,
    sums_sem,
    item_mine,
    item_other,
    item_side,
    item_row,
    item_last,
    item_sem,
    item_load_sem,
    wo_parts,
    wo_core,
    wo_row,
    wo_stack,
    wo_arrived,
    wo_side,
    wo_sem,
    wo_send,
    wo_recv,
    wq_parts,
    wq_core,
    wq_row,
    wq_stack,
    wq_arrived,
    wq_side,
    wq_sem,
    wq_side_sem,
    wq_send,
    wq_recv,
    wk_parts,
    wk_core,
    wk_row,
    wk_stack,
    wk_arrived,
    wk_side,
    wk_sem,
    wk_send,
    wk_recv,
):
    row, col, dp = lax.axis_index("row"), lax.axis_index("col"), lax.axis_index("dp")
    cols, dps = lax.axis_size("col"), lax.axis_size("dp")
    core, side, other = dp % 2, (dp // 2) % 2, 1 - row
    core_partner = dp + 1 - 2 * core
    bits = list(range(1, dps.bit_length() - 1))
    sides = len(bits)

    def across(bit):
        on = (dp // (1 << bit)) % 2
        return dp + (1 << bit) * (1 - 2 * on)

    rows, width = middle_ref.shape
    tokens, part_width = inputs_ref.shape
    heads = attended_ref.shape[1] // head_dim
    per_block = heads // 2
    query_lanes, key_lanes = query_total_ref.shape[1], keyval_total_ref.shape[1]
    block_lanes = query_lanes + key_lanes

    def part_lanes(which):
        return pl.ds(pl.multiple_of(which * part_width, 128), part_width)

    size = item_mine.shape[1]
    items = item_mine.shape[0]
    load_pairs = [
        (sum_hbm, work),
        (cot_all_hbm.at[col], cot_ref),
        (out_part_hbm, out_stack),
        (head_output_hbm, head_output_ref),
        (attended_hbm, attended_ref),
        (rot_hbm, rot_ref),
        (key_hbm, key_ref),
        (value_hbm, value_ref),
        (cosine_hbm, cosine_ref),
        (sine_hbm, sine_ref),
        (joint_hbm, joint_ref),
        (normed_hbm, normed_ref),
        (inputs_hbm, inputs_ref),
    ]
    load = [
        pltpu.make_async_copy(source, target, loads.at[n])
        for n, (source, target) in enumerate(load_pairs)
    ]

    def item_loads(at):
        chunk = at % 2
        place = pl.ds(chunk * size, size)
        if at < 2:
            sources = (up_own_hbm.at[place], (up_row_hbm, up_other_hbm)[chunk])
        else:
            sources = [down_half_hbm.at[place, part_lanes(which)] for which in (row, other)]
        return [
            pltpu.make_async_copy(source, target.at[at], item_load_sem.at[at, number])
            for number, (source, target) in enumerate(zip(sources, (item_mine, item_other)))
        ]

    inner_col = (col > 0) & (col < cols - 1)
    first_load = pltpu.make_async_copy(
        out_first_hbm, out_arrived.at[(cols - 1) * (2 - col) % cols], loads.at[13]
    )
    for copy in load[:3]:
        copy.start()
    pl.when(inner_col)(lambda: first_load.start())
    for copy in item_loads(1) + load[3:]:
        copy.start()
    for at in (0, 2, 3):
        for copy in item_loads(at):
            copy.start()

    barrier = pltpu.get_barrier_semaphore()

    def greet(**device):
        pl.semaphore_signal(
            barrier, inc=1, device_id=device, device_id_type=pl.DeviceIdType.MESH
        )

    plane = [
        dict(row=(row + there // cols) % 2, col=(col + there % cols) % cols)
        for there in range(1, 2 * cols)
    ]
    copies = [dict(dp=(dp + apart) % dps) for apart in range(1, dps)]
    for device in plane + copies:
        greet(**device)

    outs = ColSum(out_stack, out_arrived, out_send, out_recv, col, cols, range(cols))
    load[2].wait()
    pl.when(inner_col)(lambda: first_load.wait())
    pl.semaphore_wait(barrier, len(plane) + len(copies))
    outs.step(2, placed=True)

    for copy in load[:2]:
        copy.wait()
    piece = 64
    halves = [slice(h * part_width, (h + 1) * part_width) for h in range(2)]

    def norm_piece(at, mixer_sum):
        place = pl.ds(pl.multiple_of(at * piece, piece), piece)
        middle = middle_ref[place, :]
        second = jnp.concatenate([work[h, place, :] for h in range(2)], axis=1)
        scale = lax.rsqrt(jnp.mean(middle * middle, axis=1, keepdims=True) + epsilon)
        weighted = gains_ref[1:2, :] * second
        inner = jnp.sum(weighted * middle, axis=1, keepdims=True)
        grad = (
            cot_ref[place, :].astype(full)
            + scale * weighted
            - middle * (scale * scale * scale) * (inner / width)
        )
        branch[row, place, :] = grad.astype(low)
        return mixer_sum + jnp.sum(second * middle * scale, axis=0, keepdims=True)

    mixer_sum = lax.fori_loop(0, rows // piece, norm_piece, jnp.zeros((1, width), full))
    quarter_lanes = sums.shape[2]
    parts = width // quarter_lanes
    for n in range(parts):
        sums[0, parts + n : parts + n + 1, :] = mixer_sum[
            :, n * quarter_lanes : (n + 1) * quarter_lanes
        ]
    branch_copy = remote_copy(
        branch.at[row], branch.at[row], branch_sem.at[0], branch_sem.at[1], row=other
    )
    branch_copy.start()

    half_size = size // 2

    def side_rows(which):
        return pl.ds(pl.multiple_of(which * half_size, 16), half_size)

    def item_first_copies(at):
        if at == 0:
            pairs = [(item_mine.at[at], item_side.at[at])]
        else:
            there = side_rows(1 - side)
            pairs = [
                (item_mine.at[at, there], item_side.at[at, side_rows(0)]),
                (item_other.at[at, there], item_side.at[at, side_rows(1)]),
            ]
        return [
            remote_copy(
                source, target, item_sem.at[at, 2 * n], item_sem.at[at, 2 * n + 1], dp=across(1)
            )
            for n, (source, target) in enumerate(pairs)
        ]

    def item_start(at):
        for copy in item_loads(at):
            copy.wait()
        if at == 0:
            item_mine[0] = add_low(item_mine[0], item_other[0])
        for copy in item_first_copies(at):
            copy.start()

    def item_row_copy(at):
        return remote_copy(
            item_other.at[at, side_rows(side)],
            item_row.at[at],
            item_sem.at[at, 4],
            item_sem.at[at, 5],
            row=other,
        )

    def item_to_row(at):
        for copy in item_first_copies(at):
            copy.wait_recv()
        here = side_rows(side)
        item_other[at, here] = add_low(item_other[at, here], item_side[at, side_rows(1)])
        item_row_copy(at).start()
        item_mine[at, here] = add_low(item_mine[at, here], item_side[at, side_rows(0)])

    def item_extent(at):
        return pl.ds(0, size) if at == 0 else side_rows(side)

    def item_further_copy(at, number):
        extent = pl.ds(0, size if at == 0 else half_size)
        return remote_copy(
            item_mine.at[at, item_extent(at)],
            further.at[at, number - 1, extent],
            item_sem.at[at, 4 + 2 * number],
            item_sem.at[at, 5 + 2 * number],
            dp=across(bits[number]),
        )

    def item_further(at):
        extent = pl.ds(0, size if at == 0 else half_size)
        for number in range(1, sides):
            copy = item_further_copy(at, number)
            copy.start()
            copy.wait()
            landed = pltpu.make_async_copy(
                further.at[at, number - 1, extent],
                item_side.at[at, extent],
                item_load_sem.at[at, 0],
            )
            landed.start()
            landed.wait()
            here = item_extent(at)
            item_mine[at, here] = add_low(item_mine[at, here], item_side[at, extent])

    def item_last_copy(at):
        return remote_copy(
            item_mine.at[at, side_rows(side)],
            item_last.at[at],
            item_sem.at[at, 4 + 2 * sides],
            item_sem.at[at, 5 + 2 * sides],
            dp=across(1),
        )

    def item_after_row(at):
        item_row_copy(at).wait_recv()
        here = side_rows(side)
        for copy in item_first_copies(at):
            copy.wait_send()
        item_mine[at, here] = add_low(item_mine[at, here], item_row[at])
        item_further(at)
        item_last_copy(at).start()

    def item_core_copies(at):
        which, chunk = at // 2, at % 2
        total = (up_total_ref, down_total_ref)[which]
        first = core * part_width + chunk * size
        if at == 0:
            pieces = [(item_mine.at[0], pl.ds(pl.multiple_of(first, 16), size))]
        else:
            pieces = [
                (source, pl.ds(pl.multiple_of(first + of_side * half_size, 16), half_size))
                for source, of_side in (
                    (item_mine.at[at, side_rows(side)], side),
                    (item_last.at[at], 1 - side),
                )
            ]
        result = []
        for n, (source, place) in enumerate(pieces):
            base = 6 + 2 * sides + 3 * n
            result.append(
                remote_copy(
                    source,
                    total.at[place],
                    item_sem.at[at, base],
                    item_sem.at[at, base + 1],
                    dp=core_partner,
                )
            )
            result.append(
                pltpu.make_async_copy(source, total.at[place], item_sem.at[at, base + 2])
            )
        return result

    def item_finish(at):
        if at == 0:
            for copy in item_first_copies(at):
                copy.wait()
            item_mine[at] = add_low(item_mine[at], item_side[at])
            item_further(at)
        else:
            item_last_copy(at).wait_recv()
        for copy in item_core_copies(at):
            copy.start()

    def item_end(at):
        if at > 0:
            item_row_copy(at).wait_send()
            item_last_copy(at).wait_send()
        for copy in item_core_copies(at):
            copy.wait()

    item_start(1)
    for copy in load[3:]:
        copy.wait()

    branch_copy.wait_recv()
    item_to_row(1)
    item_start(0)
    outs.step(3)
    branch_all = branch[...].reshape(tokens, width)
    half_lanes = heads * head_dim // 2
    for part in range(2):
        lanes = slice(part * half_lanes, (part + 1) * half_lanes)
        grad_heads[:, lanes] = dot(branch_all, head_output_ref[lanes, :], 1, 1).astype(low)

    wo_size = wo_parts.shape[2]
    for b in range(2):
        lanes = slice(b * half_lanes, (b + 1) * half_lanes)
        value = dot(attended_ref[:, lanes], branch_all, 0, 0).astype(low)
        for part in range(2):
            wo_parts[b, part] = value[part * wo_size : (part + 1) * wo_size, :]

    def wo_core_copy(b):
        return remote_copy(
            wo_parts.at[b, 1 - core],
            wo_core.at[b],
            wo_sem.at[0, b],
            wo_sem.at[1, b],
            dp=core_partner,
        )

    for b in range(2):
        wo_core_copy(b).start()

    key_grad[...] = jnp.zeros_like(key_grad)
    value_grad[...] = jnp.zeros_like(value_grad)
    tile = tokens // 2
    window = key_ref.shape[0] - tile

    def head_step(head, carry):
        here = pl.ds(pl.multiple_of(head * head_dim, head_dim), head_dim)
        there = pl.ds(
            pl.multiple_of((head + head // per_block) * head_dim, head_dim), head_dim
        )
        for at in range(tokens // tile):
            first = at * tile
            rot = rot_ref[first : first + tile, here]
            grad = grad_heads[first : first + tile, here]
            keys = key_ref[first : first + window, :]
            values = value_ref[first : first + window, :]
            scores = dot(rot, keys, 1, 1) * head_dim ** (-0.5)
            place = lax.broadcasted_iota(jnp.int32, scores.shape, 1) + first
            query = lax.broadcasted_iota(jnp.int32, scores.shape, 0) + (first + tokens)
            allowed = (place <= query) & (place.astype(full) >= start_ref[first : first + tile, :])
            scores = jnp.where(allowed, scores, -1e30)
            lane = lax.broadcasted_iota(jnp.int32, (tile, head_dim), 1)
            logsum = jnp.sum(
                jnp.where(lane == head, logsum_ref[first : first + tile, :], 0.0),
                axis=1,
                keepdims=True,
            )
            probs = jnp.exp(scores - logsum)
            prob_grad = dot(grad, values, 1, 1)
            inner = jnp.sum(probs * prob_grad, axis=1, keepdims=True)
            score_grad = (probs * (prob_grad - inner) * head_dim ** (-0.5)).astype(low)
            rot_grad = dot(score_grad, keys)
            joint_grad[first : first + tile, there] = (
                rot_grad * cosine_ref[first : first + tile, :]
                - pltpu.roll(rot_grad, head_dim // 2, 1) * sine_ref[first : first + tile, :]
            ).astype(low)
            key_grad[first : first + window, :] += dot(score_grad, rot, 0, 0)
            value_grad[first : first + window, :] += dot(probs.astype(low), grad, 0, 0)
        return carry

    wa_size = part_width // 2
    chunk_rows = wa_size // 2

    class Lanes:
        def __init__(self, parts, core_room, row_room, sems, stretches, chunks):
            self.parts, self.core_room, self.row_room, self.sems = parts, core_room, row_room, sems
            self.stretches, self.chunks = stretches, chunks

        def core_copy(self, r0):
            return remote_copy(
                self.parts.at[r0, 1 - core],
                self.core_room.at[r0],
                self.sems.at[0, r0],
                self.sems.at[1, r0],
                dp=core_partner,
            )

        def dot(self, r0, which):
            first = pl.multiple_of(r0 * part_width + which * wa_size, 128)
            left = normed_ref[:, pl.ds(first, wa_size)]
            right = [joint_grad[:, lanes] for lanes in self.stretches]
            right = right[0] if len(right) == 1 else jnp.concatenate(right, axis=1)
            self.parts[r0, which] = dot(left, right, 0, 0).astype(low)

        def first(self):
            for r0 in (other, row):
                self.dot(r0, 1 - core)
                self.core_copy(r0).start()
            for r0 in (other, row):
                self.dot(r0, core)

        def row_copy(self, chunk):
            count = wa_size // self.chunks
            return remote_copy(
                self.parts.at[other, core, pl.ds(chunk * count, count)],
                self.row_room.at[chunk],
                self.sems.at[2, chunk],
                self.sems.at[3, chunk],
                row=other,
            )

        def to_row(self):
            self.core_copy(other).wait_recv()
            self.parts[other, core] = add_low(self.parts[other, core], self.core_room[other])
            for chunk in range(self.chunks):
                self.row_copy(chunk).start()
            self.core_copy(row).wait_recv()
            self.parts[row, core] = add_low(self.parts[row, core], self.core_room[row])

        def end(self):
            for r0 in range(2):
                self.core_copy(r0).wait_send()
            for chunk in range(self.chunks):
                self.row_copy(chunk).wait_send()

    stretches = [
        slice(b * block_lanes, b * block_lanes + query_lanes) for b in range(2)
    ]
    key_stretch = slice(query_lanes, block_lanes)
    value_stretch = slice(block_lanes + query_lanes, 2 * block_lanes)
    wq = [
        Lanes(
            wq_parts.at[b], wq_core.at[b], wq_row.at[b], wq_sem.at[b], [stretches[b]], 2
        )
        for b in range(2)
    ]
    wk = Lanes(wk_parts, wk_core, wk_row, wk_sem, [key_stretch, value_stretch], 1)

    def wo_row_copy(b):
        return remote_copy(
            wo_parts.at[b, core, :, part_lanes(other)],
            wo_row.at[b],
            wo_sem.at[2, b],
            wo_sem.at[3, b],
            row=other,
        )

    lax.fori_loop(0, 1, head_step, 0)
    for b in range(2):
        wo_core_copy(b).wait_recv()
        wo_parts[b, core] = add_low(wo_parts[b, core], wo_core[b])
        wo_row_copy(b).start()
    lax.fori_loop(1, per_block, head_step, 0)
    item_start(2)
    wq[0].first()
    lax.fori_loop(per_block, per_block + 1, head_step, 0)
    wq[0].to_row()
    lax.fori_loop(per_block + 1, heads, head_step, 0)
    pair_stage[:, :head_dim] = key_grad[:tokens, :].astype(low)
    pair_stage[:, head_dim:] = value_grad[:tokens, :].astype(low)
    odd = col % 2 == 1

    def pair_copy():
        return remote_copy(
            pair_stage, pair_arrived, pair_sem.at[0], pair_sem.at[1], col=col + 1 - 2 * (col % 2)
        )

    pl.when(odd)(lambda: pair_copy().start())
    wq[1].first()
    item_start(3)

    def over_col(lanes, stacks, arrived, send, recv, chunk, blocks):
        return ColSum(
            stacks.at[chunk], arrived.at[chunk], send.at[chunk], recv.at[chunk], col, cols, blocks
        )

    wq_total = [
        [
            over_col(
                wq[b], wq_stack.at[b], wq_arrived.at[b], wq_send.at[b], wq_recv.at[b], c, (b, 2 + b)
            )
            for c in range(2)
        ]
        for b in range(2)
    ]

    def wq_to_col(b):
        for chunk in range(2):
            wq[b].row_copy(chunk).wait_recv()
            place = pl.ds(chunk * chunk_rows, chunk_rows)
            wq_stack[b, chunk, row] = wq_parts[b, row, core, place]
            wq_stack[b, chunk, other] = wq_row[b, chunk]
            wq_total[b][chunk].step(1)

    def wq_step(b, number):
        for chunk in range(2):
            wq_total[b][chunk].step(number)

    wq[1].to_row()
    item_finish(0)
    wo_total = ColSum(wo_stack, wo_arrived, wo_send, wo_recv, col, cols, range(cols))
    for b in range(2):
        wo_row_copy(b).wait_recv()
        wo_stack[2 * row + b] = wo_parts[b, core, :, part_lanes(row)]
        wo_stack[2 * other + b] = wo_row[b]
    wo_total.step(1)
    wq_to_col(0)

    @pl.when(jnp.logical_not(odd))
    def _():
        pair_copy().wait_recv()
        key_grad[tokens:, :] += pair_arrived[:, :head_dim].astype(full)
        value_grad[tokens:, :] += pair_arrived[:, head_dim:].astype(full)

    key_total = key_grad[tokens:, :]
    joint_grad[:, key_stretch] = (
        key_total * cosine_ref[...] - pltpu.roll(key_total, head_dim // 2, 1) * sine_ref[...]
    ).astype(low)
    joint_grad[:, value_stretch] = value_grad[tokens:, :].astype(low)
    wk.first()

    normed_own = work

    def normed_dot(which):
        return dot(joint_grad[...], joint_ref[part_lanes(which), :], 1, 1)

    def normed_sums(which, value):
        product = value * normed_ref[:, part_lanes(which)].astype(full)
        gain = gains_ref[0:1, part_lanes(which)]
        total = jnp.sum(product, axis=0, keepdims=True) / gain
        for n in range(parts // 2):
            sums[0, pl.ds(which * (parts // 2) + n, 1), :] = total[
                :, n * quarter_lanes : (n + 1) * quarter_lanes
            ]
        return jnp.sum(product, axis=1, keepdims=True)

    wk.to_row()
    item_to_row(2)
    value = normed_dot(other)
    grad_heads[...] = value.astype(low)
    normed_copy = remote_copy(
        grad_heads, normed_arrived, normed_sem.at[0], normed_sem.at[1], row=other
    )
    inner = normed_sums(other, value)
    value = normed_dot(row)
    inner += normed_sums(row, value)
    for h in range(2):
        normed_own[h] = value[h * rows : (h + 1) * rows]
    inner_stage[...] = jnp.transpose(jnp.broadcast_to(inner, (tokens, head_dim)))[:8, :]
    inner_copy = remote_copy(
        inner_stage, inner_arrived, inner_sem.at[0], inner_sem.at[1], row=other
    )
    inner_copy.start()

    def sums_copies(stage):
        base = 0 if stage == 0 else len(plane)
        return [
            remote_copy(
                sums.at[stage],
                sums_arrived.at[base + n],
                sums_sem.at[base + n, 0],
                sums_sem.at[base + n, 1],
                **device,
            )
            for n, device in enumerate((plane, copies)[stage])
        ]

    def sums_start(stage):
        for copy in sums_copies(stage):
            copy.start()

    def sums_finish(stage):
        base = 0 if stage == 0 else len(plane)
        total = sums[stage]
        for n, copy in enumerate(sums_copies(stage)):
            copy.wait_recv()
            total += sums_arrived[base + n]
        sums[stage + 1] = total

    sums_start(0)
    wq_to_col(1)
    wq_step(0, 2)
    wo_total.step(2)
    wk_total = ColSum(wk_stack, wk_arrived, wk_send, wk_recv, col, cols, range(cols))
    wk.row_copy(0).wait_recv()
    for b in range(2):
        lanes = slice(b * key_lanes, (b + 1) * key_lanes)
        wk_stack[2 * row + b] = wk_parts[row, core, :, lanes]
        wk_stack[2 * other + b] = wk_row[0, :, lanes]
    wk_total.step(1)
    item_to_row(3)
    wq_step(1, 2)
    wq_step(0, 3)
    wk_total.step(2)
    normed_copy.start()
    sums_finish(0)
    sums_start(1)
    wo_total.step(3)
    wq_step(1, 3)
    wk_total.step(3)
    item_after_row(1)
    item_after_row(2)

    class Owned:
        def __init__(self, side_room, sems, targets):
            self.room, self.sems, self.targets = side_room, sems, targets

        def copy(self, number):
            return remote_copy(
                self.room.at[number % 2],
                self.room.at[2 + number],
                self.sems.at[2 * number],
                self.sems.at[2 * number + 1],
                dp=across(bits[number]),
            )

        def start(self, value):
            self.room[0] = value.astype(low)
            if sides:
                self.copy(0).start()

        def core_copies(self):
            result = []
            base, value = 2 * sides, self.room.at[sides % 2]
            return (
                remote_copy(
                    value,
                    self.targets,
                    self.sems.at[base],
                    self.sems.at[base + 1],
                    dp=core_partner,
                ),
                pltpu.make_async_copy(value, self.targets, self.sems.at[base + 2]),
            )

        def finish(self):
            for number in range(sides):
                self.copy(number).wait()
                self.room[1 - number % 2] = add_low(
                    self.room[number % 2], self.room[2 + number]
                )
                if number + 1 < sides:
                    self.copy(number + 1).start()
            for copy in self.core_copies():
                copy.start()

        def end(self):
            for copy in self.core_copies():
                copy.wait()

    def own_place(chunk, count):
        return pl.ds(pl.multiple_of(core * wa_size + chunk * count, 16), count)

    wk_owned = Owned(wk_side, wk_sem.at[4], keyval_total_ref.at[own_place(0, wa_size)])
    wq_owned = [
        Owned(wq_side.at[c], wq_side_sem.at[c], query_total_ref.at[own_place(c, chunk_rows)])
        for c in range(2)
    ]
    wo_owned = Owned(
        wo_side,
        wo_sem.at[4],
        output_total_ref.at[pl.ds(pl.multiple_of(core * wo_size, 16), wo_size)],
    )
    for b in range(2):
        for c in range(2):
            wq_total[b][c].total(wq_owned[c].start)
    wo_total.total(wo_owned.start)
    wk_total.total(wk_owned.start)

    def own_tokens(value):
        out_stack[col] = (middle_ref[...] + value).astype(low)

    outs.total(own_tokens)

    def outputs_copy():
        place = pl.ds(pl.multiple_of(row * rows, rows), rows)
        return remote_copy(
            out_stack.at[col, :, part_lanes(other)],
            outputs_ref.at[place],
            own_out_sem.at[0],
            own_out_sem.at[1],
            row=other,
        )

    outputs_copy().start()
    outputs_ref[pl.ds(pl.multiple_of(row * rows, rows), rows), :] = out_stack[
        col, :, part_lanes(row)
    ]
    item_after_row(3)
    item_finish(1)
    for c in range(2):
        wq_owned[c].finish()
    wk_owned.finish()
    wo_owned.finish()
    item_finish(2)
    sums_finish(1)
    for n in range(parts // 2):
        place = pl.ds(row * (parts // 2) + n, 1)
        lanes = slice(n * quarter_lanes, (n + 1) * quarter_lanes)
        gain_sums_ref[0:1, lanes] = sums[2, place, :]
        place = pl.ds(parts + row * (parts // 2) + n, 1)
        gain_sums_ref[1:2, lanes] = sums[2, place, :]
    item_finish(3)

    normed_copy.wait_recv()
    inner_copy.wait_recv()
    both = inner_stage[...] + inner_arrived[...]
    inner = jnp.transpose(jnp.concatenate([both] * (head_dim // 8), axis=0))[:, 0:1]
    for h in range(2):
        place = slice(h * rows, (h + 1) * rows)
        scale = scale_ref[place, :]
        normed_grad = normed_own[h] + normed_arrived[place, :].astype(full)
        input_grad_ref[place, :] = (
            branch[h, :, part_lanes(row)].astype(full)
            + scale * (gains_ref[0:1, part_lanes(row)] * normed_grad)
            - inputs_ref[place, :].astype(full) * (scale * scale) * (inner[place, :] / width)
        ).astype(low)

    branch_copy.wait_send()
    pl.when(odd)(lambda: pair_copy().wait_send())
    for b in range(2):
        wo_core_copy(b).wait_send()
        wo_row_copy(b).wait_send()
    for lanes in wq + [wk]:
        lanes.end()
    normed_copy.wait_send()
    inner_copy.wait_send()
    outputs_copy().wait()
    for stage in range(2):
        for copy in sums_copies(stage):
            copy.wait_send()
    outs.end(first=False)
    for total in [wo_total, wk_total] + wq_total[0] + wq_total[1]:
        total.end()
    for owned in wq_owned + [wk_owned, wo_owned]:
        owned.end()
    for at in range(items):
        item_end(at)


def finish_call(
    middle, gains, scale, start, logsum, sums, inputs, attended, rot, keys, values, cosine, sine,
    head_output, joint_weight, normed, cot_all, out_part, up_own, up_row, up_other, down_half, out_first,
    query_block, both_block,
):
    rows, width = middle.shape
    tokens, part_width = inputs.shape
    cols, dps = lax.axis_size("col"), lax.axis_size("dp")
    sides = dps.bit_length() - 2
    heads_width = attended.shape[1]
    reach = keys.shape[0]
    vmem = pl.BlockSpec(memory_space=pltpu.VMEM)
    anywhere = pl.BlockSpec(memory_space=pl.ANY)
    dma = pltpu.SemaphoreType.DMA
    hidden = 2 * up_own.shape[0]
    size = part_width // 2
    items = 4
    key_block = both_block - query_block
    wo_size, wa_size = query_block // 2, part_width // 2
    chunk = wa_size // 2
    shape = jax.ShapeDtypeStruct
    sums_count = 2 * cols - 1 + dps - 1
    return pl.pallas_call(
        finish_kernel,
        in_specs=[vmem] * 5 + [anywhere] * 18,
        out_specs=[vmem] * 6 + [anywhere] * 3,
        out_shape=[
            shape((tokens, part_width), low),
            shape((tokens, part_width), low),
            shape((2, part_width), full),
            shape((query_block, part_width), low),
            shape((part_width, query_block), low),
            shape((part_width, key_block), low),
            shape((hidden, part_width), low),
            shape((hidden, part_width), low),
            shape((items, max(sides - 1, 1), size, part_width), low),
        ],
        scratch_shapes=[
            pltpu.VMEM((2, rows, part_width), full),
            pltpu.VMEM((rows, width), low),
            pltpu.VMEM((tokens, part_width), low),
            pltpu.VMEM((tokens, heads_width), low),
            pltpu.VMEM((tokens, heads_width), low),
            pltpu.VMEM((reach, head_dim), low),
            pltpu.VMEM((reach, head_dim), low),
            pltpu.VMEM((tokens, head_dim), full),
            pltpu.VMEM((tokens, head_dim), full),
            pltpu.VMEM((heads_width, width), low),
            pltpu.VMEM((width, 2 * both_block), low),
            pltpu.VMEM((tokens, width), low),
            dma((14,)),
            pltpu.VMEM((2, rows, width), low),
            dma((2,)),
            pltpu.VMEM((cols, rows, width), low),
            pltpu.VMEM((cols + 1, rows, width), low),
            dma((cols,)),
            dma((cols + 1,)),
            dma((2,)),
            pltpu.VMEM((tokens, heads_width), low),
            pltpu.VMEM((tokens, 2 * both_block), low),
            pltpu.VMEM((reach, head_dim), full),
            pltpu.VMEM((reach, head_dim), full),
            pltpu.VMEM((tokens, 2 * head_dim), low),
            pltpu.VMEM((tokens, 2 * head_dim), low),
            dma((2,)),
            pltpu.VMEM((tokens, part_width), low),
            dma((2,)),
            pltpu.VMEM((8, tokens), full),
            pltpu.VMEM((8, tokens), full),
            dma((2,)),
            pltpu.VMEM((3, 8, width // 4), full),
            pltpu.VMEM((sums_count, 8, width // 4), full),
            dma((sums_count, 2)),
            pltpu.VMEM((items, size, part_width), low),
            pltpu.VMEM((items, size, part_width), low),
            pltpu.VMEM((items, size, part_width), low),
            pltpu.VMEM((items, size // 2, part_width), low),
            pltpu.VMEM((items, size // 2, part_width), low),
            dma((items, 12 + 2 * sides)),
            dma((items, 2)),
            pltpu.VMEM((2, 2, wo_size, width), low),
            pltpu.VMEM((2, wo_size, width), low),
            pltpu.VMEM((2, wo_size, part_width), low),
            pltpu.VMEM((cols, wo_size, part_width), low),
            pltpu.VMEM((cols + 1, wo_size, part_width), low),
            pltpu.VMEM((2 + sides, wo_size, part_width), low),
            dma((5, 3 + 2 * sides)),
            dma((cols,)),
            dma((cols + 1,)),
            pltpu.VMEM((2, 2, 2, wa_size, query_block), low),
            pltpu.VMEM((2, 2, wa_size, query_block), low),
            pltpu.VMEM((2, 2, chunk, query_block), low),
            pltpu.VMEM((2, 2, 2, chunk, query_block), low),
            pltpu.VMEM((2, 2, 3, chunk, query_block), low),
            pltpu.VMEM((2, 2 + sides, chunk, query_block), low),
            dma((2, 4, 2)),
            dma((2, 3 + 2 * sides)),
            dma((2, 2, 2)),
            dma((2, 2, 3)),
            pltpu.VMEM((2, 2, wa_size, 2 * key_block), low),
            pltpu.VMEM((2, wa_size, 2 * key_block), low),
            pltpu.VMEM((1, wa_size, 2 * key_block), low),
            pltpu.VMEM((cols, wa_size, key_block), low),
            pltpu.VMEM((cols + 1, wa_size, key_block), low),
            pltpu.VMEM((2 + sides, wa_size, key_block), low),
            dma((5, 3 + 2 * sides)),
            dma((cols,)),
            dma((cols + 1,)),
        ],
        compiler_params=pltpu.CompilerParams(
            collective_id=2, has_side_effects=True, vmem_limit_bytes=63 * 2**20
        ),
        cost_estimate=pl.CostEstimate(
            flops=10 * 10**9, bytes_accessed=40 * 10**6, transcendentals=4 * 10**6
        ),
    )(
        middle, gains, scale, start, logsum, sums, inputs, attended, rot, keys, values, cosine, sine,
        head_output, joint_weight, normed, cot_all, out_part, up_own, up_row, up_other, down_half, out_first,
    )


def results_kernel(*refs):
    count = len(refs) // 2
    for source, target in zip(refs[:count], refs[count:]):
        target[...] = source[...].astype(target.dtype)


def results_call(arrays, kinds, steps):
    specs = [
        pl.BlockSpec((array.shape[0] // steps, array.shape[1]), lambda i: (i, 0))
        for array in arrays
    ]
    return pl.pallas_call(
        results_kernel,
        grid=(steps,),
        in_specs=specs,
        out_specs=specs,
        out_shape=[
            jax.ShapeDtypeStruct(array.shape, kind) for array, kind in zip(arrays, kinds)
        ],
        compiler_params=pltpu.CompilerParams(vmem_limit_bytes=60 * 2**20),
    )(*arrays)


def shards(
    inputs,
    norm_gain,
    query_weight,
    key_value_matrix,
    output_weight,
    mixer_gain,
    gate_weight,
    up_weight,
    down_weight,
    lengths,
    routes,
    route_gates,
    cotangent,
):
    row, col = lax.axis_index("row"), lax.axis_index("col")
    part_width = inputs.shape[1]
    experts, _, units = gate_weight.shape
    hidden_width = experts * units
    query_block, keyval_block = query_weight.shape[1], key_value_matrix.shape[1]
    small = jnp.zeros((8, part_width), full)
    small = small.at[0].set(norm_gain).at[1].set(mixer_gain)
    sequences = lengths.shape[1]
    small = small.at[2, :sequences].set(lengths[0].astype(full))
    theta = rope_base ** (-jnp.arange(0, head_dim, 2, dtype=full) / head_dim)
    theta = jnp.concatenate([theta, theta])[None, :]
    gate_flat = gate_weight.swapaxes(1, 2).reshape(hidden_width, part_width)
    up_flat = up_weight.swapaxes(1, 2).reshape(hidden_width, part_width)
    down_flat = down_weight.reshape(hidden_width, part_width)
    (
        normed,
        first_scale,
        gains,
        keys,
        values,
        cosine,
        sine,
        start,
        logsum,
        attended,
        rot,
        joint_weight,
        head_output,
        middle,
        expert_own,
        tables,
        cot_all,
        gate_other,
        up_other_half,
        down_quarter,
    ) = prologue_call(
        inputs, small, theta, routes.T, route_gates.T, cotangent, query_weight, key_value_matrix,
        output_weight, gate_flat, up_flat, down_flat, sequences, experts,
    )
    (
        second_grad,
        out_part,
        gate_total,
        up_own,
        up_row,
        up_other,
        down_half,
        out_first,
    ) = experts_call(
        expert_own, cot_all, tables, gate_flat, gate_other, up_flat, up_other_half, down_flat, down_quarter
    )

    both_block = query_block + keyval_block
    (
        outputs,
        input_grad,
        gain_sums,
        output_total,
        query_total,
        keyval_total,
        up_total,
        down_total,
        _,
    ) = finish_call(
        middle, gains, first_scale, start, logsum, second_grad, inputs, attended, rot, keys, values,
        cosine, sine, head_output, joint_weight, normed, cot_all, out_part,
        up_own, up_row, up_other, down_half, out_first, query_block, both_block,
    )
    norm_total, mixer_total = gain_sums[0], gain_sums[1]

    arrays = [gate_total, up_total, down_total, query_total, keyval_total, output_total]
    (
        gate_total,
        up_total,
        down_total,
        query_total,
        keyval_total,
        output_total,
        outputs,
        input_grad,
    ) = results_call(arrays + [outputs, input_grad], [full] * 6 + [low] * 2, 8)

    def by_expert(flat):
        return flat.reshape(experts, units, part_width)

    gate_total = by_expert(gate_total).swapaxes(1, 2)
    up_total = by_expert(up_total).swapaxes(1, 2)
    down_total = by_expert(down_total)
    return (
        outputs,
        input_grad,
        norm_total,
        query_total,
        keyval_total,
        output_total,
        mixer_total,
        gate_total,
        up_total,
        down_total,
    )


def solution(mesh):
    return jax.shard_map(
        shards,
        mesh=mesh,
        in_specs=(
            P(("dp", "col"), "row"),
            P("row"),
            P("row", "col"),
            P("row", "col"),
            P("col", "row"),
            P("row"),
            P(None, "row", "col"),
            P(None, "row", "col"),
            P(None, "col", "row"),
            P(("dp", "row"), None),
            P("dp", None),
            P("dp", None),
            P(("dp", "col"), "row"),
        ),
        out_specs=(
            P(("dp", "col"), "row"),
            P(("dp", "col"), "row"),
            P("row"),
            P("row", "col"),
            P("row", "col"),
            P("col", "row"),
            P("row"),
            P(None, "row", "col"),
            P(None, "row", "col"),
            P(None, "col", "row"),
        ),
        check_vma=False,
    )
```

```python
import jax
import jax.numpy as jnp
import numpy as np
from jax import lax
from jax.experimental import pallas as pl
from jax.experimental.pallas import tpu as pltpu
from jax.sharding import PartitionSpec as P

epsilon = 1e-06
rope_base = 1000000.0
head_dim = 128
low = jnp.bfloat16
full = jnp.float32


def dot(left, right, left_dim=1, right_dim=0):
    return lax.dot_general(
        left, right, (((left_dim,), (right_dim,)), ((), ())), preferred_element_type=full
    )


def remote_copy(source, target, send_sem, recv_sem, **device):
    return pltpu.make_async_remote_copy(
        src_ref=source,
        dst_ref=target,
        send_sem=send_sem,
        recv_sem=recv_sem,
        device_id=device,
        device_id_type=pl.DeviceIdType.MESH,
    )


def add_low(left, right):
    return (left.astype(full) + right.astype(full)).astype(low)


class ColSum:
    def __init__(self, stack, arrived, send_sem, recv_sem, col, count, blocks):
        self.stack, self.arrived, self.send_sem, self.recv_sem = stack, arrived, send_sem, recv_sem
        self.col, self.last, self.blocks = col, count - 1, list(blocks)

    def copy(self, block, at, right):
        neighbour = at + 1 if right else at - 1
        n = self.blocks.index(block)
        slot = n if right or block != neighbour else len(self.blocks)
        return remote_copy(
            self.stack.at[n],
            self.arrived.at[slot],
            self.send_sem.at[n],
            self.recv_sem.at[slot],
            col=neighbour,
        )

    def wait(self, slot, at):
        remote_copy(
            self.arrived.at[slot],
            self.arrived.at[slot],
            self.send_sem.at[0],
            self.recv_sem.at[slot],
            col=at + 1 if at == 0 else at - 1,
        ).wait_recv()

    def step(self, number, placed=False):
        for at in range(self.last + 1):
            ways = []
            for right in (True, False):
                block = at + self.last + 1 - number if right else at - self.last - 1 + number
                if block in self.blocks:
                    ways.append((block, right))
            if not ways:
                continue

            @pl.when(self.col == at)
            def _(at=at, ways=ways):
                for block, right in ways:
                    n = self.blocks.index(block)
                    if 0 < at < self.last:
                        if not placed:
                            self.wait(n, at)
                        self.stack[n] = add_low(self.stack[n], self.arrived[n])
                    self.copy(block, at, right).start()

    def total(self, part):
        for n, at in enumerate(self.blocks):

            @pl.when(self.col == at)
            def _(n=n, at=at):
                value = self.stack[n].astype(full)
                if at > 0:
                    self.wait(n, at)
                    value += self.arrived[n].astype(full)
                if at < self.last:
                    self.wait(len(self.blocks), at)
                    value += self.arrived[len(self.blocks)].astype(full)
                part(value)

    def end(self, first=True):
        for at in range(self.last + 1):

            @pl.when(self.col == at)
            def _(at=at):
                for block in self.blocks:
                    if block != at and (first or abs(block - at) < self.last):
                        self.copy(block, at, block > at).wait_send()


def experts_kernel(
    own_ref,
    cot_ref,
    table_ref,
    gate_hbm,
    gate_other_hbm,
    up_hbm,
    up_other_hbm,
    down_hbm,
    sum_ref,
    out_part_ref,
    gate_total_ref,
    up_own_ref,
    up_row_ref,
    up_other_ref,
    down_half_ref,
    out_first_ref,
    weights,
    expert_in,
    gate_grad,
    up_grad,
    hidden,
    send_stage,
    arrived,
    parts,
    stage,
    weights_sem,
    down_sem,
    ready,
    ag_recv,
    ag_right,
    ag_left,
    rs_recv,
    rs_send,
    core_send,
    core_recv,
    row_send,
    row_recv,
    side_send,
    side_recv,
    final_sem,
    local_sem,
    out_sem,
):
    row, col, dp = lax.axis_index("row"), lax.axis_index("col"), lax.axis_index("dp")
    dps = lax.axis_size("dp")
    core, other = dp % 2, 1 - row
    core_partner = dp + 1 - 2 * core
    side_bits = list(range(1, dps.bit_length() - 1))
    sides = len(side_bits)
    last = cot_ref.shape[0] - 1
    rows, width = own_ref.shape
    half = width // 2
    size = half // 2
    inner = (col > 0) & (col < last)

    def across(bit):
        on = (dp // (1 << bit)) % 2
        return dp + (1 << bit) * (1 - 2 * on)

    def half_lanes(which):
        return pl.ds(pl.multiple_of(which * half, half), half)

    gate_ref, up_ref, down_ref = weights.at[0], weights.at[1], weights.at[2]
    sources = (gate_hbm, gate_other_hbm, up_hbm, up_other_hbm, down_hbm)
    loads = [
        pltpu.make_async_copy(
            source,
            weights.at[i // 2, :, half_lanes((row, other)[i % 2])],
            weights_sem.at[i],
        )
        for i, source in enumerate(sources)
    ]
    for copy in loads:
        copy.start()

    barrier = pltpu.get_barrier_semaphore()

    def greet(semaphore, **device):
        pl.semaphore_signal(
            semaphore, inc=1, device_id=device, device_id_type=pl.DeviceIdType.MESH
        )

    greet(barrier, dp=core_partner)
    greet(barrier, row=other)
    for bit in side_bits:
        greet(barrier, dp=across(bit))
    pl.when(col > 0)(lambda: greet(barrier, col=col - 1))
    pl.when(col < last)(lambda: greet(barrier, col=col + 1))
    expert_in[col] = own_ref[...]
    pl.when(inner)(lambda: pl.semaphore_wait(barrier, 4 + sides))
    pl.when(jnp.logical_not(inner))(lambda: pl.semaphore_wait(barrier, 3 + sides))

    def ag_copy(block, right):
        return remote_copy(
            expert_in.at[block],
            expert_in.at[block],
            (ag_right if right else ag_left).at[block],
            ag_recv.at[block],
            col=col + 1 if right else col - 1,
        )

    def rs_copy(block, part, right):
        neighbour = col + 1 if right else col - 1
        slot = block if right else jnp.where(block == neighbour, last + 1, block)
        return remote_copy(
            send_stage.at[block, part],
            arrived.at[slot, part],
            rs_send.at[block, part],
            rs_recv.at[slot, part],
            col=neighbour,
        )

    def rs_wait(slot, part):
        remote_copy(
            arrived.at[slot, part],
            arrived.at[slot, part],
            rs_send.at[0, part],
            rs_recv.at[slot, part],
            col=jnp.where(col > 0, col - 1, col + 1),
        ).wait_recv()

    pl.when(col < last)(lambda: ag_copy(col, True).start())
    pl.when(col > 0)(lambda: ag_copy(col, False).start())
    pieces = 4
    quarter_size = down_hbm.shape[0] // 4
    piece_size = quarter_size // pieces
    quarter = dp % 4

    def down_place(which, piece):
        first = which * quarter_size + piece * piece_size
        return pl.ds(pl.multiple_of(first, 16), piece_size)

    def down_row(piece):
        place = down_place(quarter, piece)
        return remote_copy(
            down_hbm.at[place],
            weights.at[2, place, half_lanes(row)],
            down_sem.at[piece, 0],
            down_sem.at[piece, 1],
            row=other,
        )

    def down_side(piece):
        there = weights.at[2, down_place(quarter, piece), half_lanes(other)]
        return remote_copy(
            there, there, down_sem.at[piece, 2], down_sem.at[piece, 3], dp=across(1)
        )

    def down_core(piece, n):
        there = weights.at[2, down_place(core + 2 * n, piece), half_lanes(other)]
        return remote_copy(
            there,
            there,
            down_sem.at[piece, 4 + 2 * n],
            down_sem.at[piece, 5 + 2 * n],
            dp=core_partner,
        )

    for piece in range(pieces):
        down_row(piece).start()
    for copy in loads[:4]:
        copy.wait()

    def products(block):
        tokens = expert_in[block]
        table = table_ref[block]
        experts = table.shape[1]
        units = width // experts
        for g in range(2):
            cols = slice(g * half, (g + 1) * half)
            gate = dot(tokens, gate_ref[cols, :], 1, 1)
            up = dot(tokens, up_ref[cols, :], 1, 1)
            lane = lax.broadcasted_iota(jnp.int32, gate.shape, 1)
            first = g * experts // 2
            chosen = jnp.broadcast_to(table[:, first : first + 1], gate.shape)
            for e in range(1, experts // 2):
                chosen = jnp.where(lane >= e * units, table[:, first + e : first + e + 1], chosen)
            sigmoid = 1.0 / (1.0 + jnp.exp(-gate))
            silu = gate * sigmoid
            up = up * chosen
            hidden[block, :, cols] = (silu * up).astype(low)
            gate_grad[block, :, cols] = (up * (sigmoid * (1.0 + gate * (1.0 - sigmoid)))).astype(low)
            up_grad[block, :, cols] = (silu * chosen).astype(low)

    def gradients(block):
        grads = cot_ref[block]
        for g in range(2):
            cols = slice(g * half, (g + 1) * half)
            grad = dot(grads, down_ref[cols, :], 1, 1)
            gate_grad[block, :, cols] = (grad * gate_grad[block, :, cols].astype(full)).astype(low)
            up_grad[block, :, cols] = (grad * up_grad[block, :, cols].astype(full)).astype(low)
        gates_now, ups_now = gate_grad[block], up_grad[block]
        for part in range(2):
            cols = slice(part * half, (part + 1) * half)
            total = dot(gates_now, gate_ref[:, cols]) + dot(ups_now, up_ref[:, cols])
            send_stage[block, part] = total.astype(low)
            pl.when((col == 0) & (block != col))(lambda: rs_copy(block, part, True).start())
            pl.when((col == last) & (block != col))(lambda: rs_copy(block, part, False).start())
        out_part_ref[block] = dot(hidden[block], down_ref[...]).astype(low)

    def block_of(i):
        return jnp.where(i % 2 == 1, col - (i + 1) // 2, col + (i + 1) // 2)

    def pass_on(apart):
        @pl.when(col - apart >= 0)
        def _():
            ag_copy(col - apart, True).wait_recv()
            pl.when(col < last)(lambda: ag_copy(col - apart, True).start())

        @pl.when(col + apart <= last)
        def _():
            ag_copy(col + apart, False).wait_recv()
            pl.when(col > 0)(lambda: ag_copy(col + apart, False).start())

    def present(block):
        return (block >= 0) & (block <= last)

    def near_products(i, carry):
        pl.when(i == 1)(lambda: pass_on(1))
        pl.when(present(block_of(i)))(lambda: products(block_of(i)))
        return carry

    lax.fori_loop(0, 1, near_products, 0)
    for piece in range(pieces):
        down_row(piece).wait_recv()
        down_side(piece).start()
    lax.fori_loop(1, 3, near_products, 0)
    for piece in range(pieces):
        down_side(piece).wait_recv()
        for n in range(2):
            down_core(piece, n).start()
    loads[4].wait()
    for piece in range(pieces):
        for n in range(2):
            down_core(piece, n).wait_recv()

    def near_gradients(n, carry):
        i = (n + 1) % 3
        pl.when(i == 0)(lambda: pass_on(2))
        pl.when(present(block_of(i)))(lambda: gradients(block_of(i)))
        return carry

    lax.fori_loop(0, 3, near_gradients, 0)

    def far_blocks(i, carry):
        pl.when(i == 5)(lambda: pass_on(3))

        @pl.when(present(block_of(i)))
        def _():
            products(block_of(i))
            gradients(block_of(i))

        return carry

    lax.fori_loop(3, 2 * last + 1, far_blocks, 0)
    for piece in range(pieces):
        down_row(piece).wait_send()
        down_side(piece).wait_send()
        for n in range(2):
            down_core(piece, n).wait_send()

    greet(ready.at[0], dp=core_partner)
    greet(ready.at[1], row=other)
    for number, bit in enumerate(side_bits):
        greet(ready.at[2 + number], dp=across(bit))

    def room(which, down, right):
        return weights.at[
            which, pl.ds(down * half, half), pl.ds(right * half, half)
        ]

    def forward(block, part, right):
        rs_wait(block, part)
        send_stage[block, part] = add_low(send_stage[block, part], arrived[block, part])
        rs_copy(block, part, right).start()

    def event(number, part):
        blocks = ((2, 1), (3, 0), (0, 3))[number]
        pl.when(col == 1)(lambda: forward(blocks[0], part, number < 2))
        pl.when(col == 2)(lambda: forward(blocks[1], part, number == 2))

    def core_copy(at):
        if at < 4:
            target = room(at // 2, 0, at % 2)
        else:
            target = room(2, 0, at - 4)
        return remote_copy(
            stage.at[at % 2], target, core_send.at[at], core_recv.at[at], dp=core_partner
        )

    def stage_free(at):
        if at >= 2:
            core_copy(at - 2).wait_send()

    def core_dot(at):
        left = (gate_grad, up_grad)[at // 2]
        right = expert_in[:, :, half_lanes(row if at % 2 else other)].reshape(-1, half)
        stage_free(at)
        stage[at % 2] = dot(
            left[:, :, half_lanes(1 - core)].reshape(-1, half), right, 0, 0
        ).astype(low)
        core_copy(at).start()
        parts[at] = dot(left[:, :, half_lanes(core)].reshape(-1, half), right, 0, 0).astype(low)

    def core_sum(at):
        core_copy(at).wait_recv()
        parts[at] = add_low(parts[at], room(at // 2, 0, at % 2)[...])

    def down_dot_partner():
        left = hidden[:, :, half_lanes(1 - core)].reshape(-1, half)
        for part in range(2):
            lanes = slice(part * half, (part + 1) * half)
            right = cot_ref[:, :, lanes].reshape(-1, half)
            stage_free(4 + part)
            stage[part] = dot(left, right, 0, 0).astype(low)
            core_copy(4 + part).start()

    def down_dot_own():
        left = hidden[:, :, half_lanes(core)].reshape(-1, half)
        for part in range(2):
            lanes = slice(part * half, (part + 1) * half)
            right = cot_ref[:, :, lanes].reshape(-1, half)
            room(2, 1, part)[...] = dot(left, right, 0, 0).astype(low)

    def down_sum():
        for part in range(2):
            core_copy(4 + part).wait_recv()
            room(2, 1, part)[...] = add_low(room(2, 1, part)[...], room(2, 0, part)[...])

    down_out = pltpu.make_async_copy(
        weights.at[2, pl.ds(half, half)], down_half_ref, local_sem.at[0]
    )
    up_out = pltpu.make_async_copy(parts.at[3], up_own_ref, local_sem.at[1])
    up_rest = pltpu.make_async_copy(
        parts.at[2, pl.ds(size, size)], up_other_ref, local_sem.at[2]
    )

    chunks = 4
    chunk_size = half // chunks

    def chunk_rows(chunk):
        return pl.ds(chunk * chunk_size, chunk_size)

    def row_copy(chunk):
        if chunk < chunks:
            source = parts.at[0, chunk_rows(chunk)]
            target = weights.at[0, pl.ds(half + chunk * chunk_size, chunk_size), pl.ds(0, half)]
        else:
            source, target = parts.at[2, pl.ds(0, size)], up_row_ref
        return remote_copy(source, target, row_send.at[chunk], row_recv.at[chunk], row=other)

    def side_room(number, chunk):
        which, right = ((0, 1), (1, 0), (1, 1))[number]
        return weights.at[
            which, pl.ds(half + chunk * chunk_size, chunk_size), pl.ds(right * half, half)
        ]

    def side_copy(chunk, number):
        return remote_copy(
            parts.at[1 - number % 2, chunk_rows(chunk)],
            side_room(number, chunk),
            side_send.at[chunk, number],
            side_recv.at[chunk, number],
            dp=across(side_bits[number]),
        )

    def after_row(chunk):
        copy = row_copy(chunk)
        copy.wait_recv()
        row_copy(chunk + 1).start()
        copy.wait_send()
        here = chunk_rows(chunk)
        landed = weights.at[0, pl.ds(half + chunk * chunk_size, chunk_size), pl.ds(0, half)]
        parts[1, here] = add_low(parts[1, here], landed[...])
        if chunk == 0 and sides:
            for number in range(sides):
                pl.semaphore_wait(ready.at[2 + number], 1)
        if sides:
            side_copy(chunk, 0).start()

    def final_copies(chunk):
        source = parts.at[1 - sides % 2, chunk_rows(chunk)]
        first = pl.multiple_of(core * half + chunk * chunk_size, 16)
        target = gate_total_ref.at[pl.ds(first, chunk_size)]
        return (
            remote_copy(
                source, target, final_sem.at[chunk, 0], final_sem.at[chunk, 1], dp=core_partner
            ),
            pltpu.make_async_copy(source, target, final_sem.at[chunk, 2]),
        )

    def after_side(chunk):
        here = chunk_rows(chunk)
        for number in range(sides):
            copy = side_copy(chunk, number)
            copy.wait_recv()
            copy.wait_send()
            parts[number % 2, here] = add_low(
                parts[1 - number % 2, here], side_room(number, chunk)[...]
            )
            if number + 1 < sides:
                side_copy(chunk, number + 1).start()
        for copy in final_copies(chunk):
            copy.start()

    def out_copy(right):
        return remote_copy(
            out_part_ref.at[last if right else 0],
            out_first_ref,
            out_sem.at[0],
            out_sem.at[1],
            col=col + 1 if right else col - 1,
        )

    pl.semaphore_wait(ready.at[0], 1)
    core_dot(0)
    event(0, 0)
    core_sum(0)
    pl.semaphore_wait(ready.at[1], 1)
    row_copy(0).start()
    event(0, 1)
    core_dot(1)
    core_sum(1)
    event(1, 0)
    core_dot(2)
    after_row(0)
    core_sum(2)
    up_rest.start()
    event(1, 1)
    core_dot(3)
    after_row(1)
    event(2, 0)
    pl.when(col == 0)(lambda: out_copy(True).start())
    pl.when(col == last)(lambda: out_copy(False).start())
    core_sum(3)
    up_out.start()
    after_side(0)
    down_dot_partner()
    event(2, 1)
    after_row(2)
    after_side(1)
    down_dot_own()
    after_row(3)
    down_sum()
    down_out.start()
    after_side(2)

    for part in range(2):
        sum_ref[part] = send_stage[col, part].astype(full)

        @pl.when(col > 0)
        def _():
            rs_wait(col, part)
            sum_ref[part] += arrived[col, part].astype(full)

        @pl.when(col < last)
        def _():
            rs_wait(last + 1, part)
            sum_ref[part] += arrived[last + 1, part].astype(full)

    after_side(3)

    for block in range(last + 1):
        pl.when((block <= col) & (col < last))(lambda: ag_copy(block, True).wait_send())
        pl.when((block >= col) & (col > 0))(lambda: ag_copy(block, False).wait_send())
        for part in range(2):
            pl.when(block > col)(lambda: rs_copy(block, part, True).wait_send())
            pl.when(block < col)(lambda: rs_copy(block, part, False).wait_send())
    for at in range(4, 6):
        core_copy(at).wait_send()
    row_copy(chunks).wait()
    pl.when(col == 0)(lambda: out_copy(True).wait_send())
    pl.when(col == last)(lambda: out_copy(False).wait_send())
    pl.when(inner)(lambda: out_copy(False).wait_recv())
    for copy in (down_out, up_out, up_rest):
        copy.wait()
    for chunk in range(chunks):
        for copy in final_copies(chunk):
            copy.wait()


def experts_call(own, cot, table, *halves):
    rows, width = own.shape
    blocks, half = cot.shape[0], width // 2
    sides = lax.axis_size("dp").bit_length() - 2
    vmem = pl.BlockSpec(memory_space=pltpu.VMEM)
    anywhere = pl.BlockSpec(memory_space=pl.ANY)
    dma = pltpu.SemaphoreType.DMA
    shape = jax.ShapeDtypeStruct
    return pl.pallas_call(
        experts_kernel,
        in_specs=[vmem] * 3 + [anywhere] * 5,
        out_specs=[vmem, vmem] + [anywhere] * 6,
        out_shape=[
            shape((2, rows, half), full),
            shape((blocks, rows, width), low),
            shape((width, half), low),
            shape((half, half), low),
            shape((half // 2, half), low),
            shape((half // 2, half), low),
            shape((half, width), low),
            shape((rows, width), low),
        ],
        scratch_shapes=[pltpu.VMEM((3, width, width), low)]
        + [pltpu.VMEM((blocks, rows, width), low)] * 4
        + [
            pltpu.VMEM((blocks, 2, rows, half), low),
            pltpu.VMEM((blocks + 1, 2, rows, half), low),
            pltpu.VMEM((4, half, half), low),
            pltpu.VMEM((2, half, half), low),
            dma((5,)),
            dma((4, 8)),
            pltpu.SemaphoreType.REGULAR((2 + max(sides, 1),)),
            dma((blocks,)),
            dma((blocks,)),
            dma((blocks,)),
            dma((blocks + 1, 2)),
            dma((blocks, 2)),
            dma((6,)),
            dma((6,)),
            dma((5,)),
            dma((5,)),
            dma((4, max(sides, 1))),
            dma((4, max(sides, 1))),
            dma((4, 3)),
            dma((3,)),
            dma((2,)),
        ],
        compiler_params=pltpu.CompilerParams(
            collective_id=1, has_side_effects=True, vmem_limit_bytes=60 * 2**20
        ),
        cost_estimate=pl.CostEstimate(
            flops=9 * 2 * blocks * rows * width * width,
            bytes_accessed=12 * width * width,
            transcendentals=blocks * rows * width,
        ),
    )(own, cot, table, *halves)


def prologue_kernel(
    inputs_ref,
    norm_ref,
    mixer_ref,
    lengths_ref,
    theta_ref,
    routes_ref,
    route_gates_ref,
    cot_ref,
    query_hbm,
    keyval_hbm,
    output_hbm,
    gate_hbm,
    up_hbm,
    normed_hbm,
    scale_ref,
    gains_ref,
    key_hbm,
    value_hbm,
    cosine_ref,
    sine_ref,
    start_ref,
    logsum_ref,
    attended_hbm,
    rot_hbm,
    joint_hbm,
    head_output_hbm,
    middle_ref,
    expert_ref,
    table_ref,
    cot_all_ref,
    gate_all_ref,
    up_all_ref,
    normed_ref,
    key_ref,
    value_ref,
    attended_ref,
    rot_ref,
    joint_ref,
    head_output_ref,
    store_sem,
    inputs_all,
    inputs_sem,
    small,
    small_sem,
    projected,
    branch_own,
    branch_stage,
    branch_arrived,
    branch_sem,
    pair_sem,
    joint_line,
    joint_load,
    joint_hop,
    joint_row,
    joint_side,
    joint_core,
    output_line,
    output_load,
    output_hop,
    output_row,
    output_side,
    output_core,
    expert_row,
    expert_side,
    expert_core,
    cot_sem,
    cot_recv,
    cot_send,
):
    row, col, dp = lax.axis_index("row"), lax.axis_index("col"), lax.axis_index("dp")
    cols = lax.axis_size("col")
    last = cols - 1
    core, side, other = dp % 2, (dp // 2) % 2, 1 - row
    quarter = dp % 4
    core_partner, side_partner = dp + 1 - 2 * core, dp + 2 - 4 * side
    tokens, part_width = inputs_ref.shape
    width, rows = 2 * part_width, tokens // 2
    query_block, keyval_block = query_hbm.shape[1], keyval_hbm.shape[1]
    block = query_block + keyval_block
    experts = table_ref.shape[2]

    barrier = pltpu.get_barrier_semaphore()

    def greet(**device):
        pl.semaphore_signal(
            barrier, inc=1, device_id=device, device_id_type=pl.DeviceIdType.MESH
        )

    greet(row=other)
    for apart in range(1, cols):
        greet(col=(col + apart) % cols)
    greet(dp=core_partner)
    greet(dp=side_partner)

    def part_lanes(which):
        return pl.ds(pl.multiple_of(which * part_width, 128), part_width)

    inputs_all[:, part_lanes(row)] = inputs_ref[...]
    small[row, 0:1, :] = norm_ref[...].reshape(1, part_width)
    small[row, 1:2, :] = mixer_ref[...].reshape(1, part_width)
    sequences = lengths_ref.shape[1]
    small[row, 2:3, :] = jnp.zeros((1, part_width), full)
    small[row, 2:3, :sequences] = lengths_ref[...].astype(full)
    small[row, 3:8, :] = jnp.zeros((5, part_width), full)
    inputs_copy = remote_copy(
        inputs_ref,
        inputs_all.at[:, part_lanes(row)],
        inputs_sem.at[0],
        inputs_sem.at[1],
        row=other,
    )
    small_copy = remote_copy(
        small.at[row], small.at[row], small_sem.at[0], small_sem.at[1], row=other
    )

    joint_size, output_size = query_hbm.shape[0] // 4, output_hbm.shape[0] // 4

    def joint_region(r0, b, which):
        return joint_ref.at[
            pl.ds(pl.multiple_of(r0 * part_width + which * joint_size, 16), joint_size),
            pl.ds(pl.multiple_of(b * block, 128), block),
        ]

    def output_region(r0, b, which):
        return head_output_ref.at[
            pl.ds(pl.multiple_of(b * query_block + which * output_size, 16), output_size),
            part_lanes(r0),
        ]

    class Gather:
        def __init__(self, line, pieces, load, hop, row_sems, side_sems, core_sems, region):
            self.line, self.region, self.hop, self.row_sems = line, region, hop, row_sems
            self.side_sems, self.core_sems = side_sems, core_sems
            self.loads = [
                pltpu.make_async_copy(source, target, load.at[n])
                for n, (source, target) in enumerate(pieces)
            ]

        def copy(self, at, right):
            return remote_copy(
                self.line.at[at],
                self.line.at[at],
                self.hop.at[at, 1 if right else 0],
                self.hop.at[at, 2],
                col=col + 1 if right else col - 1,
            )

        def row_copy(self, b):
            return remote_copy(
                self.line.at[2 * other + b],
                self.region(row, b, quarter),
                self.row_sems.at[b, 0],
                self.row_sems.at[b, 1],
                row=other,
            )

        def side_copy(self, n):
            there = self.region((row, other)[n // 2], n % 2, quarter)
            return remote_copy(
                there, there, self.side_sems.at[n, 0], self.side_sems.at[n, 1], dp=side_partner
            )

        def core_copies(self, n):
            result = []
            for part in range(2):
                there = self.region((row, other)[n // 2], n % 2, core + 2 * part)
                result.append(
                    remote_copy(
                        there,
                        there,
                        self.core_sems.at[n, 2 * part],
                        self.core_sems.at[n, 2 * part + 1],
                        dp=core_partner,
                    )
                )
            return result

        def use(self, at):
            for b in range(2):

                @pl.when(at == 2 * row + b)
                def _(b=b):
                    there = self.region(row, b, quarter)
                    there[...] = self.line[at]
                    self.side_copy(b).start()

                @pl.when(at == 2 * other + b)
                def _(b=b):
                    self.row_copy(b).start()

        def load(self):
            for copy in self.loads:
                copy.start()

        def first(self):
            for copy in self.loads:
                copy.wait()
            pl.when(col < last)(lambda: self.copy(col, True).start())
            pl.when(col > 0)(lambda: self.copy(col, False).start())
            self.use(col)

        def step(self, apart):
            @pl.when(col - apart >= 0)
            def _():
                self.copy(col - apart, True).wait_recv()
                pl.when(col < last)(lambda: self.copy(col - apart, True).start())
                self.use(col - apart)

            @pl.when(col + apart <= last)
            def _():
                self.copy(col + apart, False).wait_recv()
                pl.when(col > 0)(lambda: self.copy(col + apart, False).start())
                self.use(col + apart)

        def from_row(self):
            for b in range(2):
                self.row_copy(b).wait_recv()
                self.side_copy(2 + b).start()

        def to_core(self):
            for n in range(4):
                self.side_copy(n).wait_recv()
                for copy in self.core_copies(n):
                    copy.start()

        def ready(self):
            for n in range(4):
                for copy in self.core_copies(n):
                    copy.wait_recv()

        def end(self):
            for at in range(cols):
                pl.when((at <= col) & (col < last))(lambda: self.copy(at, True).wait_send())
                pl.when((at >= col) & (col > 0))(lambda: self.copy(at, False).wait_send())
            for b in range(2):
                self.row_copy(b).wait_send()
            for n in range(4):
                self.side_copy(n).wait_send()
                for copy in self.core_copies(n):
                    copy.wait_send()

    first_joint = pl.ds(pl.multiple_of(quarter * joint_size, 16), joint_size)
    first_output = pl.ds(pl.multiple_of(quarter * output_size, 16), output_size)
    joint = Gather(
        joint_line,
        (
            (query_hbm.at[first_joint], joint_line.at[col, :, pl.ds(0, query_block)]),
            (keyval_hbm.at[first_joint], joint_line.at[col, :, pl.ds(query_block, keyval_block)]),
        ),
        joint_load,
        joint_hop,
        joint_row,
        joint_side,
        joint_core,
        joint_region,
    )
    output = Gather(
        output_line,
        ((output_hbm.at[first_output], output_line.at[col]),),
        output_load,
        output_hop,
        output_row,
        output_side,
        output_core,
        output_region,
    )

    def token_rows(which):
        return pl.ds(pl.multiple_of(which * rows, 16), rows)

    cot_row = remote_copy(
        cot_ref.at[token_rows(other)],
        cot_all_ref.at[col, :, part_lanes(row)],
        cot_sem.at[0],
        cot_sem.at[1],
        row=other,
    )

    def cot_copy(block_at, right):
        return remote_copy(
            cot_all_ref.at[block_at],
            cot_all_ref.at[block_at],
            cot_send.at[block_at, 1 if right else 0],
            cot_recv.at[block_at],
            col=col + 1 if right else col - 1,
        )

    def cot_first():
        cot_row.wait_recv()
        pl.when(col < last)(lambda: cot_copy(col, True).start())
        pl.when(col > 0)(lambda: cot_copy(col, False).start())

    def cot_pass(apart):
        @pl.when(col - apart >= 0)
        def _():
            cot_copy(col - apart, True).wait_recv()
            pl.when(col < last)(lambda: cot_copy(col - apart, True).start())

        @pl.when(col + apart <= last)
        def _():
            cot_copy(col + apart, False).wait_recv()
            pl.when(col > 0)(lambda: cot_copy(col + apart, False).start())

    expert_size = gate_hbm.shape[0] // 4
    weights = (gate_hbm, up_hbm)
    totals = (gate_all_ref, up_all_ref)

    unit_size = expert_size // 2

    def expert_place(which, of_quarter):
        first = of_quarter * expert_size + (which % 2) * unit_size
        return pl.ds(pl.multiple_of(first, 16), unit_size)

    def expert_region(which, of_quarter):
        return totals[which // 2].at[expert_place(which, of_quarter)]

    def expert_row_copy(which):
        return remote_copy(
            weights[which // 2].at[expert_place(which, quarter)],
            expert_region(which, quarter),
            expert_row.at[which, 0],
            expert_row.at[which, 1],
            row=other,
        )

    def expert_side_copy(which):
        there = expert_region(which, quarter)
        return remote_copy(
            there, there, expert_side.at[which, 0], expert_side.at[which, 1], dp=side_partner
        )

    def expert_core_copies(which):
        result = []
        for n in range(2):
            there = expert_region(which, core + 2 * n)
            result.append(
                remote_copy(
                    there,
                    there,
                    expert_core.at[which, 2 * n],
                    expert_core.at[which, 2 * n + 1],
                    dp=core_partner,
                )
            )
        return result

    def expert_after_row(which):
        expert_row_copy(which).wait_recv()
        expert_side_copy(which).start()

    def expert_after_side(which):
        expert_side_copy(which).wait_recv()
        for copy in expert_core_copies(which):
            copy.start()

    store_pairs = (
        (normed_ref, normed_hbm),
        (key_ref, key_hbm),
        (value_ref, value_hbm),
        (attended_ref, attended_hbm),
        (rot_ref, rot_hbm),
        (joint_ref, joint_hbm),
        (head_output_ref, head_output_hbm),
    )
    stores = [
        pltpu.make_async_copy(source, target, store_sem.at[n])
        for n, (source, target) in enumerate(store_pairs)
    ]
    joint.load()
    output.load()
    pl.semaphore_wait(barrier, cols + 2)
    joint.first()
    small_copy.start()
    cot_row.start()
    cot_all_ref[col, :, part_lanes(row)] = cot_ref[token_rows(row), :]

    for at in range(cols):
        place = pl.ds(pl.multiple_of(at * tokens + row * rows, 128), rows)
        chosen, gates = routes_ref[:, place], route_gates_ref[:, place]
        expert = lax.broadcasted_iota(jnp.int32, (experts, rows), 0)
        table = jnp.zeros((experts, rows), full)
        for k in range(chosen.shape[0]):
            table += jnp.where(chosen[k : k + 1, :] == expert, gates[k : k + 1, :], 0.0)
        table_ref[at] = jnp.transpose(table)
    joint.step(1)

    small_copy.wait_recv()
    gains_ref[:, :part_width] = small[0, 0:2, :]
    gains_ref[:, part_width:] = small[1, 0:2, :]
    half = col // 2
    lens = small[half, 2:3, :]
    odd = (col % 2).astype(full)
    place = lax.broadcasted_iota(jnp.int32, (tokens, 1), 0).astype(full) + odd * tokens
    begin = jnp.zeros((tokens, 1), full)
    total = lens[:, 0:1]
    for n in range(1, sequences):
        begin = jnp.where(place >= total, total, begin)
        total = total + lens[:, n : n + 1]
    start_ref[...] = begin + (1.0 - odd) * tokens
    cot_first()
    inputs_copy.start()
    angles = (place - begin) * theta_ref[...]
    cosine_ref[...] = jnp.cos(angles)
    sine = jnp.sin(angles)
    lane = lax.broadcasted_iota(jnp.int32, sine.shape, 1)
    sine_ref[...] = jnp.where(lane < head_dim // 2, -sine, sine)

    joint.step(2)
    joint.step(3)
    output.first()
    joint.from_row()
    output.step(1)
    inputs_copy.wait_recv()
    expert_row_copy(0).start()
    expert_row_copy(1).start()

    piece = 64

    def norm_piece(at, carry):
        here = pl.ds(pl.multiple_of(at * piece, piece), piece)
        values = inputs_all[here, :].astype(full)
        scale = lax.rsqrt(jnp.mean(values * values, axis=1, keepdims=True) + epsilon)
        scale_ref[here, :] = scale
        for which in range(2):
            lanes = slice(which * part_width, (which + 1) * part_width)
            normed_ref[here, lanes] = (values[:, lanes] * scale * small[which, 0:1, :]).astype(low)
        return carry

    lax.fori_loop(0, tokens // piece, norm_piece, 0)
    joint.to_core()
    output.step(2)
    cot_pass(1)
    joint.ready()
    stores[0].start()
    stores[5].start()

    own = pl.ds(tokens, tokens)
    key = dot(normed_ref[...], joint_ref[:, query_block:block])
    key_ref[own, :] = (
        key * cosine_ref[...] + pltpu.roll(key, head_dim // 2, 1) * sine_ref[...]
    ).astype(low)
    value_ref[own, :] = dot(normed_ref[...], joint_ref[:, block + query_block :]).astype(low)

    def pair_copies():
        return [
            remote_copy(
                ref.at[own],
                ref.at[pl.ds(0, tokens)],
                pair_sem.at[n, 0],
                pair_sem.at[n, 1],
                col=col + 1 - 2 * (col % 2),
            )
            for n, ref in enumerate((key_ref, value_ref))
        ]

    @pl.when(col % 2 == 0)
    def _():
        for copy in pair_copies():
            copy.start()
        key_ref[:tokens, :] = jnp.zeros((tokens, head_dim), low)
        value_ref[:tokens, :] = jnp.zeros((tokens, head_dim), low)

    for b in range(2):
        lanes = slice(b * query_block, (b + 1) * query_block)
        projected[:, lanes] = dot(
            normed_ref[...], joint_ref[:, b * block : b * block + query_block]
        )
    output.step(3)
    output.from_row()
    expert_after_row(0)
    expert_row_copy(2).start()
    output.to_core()

    @pl.when(col % 2 == 1)
    def _():
        for copy in pair_copies():
            copy.wait_recv()

    expert_after_row(1)
    expert_row_copy(3).start()

    heads = 2 * query_block // head_dim
    tile = rows
    window = key_ref.shape[0] - tile

    def attend(which):
        first = which * tile
        here = pl.ds(pl.multiple_of(first, 16), tile)
        reach = pl.ds(pl.multiple_of(first, 16), window)

        def head_step(head, carry):
            lanes = pl.ds(pl.multiple_of(head * head_dim, head_dim), head_dim)
            pre = projected[here, lanes]
            rot = (
                pre * cosine_ref[here, :] + pltpu.roll(pre, head_dim // 2, 1) * sine_ref[here, :]
            ).astype(low)
            rot_ref[here, lanes] = rot
            scores = dot(rot, key_ref[reach, :], 1, 1) * head_dim ** (-0.5)
            key_place = lax.broadcasted_iota(jnp.int32, scores.shape, 1) + first
            query_place = lax.broadcasted_iota(jnp.int32, scores.shape, 0) + (first + tokens)
            allowed = (key_place <= query_place) & (
                key_place.astype(full) >= start_ref[here, :]
            )
            scores = jnp.where(allowed, scores, -1e30)
            most = jnp.max(scores, axis=1, keepdims=True)
            exponent = jnp.exp(scores - most)
            total = jnp.sum(exponent, axis=1, keepdims=True)
            weights = exponent / total
            attended_ref[here, lanes] = dot(weights.astype(low), value_ref[reach, :]).astype(low)
            lane = lax.broadcasted_iota(jnp.int32, (tile, head_dim), 1)
            logsum_ref[here, :] = jnp.where(
                lane == head, most + jnp.log(total), logsum_ref[here, :]
            )
            return carry

        lax.fori_loop(0, heads, head_step, 0)

    logsum_ref[...] = jnp.zeros_like(logsum_ref)
    attend(other)
    output.ready()

    def branch_copy(part):
        return remote_copy(
            branch_stage.at[part],
            branch_arrived.at[part],
            branch_sem.at[part, 0],
            branch_sem.at[part, 1],
            row=other,
        )

    theirs = attended_ref[token_rows(other), :]
    for part in range(2):
        lanes = slice(part * part_width, (part + 1) * part_width)
        branch_stage[part] = dot(theirs, head_output_ref[:, lanes]).astype(low)
        branch_copy(part).start()
    cot_pass(2)
    expert_after_row(2)
    expert_after_side(0)
    attend(row)
    mine = attended_ref[token_rows(row), :]
    branch_own[...] = dot(mine, head_output_ref[...])
    for n in (1, 2, 3, 4, 6):
        stores[n].start()
    expert_after_row(3)
    expert_after_side(1)
    for part in range(2):
        lanes = slice(part * part_width, (part + 1) * part_width)
        branch_copy(part).wait_recv()
        middle_ref[:, lanes] = (
            inputs_all[token_rows(row), lanes].astype(full)
            + branch_own[:, lanes]
            + branch_arrived[part].astype(full)
        )

    expert_after_side(2)

    def second_piece(at, carry):
        here = pl.ds(pl.multiple_of(at * piece, piece), piece)
        values = middle_ref[here, :]
        scale = lax.rsqrt(jnp.mean(values * values, axis=1, keepdims=True) + epsilon)
        expert_ref[here, :] = (values * scale * gains_ref[1:2, :]).astype(low)
        return carry

    lax.fori_loop(0, rows // piece, second_piece, 0)
    cot_pass(3)
    expert_after_side(3)

    inputs_copy.wait_send()
    small_copy.wait_send()
    joint.end()
    output.end()
    for copy in stores:
        copy.wait()
    for which in range(4):
        expert_row_copy(which).wait_send()
        expert_side_copy(which).wait_send()
        for copy in expert_core_copies(which):
            copy.wait()
    cot_row.wait_send()
    for at in range(cols):
        pl.when((at <= col) & (col < last))(lambda: cot_copy(at, True).wait_send())
        pl.when((at >= col) & (col > 0))(lambda: cot_copy(at, False).wait_send())

    @pl.when(col % 2 == 0)
    def _():
        for copy in pair_copies():
            copy.wait_send()

    for part in range(2):
        branch_copy(part).wait_send()


def prologue_call(
    inputs, norm_gain, mixer_gain, lengths, theta, routes, route_gates, cotangent, query_weight, key_value_matrix,
    output_weight, gate_flat, up_flat, experts,
):
    tokens, part_width = inputs.shape
    cols = lax.axis_size("col")
    width, rows = 2 * part_width, tokens // 2
    query_block, keyval_block = query_weight.shape[1], key_value_matrix.shape[1]
    block = query_block + keyval_block
    hidden = gate_flat.shape[0]
    vmem = pl.BlockSpec(memory_space=pltpu.VMEM)
    anywhere = pl.BlockSpec(memory_space=pl.ANY)
    dma = pltpu.SemaphoreType.DMA
    shape = jax.ShapeDtypeStruct
    return pl.pallas_call(
        prologue_kernel,
        in_specs=[vmem] * 8 + [anywhere] * 5,
        out_specs=[anywhere]
        + [vmem] * 2
        + [anywhere] * 2
        + [vmem] * 4
        + [anywhere] * 4
        + [vmem] * 4
        + [anywhere] * 2,
        out_shape=[
            shape((tokens, width), low),
            shape((tokens, 1), full),
            shape((2, width), full),
            shape((2 * tokens, head_dim), low),
            shape((2 * tokens, head_dim), low),
            shape((tokens, head_dim), full),
            shape((tokens, head_dim), full),
            shape((tokens, 1), full),
            shape((tokens, head_dim), full),
            shape((tokens, 2 * query_block), low),
            shape((tokens, 2 * query_block), low),
            shape((width, 2 * block), low),
            shape((2 * query_block, width), low),
            shape((rows, width), full),
            shape((rows, width), low),
            shape((cols, rows, experts), full),
            shape((cols, rows, width), low),
            shape((hidden, part_width), low),
            shape((hidden, part_width), low),
        ],
        scratch_shapes=[
            pltpu.VMEM((tokens, width), low),
            pltpu.VMEM((2 * tokens, head_dim), low),
            pltpu.VMEM((2 * tokens, head_dim), low),
            pltpu.VMEM((tokens, 2 * query_block), low),
            pltpu.VMEM((tokens, 2 * query_block), low),
            pltpu.VMEM((width, 2 * block), low),
            pltpu.VMEM((2 * query_block, width), low),
            dma((7,)),
            pltpu.VMEM((tokens, width), low),
            dma((2,)),
            pltpu.VMEM((2, 8, part_width), full),
            dma((2,)),
            pltpu.VMEM((tokens, 2 * query_block), full),
            pltpu.VMEM((rows, width), full),
            pltpu.VMEM((2, rows, part_width), low),
            pltpu.VMEM((2, rows, part_width), low),
            dma((2, 2)),
            dma((2, 2)),
            pltpu.VMEM((cols, part_width // 4, block), low),
            dma((2,)),
            dma((cols, 3)),
            dma((2, 2)),
            dma((4, 2)),
            dma((4, 4)),
            pltpu.VMEM((cols, query_block // 4, part_width), low),
            dma((1,)),
            dma((cols, 3)),
            dma((2, 2)),
            dma((4, 2)),
            dma((4, 4)),
            dma((4, 2)),
            dma((4, 2)),
            dma((4, 4)),
            dma((2,)),
            dma((cols,)),
            dma((cols, 2)),
        ],
        compiler_params=pltpu.CompilerParams(
            collective_id=3, has_side_effects=True, vmem_limit_bytes=60 * 2**20
        ),
        cost_estimate=pl.CostEstimate(
            flops=5 * 10**9, bytes_accessed=30 * 10**6, transcendentals=3 * 10**6
        ),
    )(
        inputs, norm_gain, mixer_gain, lengths, theta, routes, route_gates, cotangent, query_weight, key_value_matrix,
        output_weight, gate_flat, up_flat,
    )


def finish_kernel(
    middle_ref,
    gains_ref,
    scale_ref,
    start_ref,
    logsum_ref,
    sum_hbm,
    inputs_hbm,
    attended_hbm,
    rot_hbm,
    key_hbm,
    value_hbm,
    cosine_hbm,
    sine_hbm,
    head_output_hbm,
    joint_hbm,
    normed_hbm,
    cot_all_hbm,
    out_part_hbm,
    up_own_hbm,
    up_row_hbm,
    up_other_hbm,
    down_half_hbm,
    out_first_hbm,
    outputs_ref,
    input_grad_ref,
    gain_sums_ref,
    output_total_ref,
    query_total_ref,
    keyval_total_ref,
    up_total_ref,
    down_total_ref,
    further,
    work,
    cot_ref,
    inputs_ref,
    attended_ref,
    rot_ref,
    key_ref,
    value_ref,
    cosine_ref,
    sine_ref,
    head_output_ref,
    joint_ref,
    normed_ref,
    loads,
    branch,
    branch_sem,
    out_stack,
    out_arrived,
    out_send,
    out_recv,
    own_out_sem,
    grad_heads,
    joint_grad,
    key_grad,
    value_grad,
    pair_stage,
    pair_arrived,
    pair_sem,
    normed_arrived,
    normed_sem,
    inner_stage,
    inner_arrived,
    inner_sem,
    sums,
    sums_arrived,
    sums_sem,
    item_mine,
    item_other,
    item_side,
    item_row,
    item_last,
    item_sem,
    item_load_sem,
    wo_parts,
    wo_core,
    wo_row,
    wo_stack,
    wo_arrived,
    wo_side,
    wo_sem,
    wo_send,
    wo_recv,
    wq_parts,
    wq_core,
    wq_row,
    wq_stack,
    wq_arrived,
    wq_side,
    wq_sem,
    wq_side_sem,
    wq_send,
    wq_recv,
    wk_parts,
    wk_core,
    wk_row,
    wk_stack,
    wk_arrived,
    wk_side,
    wk_sem,
    wk_send,
    wk_recv,
):
    row, col, dp = lax.axis_index("row"), lax.axis_index("col"), lax.axis_index("dp")
    cols, dps = lax.axis_size("col"), lax.axis_size("dp")
    core, side, other = dp % 2, (dp // 2) % 2, 1 - row
    core_partner = dp + 1 - 2 * core
    bits = list(range(1, dps.bit_length() - 1))
    sides = len(bits)

    def across(bit):
        on = (dp // (1 << bit)) % 2
        return dp + (1 << bit) * (1 - 2 * on)

    rows, width = middle_ref.shape
    tokens, part_width = inputs_ref.shape
    heads = attended_ref.shape[1] // head_dim
    per_block = heads // 2
    query_lanes, key_lanes = query_total_ref.shape[1], keyval_total_ref.shape[1]
    block_lanes = query_lanes + key_lanes

    def part_lanes(which):
        return pl.ds(pl.multiple_of(which * part_width, 128), part_width)

    size = item_mine.shape[1]
    items = item_mine.shape[0]
    load_pairs = [
        (sum_hbm, work),
        (cot_all_hbm.at[col], cot_ref),
        (out_part_hbm, out_stack),
        (head_output_hbm, head_output_ref),
        (attended_hbm, attended_ref),
        (rot_hbm, rot_ref),
        (key_hbm, key_ref),
        (value_hbm, value_ref),
        (cosine_hbm, cosine_ref),
        (sine_hbm, sine_ref),
        (joint_hbm, joint_ref),
        (normed_hbm, normed_ref),
        (inputs_hbm, inputs_ref),
    ]
    load = [
        pltpu.make_async_copy(source, target, loads.at[n])
        for n, (source, target) in enumerate(load_pairs)
    ]

    def item_loads(at):
        chunk = at % 2
        place = pl.ds(chunk * size, size)
        if at < 2:
            sources = (up_own_hbm.at[place], (up_row_hbm, up_other_hbm)[chunk])
        else:
            sources = [down_half_hbm.at[place, part_lanes(which)] for which in (row, other)]
        return [
            pltpu.make_async_copy(source, target.at[at], item_load_sem.at[at, number])
            for number, (source, target) in enumerate(zip(sources, (item_mine, item_other)))
        ]

    inner_col = (col > 0) & (col < cols - 1)
    first_load = pltpu.make_async_copy(
        out_first_hbm, out_arrived.at[(cols - 1) * (2 - col) % cols], loads.at[13]
    )
    for copy in load[:3]:
        copy.start()
    pl.when(inner_col)(lambda: first_load.start())
    for copy in item_loads(1) + load[3:]:
        copy.start()
    for at in (0, 2, 3):
        for copy in item_loads(at):
            copy.start()

    barrier = pltpu.get_barrier_semaphore()

    def greet(**device):
        pl.semaphore_signal(
            barrier, inc=1, device_id=device, device_id_type=pl.DeviceIdType.MESH
        )

    plane = [
        dict(row=(row + there // cols) % 2, col=(col + there % cols) % cols)
        for there in range(1, 2 * cols)
    ]
    copies = [dict(dp=(dp + apart) % dps) for apart in range(1, dps)]
    for device in plane + copies:
        greet(**device)

    outs = ColSum(out_stack, out_arrived, out_send, out_recv, col, cols, range(cols))
    load[2].wait()
    pl.when(inner_col)(lambda: first_load.wait())
    pl.semaphore_wait(barrier, len(plane) + len(copies))
    outs.step(2, placed=True)

    for copy in load[:2]:
        copy.wait()
    piece = 64
    halves = [slice(h * part_width, (h + 1) * part_width) for h in range(2)]

    def norm_piece(at, mixer_sum):
        place = pl.ds(pl.multiple_of(at * piece, piece), piece)
        middle = middle_ref[place, :]
        second = jnp.concatenate([work[h, place, :] for h in range(2)], axis=1)
        scale = lax.rsqrt(jnp.mean(middle * middle, axis=1, keepdims=True) + epsilon)
        weighted = gains_ref[1:2, :] * second
        inner = jnp.sum(weighted * middle, axis=1, keepdims=True)
        grad = (
            cot_ref[place, :].astype(full)
            + scale * weighted
            - middle * (scale * scale * scale) * (inner / width)
        )
        branch[row, place, :] = grad.astype(low)
        return mixer_sum + jnp.sum(second * middle * scale, axis=0, keepdims=True)

    mixer_sum = lax.fori_loop(0, rows // piece, norm_piece, jnp.zeros((1, width), full))
    quarter_lanes = sums.shape[2]
    parts = width // quarter_lanes
    for n in range(parts):
        sums[0, parts + n : parts + n + 1, :] = mixer_sum[
            :, n * quarter_lanes : (n + 1) * quarter_lanes
        ]
    branch_copy = remote_copy(
        branch.at[row], branch.at[row], branch_sem.at[0], branch_sem.at[1], row=other
    )
    branch_copy.start()

    half_size = size // 2

    def side_rows(which):
        return pl.ds(pl.multiple_of(which * half_size, 16), half_size)

    def item_first_copies(at):
        if at == 0:
            pairs = [(item_mine.at[at], item_side.at[at])]
        else:
            there = side_rows(1 - side)
            pairs = [
                (item_mine.at[at, there], item_side.at[at, side_rows(0)]),
                (item_other.at[at, there], item_side.at[at, side_rows(1)]),
            ]
        return [
            remote_copy(
                source, target, item_sem.at[at, 2 * n], item_sem.at[at, 2 * n + 1], dp=across(1)
            )
            for n, (source, target) in enumerate(pairs)
        ]

    def item_start(at):
        for copy in item_loads(at):
            copy.wait()
        if at == 0:
            item_mine[0] = add_low(item_mine[0], item_other[0])
        for copy in item_first_copies(at):
            copy.start()

    def item_row_copy(at):
        return remote_copy(
            item_other.at[at, side_rows(side)],
            item_row.at[at],
            item_sem.at[at, 4],
            item_sem.at[at, 5],
            row=other,
        )

    def item_to_row(at):
        for copy in item_first_copies(at):
            copy.wait_recv()
        here = side_rows(side)
        item_other[at, here] = add_low(item_other[at, here], item_side[at, side_rows(1)])
        item_row_copy(at).start()
        item_mine[at, here] = add_low(item_mine[at, here], item_side[at, side_rows(0)])

    def item_extent(at):
        return pl.ds(0, size) if at == 0 else side_rows(side)

    def item_further_copy(at, number):
        extent = pl.ds(0, size if at == 0 else half_size)
        return remote_copy(
            item_mine.at[at, item_extent(at)],
            further.at[at, number - 1, extent],
            item_sem.at[at, 4 + 2 * number],
            item_sem.at[at, 5 + 2 * number],
            dp=across(bits[number]),
        )

    def item_further(at):
        extent = pl.ds(0, size if at == 0 else half_size)
        for number in range(1, sides):
            copy = item_further_copy(at, number)
            copy.start()
            copy.wait()
            landed = pltpu.make_async_copy(
                further.at[at, number - 1, extent],
                item_side.at[at, extent],
                item_load_sem.at[at, 0],
            )
            landed.start()
            landed.wait()
            here = item_extent(at)
            item_mine[at, here] = add_low(item_mine[at, here], item_side[at, extent])

    def item_last_copy(at):
        return remote_copy(
            item_mine.at[at, side_rows(side)],
            item_last.at[at],
            item_sem.at[at, 4 + 2 * sides],
            item_sem.at[at, 5 + 2 * sides],
            dp=across(1),
        )

    def item_after_row(at):
        item_row_copy(at).wait_recv()
        here = side_rows(side)
        for copy in item_first_copies(at):
            copy.wait_send()
        item_mine[at, here] = add_low(item_mine[at, here], item_row[at])
        item_further(at)
        item_last_copy(at).start()

    def item_core_copies(at):
        which, chunk = at // 2, at % 2
        total = (up_total_ref, down_total_ref)[which]
        first = core * part_width + chunk * size
        if at == 0:
            pieces = [(item_mine.at[0], pl.ds(pl.multiple_of(first, 16), size))]
        else:
            pieces = [
                (source, pl.ds(pl.multiple_of(first + of_side * half_size, 16), half_size))
                for source, of_side in (
                    (item_mine.at[at, side_rows(side)], side),
                    (item_last.at[at], 1 - side),
                )
            ]
        result = []
        for n, (source, place) in enumerate(pieces):
            base = 6 + 2 * sides + 3 * n
            result.append(
                remote_copy(
                    source,
                    total.at[place],
                    item_sem.at[at, base],
                    item_sem.at[at, base + 1],
                    dp=core_partner,
                )
            )
            result.append(
                pltpu.make_async_copy(source, total.at[place], item_sem.at[at, base + 2])
            )
        return result

    def item_finish(at):
        if at == 0:
            for copy in item_first_copies(at):
                copy.wait()
            item_mine[at] = add_low(item_mine[at], item_side[at])
            item_further(at)
        else:
            item_last_copy(at).wait_recv()
        for copy in item_core_copies(at):
            copy.start()

    def item_end(at):
        if at > 0:
            item_row_copy(at).wait_send()
            item_last_copy(at).wait_send()
        for copy in item_core_copies(at):
            copy.wait()

    item_start(1)
    for copy in load[3:]:
        copy.wait()

    branch_copy.wait_recv()
    item_to_row(1)
    item_start(0)
    outs.step(3)
    branch_all = branch[...].reshape(tokens, width)
    half_lanes = heads * head_dim // 2
    for part in range(2):
        lanes = slice(part * half_lanes, (part + 1) * half_lanes)
        grad_heads[:, lanes] = dot(branch_all, head_output_ref[lanes, :], 1, 1).astype(low)

    wo_size = wo_parts.shape[2]
    for b in range(2):
        lanes = slice(b * half_lanes, (b + 1) * half_lanes)
        value = dot(attended_ref[:, lanes], branch_all, 0, 0).astype(low)
        for part in range(2):
            wo_parts[b, part] = value[part * wo_size : (part + 1) * wo_size, :]

    def wo_core_copy(b):
        return remote_copy(
            wo_parts.at[b, 1 - core],
            wo_core.at[b],
            wo_sem.at[0, b],
            wo_sem.at[1, b],
            dp=core_partner,
        )

    for b in range(2):
        wo_core_copy(b).start()

    key_grad[...] = jnp.zeros_like(key_grad)
    value_grad[...] = jnp.zeros_like(value_grad)
    tile = tokens // 2
    window = key_ref.shape[0] - tile

    def head_step(head, carry):
        here = pl.ds(pl.multiple_of(head * head_dim, head_dim), head_dim)
        there = pl.ds(
            pl.multiple_of((head + head // per_block) * head_dim, head_dim), head_dim
        )
        for at in range(tokens // tile):
            first = at * tile
            rot = rot_ref[first : first + tile, here]
            grad = grad_heads[first : first + tile, here]
            keys = key_ref[first : first + window, :]
            values = value_ref[first : first + window, :]
            scores = dot(rot, keys, 1, 1) * head_dim ** (-0.5)
            place = lax.broadcasted_iota(jnp.int32, scores.shape, 1) + first
            query = lax.broadcasted_iota(jnp.int32, scores.shape, 0) + (first + tokens)
            allowed = (place <= query) & (place.astype(full) >= start_ref[first : first + tile, :])
            scores = jnp.where(allowed, scores, -1e30)
            lane = lax.broadcasted_iota(jnp.int32, (tile, head_dim), 1)
            logsum = jnp.sum(
                jnp.where(lane == head, logsum_ref[first : first + tile, :], 0.0),
                axis=1,
                keepdims=True,
            )
            probs = jnp.exp(scores - logsum)
            prob_grad = dot(grad, values, 1, 1)
            inner = jnp.sum(probs * prob_grad, axis=1, keepdims=True)
            score_grad = (probs * (prob_grad - inner) * head_dim ** (-0.5)).astype(low)
            rot_grad = dot(score_grad, keys)
            joint_grad[first : first + tile, there] = (
                rot_grad * cosine_ref[first : first + tile, :]
                - pltpu.roll(rot_grad, head_dim // 2, 1) * sine_ref[first : first + tile, :]
            ).astype(low)
            key_grad[first : first + window, :] += dot(score_grad, rot, 0, 0)
            value_grad[first : first + window, :] += dot(probs.astype(low), grad, 0, 0)
        return carry

    wa_size = part_width // 2
    chunk_rows = wa_size // 2

    class Lanes:
        def __init__(self, parts, core_room, row_room, sems, stretches, chunks):
            self.parts, self.core_room, self.row_room, self.sems = parts, core_room, row_room, sems
            self.stretches, self.chunks = stretches, chunks

        def core_copy(self, r0):
            return remote_copy(
                self.parts.at[r0, 1 - core],
                self.core_room.at[r0],
                self.sems.at[0, r0],
                self.sems.at[1, r0],
                dp=core_partner,
            )

        def dot(self, r0, which):
            first = pl.multiple_of(r0 * part_width + which * wa_size, 128)
            left = normed_ref[:, pl.ds(first, wa_size)]
            right = [joint_grad[:, lanes] for lanes in self.stretches]
            right = right[0] if len(right) == 1 else jnp.concatenate(right, axis=1)
            self.parts[r0, which] = dot(left, right, 0, 0).astype(low)

        def first(self):
            for r0 in (other, row):
                self.dot(r0, 1 - core)
                self.core_copy(r0).start()
            for r0 in (other, row):
                self.dot(r0, core)

        def row_copy(self, chunk):
            count = wa_size // self.chunks
            return remote_copy(
                self.parts.at[other, core, pl.ds(chunk * count, count)],
                self.row_room.at[chunk],
                self.sems.at[2, chunk],
                self.sems.at[3, chunk],
                row=other,
            )

        def to_row(self):
            self.core_copy(other).wait_recv()
            self.parts[other, core] = add_low(self.parts[other, core], self.core_room[other])
            for chunk in range(self.chunks):
                self.row_copy(chunk).start()
            self.core_copy(row).wait_recv()
            self.parts[row, core] = add_low(self.parts[row, core], self.core_room[row])

        def end(self):
            for r0 in range(2):
                self.core_copy(r0).wait_send()
            for chunk in range(self.chunks):
                self.row_copy(chunk).wait_send()

    stretches = [
        slice(b * block_lanes, b * block_lanes + query_lanes) for b in range(2)
    ]
    key_stretch = slice(query_lanes, block_lanes)
    value_stretch = slice(block_lanes + query_lanes, 2 * block_lanes)
    wq = [
        Lanes(
            wq_parts.at[b], wq_core.at[b], wq_row.at[b], wq_sem.at[b], [stretches[b]], 2
        )
        for b in range(2)
    ]
    wk = Lanes(wk_parts, wk_core, wk_row, wk_sem, [key_stretch, value_stretch], 1)

    def wo_row_copy(b):
        return remote_copy(
            wo_parts.at[b, core, :, part_lanes(other)],
            wo_row.at[b],
            wo_sem.at[2, b],
            wo_sem.at[3, b],
            row=other,
        )

    lax.fori_loop(0, 1, head_step, 0)
    for b in range(2):
        wo_core_copy(b).wait_recv()
        wo_parts[b, core] = add_low(wo_parts[b, core], wo_core[b])
        wo_row_copy(b).start()
    lax.fori_loop(1, per_block, head_step, 0)
    item_start(2)
    wq[0].first()
    lax.fori_loop(per_block, per_block + 1, head_step, 0)
    wq[0].to_row()
    lax.fori_loop(per_block + 1, heads, head_step, 0)
    pair_stage[:, :head_dim] = key_grad[:tokens, :].astype(low)
    pair_stage[:, head_dim:] = value_grad[:tokens, :].astype(low)
    odd = col % 2 == 1

    def pair_copy():
        return remote_copy(
            pair_stage, pair_arrived, pair_sem.at[0], pair_sem.at[1], col=col + 1 - 2 * (col % 2)
        )

    pl.when(odd)(lambda: pair_copy().start())
    wq[1].first()
    item_start(3)

    def over_col(lanes, stacks, arrived, send, recv, chunk, blocks):
        return ColSum(
            stacks.at[chunk], arrived.at[chunk], send.at[chunk], recv.at[chunk], col, cols, blocks
        )

    wq_total = [
        [
            over_col(
                wq[b], wq_stack.at[b], wq_arrived.at[b], wq_send.at[b], wq_recv.at[b], c, (b, 2 + b)
            )
            for c in range(2)
        ]
        for b in range(2)
    ]

    def wq_to_col(b):
        for chunk in range(2):
            wq[b].row_copy(chunk).wait_recv()
            place = pl.ds(chunk * chunk_rows, chunk_rows)
            wq_stack[b, chunk, row] = wq_parts[b, row, core, place]
            wq_stack[b, chunk, other] = wq_row[b, chunk]
            wq_total[b][chunk].step(1)

    def wq_step(b, number):
        for chunk in range(2):
            wq_total[b][chunk].step(number)

    wq[1].to_row()
    item_finish(0)
    wo_total = ColSum(wo_stack, wo_arrived, wo_send, wo_recv, col, cols, range(cols))
    for b in range(2):
        wo_row_copy(b).wait_recv()
        wo_stack[2 * row + b] = wo_parts[b, core, :, part_lanes(row)]
        wo_stack[2 * other + b] = wo_row[b]
    wo_total.step(1)
    wq_to_col(0)

    @pl.when(jnp.logical_not(odd))
    def _():
        pair_copy().wait_recv()
        key_grad[tokens:, :] += pair_arrived[:, :head_dim].astype(full)
        value_grad[tokens:, :] += pair_arrived[:, head_dim:].astype(full)

    key_total = key_grad[tokens:, :]
    joint_grad[:, key_stretch] = (
        key_total * cosine_ref[...] - pltpu.roll(key_total, head_dim // 2, 1) * sine_ref[...]
    ).astype(low)
    joint_grad[:, value_stretch] = value_grad[tokens:, :].astype(low)
    wk.first()

    normed_own = work

    def normed_dot(which):
        return dot(joint_grad[...], joint_ref[part_lanes(which), :], 1, 1)

    def normed_sums(which, value):
        product = value * normed_ref[:, part_lanes(which)].astype(full)
        gain = gains_ref[0:1, part_lanes(which)]
        total = jnp.sum(product, axis=0, keepdims=True) / gain
        for n in range(parts // 2):
            sums[0, pl.ds(which * (parts // 2) + n, 1), :] = total[
                :, n * quarter_lanes : (n + 1) * quarter_lanes
            ]
        return jnp.sum(product, axis=1, keepdims=True)

    wk.to_row()
    item_to_row(2)
    value = normed_dot(other)
    grad_heads[...] = value.astype(low)
    normed_copy = remote_copy(
        grad_heads, normed_arrived, normed_sem.at[0], normed_sem.at[1], row=other
    )
    inner = normed_sums(other, value)
    value = normed_dot(row)
    inner += normed_sums(row, value)
    for h in range(2):
        normed_own[h] = value[h * rows : (h + 1) * rows]
    inner_stage[...] = jnp.transpose(jnp.broadcast_to(inner, (tokens, head_dim)))[:8, :]
    inner_copy = remote_copy(
        inner_stage, inner_arrived, inner_sem.at[0], inner_sem.at[1], row=other
    )
    inner_copy.start()

    def sums_copies(stage):
        base = 0 if stage == 0 else len(plane)
        return [
            remote_copy(
                sums.at[stage],
                sums_arrived.at[base + n],
                sums_sem.at[base + n, 0],
                sums_sem.at[base + n, 1],
                **device,
            )
            for n, device in enumerate((plane, copies)[stage])
        ]

    def sums_start(stage):
        for copy in sums_copies(stage):
            copy.start()

    def sums_finish(stage):
        base = 0 if stage == 0 else len(plane)
        total = sums[stage]
        for n, copy in enumerate(sums_copies(stage)):
            copy.wait_recv()
            total += sums_arrived[base + n]
        sums[stage + 1] = total

    sums_start(0)
    wq_to_col(1)
    wq_step(0, 2)
    wo_total.step(2)
    wk_total = ColSum(wk_stack, wk_arrived, wk_send, wk_recv, col, cols, range(cols))
    wk.row_copy(0).wait_recv()
    for b in range(2):
        lanes = slice(b * key_lanes, (b + 1) * key_lanes)
        wk_stack[2 * row + b] = wk_parts[row, core, :, lanes]
        wk_stack[2 * other + b] = wk_row[0, :, lanes]
    wk_total.step(1)
    item_to_row(3)
    wq_step(1, 2)
    wq_step(0, 3)
    wk_total.step(2)
    normed_copy.start()
    sums_finish(0)
    sums_start(1)
    wo_total.step(3)
    wq_step(1, 3)
    wk_total.step(3)
    item_after_row(1)
    item_after_row(2)

    class Owned:
        def __init__(self, side_room, sems, targets):
            self.room, self.sems, self.targets = side_room, sems, targets

        def copy(self, number):
            return remote_copy(
                self.room.at[number % 2],
                self.room.at[2 + number],
                self.sems.at[2 * number],
                self.sems.at[2 * number + 1],
                dp=across(bits[number]),
            )

        def start(self, value):
            self.room[0] = value.astype(low)
            if sides:
                self.copy(0).start()

        def core_copies(self):
            result = []
            base, value = 2 * sides, self.room.at[sides % 2]
            return (
                remote_copy(
                    value,
                    self.targets,
                    self.sems.at[base],
                    self.sems.at[base + 1],
                    dp=core_partner,
                ),
                pltpu.make_async_copy(value, self.targets, self.sems.at[base + 2]),
            )

        def finish(self):
            for number in range(sides):
                self.copy(number).wait()
                self.room[1 - number % 2] = add_low(
                    self.room[number % 2], self.room[2 + number]
                )
                if number + 1 < sides:
                    self.copy(number + 1).start()
            for copy in self.core_copies():
                copy.start()

        def end(self):
            for copy in self.core_copies():
                copy.wait()

    def own_place(chunk, count):
        return pl.ds(pl.multiple_of(core * wa_size + chunk * count, 16), count)

    wk_owned = Owned(wk_side, wk_sem.at[4], keyval_total_ref.at[own_place(0, wa_size)])
    wq_owned = [
        Owned(wq_side.at[c], wq_side_sem.at[c], query_total_ref.at[own_place(c, chunk_rows)])
        for c in range(2)
    ]
    wo_owned = Owned(
        wo_side,
        wo_sem.at[4],
        output_total_ref.at[pl.ds(pl.multiple_of(core * wo_size, 16), wo_size)],
    )
    for b in range(2):
        for c in range(2):
            wq_total[b][c].total(wq_owned[c].start)
    wo_total.total(wo_owned.start)
    wk_total.total(wk_owned.start)

    def own_tokens(value):
        out_stack[col] = (middle_ref[...] + value).astype(low)

    outs.total(own_tokens)

    def outputs_copy():
        place = pl.ds(pl.multiple_of(row * rows, rows), rows)
        return remote_copy(
            out_stack.at[col, :, part_lanes(other)],
            outputs_ref.at[place],
            own_out_sem.at[0],
            own_out_sem.at[1],
            row=other,
        )

    outputs_copy().start()
    outputs_ref[pl.ds(pl.multiple_of(row * rows, rows), rows), :] = out_stack[
        col, :, part_lanes(row)
    ]
    item_after_row(3)
    item_finish(1)
    for c in range(2):
        wq_owned[c].finish()
    wk_owned.finish()
    wo_owned.finish()
    item_finish(2)
    sums_finish(1)
    for n in range(parts // 2):
        place = pl.ds(row * (parts // 2) + n, 1)
        lanes = slice(n * quarter_lanes, (n + 1) * quarter_lanes)
        gain_sums_ref[0:1, lanes] = sums[2, place, :]
        place = pl.ds(parts + row * (parts // 2) + n, 1)
        gain_sums_ref[1:2, lanes] = sums[2, place, :]
    item_finish(3)

    normed_copy.wait_recv()
    inner_copy.wait_recv()
    both = inner_stage[...] + inner_arrived[...]
    inner = jnp.transpose(jnp.concatenate([both] * (head_dim // 8), axis=0))[:, 0:1]
    for h in range(2):
        place = slice(h * rows, (h + 1) * rows)
        scale = scale_ref[place, :]
        normed_grad = normed_own[h] + normed_arrived[place, :].astype(full)
        input_grad_ref[place, :] = (
            branch[h, :, part_lanes(row)].astype(full)
            + scale * (gains_ref[0:1, part_lanes(row)] * normed_grad)
            - inputs_ref[place, :].astype(full) * (scale * scale) * (inner[place, :] / width)
        ).astype(low)

    branch_copy.wait_send()
    pl.when(odd)(lambda: pair_copy().wait_send())
    for b in range(2):
        wo_core_copy(b).wait_send()
        wo_row_copy(b).wait_send()
    for lanes in wq + [wk]:
        lanes.end()
    normed_copy.wait_send()
    inner_copy.wait_send()
    outputs_copy().wait()
    for stage in range(2):
        for copy in sums_copies(stage):
            copy.wait_send()
    outs.end(first=False)
    for total in [wo_total, wk_total] + wq_total[0] + wq_total[1]:
        total.end()
    for owned in wq_owned + [wk_owned, wo_owned]:
        owned.end()
    for at in range(items):
        item_end(at)


def finish_call(
    middle, gains, scale, start, logsum, sums, inputs, attended, rot, keys, values, cosine, sine,
    head_output, joint_weight, normed, cot_all, out_part, up_own, up_row, up_other, down_half, out_first,
    query_block, both_block,
):
    rows, width = middle.shape
    tokens, part_width = inputs.shape
    cols, dps = lax.axis_size("col"), lax.axis_size("dp")
    sides = dps.bit_length() - 2
    heads_width = attended.shape[1]
    reach = keys.shape[0]
    vmem = pl.BlockSpec(memory_space=pltpu.VMEM)
    anywhere = pl.BlockSpec(memory_space=pl.ANY)
    dma = pltpu.SemaphoreType.DMA
    hidden = 2 * up_own.shape[0]
    size = part_width // 2
    items = 4
    key_block = both_block - query_block
    wo_size, wa_size = query_block // 2, part_width // 2
    chunk = wa_size // 2
    shape = jax.ShapeDtypeStruct
    sums_count = 2 * cols - 1 + dps - 1
    return pl.pallas_call(
        finish_kernel,
        in_specs=[vmem] * 5 + [anywhere] * 18,
        out_specs=[vmem] * 6 + [anywhere] * 3,
        out_shape=[
            shape((tokens, part_width), low),
            shape((tokens, part_width), low),
            shape((2, part_width), full),
            shape((query_block, part_width), low),
            shape((part_width, query_block), low),
            shape((part_width, key_block), low),
            shape((hidden, part_width), low),
            shape((hidden, part_width), low),
            shape((items, max(sides - 1, 1), size, part_width), low),
        ],
        scratch_shapes=[
            pltpu.VMEM((2, rows, part_width), full),
            pltpu.VMEM((rows, width), low),
            pltpu.VMEM((tokens, part_width), low),
            pltpu.VMEM((tokens, heads_width), low),
            pltpu.VMEM((tokens, heads_width), low),
            pltpu.VMEM((reach, head_dim), low),
            pltpu.VMEM((reach, head_dim), low),
            pltpu.VMEM((tokens, head_dim), full),
            pltpu.VMEM((tokens, head_dim), full),
            pltpu.VMEM((heads_width, width), low),
            pltpu.VMEM((width, 2 * both_block), low),
            pltpu.VMEM((tokens, width), low),
            dma((14,)),
            pltpu.VMEM((2, rows, width), low),
            dma((2,)),
            pltpu.VMEM((cols, rows, width), low),
            pltpu.VMEM((cols + 1, rows, width), low),
            dma((cols,)),
            dma((cols + 1,)),
            dma((2,)),
            pltpu.VMEM((tokens, heads_width), low),
            pltpu.VMEM((tokens, 2 * both_block), low),
            pltpu.VMEM((reach, head_dim), full),
            pltpu.VMEM((reach, head_dim), full),
            pltpu.VMEM((tokens, 2 * head_dim), low),
            pltpu.VMEM((tokens, 2 * head_dim), low),
            dma((2,)),
            pltpu.VMEM((tokens, part_width), low),
            dma((2,)),
            pltpu.VMEM((8, tokens), full),
            pltpu.VMEM((8, tokens), full),
            dma((2,)),
            pltpu.VMEM((3, 8, width // 4), full),
            pltpu.VMEM((sums_count, 8, width // 4), full),
            dma((sums_count, 2)),
            pltpu.VMEM((items, size, part_width), low),
            pltpu.VMEM((items, size, part_width), low),
            pltpu.VMEM((items, size, part_width), low),
            pltpu.VMEM((items, size // 2, part_width), low),
            pltpu.VMEM((items, size // 2, part_width), low),
            dma((items, 12 + 2 * sides)),
            dma((items, 2)),
            pltpu.VMEM((2, 2, wo_size, width), low),
            pltpu.VMEM((2, wo_size, width), low),
            pltpu.VMEM((2, wo_size, part_width), low),
            pltpu.VMEM((cols, wo_size, part_width), low),
            pltpu.VMEM((cols + 1, wo_size, part_width), low),
            pltpu.VMEM((2 + sides, wo_size, part_width), low),
            dma((5, 3 + 2 * sides)),
            dma((cols,)),
            dma((cols + 1,)),
            pltpu.VMEM((2, 2, 2, wa_size, query_block), low),
            pltpu.VMEM((2, 2, wa_size, query_block), low),
            pltpu.VMEM((2, 2, chunk, query_block), low),
            pltpu.VMEM((2, 2, 2, chunk, query_block), low),
            pltpu.VMEM((2, 2, 3, chunk, query_block), low),
            pltpu.VMEM((2, 2 + sides, chunk, query_block), low),
            dma((2, 4, 2)),
            dma((2, 3 + 2 * sides)),
            dma((2, 2, 2)),
            dma((2, 2, 3)),
            pltpu.VMEM((2, 2, wa_size, 2 * key_block), low),
            pltpu.VMEM((2, wa_size, 2 * key_block), low),
            pltpu.VMEM((1, wa_size, 2 * key_block), low),
            pltpu.VMEM((cols, wa_size, key_block), low),
            pltpu.VMEM((cols + 1, wa_size, key_block), low),
            pltpu.VMEM((2 + sides, wa_size, key_block), low),
            dma((5, 3 + 2 * sides)),
            dma((cols,)),
            dma((cols + 1,)),
        ],
        compiler_params=pltpu.CompilerParams(
            collective_id=2, has_side_effects=True, vmem_limit_bytes=63 * 2**20
        ),
        cost_estimate=pl.CostEstimate(
            flops=10 * 10**9, bytes_accessed=40 * 10**6, transcendentals=4 * 10**6
        ),
    )(
        middle, gains, scale, start, logsum, sums, inputs, attended, rot, keys, values, cosine, sine,
        head_output, joint_weight, normed, cot_all, out_part, up_own, up_row, up_other, down_half, out_first,
    )


def results_kernel(*refs):
    count = len(refs) // 2
    for source, target in zip(refs[:count], refs[count:]):
        target[...] = source[...].astype(target.dtype)


def results_call(arrays, kinds, steps):
    specs = [
        pl.BlockSpec((array.shape[0] // steps, array.shape[1]), lambda i: (i, 0))
        for array in arrays
    ]
    return pl.pallas_call(
        results_kernel,
        grid=(steps,),
        in_specs=specs,
        out_specs=specs,
        out_shape=[
            jax.ShapeDtypeStruct(array.shape, kind) for array, kind in zip(arrays, kinds)
        ],
        compiler_params=pltpu.CompilerParams(vmem_limit_bytes=60 * 2**20),
    )(*arrays)


def shards(
    inputs,
    norm_gain,
    query_weight,
    key_value_matrix,
    output_weight,
    mixer_gain,
    gate_weight,
    up_weight,
    down_weight,
    lengths,
    routes,
    route_gates,
    cotangent,
):
    row, col = lax.axis_index("row"), lax.axis_index("col")
    part_width = inputs.shape[1]
    experts, _, units = gate_weight.shape
    hidden_width = experts * units
    query_block, keyval_block = query_weight.shape[1], key_value_matrix.shape[1]
    theta = rope_base ** (-np.arange(0, head_dim, 2, dtype=np.float64) / head_dim)
    theta = np.concatenate([theta, theta])[None, :].astype(np.float32)
    gate_flat = gate_weight.swapaxes(1, 2).reshape(hidden_width, part_width)
    up_flat = up_weight.swapaxes(1, 2).reshape(hidden_width, part_width)
    down_flat = down_weight.reshape(hidden_width, part_width)
    (
        normed,
        first_scale,
        gains,
        keys,
        values,
        cosine,
        sine,
        start,
        logsum,
        attended,
        rot,
        joint_weight,
        head_output,
        middle,
        expert_own,
        tables,
        cot_all,
        gate_other,
        up_other_half,
    ) = prologue_call(
        inputs, norm_gain, mixer_gain, lengths, theta, routes.T, route_gates.T, cotangent, query_weight, key_value_matrix,
        output_weight, gate_flat, up_flat, experts,
    )
    (
        second_grad,
        out_part,
        gate_total,
        up_own,
        up_row,
        up_other,
        down_half,
        out_first,
    ) = experts_call(
        expert_own, cot_all, tables, gate_flat, gate_other, up_flat, up_other_half, down_flat
    )

    both_block = query_block + keyval_block
    (
        outputs,
        input_grad,
        gain_sums,
        output_total,
        query_total,
        keyval_total,
        up_total,
        down_total,
        _,
    ) = finish_call(
        middle, gains, first_scale, start, logsum, second_grad, inputs, attended, rot, keys, values,
        cosine, sine, head_output, joint_weight, normed, cot_all, out_part,
        up_own, up_row, up_other, down_half, out_first, query_block, both_block,
    )
    norm_total, mixer_total = gain_sums[0], gain_sums[1]

    arrays = [gate_total, up_total, down_total, query_total, keyval_total, output_total]
    (
        gate_total,
        up_total,
        down_total,
        query_total,
        keyval_total,
        output_total,
        outputs,
        input_grad,
    ) = results_call(arrays + [outputs, input_grad], [full] * 6 + [low] * 2, 8)

    def by_expert(flat):
        return flat.reshape(experts, units, part_width)

    gate_total = by_expert(gate_total).swapaxes(1, 2)
    up_total = by_expert(up_total).swapaxes(1, 2)
    down_total = by_expert(down_total)
    return (
        outputs,
        input_grad,
        norm_total,
        query_total,
        keyval_total,
        output_total,
        mixer_total,
        gate_total,
        up_total,
        down_total,
    )


def solution(mesh):
    return jax.shard_map(
        shards,
        mesh=mesh,
        in_specs=(
            P(("dp", "col"), "row"),
            P("row"),
            P("row", "col"),
            P("row", "col"),
            P("col", "row"),
            P("row"),
            P(None, "row", "col"),
            P(None, "row", "col"),
            P(None, "col", "row"),
            P(("dp", "row"), None),
            P("dp", None),
            P("dp", None),
            P(("dp", "col"), "row"),
        ),
        out_specs=(
            P(("dp", "col"), "row"),
            P(("dp", "col"), "row"),
            P("row"),
            P("row", "col"),
            P("row", "col"),
            P("col", "row"),
            P("row"),
            P(None, "row", "col"),
            P(None, "row", "col"),
            P(None, "col", "row"),
        ),
        check_vma=False,
    )
```

```python
import jax
import jax.numpy as jnp
import numpy as np
from jax import lax
from jax.experimental import pallas as pl
from jax.experimental.pallas import tpu as pltpu
from jax.sharding import PartitionSpec as P

epsilon = 1e-06
rope_base = 1000000.0
head_dim = 128
low = jnp.bfloat16
full = jnp.float32


def dot(left, right, left_dim=1, right_dim=0):
    return lax.dot_general(
        left, right, (((left_dim,), (right_dim,)), ((), ())), preferred_element_type=full
    )


def remote_copy(source, target, send_sem, recv_sem, **device):
    return pltpu.make_async_remote_copy(
        src_ref=source,
        dst_ref=target,
        send_sem=send_sem,
        recv_sem=recv_sem,
        device_id=device,
        device_id_type=pl.DeviceIdType.MESH,
    )


def add_low(left, right):
    return (left.astype(full) + right.astype(full)).astype(low)


class ColSum:
    def __init__(self, stack, arrived, send_sem, recv_sem, col, count, blocks):
        self.stack, self.arrived, self.send_sem, self.recv_sem = stack, arrived, send_sem, recv_sem
        self.col, self.last, self.blocks = col, count - 1, list(blocks)

    def copy(self, block, at, right):
        neighbour = at + 1 if right else at - 1
        n = self.blocks.index(block)
        slot = n if right or block != neighbour else len(self.blocks)
        return remote_copy(
            self.stack.at[n],
            self.arrived.at[slot],
            self.send_sem.at[n],
            self.recv_sem.at[slot],
            col=neighbour,
        )

    def wait(self, slot, at):
        remote_copy(
            self.arrived.at[slot],
            self.arrived.at[slot],
            self.send_sem.at[0],
            self.recv_sem.at[slot],
            col=at + 1 if at == 0 else at - 1,
        ).wait_recv()

    def step(self, number, placed=False):
        for at in range(self.last + 1):
            ways = []
            for right in (True, False):
                block = at + self.last + 1 - number if right else at - self.last - 1 + number
                if block in self.blocks:
                    ways.append((block, right))
            if not ways:
                continue

            @pl.when(self.col == at)
            def _(at=at, ways=ways):
                for block, right in ways:
                    n = self.blocks.index(block)
                    if 0 < at < self.last:
                        if not placed:
                            self.wait(n, at)
                        self.stack[n] = add_low(self.stack[n], self.arrived[n])
                    self.copy(block, at, right).start()

    def total(self, part):
        for n, at in enumerate(self.blocks):

            @pl.when(self.col == at)
            def _(n=n, at=at):
                value = self.stack[n].astype(full)
                if at > 0:
                    self.wait(n, at)
                    value += self.arrived[n].astype(full)
                if at < self.last:
                    self.wait(len(self.blocks), at)
                    value += self.arrived[len(self.blocks)].astype(full)
                part(value)

    def end(self, first=True):
        for at in range(self.last + 1):

            @pl.when(self.col == at)
            def _(at=at):
                for block in self.blocks:
                    if block != at and (first or abs(block - at) < self.last):
                        self.copy(block, at, block > at).wait_send()


def experts_kernel(
    table_ref,
    own_hbm,
    cot_hbm,
    gate_hbm,
    gate_other_hbm,
    up_hbm,
    up_other_hbm,
    down_hbm,
    sum_ref,
    out_part_hbm,
    gate_total_ref,
    up_own_ref,
    up_row_ref,
    up_other_ref,
    down_half_ref,
    out_first_ref,
    cot_ref,
    out_part_ref,
    token_sem,
    weights,
    expert_in,
    gate_grad,
    up_grad,
    hidden,
    send_stage,
    arrived,
    parts,
    stage,
    weights_sem,
    down_sem,
    ready,
    ag_recv,
    ag_right,
    ag_left,
    rs_recv,
    rs_send,
    core_send,
    core_recv,
    row_send,
    row_recv,
    side_send,
    side_recv,
    final_sem,
    local_sem,
    out_sem,
):
    row, col, dp = lax.axis_index("row"), lax.axis_index("col"), lax.axis_index("dp")
    dps = lax.axis_size("dp")
    core, other = dp % 2, 1 - row
    core_partner = dp + 1 - 2 * core
    side_bits = list(range(1, dps.bit_length() - 1))
    sides = len(side_bits)
    last = cot_ref.shape[0] - 1
    rows, width = own_hbm.shape
    half = width // 2
    size = half // 2
    inner = (col > 0) & (col < last)

    def across(bit):
        on = (dp // (1 << bit)) % 2
        return dp + (1 << bit) * (1 - 2 * on)

    def half_lanes(which):
        return pl.ds(pl.multiple_of(which * half, half), half)

    gate_ref, up_ref, down_ref = weights.at[0], weights.at[1], weights.at[2]
    sources = (gate_hbm, gate_other_hbm, up_hbm, up_other_hbm, down_hbm)
    loads = [
        pltpu.make_async_copy(
            source,
            weights.at[i // 2, :, half_lanes((row, other)[i % 2])],
            weights_sem.at[i],
        )
        for i, source in enumerate(sources)
    ]
    own_load = pltpu.make_async_copy(own_hbm, expert_in.at[col], token_sem.at[0])
    cot_load = pltpu.make_async_copy(cot_hbm, cot_ref, token_sem.at[1])
    out_store = pltpu.make_async_copy(out_part_ref, out_part_hbm, token_sem.at[2])
    own_load.start()
    for copy in loads:
        copy.start()
    cot_load.start()

    barrier = pltpu.get_barrier_semaphore()

    def greet(semaphore, **device):
        pl.semaphore_signal(
            semaphore, inc=1, device_id=device, device_id_type=pl.DeviceIdType.MESH
        )

    greet(barrier, dp=core_partner)
    greet(barrier, row=other)
    for bit in side_bits:
        greet(barrier, dp=across(bit))
    pl.when(col > 0)(lambda: greet(barrier, col=col - 1))
    pl.when(col < last)(lambda: greet(barrier, col=col + 1))
    own_load.wait()
    pl.when(inner)(lambda: pl.semaphore_wait(barrier, 4 + sides))
    pl.when(jnp.logical_not(inner))(lambda: pl.semaphore_wait(barrier, 3 + sides))

    def ag_copy(block, right):
        return remote_copy(
            expert_in.at[block],
            expert_in.at[block],
            (ag_right if right else ag_left).at[block],
            ag_recv.at[block],
            col=col + 1 if right else col - 1,
        )

    def rs_copy(block, part, right):
        neighbour = col + 1 if right else col - 1
        slot = block if right else jnp.where(block == neighbour, last + 1, block)
        return remote_copy(
            send_stage.at[block, part],
            arrived.at[slot, part],
            rs_send.at[block, part],
            rs_recv.at[slot, part],
            col=neighbour,
        )

    def rs_wait(slot, part):
        remote_copy(
            arrived.at[slot, part],
            arrived.at[slot, part],
            rs_send.at[0, part],
            rs_recv.at[slot, part],
            col=jnp.where(col > 0, col - 1, col + 1),
        ).wait_recv()

    pl.when(col < last)(lambda: ag_copy(col, True).start())
    pl.when(col > 0)(lambda: ag_copy(col, False).start())
    pieces = 4
    quarter_size = down_hbm.shape[0] // 4
    piece_size = quarter_size // pieces
    quarter = dp % 4

    def down_place(which, piece):
        first = which * quarter_size + piece * piece_size
        return pl.ds(pl.multiple_of(first, 16), piece_size)

    def down_row(piece):
        place = down_place(quarter, piece)
        return remote_copy(
            down_hbm.at[place],
            weights.at[2, place, half_lanes(row)],
            down_sem.at[piece, 0],
            down_sem.at[piece, 1],
            row=other,
        )

    def down_side(piece):
        there = weights.at[2, down_place(quarter, piece), half_lanes(other)]
        return remote_copy(
            there, there, down_sem.at[piece, 2], down_sem.at[piece, 3], dp=across(1)
        )

    def down_core(piece, n):
        there = weights.at[2, down_place(core + 2 * n, piece), half_lanes(other)]
        return remote_copy(
            there,
            there,
            down_sem.at[piece, 4 + 2 * n],
            down_sem.at[piece, 5 + 2 * n],
            dp=core_partner,
        )

    for piece in range(pieces):
        down_row(piece).start()
    for copy in loads[:4]:
        copy.wait()

    def products(block):
        tokens = expert_in[block]
        table = table_ref[block]
        experts = table.shape[1]
        units = width // experts
        for g in range(2):
            cols = slice(g * half, (g + 1) * half)
            gate = dot(tokens, gate_ref[cols, :], 1, 1)
            up = dot(tokens, up_ref[cols, :], 1, 1)
            lane = lax.broadcasted_iota(jnp.int32, gate.shape, 1)
            first = g * experts // 2
            chosen = jnp.broadcast_to(table[:, first : first + 1], gate.shape)
            for e in range(1, experts // 2):
                chosen = jnp.where(lane >= e * units, table[:, first + e : first + e + 1], chosen)
            sigmoid = 1.0 / (1.0 + jnp.exp(-gate))
            silu = gate * sigmoid
            up = up * chosen
            hidden[block, :, cols] = (silu * up).astype(low)
            gate_grad[block, :, cols] = (up * (sigmoid * (1.0 + gate * (1.0 - sigmoid)))).astype(low)
            up_grad[block, :, cols] = (silu * chosen).astype(low)

    def gradients(block):
        grads = cot_ref[block]
        for g in range(2):
            cols = slice(g * half, (g + 1) * half)
            grad = dot(grads, down_ref[cols, :], 1, 1)
            gate_grad[block, :, cols] = (grad * gate_grad[block, :, cols].astype(full)).astype(low)
            up_grad[block, :, cols] = (grad * up_grad[block, :, cols].astype(full)).astype(low)
        gates_now, ups_now = gate_grad[block], up_grad[block]
        for part in range(2):
            cols = slice(part * half, (part + 1) * half)
            total = dot(gates_now, gate_ref[:, cols]) + dot(ups_now, up_ref[:, cols])
            send_stage[block, part] = total.astype(low)
            pl.when((col == 0) & (block != col))(lambda: rs_copy(block, part, True).start())
            pl.when((col == last) & (block != col))(lambda: rs_copy(block, part, False).start())
        out_part_ref[block] = dot(hidden[block], down_ref[...]).astype(low)

    def block_of(i):
        return jnp.where(i % 2 == 1, col - (i + 1) // 2, col + (i + 1) // 2)

    def pass_on(apart):
        @pl.when(col - apart >= 0)
        def _():
            ag_copy(col - apart, True).wait_recv()
            pl.when(col < last)(lambda: ag_copy(col - apart, True).start())

        @pl.when(col + apart <= last)
        def _():
            ag_copy(col + apart, False).wait_recv()
            pl.when(col > 0)(lambda: ag_copy(col + apart, False).start())

    def present(block):
        return (block >= 0) & (block <= last)

    def near_products(i, carry):
        pl.when(i == 1)(lambda: pass_on(1))
        pl.when(present(block_of(i)))(lambda: products(block_of(i)))
        return carry

    lax.fori_loop(0, 1, near_products, 0)
    for piece in range(pieces):
        down_row(piece).wait_recv()
        down_side(piece).start()
    lax.fori_loop(1, 3, near_products, 0)
    for piece in range(pieces):
        down_side(piece).wait_recv()
        for n in range(2):
            down_core(piece, n).start()
    loads[4].wait()
    cot_load.wait()
    for piece in range(pieces):
        for n in range(2):
            down_core(piece, n).wait_recv()

    def near_gradients(n, carry):
        i = (n + 1) % 3
        pl.when(i == 0)(lambda: pass_on(2))
        pl.when(present(block_of(i)))(lambda: gradients(block_of(i)))
        return carry

    lax.fori_loop(0, 3, near_gradients, 0)

    def far_blocks(i, carry):
        pl.when(i == 5)(lambda: pass_on(3))

        @pl.when(present(block_of(i)))
        def _():
            products(block_of(i))
            gradients(block_of(i))

        return carry

    lax.fori_loop(3, 2 * last + 1, far_blocks, 0)
    out_store.start()
    for piece in range(pieces):
        down_row(piece).wait_send()
        down_side(piece).wait_send()
        for n in range(2):
            down_core(piece, n).wait_send()

    greet(ready.at[0], dp=core_partner)
    greet(ready.at[1], row=other)
    for number, bit in enumerate(side_bits):
        greet(ready.at[2 + number], dp=across(bit))

    def room(which, down, right):
        return weights.at[
            which, pl.ds(down * half, half), pl.ds(right * half, half)
        ]

    def forward(block, part, right):
        rs_wait(block, part)
        send_stage[block, part] = add_low(send_stage[block, part], arrived[block, part])
        rs_copy(block, part, right).start()

    def event(number, part):
        blocks = ((2, 1), (3, 0), (0, 3))[number]
        pl.when(col == 1)(lambda: forward(blocks[0], part, number < 2))
        pl.when(col == 2)(lambda: forward(blocks[1], part, number == 2))

    def core_copy(at):
        if at < 4:
            target = room(at // 2, 0, at % 2)
        else:
            target = room(2, 0, at - 4)
        return remote_copy(
            stage.at[at % 2], target, core_send.at[at], core_recv.at[at], dp=core_partner
        )

    def stage_free(at):
        if at >= 2:
            core_copy(at - 2).wait_send()

    def core_dot(at):
        left = (gate_grad, up_grad)[at // 2]
        right = expert_in[:, :, half_lanes(row if at % 2 else other)].reshape(-1, half)
        stage_free(at)
        stage[at % 2] = dot(
            left[:, :, half_lanes(1 - core)].reshape(-1, half), right, 0, 0
        ).astype(low)
        core_copy(at).start()
        parts[at] = dot(left[:, :, half_lanes(core)].reshape(-1, half), right, 0, 0).astype(low)

    def core_sum(at):
        core_copy(at).wait_recv()
        parts[at] = add_low(parts[at], room(at // 2, 0, at % 2)[...])

    def down_dot_partner():
        left = hidden[:, :, half_lanes(1 - core)].reshape(-1, half)
        for part in range(2):
            lanes = slice(part * half, (part + 1) * half)
            right = cot_ref[:, :, lanes].reshape(-1, half)
            stage_free(4 + part)
            stage[part] = dot(left, right, 0, 0).astype(low)
            core_copy(4 + part).start()

    def down_dot_own():
        left = hidden[:, :, half_lanes(core)].reshape(-1, half)
        for part in range(2):
            lanes = slice(part * half, (part + 1) * half)
            right = cot_ref[:, :, lanes].reshape(-1, half)
            room(2, 1, part)[...] = dot(left, right, 0, 0).astype(low)

    def down_sum():
        for part in range(2):
            core_copy(4 + part).wait_recv()
            room(2, 1, part)[...] = add_low(room(2, 1, part)[...], room(2, 0, part)[...])

    down_out = pltpu.make_async_copy(
        weights.at[2, pl.ds(half, half)], down_half_ref, local_sem.at[0]
    )
    up_out = pltpu.make_async_copy(parts.at[3], up_own_ref, local_sem.at[1])
    up_rest = pltpu.make_async_copy(
        parts.at[2, pl.ds(size, size)], up_other_ref, local_sem.at[2]
    )

    chunks = 4
    chunk_size = half // chunks

    def chunk_rows(chunk):
        return pl.ds(chunk * chunk_size, chunk_size)

    def row_copy(chunk):
        if chunk < chunks:
            source = parts.at[0, chunk_rows(chunk)]
            target = weights.at[0, pl.ds(half + chunk * chunk_size, chunk_size), pl.ds(0, half)]
        else:
            source, target = parts.at[2, pl.ds(0, size)], up_row_ref
        return remote_copy(source, target, row_send.at[chunk], row_recv.at[chunk], row=other)

    def side_room(number, chunk):
        which, right = ((0, 1), (1, 0), (1, 1))[number]
        return weights.at[
            which, pl.ds(half + chunk * chunk_size, chunk_size), pl.ds(right * half, half)
        ]

    def side_copy(chunk, number):
        return remote_copy(
            parts.at[1 - number % 2, chunk_rows(chunk)],
            side_room(number, chunk),
            side_send.at[chunk, number],
            side_recv.at[chunk, number],
            dp=across(side_bits[number]),
        )

    def after_row(chunk):
        copy = row_copy(chunk)
        copy.wait_recv()
        if chunk + 2 <= chunks:
            row_copy(chunk + 2).start()
        copy.wait_send()
        here = chunk_rows(chunk)
        landed = weights.at[0, pl.ds(half + chunk * chunk_size, chunk_size), pl.ds(0, half)]
        parts[1, here] = add_low(parts[1, here], landed[...])
        if chunk == 0 and sides:
            for number in range(sides):
                pl.semaphore_wait(ready.at[2 + number], 1)
        if sides:
            side_copy(chunk, 0).start()

    def final_copies(chunk):
        source = parts.at[1 - sides % 2, chunk_rows(chunk)]
        first = pl.multiple_of(core * half + chunk * chunk_size, 16)
        target = gate_total_ref.at[pl.ds(first, chunk_size)]
        return (
            remote_copy(
                source, target, final_sem.at[chunk, 0], final_sem.at[chunk, 1], dp=core_partner
            ),
            pltpu.make_async_copy(source, target, final_sem.at[chunk, 2]),
        )

    def after_side(chunk):
        here = chunk_rows(chunk)
        for number in range(sides):
            copy = side_copy(chunk, number)
            copy.wait_recv()
            copy.wait_send()
            parts[number % 2, here] = add_low(
                parts[1 - number % 2, here], side_room(number, chunk)[...]
            )
            if number + 1 < sides:
                side_copy(chunk, number + 1).start()
        for copy in final_copies(chunk):
            copy.start()

    def out_copy(right):
        return remote_copy(
            out_part_ref.at[last if right else 0],
            out_first_ref,
            out_sem.at[0],
            out_sem.at[1],
            col=col + 1 if right else col - 1,
        )

    pl.semaphore_wait(ready.at[0], 1)
    core_dot(0)
    event(0, 0)
    core_sum(0)
    pl.semaphore_wait(ready.at[1], 1)
    row_copy(0).start()
    event(0, 1)
    core_dot(1)
    core_sum(1)
    row_copy(1).start()
    event(1, 0)
    core_dot(2)
    pl.when(col == 0)(lambda: out_copy(True).start())
    pl.when(col == last)(lambda: out_copy(False).start())
    after_row(0)
    core_sum(2)
    up_rest.start()
    event(1, 1)
    core_dot(3)
    after_row(1)
    event(2, 0)
    core_sum(3)
    up_out.start()
    after_side(0)
    down_dot_partner()
    event(2, 1)
    after_row(2)
    after_side(1)
    down_dot_own()
    after_row(3)
    down_sum()
    down_out.start()
    after_side(2)

    for part in range(2):
        sum_ref[part] = send_stage[col, part].astype(full)

        @pl.when(col > 0)
        def _():
            rs_wait(col, part)
            sum_ref[part] += arrived[col, part].astype(full)

        @pl.when(col < last)
        def _():
            rs_wait(last + 1, part)
            sum_ref[part] += arrived[last + 1, part].astype(full)

    after_side(3)

    for block in range(last + 1):
        pl.when((block <= col) & (col < last))(lambda: ag_copy(block, True).wait_send())
        pl.when((block >= col) & (col > 0))(lambda: ag_copy(block, False).wait_send())
        for part in range(2):
            pl.when(block > col)(lambda: rs_copy(block, part, True).wait_send())
            pl.when(block < col)(lambda: rs_copy(block, part, False).wait_send())
    for at in range(4, 6):
        core_copy(at).wait_send()
    out_store.wait()
    row_copy(chunks).wait()
    pl.when(col == 0)(lambda: out_copy(True).wait_send())
    pl.when(col == last)(lambda: out_copy(False).wait_send())
    pl.when(inner)(lambda: out_copy(False).wait_recv())
    for copy in (down_out, up_out, up_rest):
        copy.wait()
    for chunk in range(chunks):
        for copy in final_copies(chunk):
            copy.wait()


def experts_call(own, cot, table, *halves):
    rows, width = own.shape
    blocks, half = cot.shape[0], width // 2
    sides = lax.axis_size("dp").bit_length() - 2
    vmem = pl.BlockSpec(memory_space=pltpu.VMEM)
    anywhere = pl.BlockSpec(memory_space=pl.ANY)
    dma = pltpu.SemaphoreType.DMA
    shape = jax.ShapeDtypeStruct
    return pl.pallas_call(
        experts_kernel,
        in_specs=[vmem] + [anywhere] * 7,
        out_specs=[vmem] + [anywhere] * 7,
        out_shape=[
            shape((2, rows, half), full),
            shape((blocks, rows, width), low),
            shape((width, half), low),
            shape((half, half), low),
            shape((half // 2, half), low),
            shape((half // 2, half), low),
            shape((half, width), low),
            shape((rows, width), low),
        ],
        scratch_shapes=[
            pltpu.VMEM((blocks, rows, width), low),
            pltpu.VMEM((blocks, rows, width), low),
            dma((3,)),
            pltpu.VMEM((3, width, width), low),
        ]
        + [pltpu.VMEM((blocks, rows, width), low)] * 4
        + [
            pltpu.VMEM((blocks, 2, rows, half), low),
            pltpu.VMEM((blocks + 1, 2, rows, half), low),
            pltpu.VMEM((4, half, half), low),
            pltpu.VMEM((2, half, half), low),
            dma((5,)),
            dma((4, 8)),
            pltpu.SemaphoreType.REGULAR((2 + max(sides, 1),)),
            dma((blocks,)),
            dma((blocks,)),
            dma((blocks,)),
            dma((blocks + 1, 2)),
            dma((blocks, 2)),
            dma((6,)),
            dma((6,)),
            dma((5,)),
            dma((5,)),
            dma((4, max(sides, 1))),
            dma((4, max(sides, 1))),
            dma((4, 3)),
            dma((3,)),
            dma((2,)),
        ],
        compiler_params=pltpu.CompilerParams(
            collective_id=1, has_side_effects=True, vmem_limit_bytes=60 * 2**20
        ),
        cost_estimate=pl.CostEstimate(
            flops=9 * 2 * blocks * rows * width * width,
            bytes_accessed=12 * width * width,
            transcendentals=blocks * rows * width,
        ),
    )(table, own, cot, *halves)


def prologue_kernel(
    inputs_ref,
    norm_ref,
    mixer_ref,
    lengths_ref,
    theta_ref,
    routes_ref,
    route_gates_ref,
    cot_ref,
    query_hbm,
    keyval_hbm,
    output_hbm,
    gate_hbm,
    up_hbm,
    normed_hbm,
    scale_ref,
    gains_ref,
    key_hbm,
    value_hbm,
    cosine_ref,
    sine_ref,
    start_ref,
    logsum_ref,
    attended_hbm,
    rot_hbm,
    joint_hbm,
    head_output_hbm,
    middle_hbm,
    expert_hbm,
    table_ref,
    cot_all_ref,
    gate_all_ref,
    up_all_ref,
    normed_ref,
    key_ref,
    value_ref,
    attended_ref,
    rot_ref,
    joint_ref,
    head_output_ref,
    middle_ref,
    expert_ref,
    store_sem,
    inputs_all,
    inputs_sem,
    small,
    small_sem,
    projected,
    branch_own,
    branch_stage,
    branch_arrived,
    branch_sem,
    pair_sem,
    joint_line,
    joint_load,
    joint_hop,
    joint_row,
    joint_side,
    joint_core,
    output_line,
    output_load,
    output_hop,
    output_row,
    output_side,
    output_core,
    expert_row,
    expert_side,
    expert_core,
    cot_sem,
    cot_recv,
    cot_send,
):
    row, col, dp = lax.axis_index("row"), lax.axis_index("col"), lax.axis_index("dp")
    cols = lax.axis_size("col")
    last = cols - 1
    core, side, other = dp % 2, (dp // 2) % 2, 1 - row
    quarter = dp % 4
    core_partner, side_partner = dp + 1 - 2 * core, dp + 2 - 4 * side
    tokens, part_width = inputs_ref.shape
    width, rows = 2 * part_width, tokens // 2
    query_block, keyval_block = query_hbm.shape[1], keyval_hbm.shape[1]
    block = query_block + keyval_block
    experts = table_ref.shape[2]

    barrier = pltpu.get_barrier_semaphore()

    def greet(**device):
        pl.semaphore_signal(
            barrier, inc=1, device_id=device, device_id_type=pl.DeviceIdType.MESH
        )

    greet(row=other)
    for apart in range(1, cols):
        greet(col=(col + apart) % cols)
    greet(dp=core_partner)
    greet(dp=side_partner)

    def part_lanes(which):
        return pl.ds(pl.multiple_of(which * part_width, 128), part_width)

    inputs_all[:, part_lanes(row)] = inputs_ref[...]
    small[row, 0:1, :] = norm_ref[...].reshape(1, part_width)
    small[row, 1:2, :] = mixer_ref[...].reshape(1, part_width)
    sequences = lengths_ref.shape[1]
    small[row, 2:3, :] = jnp.zeros((1, part_width), full)
    small[row, 2:3, :sequences] = lengths_ref[...].astype(full)
    small[row, 3:8, :] = jnp.zeros((5, part_width), full)
    inputs_copy = remote_copy(
        inputs_ref,
        inputs_all.at[:, part_lanes(row)],
        inputs_sem.at[0],
        inputs_sem.at[1],
        row=other,
    )
    small_copy = remote_copy(
        small.at[row], small.at[row], small_sem.at[0], small_sem.at[1], row=other
    )

    joint_size, output_size = query_hbm.shape[0] // 4, output_hbm.shape[0] // 4

    def joint_region(r0, b, which):
        return joint_ref.at[
            pl.ds(pl.multiple_of(r0 * part_width + which * joint_size, 16), joint_size),
            pl.ds(pl.multiple_of(b * block, 128), block),
        ]

    def output_region(r0, b, which):
        return head_output_ref.at[
            pl.ds(pl.multiple_of(b * query_block + which * output_size, 16), output_size),
            part_lanes(r0),
        ]

    class Gather:
        def __init__(self, line, pieces, load, hop, row_sems, side_sems, core_sems, region):
            self.line, self.region, self.hop, self.row_sems = line, region, hop, row_sems
            self.side_sems, self.core_sems = side_sems, core_sems
            self.loads = [
                pltpu.make_async_copy(source, target, load.at[n])
                for n, (source, target) in enumerate(pieces)
            ]

        def copy(self, at, right):
            return remote_copy(
                self.line.at[at],
                self.line.at[at],
                self.hop.at[at, 1 if right else 0],
                self.hop.at[at, 2],
                col=col + 1 if right else col - 1,
            )

        def row_copy(self, b):
            return remote_copy(
                self.line.at[2 * other + b],
                self.region(row, b, quarter),
                self.row_sems.at[b, 0],
                self.row_sems.at[b, 1],
                row=other,
            )

        def side_copy(self, n):
            there = self.region((row, other)[n // 2], n % 2, quarter)
            return remote_copy(
                there, there, self.side_sems.at[n, 0], self.side_sems.at[n, 1], dp=side_partner
            )

        def core_copies(self, n):
            result = []
            for part in range(2):
                there = self.region((row, other)[n // 2], n % 2, core + 2 * part)
                result.append(
                    remote_copy(
                        there,
                        there,
                        self.core_sems.at[n, 2 * part],
                        self.core_sems.at[n, 2 * part + 1],
                        dp=core_partner,
                    )
                )
            return result

        def use(self, at):
            for b in range(2):

                @pl.when(at == 2 * row + b)
                def _(b=b):
                    there = self.region(row, b, quarter)
                    there[...] = self.line[at]
                    self.side_copy(b).start()

                @pl.when(at == 2 * other + b)
                def _(b=b):
                    self.row_copy(b).start()

        def load(self):
            for copy in self.loads:
                copy.start()

        def first(self):
            for copy in self.loads:
                copy.wait()
            pl.when(col < last)(lambda: self.copy(col, True).start())
            pl.when(col > 0)(lambda: self.copy(col, False).start())
            self.use(col)

        def step(self, apart):
            @pl.when(col - apart >= 0)
            def _():
                self.copy(col - apart, True).wait_recv()
                pl.when(col < last)(lambda: self.copy(col - apart, True).start())
                self.use(col - apart)

            @pl.when(col + apart <= last)
            def _():
                self.copy(col + apart, False).wait_recv()
                pl.when(col > 0)(lambda: self.copy(col + apart, False).start())
                self.use(col + apart)

        def from_row(self):
            for b in range(2):
                self.row_copy(b).wait_recv()
                self.side_copy(2 + b).start()

        def to_core(self):
            for n in range(4):
                self.side_copy(n).wait_recv()
                for copy in self.core_copies(n):
                    copy.start()

        def ready(self):
            for n in range(4):
                for copy in self.core_copies(n):
                    copy.wait_recv()

        def end(self):
            for at in range(cols):
                pl.when((at <= col) & (col < last))(lambda: self.copy(at, True).wait_send())
                pl.when((at >= col) & (col > 0))(lambda: self.copy(at, False).wait_send())
            for b in range(2):
                self.row_copy(b).wait_send()
            for n in range(4):
                self.side_copy(n).wait_send()
                for copy in self.core_copies(n):
                    copy.wait_send()

    first_joint = pl.ds(pl.multiple_of(quarter * joint_size, 16), joint_size)
    first_output = pl.ds(pl.multiple_of(quarter * output_size, 16), output_size)
    joint = Gather(
        joint_line,
        (
            (query_hbm.at[first_joint], joint_line.at[col, :, pl.ds(0, query_block)]),
            (keyval_hbm.at[first_joint], joint_line.at[col, :, pl.ds(query_block, keyval_block)]),
        ),
        joint_load,
        joint_hop,
        joint_row,
        joint_side,
        joint_core,
        joint_region,
    )
    output = Gather(
        output_line,
        ((output_hbm.at[first_output], output_line.at[col]),),
        output_load,
        output_hop,
        output_row,
        output_side,
        output_core,
        output_region,
    )

    def token_rows(which):
        return pl.ds(pl.multiple_of(which * rows, 16), rows)

    cot_row = remote_copy(
        cot_ref.at[token_rows(other)],
        cot_all_ref.at[col, :, part_lanes(row)],
        cot_sem.at[0],
        cot_sem.at[1],
        row=other,
    )

    def cot_copy(block_at, right):
        return remote_copy(
            cot_all_ref.at[block_at],
            cot_all_ref.at[block_at],
            cot_send.at[block_at, 1 if right else 0],
            cot_recv.at[block_at],
            col=col + 1 if right else col - 1,
        )

    def cot_first():
        cot_row.wait_recv()
        pl.when(col < last)(lambda: cot_copy(col, True).start())
        pl.when(col > 0)(lambda: cot_copy(col, False).start())

    def cot_pass(apart):
        @pl.when(col - apart >= 0)
        def _():
            cot_copy(col - apart, True).wait_recv()
            pl.when(col < last)(lambda: cot_copy(col - apart, True).start())

        @pl.when(col + apart <= last)
        def _():
            cot_copy(col + apart, False).wait_recv()
            pl.when(col > 0)(lambda: cot_copy(col + apart, False).start())

    expert_size = gate_hbm.shape[0] // 4
    weights = (gate_hbm, up_hbm)
    totals = (gate_all_ref, up_all_ref)

    unit_size = expert_size // 2

    def expert_place(which, of_quarter):
        first = of_quarter * expert_size + (which % 2) * unit_size
        return pl.ds(pl.multiple_of(first, 16), unit_size)

    def expert_region(which, of_quarter):
        return totals[which // 2].at[expert_place(which, of_quarter)]

    def expert_row_copy(which):
        return remote_copy(
            weights[which // 2].at[expert_place(which, quarter)],
            expert_region(which, quarter),
            expert_row.at[which, 0],
            expert_row.at[which, 1],
            row=other,
        )

    def expert_side_copy(which):
        there = expert_region(which, quarter)
        return remote_copy(
            there, there, expert_side.at[which, 0], expert_side.at[which, 1], dp=side_partner
        )

    def expert_core_copies(which):
        result = []
        for n in range(2):
            there = expert_region(which, core + 2 * n)
            result.append(
                remote_copy(
                    there,
                    there,
                    expert_core.at[which, 2 * n],
                    expert_core.at[which, 2 * n + 1],
                    dp=core_partner,
                )
            )
        return result

    def expert_after_row(which):
        expert_row_copy(which).wait_recv()
        expert_side_copy(which).start()

    def expert_after_side(which):
        expert_side_copy(which).wait_recv()
        for copy in expert_core_copies(which):
            copy.start()

    store_pairs = (
        (normed_ref, normed_hbm),
        (key_ref, key_hbm),
        (value_ref, value_hbm),
        (attended_ref, attended_hbm),
        (rot_ref, rot_hbm),
        (joint_ref, joint_hbm),
        (head_output_ref, head_output_hbm),
        (middle_ref, middle_hbm),
        (expert_ref, expert_hbm),
    )
    stores = [
        pltpu.make_async_copy(source, target, store_sem.at[n])
        for n, (source, target) in enumerate(store_pairs)
    ]
    joint.load()
    output.load()
    pl.semaphore_wait(barrier, cols + 2)
    joint.first()
    small_copy.start()
    cot_row.start()
    cot_all_ref[col, :, part_lanes(row)] = cot_ref[token_rows(row), :]

    for at in range(cols):
        place = pl.ds(pl.multiple_of(at * tokens + row * rows, 128), rows)
        chosen, gates = routes_ref[:, place], route_gates_ref[:, place]
        expert = lax.broadcasted_iota(jnp.int32, (experts, rows), 0)
        table = jnp.zeros((experts, rows), full)
        for k in range(chosen.shape[0]):
            table += jnp.where(chosen[k : k + 1, :] == expert, gates[k : k + 1, :], 0.0)
        table_ref[at] = jnp.transpose(table)
    joint.step(1)

    small_copy.wait_recv()
    gains_ref[:, :part_width] = small[0, 0:2, :]
    gains_ref[:, part_width:] = small[1, 0:2, :]
    half = col // 2
    lens = small[half, 2:3, :]
    odd = (col % 2).astype(full)
    place = lax.broadcasted_iota(jnp.int32, (tokens, 1), 0).astype(full) + odd * tokens
    begin = jnp.zeros((tokens, 1), full)
    total = lens[:, 0:1]
    for n in range(1, sequences):
        begin = jnp.where(place >= total, total, begin)
        total = total + lens[:, n : n + 1]
    start_ref[...] = begin + (1.0 - odd) * tokens
    cot_first()
    inputs_copy.start()
    angles = (place - begin) * theta_ref[...]
    cosine_ref[...] = jnp.cos(angles)
    sine = jnp.sin(angles)
    lane = lax.broadcasted_iota(jnp.int32, sine.shape, 1)
    sine_ref[...] = jnp.where(lane < head_dim // 2, -sine, sine)

    joint.step(2)
    joint.step(3)
    output.first()
    joint.from_row()
    output.step(1)
    inputs_copy.wait_recv()
    expert_row_copy(0).start()
    expert_row_copy(1).start()

    piece = 64

    def norm_piece(at, carry):
        here = pl.ds(pl.multiple_of(at * piece, piece), piece)
        values = inputs_all[here, :].astype(full)
        scale = lax.rsqrt(jnp.mean(values * values, axis=1, keepdims=True) + epsilon)
        scale_ref[here, :] = scale
        for which in range(2):
            lanes = slice(which * part_width, (which + 1) * part_width)
            normed_ref[here, lanes] = (values[:, lanes] * scale * small[which, 0:1, :]).astype(low)
        return carry

    lax.fori_loop(0, tokens // piece, norm_piece, 0)
    joint.to_core()
    output.step(2)
    cot_pass(1)
    joint.ready()
    stores[0].start()
    stores[5].start()

    own = pl.ds(tokens, tokens)
    key = dot(normed_ref[...], joint_ref[:, query_block:block])
    key_ref[own, :] = (
        key * cosine_ref[...] + pltpu.roll(key, head_dim // 2, 1) * sine_ref[...]
    ).astype(low)
    value_ref[own, :] = dot(normed_ref[...], joint_ref[:, block + query_block :]).astype(low)

    def pair_copies():
        return [
            remote_copy(
                ref.at[own],
                ref.at[pl.ds(0, tokens)],
                pair_sem.at[n, 0],
                pair_sem.at[n, 1],
                col=col + 1 - 2 * (col % 2),
            )
            for n, ref in enumerate((key_ref, value_ref))
        ]

    @pl.when(col % 2 == 0)
    def _():
        for copy in pair_copies():
            copy.start()
        key_ref[:tokens, :] = jnp.zeros((tokens, head_dim), low)
        value_ref[:tokens, :] = jnp.zeros((tokens, head_dim), low)

    for b in range(2):
        lanes = slice(b * query_block, (b + 1) * query_block)
        projected[:, lanes] = dot(
            normed_ref[...], joint_ref[:, b * block : b * block + query_block]
        )
    output.step(3)
    output.from_row()
    expert_after_row(0)
    expert_row_copy(2).start()
    expert_row_copy(3).start()
    output.to_core()

    @pl.when(col % 2 == 1)
    def _():
        for copy in pair_copies():
            copy.wait_recv()

    expert_after_row(1)

    heads = 2 * query_block // head_dim
    tile = rows
    window = key_ref.shape[0] - tile

    def attend(which):
        first = which * tile
        here = pl.ds(pl.multiple_of(first, 16), tile)
        reach = pl.ds(pl.multiple_of(first, 16), window)

        def head_step(head, carry):
            lanes = pl.ds(pl.multiple_of(head * head_dim, head_dim), head_dim)
            pre = projected[here, lanes]
            rot = (
                pre * cosine_ref[here, :] + pltpu.roll(pre, head_dim // 2, 1) * sine_ref[here, :]
            ).astype(low)
            rot_ref[here, lanes] = rot
            scores = dot(rot, key_ref[reach, :], 1, 1) * head_dim ** (-0.5)
            key_place = lax.broadcasted_iota(jnp.int32, scores.shape, 1) + first
            query_place = lax.broadcasted_iota(jnp.int32, scores.shape, 0) + (first + tokens)
            allowed = (key_place <= query_place) & (
                key_place.astype(full) >= start_ref[here, :]
            )
            scores = jnp.where(allowed, scores, -1e30)
            most = jnp.max(scores, axis=1, keepdims=True)
            exponent = jnp.exp(scores - most)
            total = jnp.sum(exponent, axis=1, keepdims=True)
            weights = exponent / total
            attended_ref[here, lanes] = dot(weights.astype(low), value_ref[reach, :]).astype(low)
            lane = lax.broadcasted_iota(jnp.int32, (tile, head_dim), 1)
            logsum_ref[here, :] = jnp.where(
                lane == head, most + jnp.log(total), logsum_ref[here, :]
            )
            return carry

        lax.fori_loop(0, heads, head_step, 0)

    logsum_ref[...] = jnp.zeros_like(logsum_ref)
    attend(other)
    output.ready()

    def branch_copy(part):
        return remote_copy(
            branch_stage.at[part],
            branch_arrived.at[part],
            branch_sem.at[part, 0],
            branch_sem.at[part, 1],
            row=other,
        )

    theirs = attended_ref[token_rows(other), :]
    for part in range(2):
        lanes = slice(part * part_width, (part + 1) * part_width)
        branch_stage[part] = dot(theirs, head_output_ref[:, lanes]).astype(low)
        branch_copy(part).start()
    cot_pass(2)
    expert_after_row(2)
    expert_after_side(0)
    attend(row)
    mine = attended_ref[token_rows(row), :]
    branch_own[...] = dot(mine, head_output_ref[...])
    for n in (1, 2, 3, 4, 6):
        stores[n].start()
    expert_after_row(3)
    expert_after_side(1)
    for part in range(2):
        lanes = slice(part * part_width, (part + 1) * part_width)
        branch_copy(part).wait_recv()
        middle_ref[:, lanes] = (
            inputs_all[token_rows(row), lanes].astype(full)
            + branch_own[:, lanes]
            + branch_arrived[part].astype(full)
        )

    stores[7].start()
    expert_after_side(2)

    def second_piece(at, carry):
        here = pl.ds(pl.multiple_of(at * piece, piece), piece)
        values = middle_ref[here, :]
        scale = lax.rsqrt(jnp.mean(values * values, axis=1, keepdims=True) + epsilon)
        expert_ref[here, :] = (values * scale * gains_ref[1:2, :]).astype(low)
        return carry

    lax.fori_loop(0, rows // piece, second_piece, 0)
    stores[8].start()
    cot_pass(3)
    expert_after_side(3)

    inputs_copy.wait_send()
    small_copy.wait_send()
    joint.end()
    output.end()
    for copy in stores:
        copy.wait()
    for which in range(4):
        expert_row_copy(which).wait_send()
        expert_side_copy(which).wait_send()
        for copy in expert_core_copies(which):
            copy.wait()
    cot_row.wait_send()
    for at in range(cols):
        pl.when((at <= col) & (col < last))(lambda: cot_copy(at, True).wait_send())
        pl.when((at >= col) & (col > 0))(lambda: cot_copy(at, False).wait_send())

    @pl.when(col % 2 == 0)
    def _():
        for copy in pair_copies():
            copy.wait_send()

    for part in range(2):
        branch_copy(part).wait_send()


def prologue_call(
    inputs, norm_gain, mixer_gain, lengths, theta, routes, route_gates, cotangent, query_weight, key_value_matrix,
    output_weight, gate_flat, up_flat, experts,
):
    tokens, part_width = inputs.shape
    cols = lax.axis_size("col")
    width, rows = 2 * part_width, tokens // 2
    query_block, keyval_block = query_weight.shape[1], key_value_matrix.shape[1]
    block = query_block + keyval_block
    hidden = gate_flat.shape[0]
    vmem = pl.BlockSpec(memory_space=pltpu.VMEM)
    anywhere = pl.BlockSpec(memory_space=pl.ANY)
    dma = pltpu.SemaphoreType.DMA
    shape = jax.ShapeDtypeStruct
    return pl.pallas_call(
        prologue_kernel,
        in_specs=[vmem] * 8 + [anywhere] * 5,
        out_specs=[anywhere]
        + [vmem] * 2
        + [anywhere] * 2
        + [vmem] * 4
        + [anywhere] * 6
        + [vmem] * 2
        + [anywhere] * 2,
        out_shape=[
            shape((tokens, width), low),
            shape((tokens, 1), full),
            shape((2, width), full),
            shape((2 * tokens, head_dim), low),
            shape((2 * tokens, head_dim), low),
            shape((tokens, head_dim), full),
            shape((tokens, head_dim), full),
            shape((tokens, 1), full),
            shape((tokens, head_dim), full),
            shape((tokens, 2 * query_block), low),
            shape((tokens, 2 * query_block), low),
            shape((width, 2 * block), low),
            shape((2 * query_block, width), low),
            shape((rows, width), full),
            shape((rows, width), low),
            shape((cols, rows, experts), full),
            shape((cols, rows, width), low),
            shape((hidden, part_width), low),
            shape((hidden, part_width), low),
        ],
        scratch_shapes=[
            pltpu.VMEM((tokens, width), low),
            pltpu.VMEM((2 * tokens, head_dim), low),
            pltpu.VMEM((2 * tokens, head_dim), low),
            pltpu.VMEM((tokens, 2 * query_block), low),
            pltpu.VMEM((tokens, 2 * query_block), low),
            pltpu.VMEM((width, 2 * block), low),
            pltpu.VMEM((2 * query_block, width), low),
            pltpu.VMEM((rows, width), full),
            pltpu.VMEM((rows, width), low),
            dma((9,)),
            pltpu.VMEM((tokens, width), low),
            dma((2,)),
            pltpu.VMEM((2, 8, part_width), full),
            dma((2,)),
            pltpu.VMEM((tokens, 2 * query_block), full),
            pltpu.VMEM((rows, width), full),
            pltpu.VMEM((2, rows, part_width), low),
            pltpu.VMEM((2, rows, part_width), low),
            dma((2, 2)),
            dma((2, 2)),
            pltpu.VMEM((cols, part_width // 4, block), low),
            dma((2,)),
            dma((cols, 3)),
            dma((2, 2)),
            dma((4, 2)),
            dma((4, 4)),
            pltpu.VMEM((cols, query_block // 4, part_width), low),
            dma((1,)),
            dma((cols, 3)),
            dma((2, 2)),
            dma((4, 2)),
            dma((4, 4)),
            dma((4, 2)),
            dma((4, 2)),
            dma((4, 4)),
            dma((2,)),
            dma((cols,)),
            dma((cols, 2)),
        ],
        compiler_params=pltpu.CompilerParams(
            collective_id=3, has_side_effects=True, vmem_limit_bytes=60 * 2**20
        ),
        cost_estimate=pl.CostEstimate(
            flops=5 * 10**9, bytes_accessed=30 * 10**6, transcendentals=3 * 10**6
        ),
    )(
        inputs, norm_gain, mixer_gain, lengths, theta, routes, route_gates, cotangent, query_weight, key_value_matrix,
        output_weight, gate_flat, up_flat,
    )


def finish_kernel(
    middle_ref,
    gains_ref,
    scale_ref,
    start_ref,
    logsum_ref,
    sum_hbm,
    inputs_hbm,
    attended_hbm,
    rot_hbm,
    key_hbm,
    value_hbm,
    cosine_hbm,
    sine_hbm,
    head_output_hbm,
    joint_hbm,
    normed_hbm,
    cot_all_hbm,
    out_part_hbm,
    up_own_hbm,
    up_row_hbm,
    up_other_hbm,
    down_half_hbm,
    out_first_hbm,
    outputs_ref,
    input_grad_ref,
    gain_sums_ref,
    output_total_ref,
    query_total_ref,
    keyval_total_ref,
    up_total_ref,
    down_total_ref,
    further,
    work,
    cot_ref,
    inputs_ref,
    attended_ref,
    rot_ref,
    key_ref,
    value_ref,
    cosine_ref,
    sine_ref,
    head_output_ref,
    joint_ref,
    normed_ref,
    loads,
    branch,
    branch_sem,
    out_stack,
    out_arrived,
    out_send,
    out_recv,
    own_out_sem,
    grad_heads,
    joint_grad,
    key_grad,
    value_grad,
    pair_stage,
    pair_arrived,
    pair_sem,
    normed_arrived,
    normed_sem,
    inner_stage,
    inner_arrived,
    inner_sem,
    sums,
    sums_arrived,
    sums_sem,
    item_mine,
    item_other,
    item_side,
    item_row,
    item_last,
    item_sem,
    item_load_sem,
    wo_parts,
    wo_core,
    wo_row,
    wo_stack,
    wo_arrived,
    wo_side,
    wo_sem,
    wo_send,
    wo_recv,
    wq_parts,
    wq_core,
    wq_row,
    wq_stack,
    wq_arrived,
    wq_side,
    wq_sem,
    wq_side_sem,
    wq_send,
    wq_recv,
    wk_parts,
    wk_core,
    wk_row,
    wk_stack,
    wk_arrived,
    wk_side,
    wk_sem,
    wk_send,
    wk_recv,
):
    row, col, dp = lax.axis_index("row"), lax.axis_index("col"), lax.axis_index("dp")
    cols, dps = lax.axis_size("col"), lax.axis_size("dp")
    core, side, other = dp % 2, (dp // 2) % 2, 1 - row
    core_partner = dp + 1 - 2 * core
    bits = list(range(1, dps.bit_length() - 1))
    sides = len(bits)

    def across(bit):
        on = (dp // (1 << bit)) % 2
        return dp + (1 << bit) * (1 - 2 * on)

    rows, width = middle_ref.shape
    tokens, part_width = inputs_ref.shape
    heads = attended_ref.shape[1] // head_dim
    per_block = heads // 2
    query_lanes, key_lanes = query_total_ref.shape[1], keyval_total_ref.shape[1]
    block_lanes = query_lanes + key_lanes

    def part_lanes(which):
        return pl.ds(pl.multiple_of(which * part_width, 128), part_width)

    size = item_mine.shape[1]
    items = item_mine.shape[0]
    load_pairs = [
        (sum_hbm, work),
        (cot_all_hbm.at[col], cot_ref),
        (out_part_hbm, out_stack),
        (head_output_hbm, head_output_ref),
        (attended_hbm, attended_ref),
        (rot_hbm, rot_ref),
        (key_hbm, key_ref),
        (value_hbm, value_ref),
        (cosine_hbm, cosine_ref),
        (sine_hbm, sine_ref),
        (joint_hbm, joint_ref),
        (normed_hbm, normed_ref),
        (inputs_hbm, inputs_ref),
    ]
    load = [
        pltpu.make_async_copy(source, target, loads.at[n])
        for n, (source, target) in enumerate(load_pairs)
    ]

    def item_loads(at):
        chunk = at % 2
        place = pl.ds(chunk * size, size)
        if at < 2:
            sources = (up_own_hbm.at[place], (up_row_hbm, up_other_hbm)[chunk])
        else:
            sources = [down_half_hbm.at[place, part_lanes(which)] for which in (row, other)]
        return [
            pltpu.make_async_copy(source, target.at[at], item_load_sem.at[at, number])
            for number, (source, target) in enumerate(zip(sources, (item_mine, item_other)))
        ]

    inner_col = (col > 0) & (col < cols - 1)
    first_load = pltpu.make_async_copy(
        out_first_hbm, out_arrived.at[(cols - 1) * (2 - col) % cols], loads.at[13]
    )
    for copy in load[:3]:
        copy.start()
    pl.when(inner_col)(lambda: first_load.start())
    for copy in item_loads(1) + load[3:]:
        copy.start()
    for at in (0, 2, 3):
        for copy in item_loads(at):
            copy.start()

    barrier = pltpu.get_barrier_semaphore()

    def greet(**device):
        pl.semaphore_signal(
            barrier, inc=1, device_id=device, device_id_type=pl.DeviceIdType.MESH
        )

    plane = [
        dict(row=(row + there // cols) % 2, col=(col + there % cols) % cols)
        for there in range(1, 2 * cols)
    ]
    copies = [dict(dp=(dp + apart) % dps) for apart in range(1, dps)]
    for device in plane + copies:
        greet(**device)

    for copy in load[:2]:
        copy.wait()
    piece = 64
    halves = [slice(h * part_width, (h + 1) * part_width) for h in range(2)]

    def norm_piece(at, mixer_sum):
        place = pl.ds(pl.multiple_of(at * piece, piece), piece)
        middle = middle_ref[place, :]
        second = jnp.concatenate([work[h, place, :] for h in range(2)], axis=1)
        scale = lax.rsqrt(jnp.mean(middle * middle, axis=1, keepdims=True) + epsilon)
        weighted = gains_ref[1:2, :] * second
        inner = jnp.sum(weighted * middle, axis=1, keepdims=True)
        grad = (
            cot_ref[place, :].astype(full)
            + scale * weighted
            - middle * (scale * scale * scale) * (inner / width)
        )
        branch[row, place, :] = grad.astype(low)
        return mixer_sum + jnp.sum(second * middle * scale, axis=0, keepdims=True)

    def branch_part(part):
        place = pl.ds(part * (rows // 2), rows // 2)
        return remote_copy(
            branch.at[row, place],
            branch.at[row, place],
            branch_sem.at[2 * part],
            branch_sem.at[2 * part + 1],
            row=other,
        )

    steps = rows // piece
    mixer_sum = lax.fori_loop(0, steps // 2, norm_piece, jnp.zeros((1, width), full))
    pl.semaphore_wait(barrier, len(plane) + len(copies))
    branch_part(0).start()
    mixer_sum = lax.fori_loop(steps // 2, steps, norm_piece, mixer_sum)
    branch_part(1).start()
    quarter_lanes = sums.shape[2]
    parts = width // quarter_lanes
    for n in range(parts):
        sums[0, parts + n : parts + n + 1, :] = mixer_sum[
            :, n * quarter_lanes : (n + 1) * quarter_lanes
        ]

    outs = ColSum(out_stack, out_arrived, out_send, out_recv, col, cols, range(cols))
    load[2].wait()
    pl.when(inner_col)(lambda: first_load.wait())
    outs.step(2, placed=True)


    half_size = size // 2

    def side_rows(which):
        return pl.ds(pl.multiple_of(which * half_size, 16), half_size)

    def item_first_copies(at):
        if at == 0:
            pairs = [(item_mine.at[at], item_side.at[at])]
        else:
            there = side_rows(1 - side)
            pairs = [
                (item_mine.at[at, there], item_side.at[at, side_rows(0)]),
                (item_other.at[at, there], item_side.at[at, side_rows(1)]),
            ]
        return [
            remote_copy(
                source, target, item_sem.at[at, 2 * n], item_sem.at[at, 2 * n + 1], dp=across(1)
            )
            for n, (source, target) in enumerate(pairs)
        ]

    def item_start(at):
        for copy in item_loads(at):
            copy.wait()
        if at == 0:
            item_mine[0] = add_low(item_mine[0], item_other[0])
        for copy in item_first_copies(at):
            copy.start()

    def item_row_copy(at):
        return remote_copy(
            item_other.at[at, side_rows(side)],
            item_row.at[at],
            item_sem.at[at, 4],
            item_sem.at[at, 5],
            row=other,
        )

    def item_to_row(at):
        for copy in item_first_copies(at):
            copy.wait_recv()
        here = side_rows(side)
        item_other[at, here] = add_low(item_other[at, here], item_side[at, side_rows(1)])
        item_row_copy(at).start()
        item_mine[at, here] = add_low(item_mine[at, here], item_side[at, side_rows(0)])

    def item_extent(at):
        return pl.ds(0, size) if at == 0 else side_rows(side)

    def item_further_copy(at, number):
        extent = pl.ds(0, size if at == 0 else half_size)
        return remote_copy(
            item_mine.at[at, item_extent(at)],
            further.at[at, number - 1, extent],
            item_sem.at[at, 4 + 2 * number],
            item_sem.at[at, 5 + 2 * number],
            dp=across(bits[number]),
        )

    def item_further(at):
        extent = pl.ds(0, size if at == 0 else half_size)
        for number in range(1, sides):
            copy = item_further_copy(at, number)
            copy.start()
            copy.wait()
            landed = pltpu.make_async_copy(
                further.at[at, number - 1, extent],
                item_side.at[at, extent],
                item_load_sem.at[at, 0],
            )
            landed.start()
            landed.wait()
            here = item_extent(at)
            item_mine[at, here] = add_low(item_mine[at, here], item_side[at, extent])

    def item_last_copy(at):
        return remote_copy(
            item_mine.at[at, side_rows(side)],
            item_last.at[at],
            item_sem.at[at, 4 + 2 * sides],
            item_sem.at[at, 5 + 2 * sides],
            dp=across(1),
        )

    def item_after_row(at):
        item_row_copy(at).wait_recv()
        here = side_rows(side)
        for copy in item_first_copies(at):
            copy.wait_send()
        item_mine[at, here] = add_low(item_mine[at, here], item_row[at])
        item_further(at)
        item_last_copy(at).start()

    def item_core_copies(at):
        which, chunk = at // 2, at % 2
        total = (up_total_ref, down_total_ref)[which]
        first = core * part_width + chunk * size
        if at == 0:
            pieces = [(item_mine.at[0], pl.ds(pl.multiple_of(first, 16), size))]
        else:
            pieces = [
                (source, pl.ds(pl.multiple_of(first + of_side * half_size, 16), half_size))
                for source, of_side in (
                    (item_mine.at[at, side_rows(side)], side),
                    (item_last.at[at], 1 - side),
                )
            ]
        result = []
        for n, (source, place) in enumerate(pieces):
            base = 6 + 2 * sides + 3 * n
            result.append(
                remote_copy(
                    source,
                    total.at[place],
                    item_sem.at[at, base],
                    item_sem.at[at, base + 1],
                    dp=core_partner,
                )
            )
            result.append(
                pltpu.make_async_copy(source, total.at[place], item_sem.at[at, base + 2])
            )
        return result

    def item_finish(at):
        if at == 0:
            for copy in item_first_copies(at):
                copy.wait()
            item_mine[at] = add_low(item_mine[at], item_side[at])
            item_further(at)
        else:
            item_last_copy(at).wait_recv()
        for copy in item_core_copies(at):
            copy.start()

    def item_end(at):
        if at > 0:
            item_row_copy(at).wait_send()
            item_last_copy(at).wait_send()
        for copy in item_core_copies(at):
            copy.wait()

    item_start(1)
    for copy in load[3:]:
        copy.wait()

    for part in range(2):
        branch_part(part).wait_recv()
    item_to_row(1)
    item_start(0)
    outs.step(3)
    branch_all = branch[...].reshape(tokens, width)
    half_lanes = heads * head_dim // 2
    for part in range(2):
        lanes = slice(part * half_lanes, (part + 1) * half_lanes)
        grad_heads[:, lanes] = dot(branch_all, head_output_ref[lanes, :], 1, 1).astype(low)

    wo_size = wo_parts.shape[2]
    for b in range(2):
        lanes = slice(b * half_lanes, (b + 1) * half_lanes)
        value = dot(attended_ref[:, lanes], branch_all, 0, 0).astype(low)
        for part in range(2):
            wo_parts[b, part] = value[part * wo_size : (part + 1) * wo_size, :]

    def wo_core_copy(b):
        return remote_copy(
            wo_parts.at[b, 1 - core],
            wo_core.at[b],
            wo_sem.at[0, b],
            wo_sem.at[1, b],
            dp=core_partner,
        )

    for b in range(2):
        wo_core_copy(b).start()

    key_grad[...] = jnp.zeros_like(key_grad)
    value_grad[...] = jnp.zeros_like(value_grad)
    tile = tokens // 2
    window = key_ref.shape[0] - tile

    def head_step(head, carry):
        here = pl.ds(pl.multiple_of(head * head_dim, head_dim), head_dim)
        there = pl.ds(
            pl.multiple_of((head + head // per_block) * head_dim, head_dim), head_dim
        )
        for at in range(tokens // tile):
            first = at * tile
            rot = rot_ref[first : first + tile, here]
            grad = grad_heads[first : first + tile, here]
            keys = key_ref[first : first + window, :]
            values = value_ref[first : first + window, :]
            scores = dot(rot, keys, 1, 1) * head_dim ** (-0.5)
            place = lax.broadcasted_iota(jnp.int32, scores.shape, 1) + first
            query = lax.broadcasted_iota(jnp.int32, scores.shape, 0) + (first + tokens)
            allowed = (place <= query) & (place.astype(full) >= start_ref[first : first + tile, :])
            scores = jnp.where(allowed, scores, -1e30)
            lane = lax.broadcasted_iota(jnp.int32, (tile, head_dim), 1)
            logsum = jnp.sum(
                jnp.where(lane == head, logsum_ref[first : first + tile, :], 0.0),
                axis=1,
                keepdims=True,
            )
            probs = jnp.exp(scores - logsum)
            prob_grad = dot(grad, values, 1, 1)
            inner = jnp.sum(probs * prob_grad, axis=1, keepdims=True)
            score_grad = (probs * (prob_grad - inner) * head_dim ** (-0.5)).astype(low)
            rot_grad = dot(score_grad, keys)
            joint_grad[first : first + tile, there] = (
                rot_grad * cosine_ref[first : first + tile, :]
                - pltpu.roll(rot_grad, head_dim // 2, 1) * sine_ref[first : first + tile, :]
            ).astype(low)
            key_grad[first : first + window, :] += dot(score_grad, rot, 0, 0)
            value_grad[first : first + window, :] += dot(probs.astype(low), grad, 0, 0)
        return carry

    wa_size = part_width // 2
    chunk_rows = wa_size // 2

    class Lanes:
        def __init__(self, parts, core_room, row_room, sems, stretches, chunks):
            self.parts, self.core_room, self.row_room, self.sems = parts, core_room, row_room, sems
            self.stretches, self.chunks = stretches, chunks

        def core_copy(self, r0):
            return remote_copy(
                self.parts.at[r0, 1 - core],
                self.core_room.at[r0],
                self.sems.at[0, r0],
                self.sems.at[1, r0],
                dp=core_partner,
            )

        def dot(self, r0, which):
            first = pl.multiple_of(r0 * part_width + which * wa_size, 128)
            left = normed_ref[:, pl.ds(first, wa_size)]
            right = [joint_grad[:, lanes] for lanes in self.stretches]
            right = right[0] if len(right) == 1 else jnp.concatenate(right, axis=1)
            self.parts[r0, which] = dot(left, right, 0, 0).astype(low)

        def first(self):
            for r0 in (other, row):
                self.dot(r0, 1 - core)
                self.core_copy(r0).start()
            for r0 in (other, row):
                self.dot(r0, core)

        def row_copy(self, chunk):
            count = wa_size // self.chunks
            return remote_copy(
                self.parts.at[other, core, pl.ds(chunk * count, count)],
                self.row_room.at[chunk],
                self.sems.at[2, chunk],
                self.sems.at[3, chunk],
                row=other,
            )

        def to_row(self):
            self.core_copy(other).wait_recv()
            self.parts[other, core] = add_low(self.parts[other, core], self.core_room[other])
            for chunk in range(self.chunks):
                self.row_copy(chunk).start()
            self.core_copy(row).wait_recv()
            self.parts[row, core] = add_low(self.parts[row, core], self.core_room[row])

        def end(self):
            for r0 in range(2):
                self.core_copy(r0).wait_send()
            for chunk in range(self.chunks):
                self.row_copy(chunk).wait_send()

    stretches = [
        slice(b * block_lanes, b * block_lanes + query_lanes) for b in range(2)
    ]
    key_stretch = slice(query_lanes, block_lanes)
    value_stretch = slice(block_lanes + query_lanes, 2 * block_lanes)
    wq = [
        Lanes(
            wq_parts.at[b], wq_core.at[b], wq_row.at[b], wq_sem.at[b], [stretches[b]], 2
        )
        for b in range(2)
    ]
    wk = Lanes(wk_parts, wk_core, wk_row, wk_sem, [key_stretch, value_stretch], 1)

    def wo_row_copy(b):
        return remote_copy(
            wo_parts.at[b, core, :, part_lanes(other)],
            wo_row.at[b],
            wo_sem.at[2, b],
            wo_sem.at[3, b],
            row=other,
        )

    lax.fori_loop(0, 1, head_step, 0)
    for b in range(2):
        wo_core_copy(b).wait_recv()
        wo_parts[b, core] = add_low(wo_parts[b, core], wo_core[b])
        wo_row_copy(b).start()
    lax.fori_loop(1, per_block, head_step, 0)
    item_start(2)
    wq[0].first()
    lax.fori_loop(per_block, per_block + 1, head_step, 0)
    wq[0].to_row()
    lax.fori_loop(per_block + 1, heads, head_step, 0)
    pair_stage[:, :head_dim] = key_grad[:tokens, :].astype(low)
    pair_stage[:, head_dim:] = value_grad[:tokens, :].astype(low)
    odd = col % 2 == 1

    def pair_copy():
        return remote_copy(
            pair_stage, pair_arrived, pair_sem.at[0], pair_sem.at[1], col=col + 1 - 2 * (col % 2)
        )

    pl.when(odd)(lambda: pair_copy().start())
    wq[1].first()
    item_start(3)

    def over_col(lanes, stacks, arrived, send, recv, chunk, blocks):
        return ColSum(
            stacks.at[chunk], arrived.at[chunk], send.at[chunk], recv.at[chunk], col, cols, blocks
        )

    wq_total = [
        [
            over_col(
                wq[b], wq_stack.at[b], wq_arrived.at[b], wq_send.at[b], wq_recv.at[b], c, (b, 2 + b)
            )
            for c in range(2)
        ]
        for b in range(2)
    ]

    def wq_to_col(b):
        for chunk in range(2):
            wq[b].row_copy(chunk).wait_recv()
            place = pl.ds(chunk * chunk_rows, chunk_rows)
            wq_stack[b, chunk, row] = wq_parts[b, row, core, place]
            wq_stack[b, chunk, other] = wq_row[b, chunk]
            wq_total[b][chunk].step(1)

    def wq_step(b, number):
        for chunk in range(2):
            wq_total[b][chunk].step(number)

    wq[1].to_row()
    item_finish(0)
    wo_total = ColSum(wo_stack, wo_arrived, wo_send, wo_recv, col, cols, range(cols))
    for b in range(2):
        wo_row_copy(b).wait_recv()
        wo_stack[2 * row + b] = wo_parts[b, core, :, part_lanes(row)]
        wo_stack[2 * other + b] = wo_row[b]
    wo_total.step(1)
    wq_to_col(0)

    @pl.when(jnp.logical_not(odd))
    def _():
        pair_copy().wait_recv()
        key_grad[tokens:, :] += pair_arrived[:, :head_dim].astype(full)
        value_grad[tokens:, :] += pair_arrived[:, head_dim:].astype(full)

    key_total = key_grad[tokens:, :]
    joint_grad[:, key_stretch] = (
        key_total * cosine_ref[...] - pltpu.roll(key_total, head_dim // 2, 1) * sine_ref[...]
    ).astype(low)
    joint_grad[:, value_stretch] = value_grad[tokens:, :].astype(low)
    wk.first()

    normed_own = work

    def normed_dot(which):
        return dot(joint_grad[...], joint_ref[part_lanes(which), :], 1, 1)

    def normed_sums(which, value):
        product = value * normed_ref[:, part_lanes(which)].astype(full)
        gain = gains_ref[0:1, part_lanes(which)]
        total = jnp.sum(product, axis=0, keepdims=True) / gain
        for n in range(parts // 2):
            sums[0, pl.ds(which * (parts // 2) + n, 1), :] = total[
                :, n * quarter_lanes : (n + 1) * quarter_lanes
            ]
        return jnp.sum(product, axis=1, keepdims=True)

    wk.to_row()
    item_to_row(2)
    value = normed_dot(other)
    grad_heads[...] = value.astype(low)
    normed_copy = remote_copy(
        grad_heads, normed_arrived, normed_sem.at[0], normed_sem.at[1], row=other
    )
    inner = normed_sums(other, value)
    value = normed_dot(row)
    inner += normed_sums(row, value)
    for h in range(2):
        normed_own[h] = value[h * rows : (h + 1) * rows]
    inner_stage[...] = jnp.transpose(jnp.broadcast_to(inner, (tokens, head_dim)))[:8, :]
    inner_copy = remote_copy(
        inner_stage, inner_arrived, inner_sem.at[0], inner_sem.at[1], row=other
    )
    inner_copy.start()

    def sums_copies(stage):
        base = 0 if stage == 0 else len(plane)
        return [
            remote_copy(
                sums.at[stage],
                sums_arrived.at[base + n],
                sums_sem.at[base + n, 0],
                sums_sem.at[base + n, 1],
                **device,
            )
            for n, device in enumerate((plane, copies)[stage])
        ]

    def sums_start(stage):
        for copy in sums_copies(stage):
            copy.start()

    def sums_finish(stage):
        base = 0 if stage == 0 else len(plane)
        total = sums[stage]
        for n, copy in enumerate(sums_copies(stage)):
            copy.wait_recv()
            total += sums_arrived[base + n]
        sums[stage + 1] = total

    sums_start(0)
    wq_to_col(1)
    wq_step(0, 2)
    wk_total = ColSum(wk_stack, wk_arrived, wk_send, wk_recv, col, cols, range(cols))
    wk.row_copy(0).wait_recv()
    for b in range(2):
        lanes = slice(b * key_lanes, (b + 1) * key_lanes)
        wk_stack[2 * row + b] = wk_parts[row, core, :, lanes]
        wk_stack[2 * other + b] = wk_row[0, :, lanes]
    wk_total.step(1)
    item_to_row(3)
    wq_step(1, 2)
    wq_step(0, 3)
    wk_total.step(2)
    wo_total.step(2)
    normed_copy.start()
    sums_finish(0)
    sums_start(1)
    wq_step(1, 3)
    wk_total.step(3)
    item_after_row(1)
    wo_total.step(3)
    item_after_row(2)

    class Owned:
        def __init__(self, side_room, sems, targets):
            self.room, self.sems, self.targets = side_room, sems, targets

        def copy(self, number):
            return remote_copy(
                self.room.at[number % 2],
                self.room.at[2 + number],
                self.sems.at[2 * number],
                self.sems.at[2 * number + 1],
                dp=across(bits[number]),
            )

        def start(self, value):
            self.room[0] = value.astype(low)
            if sides:
                self.copy(0).start()

        def core_copies(self):
            result = []
            base, value = 2 * sides, self.room.at[sides % 2]
            return (
                remote_copy(
                    value,
                    self.targets,
                    self.sems.at[base],
                    self.sems.at[base + 1],
                    dp=core_partner,
                ),
                pltpu.make_async_copy(value, self.targets, self.sems.at[base + 2]),
            )

        def finish(self):
            for number in range(sides):
                self.copy(number).wait()
                self.room[1 - number % 2] = add_low(
                    self.room[number % 2], self.room[2 + number]
                )
                if number + 1 < sides:
                    self.copy(number + 1).start()
            for copy in self.core_copies():
                copy.start()

        def end(self):
            for copy in self.core_copies():
                copy.wait()

    def own_place(chunk, count):
        return pl.ds(pl.multiple_of(core * wa_size + chunk * count, 16), count)

    wk_owned = Owned(wk_side, wk_sem.at[4], keyval_total_ref.at[own_place(0, wa_size)])
    wq_owned = [
        Owned(wq_side.at[c], wq_side_sem.at[c], query_total_ref.at[own_place(c, chunk_rows)])
        for c in range(2)
    ]
    wo_owned = Owned(
        wo_side,
        wo_sem.at[4],
        output_total_ref.at[pl.ds(pl.multiple_of(core * wo_size, 16), wo_size)],
    )
    for b in range(2):
        for c in range(2):
            wq_total[b][c].total(wq_owned[c].start)
    wo_total.total(wo_owned.start)
    wk_total.total(wk_owned.start)

    def own_tokens(value):
        out_stack[col] = (middle_ref[...] + value).astype(low)

    outs.total(own_tokens)

    def outputs_copy():
        place = pl.ds(pl.multiple_of(row * rows, rows), rows)
        return remote_copy(
            out_stack.at[col, :, part_lanes(other)],
            outputs_ref.at[place],
            own_out_sem.at[0],
            own_out_sem.at[1],
            row=other,
        )

    outputs_copy().start()
    outputs_ref[pl.ds(pl.multiple_of(row * rows, rows), rows), :] = out_stack[
        col, :, part_lanes(row)
    ]
    item_after_row(3)
    item_finish(1)
    for c in range(2):
        wq_owned[c].finish()
    wk_owned.finish()
    wo_owned.finish()
    item_finish(2)
    sums_finish(1)
    for n in range(parts // 2):
        place = pl.ds(row * (parts // 2) + n, 1)
        lanes = slice(n * quarter_lanes, (n + 1) * quarter_lanes)
        gain_sums_ref[0:1, lanes] = sums[2, place, :]
        place = pl.ds(parts + row * (parts // 2) + n, 1)
        gain_sums_ref[1:2, lanes] = sums[2, place, :]
    item_finish(3)

    normed_copy.wait_recv()
    inner_copy.wait_recv()
    both = inner_stage[...] + inner_arrived[...]
    inner = jnp.transpose(jnp.concatenate([both] * (head_dim // 8), axis=0))[:, 0:1]
    for h in range(2):
        place = slice(h * rows, (h + 1) * rows)
        scale = scale_ref[place, :]
        normed_grad = normed_own[h] + normed_arrived[place, :].astype(full)
        input_grad_ref[place, :] = (
            branch[h, :, part_lanes(row)].astype(full)
            + scale * (gains_ref[0:1, part_lanes(row)] * normed_grad)
            - inputs_ref[place, :].astype(full) * (scale * scale) * (inner[place, :] / width)
        ).astype(low)

    for part in range(2):
        branch_part(part).wait_send()
    pl.when(odd)(lambda: pair_copy().wait_send())
    for b in range(2):
        wo_core_copy(b).wait_send()
        wo_row_copy(b).wait_send()
    for lanes in wq + [wk]:
        lanes.end()
    normed_copy.wait_send()
    inner_copy.wait_send()
    outputs_copy().wait()
    for stage in range(2):
        for copy in sums_copies(stage):
            copy.wait_send()
    outs.end(first=False)
    for total in [wo_total, wk_total] + wq_total[0] + wq_total[1]:
        total.end()
    for owned in wq_owned + [wk_owned, wo_owned]:
        owned.end()
    for at in range(items):
        item_end(at)


def finish_call(
    middle, gains, scale, start, logsum, sums, inputs, attended, rot, keys, values, cosine, sine,
    head_output, joint_weight, normed, cot_all, out_part, up_own, up_row, up_other, down_half, out_first,
    query_block, both_block,
):
    rows, width = middle.shape
    tokens, part_width = inputs.shape
    cols, dps = lax.axis_size("col"), lax.axis_size("dp")
    sides = dps.bit_length() - 2
    heads_width = attended.shape[1]
    reach = keys.shape[0]
    vmem = pl.BlockSpec(memory_space=pltpu.VMEM)
    anywhere = pl.BlockSpec(memory_space=pl.ANY)
    dma = pltpu.SemaphoreType.DMA
    hidden = 2 * up_own.shape[0]
    size = part_width // 2
    items = 4
    key_block = both_block - query_block
    wo_size, wa_size = query_block // 2, part_width // 2
    chunk = wa_size // 2
    shape = jax.ShapeDtypeStruct
    sums_count = 2 * cols - 1 + dps - 1
    return pl.pallas_call(
        finish_kernel,
        in_specs=[vmem] * 5 + [anywhere] * 18,
        out_specs=[vmem] * 6 + [anywhere] * 3,
        out_shape=[
            shape((tokens, part_width), low),
            shape((tokens, part_width), low),
            shape((2, part_width), full),
            shape((query_block, part_width), low),
            shape((part_width, query_block), low),
            shape((part_width, key_block), low),
            shape((hidden, part_width), low),
            shape((hidden, part_width), low),
            shape((items, max(sides - 1, 1), size, part_width), low),
        ],
        scratch_shapes=[
            pltpu.VMEM((2, rows, part_width), full),
            pltpu.VMEM((rows, width), low),
            pltpu.VMEM((tokens, part_width), low),
            pltpu.VMEM((tokens, heads_width), low),
            pltpu.VMEM((tokens, heads_width), low),
            pltpu.VMEM((reach, head_dim), low),
            pltpu.VMEM((reach, head_dim), low),
            pltpu.VMEM((tokens, head_dim), full),
            pltpu.VMEM((tokens, head_dim), full),
            pltpu.VMEM((heads_width, width), low),
            pltpu.VMEM((width, 2 * both_block), low),
            pltpu.VMEM((tokens, width), low),
            dma((14,)),
            pltpu.VMEM((2, rows, width), low),
            dma((4,)),
            pltpu.VMEM((cols, rows, width), low),
            pltpu.VMEM((cols + 1, rows, width), low),
            dma((cols,)),
            dma((cols + 1,)),
            dma((2,)),
            pltpu.VMEM((tokens, heads_width), low),
            pltpu.VMEM((tokens, 2 * both_block), low),
            pltpu.VMEM((reach, head_dim), full),
            pltpu.VMEM((reach, head_dim), full),
            pltpu.VMEM((tokens, 2 * head_dim), low),
            pltpu.VMEM((tokens, 2 * head_dim), low),
            dma((2,)),
            pltpu.VMEM((tokens, part_width), low),
            dma((2,)),
            pltpu.VMEM((8, tokens), full),
            pltpu.VMEM((8, tokens), full),
            dma((2,)),
            pltpu.VMEM((3, 8, width // 4), full),
            pltpu.VMEM((sums_count, 8, width // 4), full),
            dma((sums_count, 2)),
            pltpu.VMEM((items, size, part_width), low),
            pltpu.VMEM((items, size, part_width), low),
            pltpu.VMEM((items, size, part_width), low),
            pltpu.VMEM((items, size // 2, part_width), low),
            pltpu.VMEM((items, size // 2, part_width), low),
            dma((items, 12 + 2 * sides)),
            dma((items, 2)),
            pltpu.VMEM((2, 2, wo_size, width), low),
            pltpu.VMEM((2, wo_size, width), low),
            pltpu.VMEM((2, wo_size, part_width), low),
            pltpu.VMEM((cols, wo_size, part_width), low),
            pltpu.VMEM((cols + 1, wo_size, part_width), low),
            pltpu.VMEM((2 + sides, wo_size, part_width), low),
            dma((5, 3 + 2 * sides)),
            dma((cols,)),
            dma((cols + 1,)),
            pltpu.VMEM((2, 2, 2, wa_size, query_block), low),
            pltpu.VMEM((2, 2, wa_size, query_block), low),
            pltpu.VMEM((2, 2, chunk, query_block), low),
            pltpu.VMEM((2, 2, 2, chunk, query_block), low),
            pltpu.VMEM((2, 2, 3, chunk, query_block), low),
            pltpu.VMEM((2, 2 + sides, chunk, query_block), low),
            dma((2, 4, 2)),
            dma((2, 3 + 2 * sides)),
            dma((2, 2, 2)),
            dma((2, 2, 3)),
            pltpu.VMEM((2, 2, wa_size, 2 * key_block), low),
            pltpu.VMEM((2, wa_size, 2 * key_block), low),
            pltpu.VMEM((1, wa_size, 2 * key_block), low),
            pltpu.VMEM((cols, wa_size, key_block), low),
            pltpu.VMEM((cols + 1, wa_size, key_block), low),
            pltpu.VMEM((2 + sides, wa_size, key_block), low),
            dma((5, 3 + 2 * sides)),
            dma((cols,)),
            dma((cols + 1,)),
        ],
        compiler_params=pltpu.CompilerParams(
            collective_id=2, has_side_effects=True, vmem_limit_bytes=63 * 2**20
        ),
        cost_estimate=pl.CostEstimate(
            flops=10 * 10**9, bytes_accessed=40 * 10**6, transcendentals=4 * 10**6
        ),
    )(
        middle, gains, scale, start, logsum, sums, inputs, attended, rot, keys, values, cosine, sine,
        head_output, joint_weight, normed, cot_all, out_part, up_own, up_row, up_other, down_half, out_first,
    )


def results_kernel(*refs):
    count = len(refs) // 2
    for source, target in zip(refs[:count], refs[count:]):
        target[...] = source[...].astype(target.dtype)


def results_call(arrays, kinds, steps):
    specs = [
        pl.BlockSpec((array.shape[0] // steps, array.shape[1]), lambda i: (i, 0))
        for array in arrays
    ]
    return pl.pallas_call(
        results_kernel,
        grid=(steps,),
        in_specs=specs,
        out_specs=specs,
        out_shape=[
            jax.ShapeDtypeStruct(array.shape, kind) for array, kind in zip(arrays, kinds)
        ],
        compiler_params=pltpu.CompilerParams(vmem_limit_bytes=60 * 2**20),
    )(*arrays)


def shards(
    inputs,
    norm_gain,
    query_weight,
    key_value_matrix,
    output_weight,
    mixer_gain,
    gate_weight,
    up_weight,
    down_weight,
    lengths,
    routes,
    route_gates,
    cotangent,
):
    row, col = lax.axis_index("row"), lax.axis_index("col")
    part_width = inputs.shape[1]
    experts, _, units = gate_weight.shape
    hidden_width = experts * units
    query_block, keyval_block = query_weight.shape[1], key_value_matrix.shape[1]
    theta = rope_base ** (-np.arange(0, head_dim, 2, dtype=np.float64) / head_dim)
    theta = np.concatenate([theta, theta])[None, :].astype(np.float32)
    gate_flat = gate_weight.swapaxes(1, 2).reshape(hidden_width, part_width)
    up_flat = up_weight.swapaxes(1, 2).reshape(hidden_width, part_width)
    down_flat = down_weight.reshape(hidden_width, part_width)
    (
        normed,
        first_scale,
        gains,
        keys,
        values,
        cosine,
        sine,
        start,
        logsum,
        attended,
        rot,
        joint_weight,
        head_output,
        middle,
        expert_own,
        tables,
        cot_all,
        gate_other,
        up_other_half,
    ) = prologue_call(
        inputs, norm_gain, mixer_gain, lengths, theta, routes.T, route_gates.T, cotangent, query_weight, key_value_matrix,
        output_weight, gate_flat, up_flat, experts,
    )
    (
        second_grad,
        out_part,
        gate_total,
        up_own,
        up_row,
        up_other,
        down_half,
        out_first,
    ) = experts_call(
        expert_own, cot_all, tables, gate_flat, gate_other, up_flat, up_other_half, down_flat
    )

    both_block = query_block + keyval_block
    (
        outputs,
        input_grad,
        gain_sums,
        output_total,
        query_total,
        keyval_total,
        up_total,
        down_total,
        _,
    ) = finish_call(
        middle, gains, first_scale, start, logsum, second_grad, inputs, attended, rot, keys, values,
        cosine, sine, head_output, joint_weight, normed, cot_all, out_part,
        up_own, up_row, up_other, down_half, out_first, query_block, both_block,
    )
    norm_total, mixer_total = gain_sums[0], gain_sums[1]

    arrays = [gate_total, up_total, down_total, query_total, keyval_total, output_total]
    (
        gate_total,
        up_total,
        down_total,
        query_total,
        keyval_total,
        output_total,
        outputs,
        input_grad,
    ) = results_call(arrays + [outputs, input_grad], [full] * 6 + [low] * 2, 4)

    def by_expert(flat):
        return flat.reshape(experts, units, part_width)

    gate_total = by_expert(gate_total).swapaxes(1, 2)
    up_total = by_expert(up_total).swapaxes(1, 2)
    down_total = by_expert(down_total)
    return (
        outputs,
        input_grad,
        norm_total,
        query_total,
        keyval_total,
        output_total,
        mixer_total,
        gate_total,
        up_total,
        down_total,
    )


def solution(mesh):
    return jax.shard_map(
        shards,
        mesh=mesh,
        in_specs=(
            P(("dp", "col"), "row"),
            P("row"),
            P("row", "col"),
            P("row", "col"),
            P("col", "row"),
            P("row"),
            P(None, "row", "col"),
            P(None, "row", "col"),
            P(None, "col", "row"),
            P(("dp", "row"), None),
            P("dp", None),
            P("dp", None),
            P(("dp", "col"), "row"),
        ),
        out_specs=(
            P(("dp", "col"), "row"),
            P(("dp", "col"), "row"),
            P("row"),
            P("row", "col"),
            P("row", "col"),
            P("col", "row"),
            P("row"),
            P(None, "row", "col"),
            P(None, "row", "col"),
            P(None, "col", "row"),
        ),
        check_vma=False,
    )
```

```python
import jax
import jax.numpy as jnp
import numpy as np
from jax import lax
from jax.experimental import pallas as pl
from jax.experimental.pallas import tpu as pltpu
from jax.sharding import PartitionSpec as P

epsilon = 1e-06
rope_base = 1000000.0
head_dim = 128
low = jnp.bfloat16
full = jnp.float32


def dot(left, right, left_dim=1, right_dim=0):
    return lax.dot_general(
        left, right, (((left_dim,), (right_dim,)), ((), ())), preferred_element_type=full
    )


def remote_copy(source, target, send_sem, recv_sem, **device):
    return pltpu.make_async_remote_copy(
        src_ref=source,
        dst_ref=target,
        send_sem=send_sem,
        recv_sem=recv_sem,
        device_id=device,
        device_id_type=pl.DeviceIdType.MESH,
    )


def add_low(left, right):
    return (left.astype(full) + right.astype(full)).astype(low)


class ColSum:
    def __init__(self, stack, arrived, send_sem, recv_sem, col, count, blocks):
        self.stack, self.arrived, self.send_sem, self.recv_sem = stack, arrived, send_sem, recv_sem
        self.col, self.last, self.blocks = col, count - 1, list(blocks)

    def copy(self, block, at, right):
        neighbour = at + 1 if right else at - 1
        n = self.blocks.index(block)
        slot = n if right or block != neighbour else len(self.blocks)
        return remote_copy(
            self.stack.at[n],
            self.arrived.at[slot],
            self.send_sem.at[n],
            self.recv_sem.at[slot],
            col=neighbour,
        )

    def wait(self, slot, at):
        remote_copy(
            self.arrived.at[slot],
            self.arrived.at[slot],
            self.send_sem.at[0],
            self.recv_sem.at[slot],
            col=at + 1 if at == 0 else at - 1,
        ).wait_recv()

    def step(self, number, placed=False):
        for at in range(self.last + 1):
            ways = []
            for right in (True, False):
                block = at + self.last + 1 - number if right else at - self.last - 1 + number
                if block in self.blocks:
                    ways.append((block, right))
            if not ways:
                continue

            @pl.when(self.col == at)
            def _(at=at, ways=ways):
                for block, right in ways:
                    n = self.blocks.index(block)
                    if 0 < at < self.last:
                        if not placed:
                            self.wait(n, at)
                        self.stack[n] = add_low(self.stack[n], self.arrived[n])
                    self.copy(block, at, right).start()

    def total(self, part):
        for n, at in enumerate(self.blocks):

            @pl.when(self.col == at)
            def _(n=n, at=at):
                value = self.stack[n].astype(full)
                if at > 0:
                    self.wait(n, at)
                    value += self.arrived[n].astype(full)
                if at < self.last:
                    self.wait(len(self.blocks), at)
                    value += self.arrived[len(self.blocks)].astype(full)
                part(value)

    def end(self, first=True):
        for at in range(self.last + 1):

            @pl.when(self.col == at)
            def _(at=at):
                for block in self.blocks:
                    if block != at and (first or abs(block - at) < self.last):
                        self.copy(block, at, block > at).wait_send()


def experts_kernel(
    table_ref,
    own_hbm,
    cot_hbm,
    gate_hbm,
    gate_other_hbm,
    up_hbm,
    up_other_hbm,
    down_hbm,
    sum_ref,
    out_part_hbm,
    gate_total_ref,
    up_own_ref,
    up_row_ref,
    up_other_ref,
    down_half_ref,
    out_first_ref,
    cot_ref,
    out_part_ref,
    token_sem,
    weights,
    expert_in,
    gate_grad,
    up_grad,
    hidden,
    send_stage,
    arrived,
    parts,
    stage,
    weights_sem,
    down_sem,
    ready,
    ag_recv,
    ag_right,
    ag_left,
    rs_recv,
    rs_send,
    core_send,
    core_recv,
    row_send,
    row_recv,
    side_send,
    side_recv,
    final_sem,
    local_sem,
    out_sem,
):
    row, col, dp = lax.axis_index("row"), lax.axis_index("col"), lax.axis_index("dp")
    dps = lax.axis_size("dp")
    core, other = dp % 2, 1 - row
    core_partner = dp + 1 - 2 * core
    side_bits = list(range(1, dps.bit_length() - 1))
    sides = len(side_bits)
    last = cot_ref.shape[0] - 1
    rows, width = own_hbm.shape
    half = width // 2
    size = half // 2
    inner = (col > 0) & (col < last)

    def across(bit):
        on = (dp // (1 << bit)) % 2
        return dp + (1 << bit) * (1 - 2 * on)

    def half_lanes(which):
        return pl.ds(pl.multiple_of(which * half, half), half)

    gate_ref, up_ref, down_ref = weights.at[0], weights.at[1], weights.at[2]
    sources = (gate_hbm, gate_other_hbm, up_hbm, up_other_hbm, down_hbm)
    loads = [
        pltpu.make_async_copy(
            source,
            weights.at[i // 2, :, half_lanes((row, other)[i % 2])],
            weights_sem.at[i],
        )
        for i, source in enumerate(sources)
    ]
    own_load = pltpu.make_async_copy(own_hbm, expert_in.at[col], token_sem.at[0])
    cot_load = pltpu.make_async_copy(cot_hbm, cot_ref, token_sem.at[1])
    out_store = pltpu.make_async_copy(out_part_ref, out_part_hbm, token_sem.at[2])
    own_load.start()
    for copy in loads:
        copy.start()
    cot_load.start()

    barrier = pltpu.get_barrier_semaphore()

    def greet(semaphore, **device):
        pl.semaphore_signal(
            semaphore, inc=1, device_id=device, device_id_type=pl.DeviceIdType.MESH
        )

    greet(barrier, dp=core_partner)
    greet(barrier, row=other)
    for bit in side_bits:
        greet(barrier, dp=across(bit))
    pl.when(col > 0)(lambda: greet(barrier, col=col - 1))
    pl.when(col < last)(lambda: greet(barrier, col=col + 1))
    own_load.wait()
    pl.when(inner)(lambda: pl.semaphore_wait(barrier, 4 + sides))
    pl.when(jnp.logical_not(inner))(lambda: pl.semaphore_wait(barrier, 3 + sides))

    def ag_copy(block, right):
        return remote_copy(
            expert_in.at[block],
            expert_in.at[block],
            (ag_right if right else ag_left).at[block],
            ag_recv.at[block],
            col=col + 1 if right else col - 1,
        )

    def rs_copy(block, part, right):
        neighbour = col + 1 if right else col - 1
        slot = block if right else jnp.where(block == neighbour, last + 1, block)
        return remote_copy(
            send_stage.at[block, part],
            arrived.at[slot, part],
            rs_send.at[block, part],
            rs_recv.at[slot, part],
            col=neighbour,
        )

    def rs_wait(slot, part):
        remote_copy(
            arrived.at[slot, part],
            arrived.at[slot, part],
            rs_send.at[0, part],
            rs_recv.at[slot, part],
            col=jnp.where(col > 0, col - 1, col + 1),
        ).wait_recv()

    pl.when(col < last)(lambda: ag_copy(col, True).start())
    pl.when(col > 0)(lambda: ag_copy(col, False).start())
    pieces = 4
    quarter_size = down_hbm.shape[0] // 4
    piece_size = quarter_size // pieces
    quarter = dp % 4

    def down_place(which, piece):
        first = which * quarter_size + piece * piece_size
        return pl.ds(pl.multiple_of(first, 16), piece_size)

    def down_row(piece):
        place = down_place(quarter, piece)
        return remote_copy(
            down_hbm.at[place],
            weights.at[2, place, half_lanes(row)],
            down_sem.at[piece, 0],
            down_sem.at[piece, 1],
            row=other,
        )

    def down_side(piece):
        there = weights.at[2, down_place(quarter, piece), half_lanes(other)]
        return remote_copy(
            there, there, down_sem.at[piece, 2], down_sem.at[piece, 3], dp=across(1)
        )

    def down_core(piece, n):
        there = weights.at[2, down_place(core + 2 * n, piece), half_lanes(other)]
        return remote_copy(
            there,
            there,
            down_sem.at[piece, 4 + 2 * n],
            down_sem.at[piece, 5 + 2 * n],
            dp=core_partner,
        )

    for piece in range(pieces):
        down_row(piece).start()
    for copy in loads[:4]:
        copy.wait()

    def products(block):
        tokens = expert_in[block]
        table = table_ref[block]
        experts = table.shape[1]
        units = width // experts
        for g in range(2):
            cols = slice(g * half, (g + 1) * half)
            gate = dot(tokens, gate_ref[cols, :], 1, 1)
            up = dot(tokens, up_ref[cols, :], 1, 1)
            lane = lax.broadcasted_iota(jnp.int32, gate.shape, 1)
            first = g * experts // 2
            chosen = jnp.broadcast_to(table[:, first : first + 1], gate.shape)
            for e in range(1, experts // 2):
                chosen = jnp.where(lane >= e * units, table[:, first + e : first + e + 1], chosen)
            sigmoid = 1.0 / (1.0 + jnp.exp(-gate))
            silu = gate * sigmoid
            up = up * chosen
            hidden[block, :, cols] = (silu * up).astype(low)
            gate_grad[block, :, cols] = (up * (sigmoid * (1.0 + gate * (1.0 - sigmoid)))).astype(low)
            up_grad[block, :, cols] = (silu * chosen).astype(low)

    def gradients(block):
        grads = cot_ref[block]
        for g in range(2):
            cols = slice(g * half, (g + 1) * half)
            grad = dot(grads, down_ref[cols, :], 1, 1)
            gate_grad[block, :, cols] = (grad * gate_grad[block, :, cols].astype(full)).astype(low)
            up_grad[block, :, cols] = (grad * up_grad[block, :, cols].astype(full)).astype(low)
        gates_now, ups_now = gate_grad[block], up_grad[block]
        for part in range(2):
            cols = slice(part * half, (part + 1) * half)
            total = dot(gates_now, gate_ref[:, cols]) + dot(ups_now, up_ref[:, cols])
            send_stage[block, part] = total.astype(low)
            pl.when((col == 0) & (block != col))(lambda: rs_copy(block, part, True).start())
            pl.when((col == last) & (block != col))(lambda: rs_copy(block, part, False).start())
        out_part_ref[block] = dot(hidden[block], down_ref[...]).astype(low)

    def block_of(i):
        return jnp.where(i % 2 == 1, col - (i + 1) // 2, col + (i + 1) // 2)

    def pass_on(apart):
        @pl.when(col - apart >= 0)
        def _():
            ag_copy(col - apart, True).wait_recv()
            pl.when(col < last)(lambda: ag_copy(col - apart, True).start())

        @pl.when(col + apart <= last)
        def _():
            ag_copy(col + apart, False).wait_recv()
            pl.when(col > 0)(lambda: ag_copy(col + apart, False).start())

    def present(block):
        return (block >= 0) & (block <= last)

    def near_products(i, carry):
        pl.when(i == 1)(lambda: pass_on(1))
        pl.when(present(block_of(i)))(lambda: products(block_of(i)))
        return carry

    lax.fori_loop(0, 1, near_products, 0)
    for piece in range(pieces):
        down_row(piece).wait_recv()
        down_side(piece).start()
    lax.fori_loop(1, 3, near_products, 0)
    for piece in range(pieces):
        down_side(piece).wait_recv()
        for n in range(2):
            down_core(piece, n).start()
    loads[4].wait()
    cot_load.wait()
    for piece in range(pieces):
        for n in range(2):
            down_core(piece, n).wait_recv()

    def near_gradients(n, carry):
        i = (n + 1) % 3
        pl.when(i == 0)(lambda: pass_on(2))
        pl.when(present(block_of(i)))(lambda: gradients(block_of(i)))
        return carry

    lax.fori_loop(0, 3, near_gradients, 0)

    def far_blocks(i, carry):
        pl.when(i == 5)(lambda: pass_on(3))

        @pl.when(present(block_of(i)))
        def _():
            products(block_of(i))
            gradients(block_of(i))

        return carry

    lax.fori_loop(3, 2 * last + 1, far_blocks, 0)
    out_store.start()
    for piece in range(pieces):
        down_row(piece).wait_send()
        down_side(piece).wait_send()
        for n in range(2):
            down_core(piece, n).wait_send()

    greet(ready.at[0], dp=core_partner)
    greet(ready.at[1], row=other)
    for number, bit in enumerate(side_bits):
        greet(ready.at[2 + number], dp=across(bit))

    def room(which, down, right):
        return weights.at[
            which, pl.ds(down * half, half), pl.ds(right * half, half)
        ]

    def forward(block, part, right):
        rs_wait(block, part)
        send_stage[block, part] = add_low(send_stage[block, part], arrived[block, part])
        rs_copy(block, part, right).start()

    def event(number, part):
        blocks = ((2, 1), (3, 0), (0, 3))[number]
        pl.when(col == 1)(lambda: forward(blocks[0], part, number < 2))
        pl.when(col == 2)(lambda: forward(blocks[1], part, number == 2))

    def core_copy(at):
        if at < 4:
            target = room(at // 2, 0, at % 2)
        else:
            target = room(2, 0, at - 4)
        return remote_copy(
            stage.at[at % 2], target, core_send.at[at], core_recv.at[at], dp=core_partner
        )

    def stage_free(at):
        if at >= 2:
            core_copy(at - 2).wait_send()

    def core_dot(at):
        left = (gate_grad, up_grad)[at // 2]
        right = expert_in[:, :, half_lanes(row if at % 2 else other)].reshape(-1, half)
        stage_free(at)
        stage[at % 2] = dot(
            left[:, :, half_lanes(1 - core)].reshape(-1, half), right, 0, 0
        ).astype(low)
        core_copy(at).start()
        parts[at] = dot(left[:, :, half_lanes(core)].reshape(-1, half), right, 0, 0).astype(low)

    def core_sum(at):
        core_copy(at).wait_recv()
        parts[at] = add_low(parts[at], room(at // 2, 0, at % 2)[...])

    def down_dot_partner():
        left = hidden[:, :, half_lanes(1 - core)].reshape(-1, half)
        for part in range(2):
            lanes = slice(part * half, (part + 1) * half)
            right = cot_ref[:, :, lanes].reshape(-1, half)
            stage_free(4 + part)
            stage[part] = dot(left, right, 0, 0).astype(low)
            core_copy(4 + part).start()

    def down_dot_own():
        left = hidden[:, :, half_lanes(core)].reshape(-1, half)
        for part in range(2):
            lanes = slice(part * half, (part + 1) * half)
            right = cot_ref[:, :, lanes].reshape(-1, half)
            room(2, 1, part)[...] = dot(left, right, 0, 0).astype(low)

    def down_sum():
        for part in range(2):
            core_copy(4 + part).wait_recv()
            room(2, 1, part)[...] = add_low(room(2, 1, part)[...], room(2, 0, part)[...])

    down_out = pltpu.make_async_copy(
        weights.at[2, pl.ds(half, half)], down_half_ref, local_sem.at[0]
    )
    up_out = pltpu.make_async_copy(parts.at[3], up_own_ref, local_sem.at[1])
    up_rest = pltpu.make_async_copy(
        parts.at[2, pl.ds(size, size)], up_other_ref, local_sem.at[2]
    )

    chunks = 4
    chunk_size = half // chunks

    def chunk_rows(chunk):
        return pl.ds(chunk * chunk_size, chunk_size)

    def row_copy(chunk):
        if chunk < chunks:
            source = parts.at[0, chunk_rows(chunk)]
            target = weights.at[0, pl.ds(half + chunk * chunk_size, chunk_size), pl.ds(0, half)]
        else:
            source, target = parts.at[2, pl.ds(0, size)], up_row_ref
        return remote_copy(source, target, row_send.at[chunk], row_recv.at[chunk], row=other)

    def side_room(number, chunk):
        which, right = ((0, 1), (1, 0), (1, 1))[number]
        return weights.at[
            which, pl.ds(half + chunk * chunk_size, chunk_size), pl.ds(right * half, half)
        ]

    def side_copy(chunk, number):
        return remote_copy(
            parts.at[1 - number % 2, chunk_rows(chunk)],
            side_room(number, chunk),
            side_send.at[chunk, number],
            side_recv.at[chunk, number],
            dp=across(side_bits[number]),
        )

    def after_row(chunk):
        copy = row_copy(chunk)
        copy.wait_recv()
        if chunk + 2 <= chunks:
            row_copy(chunk + 2).start()
        copy.wait_send()
        here = chunk_rows(chunk)
        landed = weights.at[0, pl.ds(half + chunk * chunk_size, chunk_size), pl.ds(0, half)]
        parts[1, here] = add_low(parts[1, here], landed[...])
        if chunk == 0 and sides:
            for number in range(sides):
                pl.semaphore_wait(ready.at[2 + number], 1)
        if sides:
            side_copy(chunk, 0).start()

    def final_copies(chunk):
        source = parts.at[1 - sides % 2, chunk_rows(chunk)]
        first = pl.multiple_of(core * half + chunk * chunk_size, 16)
        target = gate_total_ref.at[pl.ds(first, chunk_size)]
        return (
            remote_copy(
                source, target, final_sem.at[chunk, 0], final_sem.at[chunk, 1], dp=core_partner
            ),
            pltpu.make_async_copy(source, target, final_sem.at[chunk, 2]),
        )

    def after_side(chunk):
        here = chunk_rows(chunk)
        for number in range(sides):
            copy = side_copy(chunk, number)
            copy.wait_recv()
            copy.wait_send()
            parts[number % 2, here] = add_low(
                parts[1 - number % 2, here], side_room(number, chunk)[...]
            )
            if number + 1 < sides:
                side_copy(chunk, number + 1).start()
        for copy in final_copies(chunk):
            copy.start()

    def out_copy(right):
        return remote_copy(
            out_part_ref.at[last if right else 0],
            out_first_ref,
            out_sem.at[0],
            out_sem.at[1],
            col=col + 1 if right else col - 1,
        )

    pl.semaphore_wait(ready.at[0], 1)
    core_dot(0)
    event(0, 0)
    core_sum(0)
    pl.semaphore_wait(ready.at[1], 1)
    row_copy(0).start()
    event(0, 1)
    core_dot(1)
    core_sum(1)
    row_copy(1).start()
    event(1, 0)
    core_dot(2)
    pl.when(col == 0)(lambda: out_copy(True).start())
    pl.when(col == last)(lambda: out_copy(False).start())
    after_row(0)
    core_sum(2)
    up_rest.start()
    event(1, 1)
    core_dot(3)
    after_row(1)
    event(2, 0)
    core_sum(3)
    up_out.start()
    after_side(0)
    down_dot_partner()
    event(2, 1)
    after_row(2)
    after_side(1)
    down_dot_own()
    after_row(3)
    down_sum()
    down_out.start()
    after_side(2)

    for part in range(2):
        sum_ref[part] = send_stage[col, part].astype(full)

        @pl.when(col > 0)
        def _():
            rs_wait(col, part)
            sum_ref[part] += arrived[col, part].astype(full)

        @pl.when(col < last)
        def _():
            rs_wait(last + 1, part)
            sum_ref[part] += arrived[last + 1, part].astype(full)

    after_side(3)

    for block in range(last + 1):
        pl.when((block <= col) & (col < last))(lambda: ag_copy(block, True).wait_send())
        pl.when((block >= col) & (col > 0))(lambda: ag_copy(block, False).wait_send())
        for part in range(2):
            pl.when(block > col)(lambda: rs_copy(block, part, True).wait_send())
            pl.when(block < col)(lambda: rs_copy(block, part, False).wait_send())
    for at in range(4, 6):
        core_copy(at).wait_send()
    out_store.wait()
    row_copy(chunks).wait()
    pl.when(col == 0)(lambda: out_copy(True).wait_send())
    pl.when(col == last)(lambda: out_copy(False).wait_send())
    pl.when(inner)(lambda: out_copy(False).wait_recv())
    for copy in (down_out, up_out, up_rest):
        copy.wait()
    for chunk in range(chunks):
        for copy in final_copies(chunk):
            copy.wait()


def experts_call(own, cot, table, *halves):
    rows, width = own.shape
    blocks, half = cot.shape[0], width // 2
    sides = lax.axis_size("dp").bit_length() - 2
    vmem = pl.BlockSpec(memory_space=pltpu.VMEM)
    anywhere = pl.BlockSpec(memory_space=pl.ANY)
    dma = pltpu.SemaphoreType.DMA
    shape = jax.ShapeDtypeStruct
    return pl.pallas_call(
        experts_kernel,
        in_specs=[vmem] + [anywhere] * 7,
        out_specs=[vmem] + [anywhere] * 7,
        out_shape=[
            shape((2, rows, half), full),
            shape((blocks, rows, width), low),
            shape((width, half), low),
            shape((half, half), low),
            shape((half // 2, half), low),
            shape((half // 2, half), low),
            shape((half, width), low),
            shape((rows, width), low),
        ],
        scratch_shapes=[
            pltpu.VMEM((blocks, rows, width), low),
            pltpu.VMEM((blocks, rows, width), low),
            dma((3,)),
            pltpu.VMEM((3, width, width), low),
        ]
        + [pltpu.VMEM((blocks, rows, width), low)] * 4
        + [
            pltpu.VMEM((blocks, 2, rows, half), low),
            pltpu.VMEM((blocks + 1, 2, rows, half), low),
            pltpu.VMEM((4, half, half), low),
            pltpu.VMEM((2, half, half), low),
            dma((5,)),
            dma((4, 8)),
            pltpu.SemaphoreType.REGULAR((2 + max(sides, 1),)),
            dma((blocks,)),
            dma((blocks,)),
            dma((blocks,)),
            dma((blocks + 1, 2)),
            dma((blocks, 2)),
            dma((6,)),
            dma((6,)),
            dma((5,)),
            dma((5,)),
            dma((4, max(sides, 1))),
            dma((4, max(sides, 1))),
            dma((4, 3)),
            dma((3,)),
            dma((2,)),
        ],
        compiler_params=pltpu.CompilerParams(
            collective_id=1, has_side_effects=True, vmem_limit_bytes=60 * 2**20
        ),
        cost_estimate=pl.CostEstimate(
            flops=9 * 2 * blocks * rows * width * width,
            bytes_accessed=12 * width * width,
            transcendentals=blocks * rows * width,
        ),
    )(table, own, cot, *halves)


def prologue_kernel(
    inputs_ref,
    norm_ref,
    mixer_ref,
    lengths_ref,
    theta_ref,
    routes_ref,
    route_gates_ref,
    cot_ref,
    query_hbm,
    keyval_hbm,
    output_hbm,
    gate_hbm,
    up_hbm,
    normed_hbm,
    scale_ref,
    gains_ref,
    key_hbm,
    value_hbm,
    cosine_ref,
    sine_ref,
    start_ref,
    logsum_ref,
    attended_hbm,
    rot_hbm,
    joint_hbm,
    head_output_hbm,
    middle_hbm,
    expert_hbm,
    table_ref,
    cot_all_ref,
    gate_all_ref,
    up_all_ref,
    normed_ref,
    key_ref,
    value_ref,
    attended_ref,
    rot_ref,
    joint_ref,
    head_output_ref,
    middle_ref,
    expert_ref,
    store_sem,
    inputs_all,
    inputs_sem,
    small,
    small_sem,
    projected,
    branch_own,
    branch_stage,
    branch_arrived,
    branch_sem,
    pair_sem,
    joint_line,
    joint_load,
    joint_hop,
    joint_row,
    joint_side,
    joint_core,
    output_line,
    output_load,
    output_hop,
    output_row,
    output_side,
    output_core,
    expert_row,
    expert_side,
    expert_core,
    cot_sem,
    cot_recv,
    cot_send,
):
    row, col, dp = lax.axis_index("row"), lax.axis_index("col"), lax.axis_index("dp")
    cols = lax.axis_size("col")
    last = cols - 1
    core, side, other = dp % 2, (dp // 2) % 2, 1 - row
    quarter = dp % 4
    core_partner, side_partner = dp + 1 - 2 * core, dp + 2 - 4 * side
    tokens, part_width = inputs_ref.shape
    width, rows = 2 * part_width, tokens // 2
    query_block, keyval_block = query_hbm.shape[1], keyval_hbm.shape[1]
    block = query_block + keyval_block
    experts = table_ref.shape[2]

    barrier = pltpu.get_barrier_semaphore()

    def greet(**device):
        pl.semaphore_signal(
            barrier, inc=1, device_id=device, device_id_type=pl.DeviceIdType.MESH
        )

    greet(row=other)
    for apart in range(1, cols):
        greet(col=(col + apart) % cols)
    greet(dp=core_partner)
    greet(dp=side_partner)

    def part_lanes(which):
        return pl.ds(pl.multiple_of(which * part_width, 128), part_width)

    inputs_all[:, part_lanes(row)] = inputs_ref[...]
    small[row, 0:1, :] = norm_ref[...].reshape(1, part_width)
    small[row, 1:2, :] = mixer_ref[...].reshape(1, part_width)
    sequences = lengths_ref.shape[1]
    small[row, 2:3, :] = jnp.zeros((1, part_width), full)
    small[row, 2:3, :sequences] = lengths_ref[...].astype(full)
    small[row, 3:8, :] = jnp.zeros((5, part_width), full)
    inputs_copy = remote_copy(
        inputs_ref,
        inputs_all.at[:, part_lanes(row)],
        inputs_sem.at[0],
        inputs_sem.at[1],
        row=other,
    )
    small_copy = remote_copy(
        small.at[row], small.at[row], small_sem.at[0], small_sem.at[1], row=other
    )

    joint_size, output_size = query_hbm.shape[0] // 4, output_hbm.shape[0] // 4

    def joint_region(r0, b, which):
        return joint_ref.at[
            pl.ds(pl.multiple_of(r0 * part_width + which * joint_size, 16), joint_size),
            pl.ds(pl.multiple_of(b * block, 128), block),
        ]

    def output_region(r0, b, which):
        return head_output_ref.at[
            pl.ds(pl.multiple_of(b * query_block + which * output_size, 16), output_size),
            part_lanes(r0),
        ]

    class Gather:
        def __init__(self, line, pieces, load, hop, row_sems, side_sems, core_sems, region):
            self.line, self.region, self.hop, self.row_sems = line, region, hop, row_sems
            self.side_sems, self.core_sems = side_sems, core_sems
            self.loads = [
                pltpu.make_async_copy(source, target, load.at[n])
                for n, (source, target) in enumerate(pieces)
            ]

        def copy(self, at, right):
            return remote_copy(
                self.line.at[at],
                self.line.at[at],
                self.hop.at[at, 1 if right else 0],
                self.hop.at[at, 2],
                col=col + 1 if right else col - 1,
            )

        def row_copy(self, b):
            return remote_copy(
                self.line.at[2 * other + b],
                self.region(row, b, quarter),
                self.row_sems.at[b, 0],
                self.row_sems.at[b, 1],
                row=other,
            )

        def side_copy(self, n):
            there = self.region((row, other)[n // 2], n % 2, quarter)
            return remote_copy(
                there, there, self.side_sems.at[n, 0], self.side_sems.at[n, 1], dp=side_partner
            )

        def core_copies(self, n):
            result = []
            for part in range(2):
                there = self.region((row, other)[n // 2], n % 2, core + 2 * part)
                result.append(
                    remote_copy(
                        there,
                        there,
                        self.core_sems.at[n, 2 * part],
                        self.core_sems.at[n, 2 * part + 1],
                        dp=core_partner,
                    )
                )
            return result

        def use(self, at):
            for b in range(2):

                @pl.when(at == 2 * row + b)
                def _(b=b):
                    there = self.region(row, b, quarter)
                    there[...] = self.line[at]
                    self.side_copy(b).start()

                @pl.when(at == 2 * other + b)
                def _(b=b):
                    self.row_copy(b).start()

        def load(self):
            for copy in self.loads:
                copy.start()

        def first(self):
            for copy in self.loads:
                copy.wait()
            pl.when(col < last)(lambda: self.copy(col, True).start())
            pl.when(col > 0)(lambda: self.copy(col, False).start())
            self.use(col)

        def step(self, apart):
            @pl.when(col - apart >= 0)
            def _():
                self.copy(col - apart, True).wait_recv()
                pl.when(col < last)(lambda: self.copy(col - apart, True).start())
                self.use(col - apart)

            @pl.when(col + apart <= last)
            def _():
                self.copy(col + apart, False).wait_recv()
                pl.when(col > 0)(lambda: self.copy(col + apart, False).start())
                self.use(col + apart)

        def from_row(self):
            for b in range(2):
                self.row_copy(b).wait_recv()
                self.side_copy(2 + b).start()

        def to_core(self):
            for n in range(4):
                self.side_copy(n).wait_recv()
                for copy in self.core_copies(n):
                    copy.start()

        def ready(self):
            for n in range(4):
                for copy in self.core_copies(n):
                    copy.wait_recv()

        def end(self):
            for at in range(cols):
                pl.when((at <= col) & (col < last))(lambda: self.copy(at, True).wait_send())
                pl.when((at >= col) & (col > 0))(lambda: self.copy(at, False).wait_send())
            for b in range(2):
                self.row_copy(b).wait_send()
            for n in range(4):
                self.side_copy(n).wait_send()
                for copy in self.core_copies(n):
                    copy.wait_send()

    first_joint = pl.ds(pl.multiple_of(quarter * joint_size, 16), joint_size)
    first_output = pl.ds(pl.multiple_of(quarter * output_size, 16), output_size)
    joint = Gather(
        joint_line,
        (
            (query_hbm.at[first_joint], joint_line.at[col, :, pl.ds(0, query_block)]),
            (keyval_hbm.at[first_joint], joint_line.at[col, :, pl.ds(query_block, keyval_block)]),
        ),
        joint_load,
        joint_hop,
        joint_row,
        joint_side,
        joint_core,
        joint_region,
    )
    output = Gather(
        output_line,
        ((output_hbm.at[first_output], output_line.at[col]),),
        output_load,
        output_hop,
        output_row,
        output_side,
        output_core,
        output_region,
    )

    def token_rows(which):
        return pl.ds(pl.multiple_of(which * rows, 16), rows)

    cot_row = remote_copy(
        cot_ref.at[token_rows(other)],
        cot_all_ref.at[col, :, part_lanes(row)],
        cot_sem.at[0],
        cot_sem.at[1],
        row=other,
    )

    def cot_copy(block_at, right):
        return remote_copy(
            cot_all_ref.at[block_at],
            cot_all_ref.at[block_at],
            cot_send.at[block_at, 1 if right else 0],
            cot_recv.at[block_at],
            col=col + 1 if right else col - 1,
        )

    def cot_first():
        cot_row.wait_recv()
        pl.when(col < last)(lambda: cot_copy(col, True).start())
        pl.when(col > 0)(lambda: cot_copy(col, False).start())

    def cot_pass(apart):
        @pl.when(col - apart >= 0)
        def _():
            cot_copy(col - apart, True).wait_recv()
            pl.when(col < last)(lambda: cot_copy(col - apart, True).start())

        @pl.when(col + apart <= last)
        def _():
            cot_copy(col + apart, False).wait_recv()
            pl.when(col > 0)(lambda: cot_copy(col + apart, False).start())

    expert_size = gate_hbm.shape[0] // 4
    weights = (gate_hbm, up_hbm)
    totals = (gate_all_ref, up_all_ref)

    unit_size = expert_size // 2

    def expert_place(which, of_quarter):
        first = of_quarter * expert_size + (which % 2) * unit_size
        return pl.ds(pl.multiple_of(first, 16), unit_size)

    def expert_region(which, of_quarter):
        return totals[which // 2].at[expert_place(which, of_quarter)]

    def expert_row_copy(which):
        return remote_copy(
            weights[which // 2].at[expert_place(which, quarter)],
            expert_region(which, quarter),
            expert_row.at[which, 0],
            expert_row.at[which, 1],
            row=other,
        )

    def expert_side_copy(which):
        there = expert_region(which, quarter)
        return remote_copy(
            there, there, expert_side.at[which, 0], expert_side.at[which, 1], dp=side_partner
        )

    def expert_core_copies(which):
        result = []
        for n in range(2):
            there = expert_region(which, core + 2 * n)
            result.append(
                remote_copy(
                    there,
                    there,
                    expert_core.at[which, 2 * n],
                    expert_core.at[which, 2 * n + 1],
                    dp=core_partner,
                )
            )
        return result

    def expert_after_row(which):
        expert_row_copy(which).wait_recv()
        expert_side_copy(which).start()

    def expert_after_side(which):
        expert_side_copy(which).wait_recv()
        for copy in expert_core_copies(which):
            copy.start()

    store_pairs = (
        (normed_ref, normed_hbm),
        (key_ref, key_hbm),
        (value_ref, value_hbm),
        (attended_ref, attended_hbm),
        (rot_ref, rot_hbm),
        (joint_ref, joint_hbm),
        (head_output_ref, head_output_hbm),
        (middle_ref, middle_hbm),
        (expert_ref, expert_hbm),
    )
    stores = [
        pltpu.make_async_copy(source, target, store_sem.at[n])
        for n, (source, target) in enumerate(store_pairs)
    ]
    joint.load()
    output.load()
    pl.semaphore_wait(barrier, cols + 2)
    joint.first()
    small_copy.start()
    cot_row.start()
    cot_all_ref[col, :, part_lanes(row)] = cot_ref[token_rows(row), :]

    for at in range(cols):
        place = pl.ds(pl.multiple_of(at * tokens + row * rows, 128), rows)
        chosen, gates = routes_ref[:, place], route_gates_ref[:, place]
        expert = lax.broadcasted_iota(jnp.int32, (experts, rows), 0)
        table = jnp.zeros((experts, rows), full)
        for k in range(chosen.shape[0]):
            table += jnp.where(chosen[k : k + 1, :] == expert, gates[k : k + 1, :], 0.0)
        table_ref[at] = jnp.transpose(table)
    joint.step(1)

    small_copy.wait_recv()
    gains_ref[:, :part_width] = small[0, 0:2, :]
    gains_ref[:, part_width:] = small[1, 0:2, :]
    half = col // 2
    lens = small[half, 2:3, :]
    odd = (col % 2).astype(full)
    place = lax.broadcasted_iota(jnp.int32, (tokens, 1), 0).astype(full) + odd * tokens
    begin = jnp.zeros((tokens, 1), full)
    total = lens[:, 0:1]
    for n in range(1, sequences):
        begin = jnp.where(place >= total, total, begin)
        total = total + lens[:, n : n + 1]
    start_ref[...] = begin + (1.0 - odd) * tokens
    cot_first()
    inputs_copy.start()
    angles = (place - begin) * theta_ref[...]
    cosine_ref[...] = jnp.cos(angles)
    sine = jnp.sin(angles)
    lane = lax.broadcasted_iota(jnp.int32, sine.shape, 1)
    sine_ref[...] = jnp.where(lane < head_dim // 2, -sine, sine)

    joint.step(2)
    joint.step(3)
    output.first()
    joint.from_row()
    output.step(1)
    inputs_copy.wait_recv()
    expert_row_copy(0).start()
    expert_row_copy(1).start()

    piece = 64

    def norm_piece(at, carry):
        here = pl.ds(pl.multiple_of(at * piece, piece), piece)
        values = inputs_all[here, :].astype(full)
        scale = lax.rsqrt(jnp.mean(values * values, axis=1, keepdims=True) + epsilon)
        scale_ref[here, :] = scale
        for which in range(2):
            lanes = slice(which * part_width, (which + 1) * part_width)
            normed_ref[here, lanes] = (values[:, lanes] * scale * small[which, 0:1, :]).astype(low)
        return carry

    lax.fori_loop(0, tokens // piece, norm_piece, 0)
    joint.to_core()
    output.step(2)
    cot_pass(1)
    joint.ready()
    stores[0].start()
    stores[5].start()

    own = pl.ds(tokens, tokens)
    key = dot(normed_ref[...], joint_ref[:, query_block:block])
    key_ref[own, :] = (
        key * cosine_ref[...] + pltpu.roll(key, head_dim // 2, 1) * sine_ref[...]
    ).astype(low)
    value_ref[own, :] = dot(normed_ref[...], joint_ref[:, block + query_block :]).astype(low)

    def pair_copies():
        return [
            remote_copy(
                ref.at[own],
                ref.at[pl.ds(0, tokens)],
                pair_sem.at[n, 0],
                pair_sem.at[n, 1],
                col=col + 1 - 2 * (col % 2),
            )
            for n, ref in enumerate((key_ref, value_ref))
        ]

    @pl.when(col % 2 == 0)
    def _():
        for copy in pair_copies():
            copy.start()
        key_ref[:tokens, :] = jnp.zeros((tokens, head_dim), low)
        value_ref[:tokens, :] = jnp.zeros((tokens, head_dim), low)

    for b in range(2):
        lanes = slice(b * query_block, (b + 1) * query_block)
        projected[:, lanes] = dot(
            normed_ref[...], joint_ref[:, b * block : b * block + query_block]
        )
    output.step(3)
    output.from_row()
    expert_after_row(0)
    expert_row_copy(2).start()
    expert_row_copy(3).start()
    output.to_core()

    @pl.when(col % 2 == 1)
    def _():
        for copy in pair_copies():
            copy.wait_recv()

    expert_after_row(1)

    heads = 2 * query_block // head_dim
    tile = rows
    window = key_ref.shape[0] - tile

    def attend(which):
        first = which * tile
        here = pl.ds(pl.multiple_of(first, 16), tile)
        reach = pl.ds(pl.multiple_of(first, 16), window)

        def head_step(head, carry):
            lanes = pl.ds(pl.multiple_of(head * head_dim, head_dim), head_dim)
            pre = projected[here, lanes]
            rot = (
                pre * cosine_ref[here, :] + pltpu.roll(pre, head_dim // 2, 1) * sine_ref[here, :]
            ).astype(low)
            rot_ref[here, lanes] = rot
            scores = dot(rot, key_ref[reach, :], 1, 1) * head_dim ** (-0.5)
            key_place = lax.broadcasted_iota(jnp.int32, scores.shape, 1) + first
            query_place = lax.broadcasted_iota(jnp.int32, scores.shape, 0) + (first + tokens)
            allowed = (key_place <= query_place) & (
                key_place.astype(full) >= start_ref[here, :]
            )
            scores = jnp.where(allowed, scores, -1e30)
            most = jnp.max(scores, axis=1, keepdims=True)
            exponent = jnp.exp(scores - most)
            total = jnp.sum(exponent, axis=1, keepdims=True)
            weights = exponent / total
            attended_ref[here, lanes] = dot(weights.astype(low), value_ref[reach, :]).astype(low)
            lane = lax.broadcasted_iota(jnp.int32, (tile, head_dim), 1)
            logsum_ref[here, :] = jnp.where(
                lane == head, most + jnp.log(total), logsum_ref[here, :]
            )
            return carry

        lax.fori_loop(0, heads, head_step, 0)

    logsum_ref[...] = jnp.zeros_like(logsum_ref)
    attend(other)
    output.ready()

    def branch_copy(part):
        return remote_copy(
            branch_stage.at[part],
            branch_arrived.at[part],
            branch_sem.at[part, 0],
            branch_sem.at[part, 1],
            row=other,
        )

    theirs = attended_ref[token_rows(other), :]
    for part in range(2):
        lanes = slice(part * part_width, (part + 1) * part_width)
        branch_stage[part] = dot(theirs, head_output_ref[:, lanes]).astype(low)
        branch_copy(part).start()
    cot_pass(2)
    expert_after_row(2)
    expert_after_side(0)
    attend(row)
    mine = attended_ref[token_rows(row), :]
    branch_own[...] = dot(mine, head_output_ref[...])
    for n in (1, 2, 3, 4, 6):
        stores[n].start()
    expert_after_row(3)
    expert_after_side(1)
    for part in range(2):
        lanes = slice(part * part_width, (part + 1) * part_width)
        branch_copy(part).wait_recv()
        middle_ref[:, lanes] = (
            inputs_all[token_rows(row), lanes].astype(full)
            + branch_own[:, lanes]
            + branch_arrived[part].astype(full)
        )

    stores[7].start()
    expert_after_side(2)

    def second_piece(at, carry):
        here = pl.ds(pl.multiple_of(at * piece, piece), piece)
        values = middle_ref[here, :]
        scale = lax.rsqrt(jnp.mean(values * values, axis=1, keepdims=True) + epsilon)
        expert_ref[here, :] = (values * scale * gains_ref[1:2, :]).astype(low)
        return carry

    lax.fori_loop(0, rows // piece, second_piece, 0)
    stores[8].start()
    cot_pass(3)
    expert_after_side(3)

    inputs_copy.wait_send()
    small_copy.wait_send()
    joint.end()
    output.end()
    for copy in stores:
        copy.wait()
    for which in range(4):
        expert_row_copy(which).wait_send()
        expert_side_copy(which).wait_send()
        for copy in expert_core_copies(which):
            copy.wait()
    cot_row.wait_send()
    for at in range(cols):
        pl.when((at <= col) & (col < last))(lambda: cot_copy(at, True).wait_send())
        pl.when((at >= col) & (col > 0))(lambda: cot_copy(at, False).wait_send())

    @pl.when(col % 2 == 0)
    def _():
        for copy in pair_copies():
            copy.wait_send()

    for part in range(2):
        branch_copy(part).wait_send()


def prologue_call(
    inputs, norm_gain, mixer_gain, lengths, theta, routes, route_gates, cotangent, query_weight, key_value_matrix,
    output_weight, gate_flat, up_flat, experts,
):
    tokens, part_width = inputs.shape
    cols = lax.axis_size("col")
    width, rows = 2 * part_width, tokens // 2
    query_block, keyval_block = query_weight.shape[1], key_value_matrix.shape[1]
    block = query_block + keyval_block
    hidden = gate_flat.shape[0]
    vmem = pl.BlockSpec(memory_space=pltpu.VMEM)
    anywhere = pl.BlockSpec(memory_space=pl.ANY)
    dma = pltpu.SemaphoreType.DMA
    shape = jax.ShapeDtypeStruct
    return pl.pallas_call(
        prologue_kernel,
        in_specs=[vmem] * 8 + [anywhere] * 5,
        out_specs=[anywhere]
        + [vmem] * 2
        + [anywhere] * 2
        + [vmem] * 4
        + [anywhere] * 6
        + [vmem] * 2
        + [anywhere] * 2,
        out_shape=[
            shape((tokens, width), low),
            shape((tokens, 1), full),
            shape((2, width), full),
            shape((2 * tokens, head_dim), low),
            shape((2 * tokens, head_dim), low),
            shape((tokens, head_dim), full),
            shape((tokens, head_dim), full),
            shape((tokens, 1), full),
            shape((tokens, head_dim), full),
            shape((tokens, 2 * query_block), low),
            shape((tokens, 2 * query_block), low),
            shape((width, 2 * block), low),
            shape((2 * query_block, width), low),
            shape((rows, width), full),
            shape((rows, width), low),
            shape((cols, rows, experts), full),
            shape((cols, rows, width), low),
            shape((hidden, part_width), low),
            shape((hidden, part_width), low),
        ],
        scratch_shapes=[
            pltpu.VMEM((tokens, width), low),
            pltpu.VMEM((2 * tokens, head_dim), low),
            pltpu.VMEM((2 * tokens, head_dim), low),
            pltpu.VMEM((tokens, 2 * query_block), low),
            pltpu.VMEM((tokens, 2 * query_block), low),
            pltpu.VMEM((width, 2 * block), low),
            pltpu.VMEM((2 * query_block, width), low),
            pltpu.VMEM((rows, width), full),
            pltpu.VMEM((rows, width), low),
            dma((9,)),
            pltpu.VMEM((tokens, width), low),
            dma((2,)),
            pltpu.VMEM((2, 8, part_width), full),
            dma((2,)),
            pltpu.VMEM((tokens, 2 * query_block), full),
            pltpu.VMEM((rows, width), full),
            pltpu.VMEM((2, rows, part_width), low),
            pltpu.VMEM((2, rows, part_width), low),
            dma((2, 2)),
            dma((2, 2)),
            pltpu.VMEM((cols, part_width // 4, block), low),
            dma((2,)),
            dma((cols, 3)),
            dma((2, 2)),
            dma((4, 2)),
            dma((4, 4)),
            pltpu.VMEM((cols, query_block // 4, part_width), low),
            dma((1,)),
            dma((cols, 3)),
            dma((2, 2)),
            dma((4, 2)),
            dma((4, 4)),
            dma((4, 2)),
            dma((4, 2)),
            dma((4, 4)),
            dma((2,)),
            dma((cols,)),
            dma((cols, 2)),
        ],
        compiler_params=pltpu.CompilerParams(
            collective_id=3, has_side_effects=True, vmem_limit_bytes=60 * 2**20
        ),
        cost_estimate=pl.CostEstimate(
            flops=5 * 10**9, bytes_accessed=30 * 10**6, transcendentals=3 * 10**6
        ),
    )(
        inputs, norm_gain, mixer_gain, lengths, theta, routes, route_gates, cotangent, query_weight, key_value_matrix,
        output_weight, gate_flat, up_flat,
    )


def finish_kernel(
    middle_ref,
    gains_ref,
    scale_ref,
    start_ref,
    logsum_ref,
    sum_hbm,
    inputs_hbm,
    attended_hbm,
    rot_hbm,
    key_hbm,
    value_hbm,
    cosine_hbm,
    sine_hbm,
    head_output_hbm,
    joint_hbm,
    normed_hbm,
    cot_all_hbm,
    out_part_hbm,
    up_own_hbm,
    up_row_hbm,
    up_other_hbm,
    down_half_hbm,
    out_first_hbm,
    outputs_ref,
    input_grad_ref,
    gain_sums_ref,
    output_total_ref,
    query_total_ref,
    keyval_total_ref,
    up_total_ref,
    down_total_ref,
    further,
    work,
    cot_ref,
    inputs_ref,
    attended_ref,
    rot_ref,
    key_ref,
    value_ref,
    cosine_ref,
    sine_ref,
    head_output_ref,
    joint_ref,
    normed_ref,
    loads,
    branch,
    branch_sem,
    out_stack,
    out_arrived,
    out_send,
    out_recv,
    own_out_sem,
    grad_heads,
    joint_grad,
    key_grad,
    value_grad,
    pair_stage,
    pair_arrived,
    pair_sem,
    normed_arrived,
    normed_sem,
    inner_stage,
    inner_arrived,
    inner_sem,
    sums,
    sums_arrived,
    sums_sem,
    item_mine,
    item_other,
    item_side,
    item_row,
    item_last,
    item_sem,
    item_load_sem,
    wo_parts,
    wo_core,
    wo_row,
    wo_stack,
    wo_arrived,
    wo_side,
    wo_sem,
    wo_send,
    wo_recv,
    wq_parts,
    wq_core,
    wq_row,
    wq_stack,
    wq_arrived,
    wq_side,
    wq_sem,
    wq_side_sem,
    wq_send,
    wq_recv,
    wk_parts,
    wk_core,
    wk_row,
    wk_stack,
    wk_arrived,
    wk_side,
    wk_sem,
    wk_send,
    wk_recv,
):
    row, col, dp = lax.axis_index("row"), lax.axis_index("col"), lax.axis_index("dp")
    cols, dps = lax.axis_size("col"), lax.axis_size("dp")
    core, side, other = dp % 2, (dp // 2) % 2, 1 - row
    core_partner = dp + 1 - 2 * core
    bits = list(range(1, dps.bit_length() - 1))
    sides = len(bits)

    def across(bit):
        on = (dp // (1 << bit)) % 2
        return dp + (1 << bit) * (1 - 2 * on)

    rows, width = middle_ref.shape
    tokens, part_width = inputs_ref.shape
    heads = attended_ref.shape[1] // head_dim
    per_block = heads // 2
    query_lanes, key_lanes = query_total_ref.shape[1], keyval_total_ref.shape[1]
    block_lanes = query_lanes + key_lanes

    def part_lanes(which):
        return pl.ds(pl.multiple_of(which * part_width, 128), part_width)

    size = item_mine.shape[1]
    items = item_mine.shape[0]
    load_pairs = [
        (sum_hbm, work),
        (cot_all_hbm.at[col], cot_ref),
        (out_part_hbm, out_stack),
        (head_output_hbm, head_output_ref),
        (attended_hbm, attended_ref),
        (rot_hbm, rot_ref),
        (key_hbm, key_ref),
        (value_hbm, value_ref),
        (cosine_hbm, cosine_ref),
        (sine_hbm, sine_ref),
        (joint_hbm, joint_ref),
        (normed_hbm, normed_ref),
        (inputs_hbm, inputs_ref),
    ]
    load = [
        pltpu.make_async_copy(source, target, loads.at[n])
        for n, (source, target) in enumerate(load_pairs)
    ]

    def item_loads(at):
        chunk = at % 2
        place = pl.ds(chunk * size, size)
        if at < 2:
            sources = (up_own_hbm.at[place], (up_row_hbm, up_other_hbm)[chunk])
        else:
            sources = [down_half_hbm.at[place, part_lanes(which)] for which in (row, other)]
        return [
            pltpu.make_async_copy(source, target.at[at], item_load_sem.at[at, number])
            for number, (source, target) in enumerate(zip(sources, (item_mine, item_other)))
        ]

    inner_col = (col > 0) & (col < cols - 1)
    first_load = pltpu.make_async_copy(
        out_first_hbm, out_arrived.at[(cols - 1) * (2 - col) % cols], loads.at[13]
    )
    for copy in load[:3]:
        copy.start()
    pl.when(inner_col)(lambda: first_load.start())
    for copy in item_loads(1) + load[3:]:
        copy.start()
    for at in (0, 2, 3):
        for copy in item_loads(at):
            copy.start()

    barrier = pltpu.get_barrier_semaphore()

    def greet(**device):
        pl.semaphore_signal(
            barrier, inc=1, device_id=device, device_id_type=pl.DeviceIdType.MESH
        )

    plane = [
        dict(row=(row + there // cols) % 2, col=(col + there % cols) % cols)
        for there in range(1, 2 * cols)
    ]
    copies = [dict(dp=(dp + apart) % dps) for apart in range(1, dps)]
    for device in plane + copies:
        greet(**device)

    for copy in load[:2]:
        copy.wait()
    piece = 64
    halves = [slice(h * part_width, (h + 1) * part_width) for h in range(2)]

    def norm_piece(at, mixer_sum):
        place = pl.ds(pl.multiple_of(at * piece, piece), piece)
        middle = middle_ref[place, :]
        second = jnp.concatenate([work[h, place, :] for h in range(2)], axis=1)
        scale = lax.rsqrt(jnp.mean(middle * middle, axis=1, keepdims=True) + epsilon)
        weighted = gains_ref[1:2, :] * second
        inner = jnp.sum(weighted * middle, axis=1, keepdims=True)
        grad = (
            cot_ref[place, :].astype(full)
            + scale * weighted
            - middle * (scale * scale * scale) * (inner / width)
        )
        branch[row, place, :] = grad.astype(low)
        return mixer_sum + jnp.sum(second * middle * scale, axis=0, keepdims=True)

    def branch_part(part):
        place = pl.ds(part * (rows // 2), rows // 2)
        return remote_copy(
            branch.at[row, place],
            branch.at[row, place],
            branch_sem.at[2 * part],
            branch_sem.at[2 * part + 1],
            row=other,
        )

    steps = rows // piece
    mixer_sum = lax.fori_loop(0, steps // 2, norm_piece, jnp.zeros((1, width), full))
    pl.semaphore_wait(barrier, len(plane) + len(copies))
    branch_part(0).start()
    mixer_sum = lax.fori_loop(steps // 2, steps, norm_piece, mixer_sum)
    branch_part(1).start()
    quarter_lanes = sums.shape[2]
    parts = width // quarter_lanes
    for n in range(parts):
        sums[0, parts + n : parts + n + 1, :] = mixer_sum[
            :, n * quarter_lanes : (n + 1) * quarter_lanes
        ]

    outs = ColSum(out_stack, out_arrived, out_send, out_recv, col, cols, range(cols))
    load[2].wait()
    pl.when(inner_col)(lambda: first_load.wait())
    outs.step(2, placed=True)


    half_size = size // 2

    def side_rows(which):
        return pl.ds(pl.multiple_of(which * half_size, 16), half_size)

    def item_first_copies(at):
        if at == 0:
            pairs = [(item_mine.at[at], item_side.at[at])]
        else:
            there = side_rows(1 - side)
            pairs = [
                (item_mine.at[at, there], item_side.at[at, side_rows(0)]),
                (item_other.at[at, there], item_side.at[at, side_rows(1)]),
            ]
        return [
            remote_copy(
                source, target, item_sem.at[at, 2 * n], item_sem.at[at, 2 * n + 1], dp=across(1)
            )
            for n, (source, target) in enumerate(pairs)
        ]

    def item_start(at):
        for copy in item_loads(at):
            copy.wait()
        if at == 0:
            item_mine[0] = add_low(item_mine[0], item_other[0])
        for copy in item_first_copies(at):
            copy.start()

    def item_row_copy(at):
        return remote_copy(
            item_other.at[at, side_rows(side)],
            item_row.at[at],
            item_sem.at[at, 4],
            item_sem.at[at, 5],
            row=other,
        )

    def item_to_row(at):
        for copy in item_first_copies(at):
            copy.wait_recv()
        here = side_rows(side)
        item_other[at, here] = add_low(item_other[at, here], item_side[at, side_rows(1)])
        item_row_copy(at).start()
        item_mine[at, here] = add_low(item_mine[at, here], item_side[at, side_rows(0)])

    def item_extent(at):
        return pl.ds(0, size) if at == 0 else side_rows(side)

    def item_further_copy(at, number):
        extent = pl.ds(0, size if at == 0 else half_size)
        return remote_copy(
            item_mine.at[at, item_extent(at)],
            further.at[at, number - 1, extent],
            item_sem.at[at, 4 + 2 * number],
            item_sem.at[at, 5 + 2 * number],
            dp=across(bits[number]),
        )

    def item_further(at):
        extent = pl.ds(0, size if at == 0 else half_size)
        for number in range(1, sides):
            copy = item_further_copy(at, number)
            copy.start()
            copy.wait()
            landed = pltpu.make_async_copy(
                further.at[at, number - 1, extent],
                item_side.at[at, extent],
                item_load_sem.at[at, 0],
            )
            landed.start()
            landed.wait()
            here = item_extent(at)
            item_mine[at, here] = add_low(item_mine[at, here], item_side[at, extent])

    def item_last_copy(at):
        return remote_copy(
            item_mine.at[at, side_rows(side)],
            item_last.at[at],
            item_sem.at[at, 4 + 2 * sides],
            item_sem.at[at, 5 + 2 * sides],
            dp=across(1),
        )

    def item_after_row(at):
        item_row_copy(at).wait_recv()
        here = side_rows(side)
        for copy in item_first_copies(at):
            copy.wait_send()
        item_mine[at, here] = add_low(item_mine[at, here], item_row[at])
        item_further(at)
        item_last_copy(at).start()

    def item_core_copies(at):
        which, chunk = at // 2, at % 2
        total = (up_total_ref, down_total_ref)[which]
        first = core * part_width + chunk * size
        if at == 0:
            pieces = [(item_mine.at[0], pl.ds(pl.multiple_of(first, 16), size))]
        else:
            pieces = [
                (source, pl.ds(pl.multiple_of(first + of_side * half_size, 16), half_size))
                for source, of_side in (
                    (item_mine.at[at, side_rows(side)], side),
                    (item_last.at[at], 1 - side),
                )
            ]
        result = []
        for n, (source, place) in enumerate(pieces):
            base = 6 + 2 * sides + 3 * n
            result.append(
                remote_copy(
                    source,
                    total.at[place],
                    item_sem.at[at, base],
                    item_sem.at[at, base + 1],
                    dp=core_partner,
                )
            )
            result.append(
                pltpu.make_async_copy(source, total.at[place], item_sem.at[at, base + 2])
            )
        return result

    def item_finish(at):
        if at == 0:
            for copy in item_first_copies(at):
                copy.wait()
            item_mine[at] = add_low(item_mine[at], item_side[at])
            item_further(at)
        else:
            item_last_copy(at).wait_recv()
        for copy in item_core_copies(at):
            copy.start()

    def item_end(at):
        if at > 0:
            item_row_copy(at).wait_send()
            item_last_copy(at).wait_send()
        for copy in item_core_copies(at):
            copy.wait()

    item_start(1)
    for copy in load[3:]:
        copy.wait()

    for part in range(2):
        branch_part(part).wait_recv()
    item_to_row(1)
    item_start(0)
    outs.step(3)
    branch_all = branch[...].reshape(tokens, width)
    half_lanes = heads * head_dim // 2
    for part in range(2):
        lanes = slice(part * half_lanes, (part + 1) * half_lanes)
        grad_heads[:, lanes] = dot(branch_all, head_output_ref[lanes, :], 1, 1).astype(low)

    wo_size = wo_parts.shape[2]
    for b in range(2):
        lanes = slice(b * half_lanes, (b + 1) * half_lanes)
        value = dot(attended_ref[:, lanes], branch_all, 0, 0).astype(low)
        for part in range(2):
            wo_parts[b, part] = value[part * wo_size : (part + 1) * wo_size, :]

    def wo_core_copy(b):
        return remote_copy(
            wo_parts.at[b, 1 - core],
            wo_core.at[b],
            wo_sem.at[0, b],
            wo_sem.at[1, b],
            dp=core_partner,
        )

    for b in range(2):
        wo_core_copy(b).start()

    key_grad[...] = jnp.zeros_like(key_grad)
    value_grad[...] = jnp.zeros_like(value_grad)
    tile = tokens // 2
    window = key_ref.shape[0] - tile

    def head_step(head, carry):
        here = pl.ds(pl.multiple_of(head * head_dim, head_dim), head_dim)
        there = pl.ds(
            pl.multiple_of((head + head // per_block) * head_dim, head_dim), head_dim
        )
        for at in range(tokens // tile):
            first = at * tile
            rot = rot_ref[first : first + tile, here]
            grad = grad_heads[first : first + tile, here]
            keys = key_ref[first : first + window, :]
            values = value_ref[first : first + window, :]
            scores = dot(rot, keys, 1, 1) * head_dim ** (-0.5)
            place = lax.broadcasted_iota(jnp.int32, scores.shape, 1) + first
            query = lax.broadcasted_iota(jnp.int32, scores.shape, 0) + (first + tokens)
            allowed = (place <= query) & (place.astype(full) >= start_ref[first : first + tile, :])
            scores = jnp.where(allowed, scores, -1e30)
            lane = lax.broadcasted_iota(jnp.int32, (tile, head_dim), 1)
            logsum = jnp.sum(
                jnp.where(lane == head, logsum_ref[first : first + tile, :], 0.0),
                axis=1,
                keepdims=True,
            )
            probs = jnp.exp(scores - logsum)
            prob_grad = dot(grad, values, 1, 1)
            inner = jnp.sum(probs * prob_grad, axis=1, keepdims=True)
            score_grad = (probs * (prob_grad - inner) * head_dim ** (-0.5)).astype(low)
            rot_grad = dot(score_grad, keys)
            joint_grad[first : first + tile, there] = (
                rot_grad * cosine_ref[first : first + tile, :]
                - pltpu.roll(rot_grad, head_dim // 2, 1) * sine_ref[first : first + tile, :]
            ).astype(low)
            key_grad[first : first + window, :] += dot(score_grad, rot, 0, 0)
            value_grad[first : first + window, :] += dot(probs.astype(low), grad, 0, 0)
        return carry

    wa_size = part_width // 2
    chunk_rows = wa_size // 2

    class Lanes:
        def __init__(self, parts, core_room, row_room, sems, stretches, chunks):
            self.parts, self.core_room, self.row_room, self.sems = parts, core_room, row_room, sems
            self.stretches, self.chunks = stretches, chunks

        def core_copy(self, r0):
            return remote_copy(
                self.parts.at[r0, 1 - core],
                self.core_room.at[r0],
                self.sems.at[0, r0],
                self.sems.at[1, r0],
                dp=core_partner,
            )

        def dot(self, r0, which):
            first = pl.multiple_of(r0 * part_width + which * wa_size, 128)
            left = normed_ref[:, pl.ds(first, wa_size)]
            right = [joint_grad[:, lanes] for lanes in self.stretches]
            right = right[0] if len(right) == 1 else jnp.concatenate(right, axis=1)
            self.parts[r0, which] = dot(left, right, 0, 0).astype(low)

        def first(self):
            for r0 in (other, row):
                self.dot(r0, 1 - core)
                self.core_copy(r0).start()
            for r0 in (other, row):
                self.dot(r0, core)

        def row_copy(self, chunk):
            count = wa_size // self.chunks
            return remote_copy(
                self.parts.at[other, core, pl.ds(chunk * count, count)],
                self.row_room.at[chunk],
                self.sems.at[2, chunk],
                self.sems.at[3, chunk],
                row=other,
            )

        def to_row(self):
            self.core_copy(other).wait_recv()
            self.parts[other, core] = add_low(self.parts[other, core], self.core_room[other])
            for chunk in range(self.chunks):
                self.row_copy(chunk).start()
            self.core_copy(row).wait_recv()
            self.parts[row, core] = add_low(self.parts[row, core], self.core_room[row])

        def end(self):
            for r0 in range(2):
                self.core_copy(r0).wait_send()
            for chunk in range(self.chunks):
                self.row_copy(chunk).wait_send()

    stretches = [
        slice(b * block_lanes, b * block_lanes + query_lanes) for b in range(2)
    ]
    key_stretch = slice(query_lanes, block_lanes)
    value_stretch = slice(block_lanes + query_lanes, 2 * block_lanes)
    wq = [
        Lanes(
            wq_parts.at[b], wq_core.at[b], wq_row.at[b], wq_sem.at[b], [stretches[b]], 2
        )
        for b in range(2)
    ]
    wk = Lanes(wk_parts, wk_core, wk_row, wk_sem, [key_stretch, value_stretch], 1)

    def wo_row_copy(b):
        return remote_copy(
            wo_parts.at[b, core, :, part_lanes(other)],
            wo_row.at[b],
            wo_sem.at[2, b],
            wo_sem.at[3, b],
            row=other,
        )

    lax.fori_loop(0, 1, head_step, 0)
    for b in range(2):
        wo_core_copy(b).wait_recv()
        wo_parts[b, core] = add_low(wo_parts[b, core], wo_core[b])
        wo_row_copy(b).start()
    lax.fori_loop(1, per_block, head_step, 0)
    item_start(2)
    wq[0].first()
    lax.fori_loop(per_block, per_block + 1, head_step, 0)
    wq[0].to_row()
    lax.fori_loop(per_block + 1, heads, head_step, 0)
    pair_stage[:, :head_dim] = key_grad[:tokens, :].astype(low)
    pair_stage[:, head_dim:] = value_grad[:tokens, :].astype(low)
    odd = col % 2 == 1

    def pair_copy():
        return remote_copy(
            pair_stage, pair_arrived, pair_sem.at[0], pair_sem.at[1], col=col + 1 - 2 * (col % 2)
        )

    pl.when(odd)(lambda: pair_copy().start())
    wq[1].first()
    item_start(3)

    def over_col(lanes, stacks, arrived, send, recv, chunk, blocks):
        return ColSum(
            stacks.at[chunk], arrived.at[chunk], send.at[chunk], recv.at[chunk], col, cols, blocks
        )

    wq_total = [
        [
            over_col(
                wq[b], wq_stack.at[b], wq_arrived.at[b], wq_send.at[b], wq_recv.at[b], c, (b, 2 + b)
            )
            for c in range(2)
        ]
        for b in range(2)
    ]

    def wq_to_col(b):
        for chunk in range(2):
            wq[b].row_copy(chunk).wait_recv()
            place = pl.ds(chunk * chunk_rows, chunk_rows)
            wq_stack[b, chunk, row] = wq_parts[b, row, core, place]
            wq_stack[b, chunk, other] = wq_row[b, chunk]
            wq_total[b][chunk].step(1)

    def wq_step(b, number):
        for chunk in range(2):
            wq_total[b][chunk].step(number)

    wq[1].to_row()
    item_finish(0)
    wo_total = ColSum(wo_stack, wo_arrived, wo_send, wo_recv, col, cols, range(cols))
    for b in range(2):
        wo_row_copy(b).wait_recv()
        wo_stack[2 * row + b] = wo_parts[b, core, :, part_lanes(row)]
        wo_stack[2 * other + b] = wo_row[b]
    wo_total.step(1)
    wq_to_col(0)

    @pl.when(jnp.logical_not(odd))
    def _():
        pair_copy().wait_recv()
        key_grad[tokens:, :] += pair_arrived[:, :head_dim].astype(full)
        value_grad[tokens:, :] += pair_arrived[:, head_dim:].astype(full)

    key_total = key_grad[tokens:, :]
    joint_grad[:, key_stretch] = (
        key_total * cosine_ref[...] - pltpu.roll(key_total, head_dim // 2, 1) * sine_ref[...]
    ).astype(low)
    joint_grad[:, value_stretch] = value_grad[tokens:, :].astype(low)
    wk.first()

    normed_own = work

    def normed_dot(which):
        return dot(joint_grad[...], joint_ref[part_lanes(which), :], 1, 1)

    def normed_sums(which, value):
        product = value * normed_ref[:, part_lanes(which)].astype(full)
        gain = gains_ref[0:1, part_lanes(which)]
        total = jnp.sum(product, axis=0, keepdims=True) / gain
        for n in range(parts // 2):
            sums[0, pl.ds(which * (parts // 2) + n, 1), :] = total[
                :, n * quarter_lanes : (n + 1) * quarter_lanes
            ]
        return jnp.sum(product, axis=1, keepdims=True)

    wk.to_row()
    item_to_row(2)
    value = normed_dot(other)
    grad_heads[...] = value.astype(low)
    normed_copy = remote_copy(
        grad_heads, normed_arrived, normed_sem.at[0], normed_sem.at[1], row=other
    )
    inner = normed_sums(other, value)
    value = normed_dot(row)
    inner += normed_sums(row, value)
    for h in range(2):
        normed_own[h] = value[h * rows : (h + 1) * rows]
    inner_stage[...] = jnp.transpose(jnp.broadcast_to(inner, (tokens, head_dim)))[:8, :]
    inner_copy = remote_copy(
        inner_stage, inner_arrived, inner_sem.at[0], inner_sem.at[1], row=other
    )
    inner_copy.start()

    def sums_copies(stage):
        base = 0 if stage == 0 else len(plane)
        return [
            remote_copy(
                sums.at[stage],
                sums_arrived.at[base + n],
                sums_sem.at[base + n, 0],
                sums_sem.at[base + n, 1],
                **device,
            )
            for n, device in enumerate((plane, copies)[stage])
        ]

    def sums_start(stage):
        for copy in sums_copies(stage):
            copy.start()

    def sums_finish(stage):
        base = 0 if stage == 0 else len(plane)
        total = sums[stage]
        for n, copy in enumerate(sums_copies(stage)):
            copy.wait_recv()
            total += sums_arrived[base + n]
        sums[stage + 1] = total

    sums_start(0)
    wq_to_col(1)
    wq_step(0, 2)
    wk_total = ColSum(wk_stack, wk_arrived, wk_send, wk_recv, col, cols, range(cols))
    wk.row_copy(0).wait_recv()
    for b in range(2):
        lanes = slice(b * key_lanes, (b + 1) * key_lanes)
        wk_stack[2 * row + b] = wk_parts[row, core, :, lanes]
        wk_stack[2 * other + b] = wk_row[0, :, lanes]
    wk_total.step(1)
    item_to_row(3)
    wq_step(1, 2)
    wq_step(0, 3)
    wk_total.step(2)
    wo_total.step(2)
    normed_copy.start()
    sums_finish(0)
    sums_start(1)
    wq_step(1, 3)
    wk_total.step(3)
    item_after_row(1)
    wo_total.step(3)
    item_after_row(2)

    class Owned:
        def __init__(self, side_room, sems, targets):
            self.room, self.sems, self.targets = side_room, sems, targets

        def copy(self, number):
            return remote_copy(
                self.room.at[number % 2],
                self.room.at[2 + number],
                self.sems.at[2 * number],
                self.sems.at[2 * number + 1],
                dp=across(bits[number]),
            )

        def start(self, value):
            self.room[0] = value.astype(low)
            if sides:
                self.copy(0).start()

        def core_copies(self):
            result = []
            base, value = 2 * sides, self.room.at[sides % 2]
            return (
                remote_copy(
                    value,
                    self.targets,
                    self.sems.at[base],
                    self.sems.at[base + 1],
                    dp=core_partner,
                ),
                pltpu.make_async_copy(value, self.targets, self.sems.at[base + 2]),
            )

        def finish(self):
            for number in range(sides):
                self.copy(number).wait()
                self.room[1 - number % 2] = add_low(
                    self.room[number % 2], self.room[2 + number]
                )
                if number + 1 < sides:
                    self.copy(number + 1).start()
            for copy in self.core_copies():
                copy.start()

        def end(self):
            for copy in self.core_copies():
                copy.wait()

    def own_place(chunk, count):
        return pl.ds(pl.multiple_of(core * wa_size + chunk * count, 16), count)

    wk_owned = Owned(wk_side, wk_sem.at[4], keyval_total_ref.at[own_place(0, wa_size)])
    wq_owned = [
        Owned(wq_side.at[c], wq_side_sem.at[c], query_total_ref.at[own_place(c, chunk_rows)])
        for c in range(2)
    ]
    wo_owned = Owned(
        wo_side,
        wo_sem.at[4],
        output_total_ref.at[pl.ds(pl.multiple_of(core * wo_size, 16), wo_size)],
    )
    for b in range(2):
        for c in range(2):
            wq_total[b][c].total(wq_owned[c].start)
    wk_total.total(wk_owned.start)

    def own_tokens(value):
        out_stack[col] = (middle_ref[...] + value).astype(low)

    outs.total(own_tokens)

    def outputs_copy():
        place = pl.ds(pl.multiple_of(row * rows, rows), rows)
        return remote_copy(
            out_stack.at[col, :, part_lanes(other)],
            outputs_ref.at[place],
            own_out_sem.at[0],
            own_out_sem.at[1],
            row=other,
        )

    outputs_copy().start()
    outputs_ref[pl.ds(pl.multiple_of(row * rows, rows), rows), :] = out_stack[
        col, :, part_lanes(row)
    ]
    item_after_row(3)
    wo_total.total(wo_owned.start)
    item_finish(1)
    for c in range(2):
        wq_owned[c].finish()
    wk_owned.finish()
    wo_owned.finish()
    item_finish(2)
    sums_finish(1)
    for n in range(parts // 2):
        place = pl.ds(row * (parts // 2) + n, 1)
        lanes = slice(n * quarter_lanes, (n + 1) * quarter_lanes)
        gain_sums_ref[0:1, lanes] = sums[2, place, :]
        place = pl.ds(parts + row * (parts // 2) + n, 1)
        gain_sums_ref[1:2, lanes] = sums[2, place, :]
    item_finish(3)

    normed_copy.wait_recv()
    inner_copy.wait_recv()
    both = inner_stage[...] + inner_arrived[...]
    inner = jnp.transpose(jnp.concatenate([both] * (head_dim // 8), axis=0))[:, 0:1]
    for h in range(2):
        place = slice(h * rows, (h + 1) * rows)
        scale = scale_ref[place, :]
        normed_grad = normed_own[h] + normed_arrived[place, :].astype(full)
        input_grad_ref[place, :] = (
            branch[h, :, part_lanes(row)].astype(full)
            + scale * (gains_ref[0:1, part_lanes(row)] * normed_grad)
            - inputs_ref[place, :].astype(full) * (scale * scale) * (inner[place, :] / width)
        ).astype(low)

    for part in range(2):
        branch_part(part).wait_send()
    pl.when(odd)(lambda: pair_copy().wait_send())
    for b in range(2):
        wo_core_copy(b).wait_send()
        wo_row_copy(b).wait_send()
    for lanes in wq + [wk]:
        lanes.end()
    normed_copy.wait_send()
    inner_copy.wait_send()
    outputs_copy().wait()
    for stage in range(2):
        for copy in sums_copies(stage):
            copy.wait_send()
    outs.end(first=False)
    for total in [wo_total, wk_total] + wq_total[0] + wq_total[1]:
        total.end()
    for owned in wq_owned + [wk_owned, wo_owned]:
        owned.end()
    for at in range(items):
        item_end(at)


def finish_call(
    middle, gains, scale, start, logsum, sums, inputs, attended, rot, keys, values, cosine, sine,
    head_output, joint_weight, normed, cot_all, out_part, up_own, up_row, up_other, down_half, out_first,
    query_block, both_block,
):
    rows, width = middle.shape
    tokens, part_width = inputs.shape
    cols, dps = lax.axis_size("col"), lax.axis_size("dp")
    sides = dps.bit_length() - 2
    heads_width = attended.shape[1]
    reach = keys.shape[0]
    vmem = pl.BlockSpec(memory_space=pltpu.VMEM)
    anywhere = pl.BlockSpec(memory_space=pl.ANY)
    dma = pltpu.SemaphoreType.DMA
    hidden = 2 * up_own.shape[0]
    size = part_width // 2
    items = 4
    key_block = both_block - query_block
    wo_size, wa_size = query_block // 2, part_width // 2
    chunk = wa_size // 2
    shape = jax.ShapeDtypeStruct
    sums_count = 2 * cols - 1 + dps - 1
    return pl.pallas_call(
        finish_kernel,
        in_specs=[vmem] * 5 + [anywhere] * 18,
        out_specs=[vmem] * 6 + [anywhere] * 3,
        out_shape=[
            shape((tokens, part_width), low),
            shape((tokens, part_width), low),
            shape((2, part_width), full),
            shape((query_block, part_width), low),
            shape((part_width, query_block), low),
            shape((part_width, key_block), low),
            shape((hidden, part_width), low),
            shape((hidden, part_width), low),
            shape((items, max(sides - 1, 1), size, part_width), low),
        ],
        scratch_shapes=[
            pltpu.VMEM((2, rows, part_width), full),
            pltpu.VMEM((rows, width), low),
            pltpu.VMEM((tokens, part_width), low),
            pltpu.VMEM((tokens, heads_width), low),
            pltpu.VMEM((tokens, heads_width), low),
            pltpu.VMEM((reach, head_dim), low),
            pltpu.VMEM((reach, head_dim), low),
            pltpu.VMEM((tokens, head_dim), full),
            pltpu.VMEM((tokens, head_dim), full),
            pltpu.VMEM((heads_width, width), low),
            pltpu.VMEM((width, 2 * both_block), low),
            pltpu.VMEM((tokens, width), low),
            dma((14,)),
            pltpu.VMEM((2, rows, width), low),
            dma((4,)),
            pltpu.VMEM((cols, rows, width), low),
            pltpu.VMEM((cols + 1, rows, width), low),
            dma((cols,)),
            dma((cols + 1,)),
            dma((2,)),
            pltpu.VMEM((tokens, heads_width), low),
            pltpu.VMEM((tokens, 2 * both_block), low),
            pltpu.VMEM((reach, head_dim), full),
            pltpu.VMEM((reach, head_dim), full),
            pltpu.VMEM((tokens, 2 * head_dim), low),
            pltpu.VMEM((tokens, 2 * head_dim), low),
            dma((2,)),
            pltpu.VMEM((tokens, part_width), low),
            dma((2,)),
            pltpu.VMEM((8, tokens), full),
            pltpu.VMEM((8, tokens), full),
            dma((2,)),
            pltpu.VMEM((3, 8, width // 4), full),
            pltpu.VMEM((sums_count, 8, width // 4), full),
            dma((sums_count, 2)),
            pltpu.VMEM((items, size, part_width), low),
            pltpu.VMEM((items, size, part_width), low),
            pltpu.VMEM((items, size, part_width), low),
            pltpu.VMEM((items, size // 2, part_width), low),
            pltpu.VMEM((items, size // 2, part_width), low),
            dma((items, 12 + 2 * sides)),
            dma((items, 2)),
            pltpu.VMEM((2, 2, wo_size, width), low),
            pltpu.VMEM((2, wo_size, width), low),
            pltpu.VMEM((2, wo_size, part_width), low),
            pltpu.VMEM((cols, wo_size, part_width), low),
            pltpu.VMEM((cols + 1, wo_size, part_width), low),
            pltpu.VMEM((2 + sides, wo_size, part_width), low),
            dma((5, 3 + 2 * sides)),
            dma((cols,)),
            dma((cols + 1,)),
            pltpu.VMEM((2, 2, 2, wa_size, query_block), low),
            pltpu.VMEM((2, 2, wa_size, query_block), low),
            pltpu.VMEM((2, 2, chunk, query_block), low),
            pltpu.VMEM((2, 2, 2, chunk, query_block), low),
            pltpu.VMEM((2, 2, 3, chunk, query_block), low),
            pltpu.VMEM((2, 2 + sides, chunk, query_block), low),
            dma((2, 4, 2)),
            dma((2, 3 + 2 * sides)),
            dma((2, 2, 2)),
            dma((2, 2, 3)),
            pltpu.VMEM((2, 2, wa_size, 2 * key_block), low),
            pltpu.VMEM((2, wa_size, 2 * key_block), low),
            pltpu.VMEM((1, wa_size, 2 * key_block), low),
            pltpu.VMEM((cols, wa_size, key_block), low),
            pltpu.VMEM((cols + 1, wa_size, key_block), low),
            pltpu.VMEM((2 + sides, wa_size, key_block), low),
            dma((5, 3 + 2 * sides)),
            dma((cols,)),
            dma((cols + 1,)),
        ],
        compiler_params=pltpu.CompilerParams(
            collective_id=2, has_side_effects=True, vmem_limit_bytes=63 * 2**20
        ),
        cost_estimate=pl.CostEstimate(
            flops=10 * 10**9, bytes_accessed=40 * 10**6, transcendentals=4 * 10**6
        ),
    )(
        middle, gains, scale, start, logsum, sums, inputs, attended, rot, keys, values, cosine, sine,
        head_output, joint_weight, normed, cot_all, out_part, up_own, up_row, up_other, down_half, out_first,
    )


def results_kernel(*refs):
    count = len(refs) // 2
    for source, target in zip(refs[:count], refs[count:]):
        target[...] = source[...].astype(target.dtype)


def results_call(arrays, kinds, steps):
    specs = [
        pl.BlockSpec((array.shape[0] // steps, array.shape[1]), lambda i: (i, 0))
        for array in arrays
    ]
    return pl.pallas_call(
        results_kernel,
        grid=(steps,),
        in_specs=specs,
        out_specs=specs,
        out_shape=[
            jax.ShapeDtypeStruct(array.shape, kind) for array, kind in zip(arrays, kinds)
        ],
        compiler_params=pltpu.CompilerParams(vmem_limit_bytes=60 * 2**20),
    )(*arrays)


def shards(
    inputs,
    norm_gain,
    query_weight,
    key_value_matrix,
    output_weight,
    mixer_gain,
    gate_weight,
    up_weight,
    down_weight,
    lengths,
    routes,
    route_gates,
    cotangent,
):
    row, col = lax.axis_index("row"), lax.axis_index("col")
    part_width = inputs.shape[1]
    experts, _, units = gate_weight.shape
    hidden_width = experts * units
    query_block, keyval_block = query_weight.shape[1], key_value_matrix.shape[1]
    theta = rope_base ** (-np.arange(0, head_dim, 2, dtype=np.float64) / head_dim)
    theta = np.concatenate([theta, theta])[None, :].astype(np.float32)
    gate_flat = gate_weight.swapaxes(1, 2).reshape(hidden_width, part_width)
    up_flat = up_weight.swapaxes(1, 2).reshape(hidden_width, part_width)
    down_flat = down_weight.reshape(hidden_width, part_width)
    (
        normed,
        first_scale,
        gains,
        keys,
        values,
        cosine,
        sine,
        start,
        logsum,
        attended,
        rot,
        joint_weight,
        head_output,
        middle,
        expert_own,
        tables,
        cot_all,
        gate_other,
        up_other_half,
    ) = prologue_call(
        inputs, norm_gain, mixer_gain, lengths, theta, routes.T, route_gates.T, cotangent, query_weight, key_value_matrix,
        output_weight, gate_flat, up_flat, experts,
    )
    (
        second_grad,
        out_part,
        gate_total,
        up_own,
        up_row,
        up_other,
        down_half,
        out_first,
    ) = experts_call(
        expert_own, cot_all, tables, gate_flat, gate_other, up_flat, up_other_half, down_flat
    )

    both_block = query_block + keyval_block
    (
        outputs,
        input_grad,
        gain_sums,
        output_total,
        query_total,
        keyval_total,
        up_total,
        down_total,
        _,
    ) = finish_call(
        middle, gains, first_scale, start, logsum, second_grad, inputs, attended, rot, keys, values,
        cosine, sine, head_output, joint_weight, normed, cot_all, out_part,
        up_own, up_row, up_other, down_half, out_first, query_block, both_block,
    )
    norm_total, mixer_total = gain_sums[0], gain_sums[1]

    arrays = [gate_total, up_total, down_total, query_total, keyval_total, output_total]
    (
        gate_total,
        up_total,
        down_total,
        query_total,
        keyval_total,
        output_total,
        outputs,
        input_grad,
    ) = results_call(arrays + [outputs, input_grad], [full] * 6 + [low] * 2, 4)

    def by_expert(flat):
        return flat.reshape(experts, units, part_width)

    gate_total = by_expert(gate_total).swapaxes(1, 2)
    up_total = by_expert(up_total).swapaxes(1, 2)
    down_total = by_expert(down_total)
    return (
        outputs,
        input_grad,
        norm_total,
        query_total,
        keyval_total,
        output_total,
        mixer_total,
        gate_total,
        up_total,
        down_total,
    )


def solution(mesh):
    return jax.shard_map(
        shards,
        mesh=mesh,
        in_specs=(
            P(("dp", "col"), "row"),
            P("row"),
            P("row", "col"),
            P("row", "col"),
            P("col", "row"),
            P("row"),
            P(None, "row", "col"),
            P(None, "row", "col"),
            P(None, "col", "row"),
            P(("dp", "row"), None),
            P("dp", None),
            P("dp", None),
            P(("dp", "col"), "row"),
        ),
        out_specs=(
            P(("dp", "col"), "row"),
            P(("dp", "col"), "row"),
            P("row"),
            P("row", "col"),
            P("row", "col"),
            P("col", "row"),
            P("row"),
            P(None, "row", "col"),
            P(None, "row", "col"),
            P(None, "col", "row"),
        ),
        check_vma=False,
    )
```
